32 devices in a mesh: groups: 2 (over y), gx: 8 (over z, x), gy: 2 (over core).
Axes of the slice: x: 2, y: 2, z: 4, core: 2. Of those that a mesh axis runs over, the one named last changes fastest.
Arguments:
- activations: bfloat16 [16, 16384], P(('groups', 'gy'), 'gx'), parts along dimension 0, may hold values from -60 to 60
- w_query: bfloat16 [16384, 8192], P('gx', 'gy'), may hold values from -0.046875 to 0.046875
- key_weight: bfloat16 [16384, 512], P('gx', 'gy'), may hold values from -0.046875 to 0.046875
- value_weight: bfloat16 [16384, 512], P('gx', 'gy'), may hold values from -0.046875 to 0.046875
- w_out: bfloat16 [8192, 16384], P('gy', 'gx'), may hold values from -0.5 to 0.5
- k_cache: bfloat16 [16, 4, 2048, 128], P(('groups', 'gx'), 'gy'), parts along dimension 0, may hold values from -800 to 800
- value_cache: bfloat16 [16, 4, 2048, 128], P(('groups', 'gx'), 'gy'), parts along dimension 0, may hold values from -6 to 6
- lengths: int32 [16], P(('groups', 'gx')), parts along dimension 0, may hold values from 1 to 2048, as said below
Outputs:
- attn_out: bfloat16 [16, 16384], P(('groups', 'gy'), 'gx'), parts along dimension 0
The draws below stay inside these ranges and needn't reach their ends.
There are 2 independent parts, one for each index of `groups`. The reference program is written for one: setup_inputs(seed, part) draws one part's arguments, and reference() takes and returns one part's arrays. A program takes and returns all parts, laid end to end along the dimension named above; an argument that names none is the same for every part. Nothing has to cross between parts.
Inputs may be any that keep to these rules, and one draw needn't show every extreme that they name: `lengths`: one row of every part has exactly 2048 cached tokens.
All inputs are finite; a program needn't handle non-finite values.
Results may differ from the reference program's by a relative error of at most 0.011.
Values may be sent and summed in bfloat16 or wider, within the bound.
No kernel may reach another device: no remote copies, remote signals or barrier semaphores. Data moves between devices by JAX's collectives and lax.ppermute only.
A program may use at most 128 MiB of HBM per device.

```python
import math
import jax
import jax.numpy as jnp
from jax import lax

MODEL_WIDTH = 16384
QUERY_HEADS = 64
KEY_VALUE_HEADS = 4
HEAD_SIZE = 128
CACHE_SLOTS = 2048
BATCH_ROWS = 8


def length_draw(key):
    key = jax.random.fold_in(key, 17)
    first_halfpart, second_halfpart = jax.random.split(key)
    drawn = jax.random.randint(first_halfpart, (BATCH_ROWS,), 1, CACHE_SLOTS + 1)
    longest = jax.random.randint(second_halfpart, (), 0, BATCH_ROWS)
    return jnp.where(jnp.arange(BATCH_ROWS) == longest, CACHE_SLOTS, drawn).astype(jnp.int32)


def draw_lengths(key, part):
    return length_draw(key)


def draw_k_cache(key, part):
    key = jax.random.fold_in(key, 3)
    split_parts = jax.random.split(key, 1)
    array_shape = (BATCH_ROWS, KEY_VALUE_HEADS, CACHE_SLOTS, HEAD_SIZE)
    base = jnp.clip(jax.random.normal(split_parts[0], array_shape, jnp.float32), -5.0, 5.0)
    return base.astype(jnp.bfloat16)


def draw_activations(key, part):
    key = jax.random.fold_in(key, 5)
    split_parts = jax.random.split(key, 3)
    row_scale = jnp.exp(jax.random.uniform(split_parts[0], (BATCH_ROWS, 1), jnp.float32, math.log(0.3), math.log(3.0)))
    col_scale = jnp.exp(jax.random.uniform(split_parts[1], (1, MODEL_WIDTH), jnp.float32, math.log(0.3), math.log(3.0)))
    ramp = 0.5 + jnp.arange(MODEL_WIDTH, dtype=jnp.float32)[None, :] / MODEL_WIDTH
    noise = jnp.clip(jax.random.normal(split_parts[2], (BATCH_ROWS, MODEL_WIDTH), jnp.float32), -4.0, 4.0)
    return (row_scale * col_scale * ramp * noise).astype(jnp.bfloat16)


def level_of(own_key, dims, pieces, low, largest):
    def one(axis_at, blocks):
        draws = jax.random.uniform(jax.random.fold_in(jax.random.fold_in(own_key, 6), axis_at), (blocks,), jnp.float32, low / len(pieces), largest / len(pieces))
        return jnp.repeat(jnp.exp(draws), dims[axis_at] // blocks).reshape((-1,) + (1,) * (len(dims) - axis_at - 1))

    level = one(*pieces[0])
    for cut in pieces[1:]:
        level = level * one(*cut)
    return level


def normal_values(key, dims, deviation, bound, shards=(), kind=jnp.bfloat16):
    loudness = level_of(key, dims, shards, -0.22, 0.18) if shards else 1.0
    result = jax.random.normal(key, dims, jnp.float32) * deviation * loudness
    return jnp.minimum(jnp.maximum(result, -bound), bound).astype(kind)


def setup_inputs(seed: int = 0, part: int = 0) -> dict:
    key_list = jax.random.split(jax.random.key(seed), 9)
    part_splits = jax.random.split(jax.random.fold_in(key_list[8], part), 9)
    return {
        "activations": draw_activations(jax.random.fold_in(jax.random.fold_in(key_list[8], part), 71), part),
        "w_query": normal_values(key_list[1], (MODEL_WIDTH, QUERY_HEADS * HEAD_SIZE), MODEL_WIDTH ** -0.5, 0.046875, ((0, 8), (1, 2))),
        "key_weight": normal_values(key_list[2], (MODEL_WIDTH, KEY_VALUE_HEADS * HEAD_SIZE), MODEL_WIDTH ** -0.5, 0.046875, ((0, 8), (1, 2))),
        "value_weight": normal_values(key_list[3], (MODEL_WIDTH, KEY_VALUE_HEADS * HEAD_SIZE), MODEL_WIDTH ** -0.5, 0.046875, ((0, 8), (1, 2))),
        "w_out": normal_values(key_list[4], (QUERY_HEADS * HEAD_SIZE, MODEL_WIDTH), HEAD_SIZE ** -0.5, 0.5, ((0, 2), (1, 8))),
        "k_cache": draw_k_cache(jax.random.fold_in(jax.random.fold_in(key_list[8], part), 71), part),
        "value_cache": normal_values(part_splits[6], (BATCH_ROWS, KEY_VALUE_HEADS, CACHE_SLOTS, HEAD_SIZE), 1.0, 6.0, ((0, 8), (1, 2))),
        "lengths": draw_lengths(jax.random.fold_in(jax.random.fold_in(key_list[8], part), 71), part),
    }


def apply_rotary(vectors, token_positions):
    half = vectors.shape[-1] // 2
    frequency = jnp.power(jnp.float32(500000.0), -2.0 * jnp.arange(half, dtype=jnp.float32) / vectors.shape[-1])
    angle = token_positions[:, None, None] * frequency
    cosine = jnp.cos(angle)
    sine = jnp.sin(angle)
    first_halfpart = vectors[..., :half]
    second_halfpart = vectors[..., half:]
    return jnp.concatenate([first_halfpart * cosine - second_halfpart * sine, second_halfpart * cosine + first_halfpart * sine], axis=-1)

def reference(activations, w_query, key_weight, value_weight, w_out, k_cache, value_cache, lengths):
    batch_indices = activations.shape[0]
    widened = activations.astype(jnp.float32)
    scale_rows = lax.rsqrt(lax.optimization_barrier(jnp.sum(widened * widened, axis=1)) / MODEL_WIDTH + 1e-05)
    query_rows = jnp.dot(activations, w_query, preferred_element_type=jnp.float32) * scale_rows[:, None]
    fresh_keys = jnp.dot(activations, key_weight, preferred_element_type=jnp.float32) * scale_rows[:, None]
    fresh_values = jnp.dot(activations, value_weight, preferred_element_type=jnp.float32) * scale_rows[:, None]
    token_positions = lengths.astype(jnp.float32)
    query_rows = apply_rotary(query_rows.reshape(batch_indices, QUERY_HEADS, HEAD_SIZE), token_positions).astype(jnp.bfloat16)
    fresh_keys = apply_rotary(fresh_keys.reshape(batch_indices, KEY_VALUE_HEADS, HEAD_SIZE), token_positions).astype(jnp.bfloat16)
    fresh_values = fresh_values.reshape(batch_indices, KEY_VALUE_HEADS, HEAD_SIZE).astype(jnp.bfloat16)
    grouped_queries = query_rows.reshape(batch_indices, KEY_VALUE_HEADS, QUERY_HEADS // KEY_VALUE_HEADS, HEAD_SIZE).astype(jnp.float32)
    factor = 1.0 / math.sqrt(HEAD_SIZE)
    scores = jnp.einsum('rhgd,rhtd->rhgt', grouped_queries, k_cache.astype(jnp.float32)) * factor
    own = jnp.einsum('rhgd,rhd->rhg', grouped_queries, fresh_keys.astype(jnp.float32)) * factor
    live = jnp.arange(CACHE_SLOTS)[None, None, None, :] < lengths[:, None, None, None]
    scores = jnp.where(live, scores, -jnp.inf)
    top = jnp.maximum(lax.optimization_barrier(jnp.max(scores, axis=-1)), own)
    exponent = jnp.exp(scores - top[..., None])
    own_exp = jnp.exp(own - top)
    total = lax.optimization_barrier(jnp.sum(exponent, axis=-1)) + own_exp
    weights = (exponent / total[..., None]).astype(jnp.bfloat16)
    own_weight = (own_exp / total).astype(jnp.bfloat16)
    heads = jnp.einsum('rhgt,rhtd->rhgd', weights.astype(jnp.float32), value_cache.astype(jnp.float32))
    heads = heads + own_weight.astype(jnp.float32)[..., None] * fresh_values.astype(jnp.float32)[:, :, None, :]
    heads = heads.astype(jnp.bfloat16).reshape(batch_indices, QUERY_HEADS * HEAD_SIZE)
    return jnp.dot(heads, w_out, preferred_element_type=jnp.float32).astype(jnp.bfloat16)
```

```python
import math

import jax
import jax.numpy as jnp
from jax import lax
from jax.sharding import PartitionSpec as P

MODEL_WIDTH = 16384
HEAD_SIZE = 128


def apply_rotary(vectors, token_positions):
    half = vectors.shape[-1] // 2
    frequency = jnp.power(
        jnp.float32(500000.0), -2.0 * jnp.arange(half, dtype=jnp.float32) / vectors.shape[-1]
    )
    angle = token_positions[:, None, None] * frequency
    cosine = jnp.cos(angle)
    sine = jnp.sin(angle)
    first_halfpart = vectors[..., :half]
    second_halfpart = vectors[..., half:]
    return jnp.concatenate(
        [
            first_halfpart * cosine - second_halfpart * sine,
            second_halfpart * cosine + first_halfpart * sine,
        ],
        axis=-1,
    )


def softmax_weights(scores, own):
    top = jnp.maximum(jnp.max(scores, axis=-1), own)
    exponent = jnp.exp(scores - top[..., None])
    own_exp = jnp.exp(own - top)
    total = jnp.sum(exponent, axis=-1) + own_exp
    return (
        (exponent / total[..., None]).astype(jnp.bfloat16),
        (own_exp / total).astype(jnp.bfloat16),
    )


def swap_pair(block):
    return lax.ppermute(block, "gy", [(0, 1), (1, 0)])


def to_owner(pieces, devices):
    total = pieces[0]
    moved = [
        lax.ppermute(pieces[k], "gx", [(i, (i + k) % devices) for i in range(devices)])
        for k in range(1, devices)
    ]
    for piece in moved:
        total = total + piece
    return total


def body(devices, activations, w_query, key_weight, value_weight, w_out, k_cache, value_cache, lengths):
    gx = lax.axis_index("gx")
    gy = lax.axis_index("gy")
    other = swap_pair(activations)
    rows_all = jnp.where(
        gy == 0,
        jnp.concatenate([activations, other], axis=0),
        jnp.concatenate([other, activations], axis=0),
    )
    widened = rows_all.astype(jnp.float32)
    squares = jnp.sum(widened * widened, axis=1, keepdims=True)
    rows_dev = k_cache.shape[0]
    kv_local = k_cache.shape[1]
    cache_len = k_cache.shape[2]
    query_width = w_query.shape[1]
    key_width = key_weight.shape[1]
    partial = jnp.concatenate(
        [
            jnp.dot(rows_all, w_query, preferred_element_type=jnp.float32),
            jnp.dot(rows_all, key_weight, preferred_element_type=jnp.float32),
            jnp.dot(rows_all, value_weight, preferred_element_type=jnp.float32),
            jnp.broadcast_to(squares, (squares.shape[0], HEAD_SIZE)),
        ],
        axis=1,
    )
    pieces = [
        lax.dynamic_slice_in_dim(partial, lax.rem(gx + k, devices) * rows_dev, rows_dev, 0)
        for k in range(devices)
    ]
    owned = to_owner(pieces, devices)
    scale_rows = lax.rsqrt(owned[:, -1] / MODEL_WIDTH + 1e-05)
    owned = owned[:, :-HEAD_SIZE] * scale_rows[:, None]
    token_positions = lengths.astype(jnp.float32)
    query_rows = apply_rotary(
        owned[:, :query_width].reshape(rows_dev, -1, HEAD_SIZE), token_positions
    ).astype(jnp.bfloat16)
    fresh_keys = apply_rotary(
        owned[:, query_width : query_width + key_width].reshape(rows_dev, kv_local, HEAD_SIZE),
        token_positions,
    ).astype(jnp.bfloat16)
    fresh_values = (
        owned[:, query_width + key_width :]
        .reshape(rows_dev, kv_local, HEAD_SIZE)
        .astype(jnp.bfloat16)
    )
    grouped_queries = query_rows.reshape(rows_dev, kv_local, -1, HEAD_SIZE)
    factor = 1.0 / math.sqrt(HEAD_SIZE)
    own = (
        jnp.einsum("rhgd,rhd->rhg", grouped_queries, fresh_keys, preferred_element_type=jnp.float32)
        * factor
    )
    slots = jnp.arange(cache_len)[None, None, None, :] < lengths[:, None, None, None]
    scores = (
        jnp.einsum("rhgd,rhtd->rhgt", grouped_queries, k_cache, preferred_element_type=jnp.float32)
        * factor
    )
    scores = jnp.where(slots, scores, -jnp.inf)
    weights, own_weight = softmax_weights(scores, own)
    heads = jnp.einsum("rhgt,rhtd->rhgd", weights, value_cache, preferred_element_type=jnp.float32)
    heads = (
        heads
        + own_weight.astype(jnp.float32)[..., None]
        * fresh_values.astype(jnp.float32)[:, :, None, :]
    )
    heads = heads.astype(jnp.bfloat16).reshape(rows_dev, query_width)
    arrived = [heads] + [
        lax.ppermute(heads, "gx", [(i, (i - k) % devices) for i in range(devices)])
        for k in range(1, devices)
    ]
    turned = jnp.concatenate(arrived, axis=0)
    partial_out = jnp.dot(turned, w_out, preferred_element_type=jnp.float32)
    partial_out = jnp.roll(partial_out, gx * rows_dev, axis=0)
    half = partial_out.shape[0] // 2
    mine = lax.dynamic_slice_in_dim(partial_out, gy * half, half, 0)
    theirs = lax.dynamic_slice_in_dim(partial_out, (1 - gy) * half, half, 0)
    return (mine + swap_pair(theirs)).astype(jnp.bfloat16)


def solution(mesh):
    placed = (
        P(("groups", "gy"), "gx"),
        P("gx", "gy"),
        P("gx", "gy"),
        P("gx", "gy"),
        P("gy", "gx"),
        P(("groups", "gx"), "gy", None, None),
        P(("groups", "gx"), "gy", None, None),
        P(("groups", "gx")),
    )

    def run(*args):
        return body(mesh.shape["gx"], *args)

    return jax.shard_map(
        run, mesh=mesh, in_specs=placed, out_specs=P(("groups", "gy"), "gx"), check_vma=False
    )
```

```python
import math

import jax
import jax.numpy as jnp
from jax import lax
from jax.sharding import PartitionSpec as P

MODEL_WIDTH = 16384
HEAD_SIZE = 128


def apply_rotary(vectors, token_positions):
    half = vectors.shape[-1] // 2
    frequency = jnp.power(
        jnp.float32(500000.0), -2.0 * jnp.arange(half, dtype=jnp.float32) / vectors.shape[-1]
    )
    angle = token_positions[:, None, None] * frequency
    cosine = jnp.cos(angle)
    sine = jnp.sin(angle)
    first_halfpart = vectors[..., :half]
    second_halfpart = vectors[..., half:]
    return jnp.concatenate(
        [
            first_halfpart * cosine - second_halfpart * sine,
            second_halfpart * cosine + first_halfpart * sine,
        ],
        axis=-1,
    )


def softmax_weights(scores, own):
    top = jnp.maximum(jnp.max(scores, axis=-1), own)
    exponent = jnp.exp(scores - top[..., None])
    own_exp = jnp.exp(own - top)
    total = jnp.sum(exponent, axis=-1) + own_exp
    return (
        (exponent / total[..., None]).astype(jnp.bfloat16),
        (own_exp / total).astype(jnp.bfloat16),
    )


def swap_pair(block):
    return lax.ppermute(block, "gy", [(0, 1), (1, 0)])


def body(devices, activations, w_query, key_weight, value_weight, w_out, k_cache, value_cache, lengths):
    gy = lax.axis_index("gy")
    other = swap_pair(activations)
    rows_all = jnp.where(
        gy == 0,
        jnp.concatenate([activations, other], axis=0),
        jnp.concatenate([other, activations], axis=0),
    )
    widened = rows_all.astype(jnp.float32)
    squares = jnp.sum(widened * widened, axis=1, keepdims=True)
    rows_dev = k_cache.shape[0]
    kv_local = k_cache.shape[1]
    cache_len = k_cache.shape[2]
    query_width = w_query.shape[1]
    key_width = key_weight.shape[1]
    partial = jnp.concatenate(
        [
            jnp.dot(rows_all, w_query, preferred_element_type=jnp.float32),
            jnp.dot(rows_all, key_weight, preferred_element_type=jnp.float32),
            jnp.dot(rows_all, value_weight, preferred_element_type=jnp.float32),
            jnp.broadcast_to(squares, (squares.shape[0], HEAD_SIZE)),
        ],
        axis=1,
    )
    blocks = partial.reshape(devices, rows_dev, partial.shape[1])
    owned = jnp.sum(lax.all_to_all(blocks, "gx", 0, 0, tiled=True), axis=0)
    scale_rows = lax.rsqrt(owned[:, -1] / MODEL_WIDTH + 1e-05)
    owned = owned[:, :-HEAD_SIZE] * scale_rows[:, None]
    token_positions = lengths.astype(jnp.float32)
    query_rows = apply_rotary(
        owned[:, :query_width].reshape(rows_dev, -1, HEAD_SIZE), token_positions
    ).astype(jnp.bfloat16)
    fresh_keys = apply_rotary(
        owned[:, query_width : query_width + key_width].reshape(rows_dev, kv_local, HEAD_SIZE),
        token_positions,
    ).astype(jnp.bfloat16)
    fresh_values = (
        owned[:, query_width + key_width :]
        .reshape(rows_dev, kv_local, HEAD_SIZE)
        .astype(jnp.bfloat16)
    )
    grouped_queries = query_rows.reshape(rows_dev, kv_local, -1, HEAD_SIZE)
    factor = 1.0 / math.sqrt(HEAD_SIZE)
    own = (
        jnp.einsum("rhgd,rhd->rhg", grouped_queries, fresh_keys, preferred_element_type=jnp.float32)
        * factor
    )
    slots = jnp.arange(cache_len)[None, None, None, :] < lengths[:, None, None, None]
    scores = (
        jnp.einsum("rhgd,rhtd->rhgt", grouped_queries, k_cache, preferred_element_type=jnp.float32)
        * factor
    )
    scores = jnp.where(slots, scores, -jnp.inf)
    weights, own_weight = softmax_weights(scores, own)
    heads = jnp.einsum("rhgt,rhtd->rhgd", weights, value_cache, preferred_element_type=jnp.float32)
    heads = (
        heads
        + own_weight.astype(jnp.float32)[..., None]
        * fresh_values.astype(jnp.float32)[:, :, None, :]
    )
    heads = heads.astype(jnp.bfloat16).reshape(rows_dev, query_width)
    copies = jnp.broadcast_to(heads, (devices, rows_dev, query_width))
    everyone = lax.all_to_all(copies, "gx", 0, 0, tiled=True).reshape(-1, query_width)
    partial_out = jnp.dot(everyone, w_out, preferred_element_type=jnp.float32)
    half = partial_out.shape[0] // 2
    mine = lax.dynamic_slice_in_dim(partial_out, gy * half, half, 0)
    theirs = lax.dynamic_slice_in_dim(partial_out, (1 - gy) * half, half, 0)
    return (mine + swap_pair(theirs)).astype(jnp.bfloat16)


def solution(mesh):
    placed = (
        P(("groups", "gy"), "gx"),
        P("gx", "gy"),
        P("gx", "gy"),
        P("gx", "gy"),
        P("gy", "gx"),
        P(("groups", "gx"), "gy", None, None),
        P(("groups", "gx"), "gy", None, None),
        P(("groups", "gx")),
    )

    def run(*args):
        return body(mesh.shape["gx"], *args)

    return jax.shard_map(
        run, mesh=mesh, in_specs=placed, out_specs=P(("groups", "gy"), "gx"), check_vma=False
    )
```

```python
import functools
import math

import jax
import jax.numpy as jnp
from jax import lax
from jax.experimental import pallas as pl
from jax.experimental.pallas import tpu as pltpu
from jax.sharding import PartitionSpec as P

MODEL_WIDTH = 16384
LANES = 128
HEAD_SIZE = 128
CHUNK = 256
STAGE_VMEM = 8 * 2**20
PROJECT_VMEM = 50 * 2**20
OUTPUT_VMEM = 50 * 2**20


def bit_reverse(value, bits):
    turned = 0
    for bit in range(bits):
        turned = turned | (((value >> bit) & 1) << (bits - 1 - bit))
    return turned


def stage_kernel(*refs):
    count = len(refs) // 2
    sems = refs[-1]
    copies = [
        pltpu.make_async_copy(refs[i], refs[count + i], sems.at[i]) for i in range(count)
    ]
    for copy in copies:
        copy.start()
    for copy in copies:
        copy.wait()


def stage(*arrays):
    return pl.pallas_call(
        stage_kernel,
        out_shape=tuple(jax.ShapeDtypeStruct(a.shape, a.dtype) for a in arrays),
        in_specs=[pl.BlockSpec(memory_space=pltpu.HBM)] * len(arrays),
        out_specs=tuple(pl.BlockSpec(memory_space=pltpu.VMEM) for _ in arrays),
        scratch_shapes=[pltpu.SemaphoreType.DMA((len(arrays),))],
        compiler_params=pltpu.CompilerParams(vmem_limit_bytes=STAGE_VMEM),
        cost_estimate=pl.CostEstimate(
            flops=0, bytes_accessed=sum(2 * a.size for a in arrays), transcendentals=0
        ),
        name="stage",
    )(*arrays)


def project_kernel(
    bits, rows_ref, other_ref, wq_hbm, wk, wv, send_ref, keep_ref, wq, rows, out, sems
):
    depth = wq.shape[0]
    chunk = min(CHUNK, depth)
    steps = depth // chunk
    copies = []
    for step in range(steps):
        part = pl.ds(step * chunk, chunk)
        copies.append(pltpu.make_async_copy(wq_hbm.at[part], wq.at[part], sems.at[step]))
        copies[-1].start()

    slots = rows.shape[0]
    half = slots // 2
    turn = bit_reverse(lax.axis_index("gx"), bits)
    gy = lax.axis_index("gy")
    for ref, side in ((rows_ref, gy), (other_ref, 1 - gy)):
        block = ref[...].astype(jnp.float32)
        for t in range(half):
            slot = bit_reverse(t, bits) ^ turn ^ side
            rows[pl.ds(slot, 1), :] = block[t : t + 1, :]
    wide = rows[...]
    squares = jnp.sum(wide * wide, axis=1, keepdims=True)
    narrow = wide.astype(jnp.bfloat16)

    fresh = [jnp.dot(narrow, w[...], preferred_element_type=jnp.float32) for w in (wk, wv)]
    sums = None
    for step, copy in enumerate(copies):
        part = slice(step * chunk, (step + 1) * chunk)
        copy.wait()
        term = jnp.dot(narrow[:, part], wq[part, :], preferred_element_type=jnp.float32)
        sums = term if sums is None else sums + term

    total = out.shape[1]
    blocks = []
    for part in (sums, *fresh):
        blocks += [part[:, i : i + LANES] for i in range(0, part.shape[1], LANES)]
    blocks.append(jnp.broadcast_to(squares, (slots, LANES)))
    blocks += [jnp.zeros((slots, LANES), jnp.float32)] * (total - len(blocks))
    flat = out.reshape(slots * total, LANES)
    for i, block in enumerate(blocks):
        flat[pl.ds(i, slots, stride=total), :] = block
    keep_ref[...] = out[:half]
    send_ref[...] = out[half:]


def project(rows, other, w_query, key_weight, value_weight, slots):
    bits = slots.bit_length() - 1
    depth, query_width = w_query.shape
    kv_width = key_weight.shape[1]
    used = (query_width + 2 * kv_width) // LANES + 1
    total = -(-used // 8) * 8
    piece = jax.ShapeDtypeStruct((slots // 2, total, LANES), jnp.float32)
    whole = pl.BlockSpec(memory_space=pltpu.VMEM)
    stay = pl.BlockSpec(memory_space=pltpu.HBM)
    steps = depth // min(CHUNK, depth)
    return pl.pallas_call(
        functools.partial(project_kernel, bits),
        out_shape=(piece, piece),
        in_specs=[whole, whole, stay, whole, whole],
        out_specs=(whole, whole),
        scratch_shapes=[
            pltpu.VMEM(w_query.shape, jnp.bfloat16),
            pltpu.VMEM((slots, depth), jnp.float32),
            pltpu.VMEM((slots, total, LANES), jnp.float32),
            pltpu.SemaphoreType.DMA((steps,)),
        ],
        compiler_params=pltpu.CompilerParams(vmem_limit_bytes=PROJECT_VMEM),
        cost_estimate=pl.CostEstimate(
            flops=2 * slots * depth * (query_width + 2 * kv_width),
            bytes_accessed=2 * depth * (query_width + 2 * kv_width),
            transcendentals=0,
        ),
        name="project",
    )(rows, other, w_query, key_weight, value_weight)


def attend_kernel(
    query_heads, kv_heads, length_ref, mine_ref, arrived_ref, cosine_ref, sine_ref, k_ref, v_ref, heads_ref
):
    total = mine_ref[0] + arrived_ref[0]
    at = query_heads + 2 * kv_heads
    scale = lax.rsqrt(total[at : at + 1, :] / MODEL_WIDTH + 1e-05)
    turned = total[: query_heads + kv_heads] * scale
    half = HEAD_SIZE // 2
    swapped = jnp.concatenate([turned[:, half:], turned[:, :half]], axis=1)
    turned = (turned * cosine_ref[...] + swapped * sine_ref[...]).astype(jnp.bfloat16)
    fresh_values = (total[query_heads + kv_heads : at] * scale).astype(jnp.bfloat16)
    group = query_heads // kv_heads
    factor = 1.0 / math.sqrt(HEAD_SIZE)
    length = length_ref[0]
    for head in range(kv_heads):
        queries = turned[head * group : (head + 1) * group]
        fresh_key = turned[query_heads + head : query_heads + head + 1].astype(jnp.float32)
        own = jnp.sum(queries.astype(jnp.float32) * fresh_key, axis=1, keepdims=True) * factor
        scores = (
            lax.dot_general(
                queries,
                k_ref[0, head],
                (((1,), (1,)), ((), ())),
                preferred_element_type=jnp.float32,
            )
            * factor
        )
        slot = lax.broadcasted_iota(jnp.int32, scores.shape, 1)
        scores = jnp.where(slot < length, scores, -jnp.inf)
        top = jnp.maximum(jnp.max(scores, axis=1, keepdims=True), own)
        exponent = jnp.exp(scores - top)
        own_exp = jnp.exp(own - top)
        share = 1.0 / (jnp.sum(exponent, axis=1, keepdims=True) + own_exp)
        weights = (exponent * share).astype(jnp.bfloat16)
        own_weight = (own_exp * share).astype(jnp.bfloat16)
        mixed = jnp.dot(weights, v_ref[0, head], preferred_element_type=jnp.float32)
        mixed = mixed + own_weight.astype(jnp.float32) * fresh_values[head : head + 1].astype(
            jnp.float32
        )
        heads_ref[0, pl.ds(head * group, group), :] = mixed.astype(jnp.bfloat16)


def attend(mine, arrived, cosine, sine, k_cache, value_cache, lengths, query_heads):
    kv_heads, cache_len = k_cache.shape[1:3]
    whole = pl.BlockSpec(memory_space=pltpu.VMEM)
    return pl.pallas_call(
        functools.partial(attend_kernel, query_heads, kv_heads),
        out_shape=jax.ShapeDtypeStruct((1, query_heads, HEAD_SIZE), jnp.bfloat16),
        in_specs=[pl.BlockSpec(memory_space=pltpu.SMEM)] + [whole] * 6,
        out_specs=whole,
        compiler_params=pltpu.CompilerParams(vmem_limit_bytes=12 * 2**20),
        cost_estimate=pl.CostEstimate(
            flops=4 * query_heads * cache_len * HEAD_SIZE,
            bytes_accessed=64 * kv_heads * cache_len * HEAD_SIZE,
            transcendentals=query_heads * cache_len,
        ),
        name="attend",
    )(lengths, mine, arrived, cosine, sine, k_cache, value_cache)


def output_kernel(bits, pieces, *refs):
    parts = refs[:pieces]
    w_hbm, mine_ref, theirs_ref, w_ref, flat, left, sums, sems = refs[pieces:]
    depth = w_ref.shape[0]
    chunk = min(2 * CHUNK, depth)
    copies = []
    for step in range(depth // chunk):
        part = pl.ds(step * chunk, chunk)
        copies.append(pltpu.make_async_copy(w_hbm.at[part], w_ref.at[part], sems.at[step]))
        copies[-1].start()
    slots = left.shape[0]
    heads = flat.shape[0] // slots
    at = 0
    for ref in parts:
        for i in range(ref.shape[0]):
            flat[at : at + heads, :] = ref[i].astype(jnp.float32)
            at += heads
    for head in range(heads):
        left[:, head * HEAD_SIZE : (head + 1) * HEAD_SIZE] = flat[
            pl.ds(head, slots, stride=heads), :
        ].astype(jnp.bfloat16)
    total = None
    for step, copy in enumerate(copies):
        part = slice(step * chunk, (step + 1) * chunk)
        copy.wait()
        term = jnp.dot(left[:, part], w_ref[part, :], preferred_element_type=jnp.float32)
        total = term if total is None else total + term
    sums[...] = total
    half = slots // 2
    turn = bit_reverse(lax.axis_index("gx"), bits)
    gy = lax.axis_index("gy")
    for ref, side in ((mine_ref, gy), (theirs_ref, 1 - gy)):
        for t in range(half):
            slot = bit_reverse(t, bits) ^ turn ^ side
            ref[t : t + 1, :] = sums[pl.ds(slot, 1), :]


def output(parts, w_out, slots):
    bits = slots.bit_length() - 1
    depth, width = w_out.shape
    heads = depth // HEAD_SIZE
    whole = pl.BlockSpec(memory_space=pltpu.VMEM)
    piece = jax.ShapeDtypeStruct((slots // 2, width), jnp.float32)
    return pl.pallas_call(
        functools.partial(output_kernel, bits, len(parts)),
        out_shape=(piece, piece),
        in_specs=[whole] * len(parts) + [pl.BlockSpec(memory_space=pltpu.HBM)],
        out_specs=(whole, whole),
        scratch_shapes=[
            pltpu.VMEM(w_out.shape, jnp.bfloat16),
            pltpu.VMEM((slots * heads, HEAD_SIZE), jnp.float32),
            pltpu.VMEM((slots, depth), jnp.bfloat16),
            pltpu.VMEM((slots, width), jnp.float32),
            pltpu.SemaphoreType.DMA((depth // min(2 * CHUNK, depth),)),
        ],
        compiler_params=pltpu.CompilerParams(vmem_limit_bytes=OUTPUT_VMEM),
        cost_estimate=pl.CostEstimate(
            flops=2 * slots * depth * width, bytes_accessed=2 * depth * width, transcendentals=0
        ),
        name="output",
    )(*parts, w_out)


def swap(block, axis, devices, mask):
    return lax.ppermute(block, axis, [(i, i ^ mask) for i in range(devices)])


def body(devices, activations, w_query, key_weight, value_weight, w_out, k_cache, value_cache, lengths):
    slots = devices
    query_heads = w_query.shape[1] // HEAD_SIZE
    half = HEAD_SIZE // 2
    frequency = jnp.power(
        jnp.float32(500000.0), -2.0 * jnp.arange(half, dtype=jnp.float32) / HEAD_SIZE
    )
    angle = lengths.astype(jnp.float32)[:, None] * frequency
    cosine = jnp.cos(angle)
    sine = jnp.sin(angle)
    cosine = jnp.concatenate([cosine, cosine], axis=1)
    sine = jnp.concatenate([-sine, sine], axis=1)

    other = swap(activations, "gy", 2, 1)
    key_weight, value_weight, k_cache, value_cache = stage(
        key_weight, value_weight, k_cache, value_cache
    )
    send, keep = project(activations, other, w_query, key_weight, value_weight, slots)
    mask = 1
    while send.shape[0] > 1:
        arrived = swap(send, "gx", devices, mask)
        rest = keep.shape[0] // 2
        send = keep[rest:] + arrived[rest:]
        keep = keep[:rest] + arrived[:rest]
        mask *= 2
    arrived = swap(send, "gx", devices, mask)
    heads = attend(keep, arrived, cosine, sine, k_cache, value_cache, lengths, query_heads)
    parts = [heads]
    while mask:
        held = parts[0] if len(parts) == 1 else jnp.concatenate(parts, axis=0)
        parts.append(swap(held, "gx", devices, mask))
        mask //= 2
    mine, theirs = output(parts, w_out, slots)
    return (mine + swap(theirs, "gy", 2, 1)).astype(jnp.bfloat16)


def solution(mesh):
    placed = (
        P(("groups", "gy"), "gx"),
        P("gx", "gy"),
        P("gx", "gy"),
        P("gx", "gy"),
        P("gy", "gx"),
        P(("groups", "gx"), "gy", None, None),
        P(("groups", "gx"), "gy", None, None),
        P(("groups", "gx")),
    )
    return jax.shard_map(
        functools.partial(body, mesh.shape["gx"]),
        mesh=mesh,
        in_specs=placed,
        out_specs=P(("groups", "gy"), "gx"),
        check_vma=False,
    )
```

```python
import functools
import math

import jax
import jax.numpy as jnp
from jax import lax
from jax.experimental import pallas as pl
from jax.experimental.pallas import tpu as pltpu
from jax.sharding import PartitionSpec as P

MODEL_WIDTH = 16384
LANES = 128
HEAD_SIZE = 128
CHUNK = 256
MIB = 2**20


def bit_reverse(value, bits):
    turned = 0
    for bit in range(bits):
        turned = turned | (((value >> bit) & 1) << (bits - 1 - bit))
    return turned


def in_hbm(array):
    return pltpu.with_memory_space_constraint(array, pltpu.HBM)


def stage_kernel(parts, *refs):
    count = len(parts)
    sems = refs[-1]
    copies = [
        pltpu.make_async_copy(refs[i].at[pl.ds(*part)], refs[count + i], sems.at[i])
        for i, part in enumerate(parts)
    ]
    for copy in copies:
        copy.start()
    for copy in copies:
        copy.wait()


def stage(arrays, parts):
    shapes = tuple(
        jax.ShapeDtypeStruct((part[1], *a.shape[1:]), a.dtype) for a, part in zip(arrays, parts)
    )
    return pl.pallas_call(
        functools.partial(stage_kernel, parts),
        out_shape=shapes,
        in_specs=[pl.BlockSpec(memory_space=pltpu.HBM)] * len(arrays),
        out_specs=tuple(pl.BlockSpec(memory_space=pltpu.VMEM) for _ in arrays),
        scratch_shapes=[pltpu.SemaphoreType.DMA((len(arrays),))],
        compiler_params=pltpu.CompilerParams(vmem_limit_bytes=16 * MIB),
        cost_estimate=pl.CostEstimate(
            flops=0, bytes_accessed=sum(2 * math.prod(x.shape) for x in shapes), transcendentals=0
        ),
        name="stage",
    )(*[in_hbm(a) for a in arrays])


def spread(depth, skip, chunk):
    return [(at, min(chunk, depth - at)) for at in range(skip, depth, chunk)]


def project_kernel(
    bits, rows_ref, other_ref, wq_hbm, first, wk, wv, send_ref, keep_ref, wq, rows, sems
):
    skip = first.shape[0]
    ranges = spread(wq_hbm.shape[0], skip, CHUNK)
    copies = []
    for i, (start, size) in enumerate(ranges):
        copies.append(
            pltpu.make_async_copy(
                wq_hbm.at[pl.ds(start, size)], wq.at[pl.ds(start - skip, size)], sems.at[i]
            )
        )
        copies[-1].start()

    slots = rows.shape[0]
    half = slots // 2
    turn = bit_reverse(lax.axis_index("gx"), bits)
    gy = lax.axis_index("gy")
    for ref, side in ((rows_ref, gy), (other_ref, 1 - gy)):
        block = ref[...].astype(jnp.float32)
        for t in range(half):
            slot = bit_reverse(t, bits) ^ turn ^ side
            rows[pl.ds(slot, 1), :] = block[t : t + 1, :]
    wide = rows[...]
    squares = jnp.sum(wide * wide, axis=1, keepdims=True)
    narrow = wide.astype(jnp.bfloat16)

    fresh = [jnp.dot(narrow, w[...], preferred_element_type=jnp.float32) for w in (wk, wv)]
    sums = jnp.dot(narrow[:, :skip], first[...], preferred_element_type=jnp.float32)
    for (start, size), copy in zip(ranges, copies):
        copy.wait()
        sums = sums + jnp.dot(
            narrow[:, start : start + size],
            wq[start - skip : start - skip + size, :],
            preferred_element_type=jnp.float32,
        )

    total = keep_ref.shape[1]
    blocks = []
    for part in (sums, *fresh):
        blocks += [part[:, i : i + LANES] for i in range(0, part.shape[1], LANES)]
    blocks.append(jnp.broadcast_to(squares, (slots, LANES)))
    blocks += [jnp.zeros((slots, LANES), jnp.float32)] * (total - len(blocks))
    for ref, rows_at in ((keep_ref, 0), (send_ref, half)):
        flat = ref.reshape(half * total, LANES)
        for i, block in enumerate(blocks):
            flat[pl.ds(i, half, stride=total), :] = block[rows_at : rows_at + half]


def project(rows, other, w_query, first, key_weight, value_weight, slots):
    bits = slots.bit_length() - 1
    depth, query_width = w_query.shape
    kv_width = key_weight.shape[1]
    used = (query_width + 2 * kv_width) // LANES + 1
    total = -(-used // 8) * 8
    skip = first.shape[0]
    piece = jax.ShapeDtypeStruct((slots // 2, total, LANES), jnp.float32)
    whole = pl.BlockSpec(memory_space=pltpu.VMEM)
    return pl.pallas_call(
        functools.partial(project_kernel, bits),
        out_shape=(piece, piece),
        in_specs=[whole, whole, pl.BlockSpec(memory_space=pltpu.HBM), whole, whole, whole],
        out_specs=(whole, whole),
        scratch_shapes=[
            pltpu.VMEM((max(depth - skip, 16), query_width), jnp.bfloat16),
            pltpu.VMEM((slots, depth), jnp.float32),
            pltpu.SemaphoreType.DMA((max(1, len(spread(depth, skip, CHUNK))),)),
        ],
        compiler_params=pltpu.CompilerParams(vmem_limit_bytes=32 * MIB),
        cost_estimate=pl.CostEstimate(
            flops=2 * slots * depth * (query_width + 2 * kv_width),
            bytes_accessed=2 * depth * (query_width + 2 * kv_width),
            transcendentals=0,
        ),
        name="project",
    )(rows, other, in_hbm(w_query), first, key_weight, value_weight)


def attend_kernel(
    query_heads, kv_heads, pieces, length_ref, cosine_ref, sine_ref, k_ref, v_ref, *refs
):
    heads_ref = refs[pieces]
    total = refs[0][0]
    for ref in refs[1:pieces]:
        total = total + ref[0]
    at = query_heads + 2 * kv_heads
    scale = lax.rsqrt(total[at : at + 1, :] / MODEL_WIDTH + 1e-05)
    turned = total[: query_heads + kv_heads] * scale
    half = HEAD_SIZE // 2
    swapped = jnp.concatenate([turned[:, half:], turned[:, :half]], axis=1)
    turned = (turned * cosine_ref[...] + swapped * sine_ref[...]).astype(jnp.bfloat16)
    fresh_values = (total[query_heads + kv_heads : at] * scale).astype(jnp.bfloat16)
    group = query_heads // kv_heads
    factor = 1.0 / math.sqrt(HEAD_SIZE)
    length = length_ref[0]
    for head in range(kv_heads):
        queries = turned[head * group : (head + 1) * group]
        fresh_key = turned[query_heads + head : query_heads + head + 1].astype(jnp.float32)
        own = jnp.sum(queries.astype(jnp.float32) * fresh_key, axis=1, keepdims=True) * factor
        scores = (
            lax.dot_general(
                queries,
                k_ref[0, head],
                (((1,), (1,)), ((), ())),
                preferred_element_type=jnp.float32,
            )
            * factor
        )
        slot = lax.broadcasted_iota(jnp.int32, scores.shape, 1)
        scores = jnp.where(slot < length, scores, -jnp.inf)
        top = jnp.maximum(jnp.max(scores, axis=1, keepdims=True), own)
        exponent = jnp.exp(scores - top)
        own_exp = jnp.exp(own - top)
        share = 1.0 / (jnp.sum(exponent, axis=1, keepdims=True) + own_exp)
        weights = (exponent * share).astype(jnp.bfloat16)
        own_weight = (own_exp * share).astype(jnp.bfloat16)
        mixed = jnp.dot(weights, v_ref[0, head], preferred_element_type=jnp.float32)
        mixed = mixed + own_weight.astype(jnp.float32) * fresh_values[head : head + 1].astype(
            jnp.float32
        )
        heads_ref[0, pl.ds(head * group, group), :] = mixed.astype(jnp.bfloat16)


def attend(parts, cosine, sine, k_cache, value_cache, lengths, query_heads):
    kv_heads, cache_len = k_cache.shape[1:3]
    whole = pl.BlockSpec(memory_space=pltpu.VMEM)
    return pl.pallas_call(
        functools.partial(attend_kernel, query_heads, kv_heads, len(parts)),
        out_shape=jax.ShapeDtypeStruct((1, query_heads, HEAD_SIZE), jnp.bfloat16),
        in_specs=[pl.BlockSpec(memory_space=pltpu.SMEM)] + [whole] * (4 + len(parts)),
        out_specs=whole,
        compiler_params=pltpu.CompilerParams(vmem_limit_bytes=12 * MIB),
        cost_estimate=pl.CostEstimate(
            flops=4 * query_heads * cache_len * HEAD_SIZE,
            bytes_accessed=4 * kv_heads * cache_len * HEAD_SIZE,
            transcendentals=query_heads * cache_len,
        ),
        name="attend",
    )(lengths, cosine, sine, k_cache, value_cache, *parts)


def output_kernel(bits, pieces, staged, *refs):
    parts = refs[:pieces]
    ready = refs[pieces : pieces + staged]
    w_hbm, mine_ref, theirs_ref, rest, flat, left, sums, sems = refs[pieces + staged :]
    skip = sum(ref.shape[0] for ref in ready)
    ranges = spread(w_hbm.shape[0], skip, 2 * CHUNK)
    copies = []
    for i, (start, size) in enumerate(ranges):
        copies.append(
            pltpu.make_async_copy(
                w_hbm.at[pl.ds(start, size)], rest.at[pl.ds(start - skip, size)], sems.at[i]
            )
        )
        copies[-1].start()
    slots = left.shape[0]
    heads = flat.shape[0] // slots
    at = 0
    for ref in parts:
        for i in range(ref.shape[0]):
            flat[at : at + heads, :] = ref[i].astype(jnp.float32)
            at += heads
    for head in range(heads):
        left[:, head * HEAD_SIZE : (head + 1) * HEAD_SIZE] = flat[
            pl.ds(head, slots, stride=heads), :
        ].astype(jnp.bfloat16)
    total = None
    at = 0
    for ref in ready:
        size = ref.shape[0]
        term = jnp.dot(left[:, at : at + size], ref[...], preferred_element_type=jnp.float32)
        total = term if total is None else total + term
        at += size
    for (start, size), copy in zip(ranges, copies):
        copy.wait()
        term = jnp.dot(
            left[:, start : start + size],
            rest[start - skip : start - skip + size, :],
            preferred_element_type=jnp.float32,
        )
        total = term if total is None else total + term
    sums[...] = total
    half = slots // 2
    turn = bit_reverse(lax.axis_index("gx"), bits)
    gy = lax.axis_index("gy")
    for ref, side in ((mine_ref, gy), (theirs_ref, 1 - gy)):
        for t in range(half):
            slot = bit_reverse(t, bits) ^ turn ^ side
            ref[t : t + 1, :] = sums[pl.ds(slot, 1), :]


def output(parts, ready, w_out, slots):
    bits = slots.bit_length() - 1
    depth, width = w_out.shape
    heads = depth // HEAD_SIZE
    skip = sum(x.shape[0] for x in ready)
    whole = pl.BlockSpec(memory_space=pltpu.VMEM)
    piece = jax.ShapeDtypeStruct((slots // 2, width), jnp.float32)
    return pl.pallas_call(
        functools.partial(output_kernel, bits, len(parts), len(ready)),
        out_shape=(piece, piece),
        in_specs=[whole] * (len(parts) + len(ready)) + [pl.BlockSpec(memory_space=pltpu.HBM)],
        out_specs=(whole, whole),
        scratch_shapes=[
            pltpu.VMEM((max(depth - skip, 16), width), jnp.bfloat16),
            pltpu.VMEM((slots * heads, HEAD_SIZE), jnp.float32),
            pltpu.VMEM((slots, depth), jnp.bfloat16),
            pltpu.VMEM((slots, width), jnp.float32),
            pltpu.SemaphoreType.DMA((max(1, len(spread(depth, skip, 2 * CHUNK))),)),
        ],
        compiler_params=pltpu.CompilerParams(vmem_limit_bytes=24 * MIB),
        cost_estimate=pl.CostEstimate(
            flops=2 * slots * depth * width, bytes_accessed=2 * depth * width, transcendentals=0
        ),
        name="output",
    )(*parts, *ready, in_hbm(w_out))


def swap(block, axis, devices, mask):
    return lax.ppermute(block, axis, [(i, i ^ mask) for i in range(devices)])


def body(devices, activations, w_query, key_weight, value_weight, w_out, k_cache, value_cache, lengths):
    slots = devices
    query_heads = w_query.shape[1] // HEAD_SIZE
    half = HEAD_SIZE // 2
    frequency = jnp.power(
        jnp.float32(500000.0), -2.0 * jnp.arange(half, dtype=jnp.float32) / HEAD_SIZE
    )
    angle = lengths.astype(jnp.float32)[:, None] * frequency
    cosine = jnp.cos(angle)
    sine = jnp.sin(angle)
    cosine = jnp.concatenate([cosine, cosine], axis=1)
    sine = jnp.concatenate([-sine, sine], axis=1)

    bits = slots.bit_length() - 1
    direct = min(slots, 4)

    other = swap(activations, "gy", 2, 1)
    depth = w_query.shape[0]
    first, key_weight, value_weight = stage(
        (w_query, key_weight, value_weight), ((0, min(CHUNK, depth)), (0, depth), (0, depth))
    )
    send, keep = project(activations, other, w_query, first, key_weight, value_weight, slots)

    w_out, keep = lax.optimization_barrier((w_out, keep))
    rows_out = w_out.shape[0]
    third = rows_out * 3 // 8
    k_cache, value_cache, ready_one = stage(
        (k_cache, value_cache, w_out),
        ((0, k_cache.shape[0]), (0, value_cache.shape[0]), (0, third)),
    )
    mask = 1
    while True:
        arrived = swap(send, "gx", devices, mask)
        total = keep + arrived
        mask *= 2
        if total.shape[0] <= direct:
            break
        rest = total.shape[0] // 2
        keep, send = total[:rest], total[rest:]
    w_out, total = lax.optimization_barrier((w_out, total))
    (ready_two,) = stage((w_out,), ((third, third),))
    parts = [total[:1]] + [
        swap(total[j : j + 1], "gx", devices, bit_reverse(j, bits)) for j in range(1, direct)
    ]
    heads = attend(parts, cosine, sine, k_cache, value_cache, lengths, query_heads)

    parts = [heads] + [
        swap(heads, "gx", devices, bit_reverse(j, bits)) for j in range(1, direct)
    ]
    mask //= 2
    while mask:
        parts.append(swap(jnp.concatenate(parts, axis=0), "gx", devices, mask))
        mask //= 2
    mine, theirs = output(parts, (ready_one, ready_two), w_out, slots)
    return (mine + swap(theirs, "gy", 2, 1)).astype(jnp.bfloat16)


def solution(mesh):
    placed = (
        P(("groups", "gy"), "gx"),
        P("gx", "gy"),
        P("gx", "gy"),
        P("gx", "gy"),
        P("gy", "gx"),
        P(("groups", "gx"), "gy", None, None),
        P(("groups", "gx"), "gy", None, None),
        P(("groups", "gx")),
    )
    return jax.shard_map(
        functools.partial(body, mesh.shape["gx"]),
        mesh=mesh,
        in_specs=placed,
        out_specs=P(("groups", "gy"), "gx"),
        check_vma=False,
    )
```

```python
import functools
import math

import jax
import jax.numpy as jnp
from jax import lax
from jax.experimental import pallas as pl
from jax.experimental.pallas import tpu as pltpu
from jax.sharding import PartitionSpec as P

MODEL_WIDTH = 16384
LANES = 128
HEAD_SIZE = 128
CHUNK = 256
FAN = 4
MIB = 2**20


def bit_reverse(value, bits):
    turned = 0
    for bit in range(bits):
        turned = turned | (((value >> bit) & 1) << (bits - 1 - bit))
    return turned


def in_hbm(array):
    return pltpu.with_memory_space_constraint(array, pltpu.HBM)


def stage_kernel(parts, *refs):
    count = len(parts)
    sems = refs[-1]
    copies = [
        pltpu.make_async_copy(refs[i].at[pl.ds(*part)], refs[count + i], sems.at[i])
        for i, part in enumerate(parts)
    ]
    for copy in copies:
        copy.start()
    for copy in copies:
        copy.wait()


def stage(arrays, parts):
    shapes = tuple(
        jax.ShapeDtypeStruct((part[1], *a.shape[1:]), a.dtype) for a, part in zip(arrays, parts)
    )
    return pl.pallas_call(
        functools.partial(stage_kernel, parts),
        out_shape=shapes,
        in_specs=[pl.BlockSpec(memory_space=pltpu.HBM)] * len(arrays),
        out_specs=tuple(pl.BlockSpec(memory_space=pltpu.VMEM) for _ in arrays),
        scratch_shapes=[pltpu.SemaphoreType.DMA((len(arrays),))],
        compiler_params=pltpu.CompilerParams(vmem_limit_bytes=16 * MIB),
        cost_estimate=pl.CostEstimate(
            flops=0, bytes_accessed=sum(2 * math.prod(x.shape) for x in shapes), transcendentals=0
        ),
        name="stage",
    )(*[in_hbm(a) for a in arrays])


def spread(depth, skip, chunk):
    return [(at, min(chunk, depth - at)) for at in range(skip, depth, chunk)]


def project_kernel(
    bits, length_ref, rows_ref, other_ref, frequency_ref, wq_hbm, first, wk, wv, *refs
):
    pieces, (turn_ref, wq, rows, sems) = refs[:FAN], refs[FAN:]
    skip = first.shape[0]
    ranges = spread(wq_hbm.shape[0], skip, CHUNK)
    copies = []
    for i, (start, size) in enumerate(ranges):
        copies.append(
            pltpu.make_async_copy(
                wq_hbm.at[pl.ds(start, size)], wq.at[pl.ds(start - skip, size)], sems.at[i]
            )
        )
        copies[-1].start()

    slots = rows.shape[0]
    half = slots // 2
    turn = bit_reverse(lax.axis_index("gx"), bits)
    gy = lax.axis_index("gy")
    for ref, side in ((rows_ref, gy), (other_ref, 1 - gy)):
        block = ref[...].astype(jnp.float32)
        for t in range(half):
            slot = bit_reverse(t, bits) ^ turn ^ side
            rows[pl.ds(slot, 1), :] = block[t : t + 1, :]
    wide = rows[...]
    squares = jnp.sum(wide * wide, axis=1, keepdims=True)
    narrow = wide.astype(jnp.bfloat16)

    position = length_ref[0].astype(jnp.float32)
    angle = position * frequency_ref[...]
    lane = lax.broadcasted_iota(jnp.int32, angle.shape, 1)
    sine = jnp.sin(angle)
    turn_ref[0:1, :] = jnp.cos(angle)
    turn_ref[1:2, :] = jnp.where(lane < HEAD_SIZE // 2, -sine, sine)
    turn_ref[2:3, :] = jnp.full(angle.shape, position)

    fresh = [jnp.dot(narrow, w[...], preferred_element_type=jnp.float32) for w in (wk, wv)]
    sums = jnp.dot(narrow[:, :skip], first[...], preferred_element_type=jnp.float32)
    for (start, size), copy in zip(ranges, copies):
        copy.wait()
        sums = sums + jnp.dot(
            narrow[:, start : start + size],
            wq[start - skip : start - skip + size, :],
            preferred_element_type=jnp.float32,
        )

    total = pieces[0].shape[1]
    blocks = []
    for part in (sums, *fresh):
        blocks += [part[:, i : i + LANES] for i in range(0, part.shape[1], LANES)]
    blocks.append(jnp.broadcast_to(squares, (slots, LANES)))
    blocks += [jnp.zeros((slots, LANES), jnp.float32)] * (total - len(blocks))
    size = slots // FAN
    for at, ref in enumerate(pieces):
        flat = ref.reshape(size * total, LANES)
        for i, block in enumerate(blocks):
            flat[pl.ds(i, size, stride=total), :] = block[at * size : (at + 1) * size]


def project(lengths, rows, other, frequency, w_query, first, key_weight, value_weight, slots):
    bits = slots.bit_length() - 1
    depth, query_width = w_query.shape
    kv_width = key_weight.shape[1]
    used = (query_width + 2 * kv_width) // LANES + 1
    total = -(-used // 8) * 8
    skip = first.shape[0]
    piece = jax.ShapeDtypeStruct((slots // FAN, total, LANES), jnp.float32)
    hbm = pl.BlockSpec(memory_space=pltpu.HBM)
    whole = pl.BlockSpec(memory_space=pltpu.VMEM)
    return pl.pallas_call(
        functools.partial(project_kernel, bits),
        out_shape=(piece,) * FAN + (jax.ShapeDtypeStruct((8, HEAD_SIZE), jnp.float32),),
        in_specs=[pl.BlockSpec(memory_space=pltpu.SMEM), whole, whole, whole, hbm, whole, whole, whole],
        out_specs=(whole,) * (FAN + 1),
        scratch_shapes=[
            pltpu.VMEM((max(depth - skip, 16), query_width), jnp.bfloat16),
            pltpu.VMEM((slots, depth), jnp.float32),
            pltpu.SemaphoreType.DMA((max(1, len(spread(depth, skip, CHUNK))),)),
        ],
        compiler_params=pltpu.CompilerParams(vmem_limit_bytes=32 * MIB),
        cost_estimate=pl.CostEstimate(
            flops=2 * slots * depth * (query_width + 2 * kv_width),
            bytes_accessed=2 * depth * (query_width + 2 * kv_width),
            transcendentals=0,
        ),
        name="project",
    )(lengths, rows, other, frequency, in_hbm(w_query), first, key_weight, value_weight)


def attend_kernel(
    query_heads, kv_heads, pieces, turn_ref, k_ref, v_ref, *refs
):
    heads_ref = refs[pieces]
    total = refs[0][0]
    for ref in refs[1:pieces]:
        total = total + ref[0]
    at = query_heads + 2 * kv_heads
    scale = lax.rsqrt(total[at : at + 1, :] / MODEL_WIDTH + 1e-05)
    turned = total[: query_heads + kv_heads] * scale
    half = HEAD_SIZE // 2
    swapped = jnp.concatenate([turned[:, half:], turned[:, :half]], axis=1)
    turned = (turned * turn_ref[0:1, :] + swapped * turn_ref[1:2, :]).astype(jnp.bfloat16)
    fresh_values = (total[query_heads + kv_heads : at] * scale).astype(jnp.bfloat16)
    group = query_heads // kv_heads
    factor = 1.0 / math.sqrt(HEAD_SIZE)
    length = turn_ref[2:3, 0:1].astype(jnp.int32)
    for head in range(kv_heads):
        queries = turned[head * group : (head + 1) * group]
        fresh_key = turned[query_heads + head : query_heads + head + 1].astype(jnp.float32)
        own = jnp.sum(queries.astype(jnp.float32) * fresh_key, axis=1, keepdims=True) * factor
        scores = (
            lax.dot_general(
                queries,
                k_ref[0, head],
                (((1,), (1,)), ((), ())),
                preferred_element_type=jnp.float32,
            )
            * factor
        )
        slot = lax.broadcasted_iota(jnp.int32, scores.shape, 1)
        scores = jnp.where(slot < length, scores, -jnp.inf)
        top = jnp.maximum(jnp.max(scores, axis=1, keepdims=True), own)
        exponent = jnp.exp(scores - top)
        own_exp = jnp.exp(own - top)
        share = 1.0 / (jnp.sum(exponent, axis=1, keepdims=True) + own_exp)
        weights = (exponent * share).astype(jnp.bfloat16)
        own_weight = (own_exp * share).astype(jnp.bfloat16)
        mixed = jnp.dot(weights, v_ref[0, head], preferred_element_type=jnp.float32)
        mixed = mixed + own_weight.astype(jnp.float32) * fresh_values[head : head + 1].astype(
            jnp.float32
        )
        heads_ref[0, pl.ds(head * group, group), :] = mixed.astype(jnp.bfloat16)


def attend(parts, turn, k_cache, value_cache, query_heads):
    kv_heads, cache_len = k_cache.shape[1:3]
    whole = pl.BlockSpec(memory_space=pltpu.VMEM)
    return pl.pallas_call(
        functools.partial(attend_kernel, query_heads, kv_heads, len(parts)),
        out_shape=jax.ShapeDtypeStruct((1, query_heads, HEAD_SIZE), jnp.bfloat16),
        in_specs=[whole] * (3 + len(parts)),
        out_specs=whole,
        compiler_params=pltpu.CompilerParams(vmem_limit_bytes=12 * MIB),
        cost_estimate=pl.CostEstimate(
            flops=4 * query_heads * cache_len * HEAD_SIZE,
            bytes_accessed=4 * kv_heads * cache_len * HEAD_SIZE,
            transcendentals=query_heads * cache_len,
        ),
        name="attend",
    )(turn, k_cache, value_cache, *parts)


def output_kernel(bits, pieces, staged, *refs):
    parts = refs[:pieces]
    ready = refs[pieces : pieces + staged]
    w_hbm, mine_ref, theirs_ref, rest, flat, left, sums, sems = refs[pieces + staged :]
    skip = sum(ref.shape[0] for ref in ready)
    ranges = spread(w_hbm.shape[0], skip, 2 * CHUNK)
    copies = []
    for i, (start, size) in enumerate(ranges):
        copies.append(
            pltpu.make_async_copy(
                w_hbm.at[pl.ds(start, size)], rest.at[pl.ds(start - skip, size)], sems.at[i]
            )
        )
        copies[-1].start()
    slots = left.shape[0]
    heads = flat.shape[0] // slots
    at = 0
    for ref in parts:
        for i in range(ref.shape[0]):
            flat[at : at + heads, :] = ref[i].astype(jnp.float32)
            at += heads
    for head in range(heads):
        left[:, head * HEAD_SIZE : (head + 1) * HEAD_SIZE] = flat[
            pl.ds(head, slots, stride=heads), :
        ].astype(jnp.bfloat16)
    total = None
    at = 0
    for ref in ready:
        size = ref.shape[0]
        term = jnp.dot(left[:, at : at + size], ref[...], preferred_element_type=jnp.float32)
        total = term if total is None else total + term
        at += size
    for (start, size), copy in zip(ranges, copies):
        copy.wait()
        term = jnp.dot(
            left[:, start : start + size],
            rest[start - skip : start - skip + size, :],
            preferred_element_type=jnp.float32,
        )
        total = term if total is None else total + term
    sums[...] = total
    half = slots // 2
    turn = bit_reverse(lax.axis_index("gx"), bits)
    gy = lax.axis_index("gy")
    for ref, side in ((mine_ref, gy), (theirs_ref, 1 - gy)):
        for t in range(half):
            slot = bit_reverse(t, bits) ^ turn ^ side
            ref[t : t + 1, :] = sums[pl.ds(slot, 1), :]


def output(parts, ready, w_out, slots):
    bits = slots.bit_length() - 1
    depth, width = w_out.shape
    heads = depth // HEAD_SIZE
    skip = sum(x.shape[0] for x in ready)
    whole = pl.BlockSpec(memory_space=pltpu.VMEM)
    piece = jax.ShapeDtypeStruct((slots // 2, width), jnp.float32)
    return pl.pallas_call(
        functools.partial(output_kernel, bits, len(parts), len(ready)),
        out_shape=(piece, piece),
        in_specs=[whole] * (len(parts) + len(ready)) + [pl.BlockSpec(memory_space=pltpu.HBM)],
        out_specs=(whole, whole),
        scratch_shapes=[
            pltpu.VMEM((max(depth - skip, 16), width), jnp.bfloat16),
            pltpu.VMEM((slots * heads, HEAD_SIZE), jnp.float32),
            pltpu.VMEM((slots, depth), jnp.bfloat16),
            pltpu.VMEM((slots, width), jnp.float32),
            pltpu.SemaphoreType.DMA((max(1, len(spread(depth, skip, 2 * CHUNK))),)),
        ],
        compiler_params=pltpu.CompilerParams(vmem_limit_bytes=24 * MIB),
        cost_estimate=pl.CostEstimate(
            flops=2 * slots * depth * width, bytes_accessed=2 * depth * width, transcendentals=0
        ),
        name="output",
    )(*parts, *ready, in_hbm(w_out))


def swap(block, axis, devices, mask):
    return lax.ppermute(block, axis, [(i, i ^ mask) for i in range(devices)])


def fan(pieces, devices):
    masks = [bit_reverse(q, 2) for q in range(FAN)]
    arrived = [None] * FAN
    for q in sorted(range(1, FAN), key=lambda q: (masks[q] + 1) % FAN):
        arrived[q] = swap(pieces[q], "gx", devices, masks[q])
    return arrived[1:]


def body(devices, activations, w_query, key_weight, value_weight, w_out, k_cache, value_cache, lengths):
    slots = devices
    query_heads = w_query.shape[1] // HEAD_SIZE
    other = swap(activations, "gy", 2, 1)
    depth = w_query.shape[0]
    first, key_weight, value_weight = stage(
        (w_query, key_weight, value_weight), ((0, min(CHUNK, depth)), (0, depth), (0, depth))
    )
    half = HEAD_SIZE // 2
    frequency = jnp.power(
        jnp.float32(500000.0), -2.0 * jnp.arange(half, dtype=jnp.float32) / HEAD_SIZE
    )
    frequency = jnp.concatenate([frequency, frequency])[None, :]
    *pieces, turn = project(
        lengths, activations, other, frequency, w_query, first, key_weight, value_weight, slots
    )

    rows_out = w_out.shape[0]
    few, most = rows_out // 8, rows_out * 3 // 8
    arrived = fan(pieces, devices)
    k_cache, value_cache, ready_one = stage(
        (k_cache, value_cache, w_out),
        ((0, k_cache.shape[0]), (0, value_cache.shape[0]), (0, few)),
    )
    total = pieces[0] + (arrived[2] + (arrived[1] + arrived[0]))
    mask = FAN
    while total.shape[0] > 2:
        rest = total.shape[0] // 2
        total = total[:rest] + swap(total[rest:], "gx", devices, mask)
        mask *= 2
    total, w_out, k_cache, value_cache, ready_one = lax.optimization_barrier(
        (total, w_out, k_cache, value_cache, ready_one)
    )
    (ready_two,) = stage((w_out,), ((few, most),))
    parts = [total[:1], swap(total[1:], "gx", devices, mask)]
    parts[1], ready_two = lax.optimization_barrier((parts[1], ready_two))
    heads = attend(parts, turn, k_cache, value_cache, query_heads)

    heads, w_out = lax.optimization_barrier((heads, w_out))
    (ready_three,) = stage((w_out,), ((few + most, most),))
    parts = [heads, swap(heads, "gx", devices, mask)]
    parts[1], ready_three = lax.optimization_barrier((parts[1], ready_three))
    while mask > FAN:
        mask //= 2
        parts.append(swap(jnp.concatenate(parts, axis=0), "gx", devices, mask))
    held = jnp.concatenate(parts, axis=0)
    parts += fan([held] * FAN, devices)
    mine, theirs = output(parts, (ready_one, ready_two, ready_three), w_out, slots)
    return (mine + swap(theirs, "gy", 2, 1)).astype(jnp.bfloat16)


def solution(mesh):
    placed = (
        P(("groups", "gy"), "gx"),
        P("gx", "gy"),
        P("gx", "gy"),
        P("gx", "gy"),
        P("gy", "gx"),
        P(("groups", "gx"), "gy", None, None),
        P(("groups", "gx"), "gy", None, None),
        P(("groups", "gx")),
    )
    return jax.shard_map(
        functools.partial(body, mesh.shape["gx"]),
        mesh=mesh,
        in_specs=placed,
        out_specs=P(("groups", "gy"), "gx"),
        check_vma=False,
    )
```

```python
import functools
import math

import jax
import jax.numpy as jnp
from jax import lax
from jax.experimental import pallas as pl
from jax.experimental.pallas import tpu as pltpu
from jax.sharding import PartitionSpec as P

MODEL_WIDTH = 16384
LANES = 128
HEAD_SIZE = 128
CHUNK = 256
PIECES = 4
FAN = 4
MIB = 2**20


def bit_reverse(value, bits):
    turned = 0
    for bit in range(bits):
        turned = turned | (((value >> bit) & 1) << (bits - 1 - bit))
    return turned


def in_hbm(array):
    return pltpu.with_memory_space_constraint(array, pltpu.HBM)


def cut(start, size):
    if size % (16 * PIECES):
        return [(start, size)]
    return [(start + i * (size // PIECES), size // PIECES) for i in range(PIECES)]


def copies_in(src, dst, sems, start, size, offset):
    return [
        pltpu.make_async_copy(
            src.at[pl.ds(at, rows)], dst.at[pl.ds(at - start + offset, rows)], sems.at[i]
        )
        for i, (at, rows) in enumerate(cut(start, size))
    ]


def stage_kernel(parts, *refs):
    count = len(parts)
    sems = refs[-1]
    copies = []
    for i, (start, size) in enumerate(parts):
        copies += copies_in(refs[i], refs[count + i], sems.at[i], start, size, 0)
    for copy in copies:
        copy.start()
    return copies


def plain_stage_kernel(parts, *refs):
    for copy in stage_kernel(parts, *refs):
        copy.wait()


def turning_stage_kernel(parts, length_ref, frequency_ref, turn_ref, *refs):
    copies = stage_kernel(parts, *refs)
    position = length_ref[0].astype(jnp.float32)
    angle = position * frequency_ref[...]
    lane = lax.broadcasted_iota(jnp.int32, angle.shape, 1)
    sine = jnp.sin(angle)
    turn_ref[0:1, :] = jnp.cos(angle)
    turn_ref[1:2, :] = jnp.where(lane < HEAD_SIZE // 2, -sine, sine)
    turn_ref[2:3, :] = jnp.full(angle.shape, position)
    for copy in copies:
        copy.wait()


def stage(arrays, parts, lengths=None, frequency=None):
    shapes = tuple(
        jax.ShapeDtypeStruct((part[1], *a.shape[1:]), a.dtype) for a, part in zip(arrays, parts)
    )
    vmem = pl.BlockSpec(memory_space=pltpu.VMEM)
    in_specs = [pl.BlockSpec(memory_space=pltpu.HBM)] * len(arrays)
    out_specs = [vmem] * len(arrays)
    kernel = functools.partial(plain_stage_kernel, parts)
    pinned = [in_hbm(a) for a in arrays]
    out_shape = shapes
    if lengths is not None:
        count = len(arrays)

        def kernel(length_ref, frequency_ref, *refs):
            turn_ref = refs[count]
            turning_stage_kernel(
                parts, length_ref, frequency_ref, turn_ref, *refs[:count], *refs[count + 1 :]
            )

        in_specs = [pl.BlockSpec(memory_space=pltpu.SMEM), vmem] + in_specs
        out_specs = [vmem] + out_specs
        out_shape = (jax.ShapeDtypeStruct((8, HEAD_SIZE), jnp.float32), *shapes)
        pinned = [lengths, frequency] + pinned
    return pl.pallas_call(
        kernel,
        out_shape=out_shape,
        in_specs=in_specs,
        out_specs=tuple(out_specs),
        scratch_shapes=[pltpu.SemaphoreType.DMA((len(arrays), PIECES))],
        compiler_params=pltpu.CompilerParams(vmem_limit_bytes=16 * MIB),
        cost_estimate=pl.CostEstimate(
            flops=0, bytes_accessed=sum(2 * math.prod(x.shape) for x in shapes), transcendentals=0
        ),
        name="stage",
    )(*pinned)


def spread(depth, skip, chunk):
    ranges = [(at, min(chunk, depth - at)) for at in range(skip, depth, chunk)]
    if ranges and ranges[-1][1] >= 2 * LANES:
        start, size = ranges.pop()
        ranges += [(start, size - LANES), (start + size - LANES, LANES)]
    return ranges


def project_kernel(
    bits, rows_ref, other_ref, wq_hbm, first, wk, wv, *refs
):
    pieces, (wq, rows, sems) = refs[:FAN], refs[FAN:]
    skip = first.shape[0]
    ranges = spread(wq_hbm.shape[0], skip, CHUNK)
    copies = [
        copies_in(wq_hbm, wq, sems.at[i], start, size, start - skip)
        for i, (start, size) in enumerate(ranges)
    ]
    for group in copies:
        for copy in group:
            copy.start()

    slots = rows.shape[0]
    half = slots // 2
    turn = bit_reverse(lax.axis_index("gx"), bits)
    gy = lax.axis_index("gy")
    for ref, side in ((rows_ref, gy), (other_ref, 1 - gy)):
        block = ref[...].astype(jnp.float32)
        for t in range(half):
            slot = bit_reverse(t, bits) ^ turn ^ side
            rows[pl.ds(slot, 1), :] = block[t : t + 1, :]
    wide = rows[...]
    squares = jnp.sum(wide * wide, axis=1, keepdims=True)
    narrow = wide.astype(jnp.bfloat16)

    fresh = [jnp.dot(narrow, w[...], preferred_element_type=jnp.float32) for w in (wk, wv)]
    sums = jnp.dot(narrow[:, :skip], first[...], preferred_element_type=jnp.float32)
    for (start, size), group in zip(ranges, copies):
        for copy in group:
            copy.wait()
        sums = sums + jnp.dot(
            narrow[:, start : start + size],
            wq[start - skip : start - skip + size, :],
            preferred_element_type=jnp.float32,
        )

    total = pieces[0].shape[1]
    blocks = []
    for part in (sums, *fresh):
        blocks += [part[:, i : i + LANES] for i in range(0, part.shape[1], LANES)]
    blocks.append(jnp.broadcast_to(squares, (slots, LANES)))
    blocks += [jnp.zeros((slots, LANES), jnp.float32)] * (total - len(blocks))
    size = slots // FAN
    for at, ref in enumerate(pieces):
        flat = ref.reshape(size * total, LANES)
        for i, block in enumerate(blocks):
            flat[pl.ds(i, size, stride=total), :] = block[at * size : (at + 1) * size]


def project(rows, other, w_query, first, key_weight, value_weight, slots):
    bits = slots.bit_length() - 1
    depth, query_width = w_query.shape
    kv_width = key_weight.shape[1]
    used = (query_width + 2 * kv_width) // LANES + 1
    total = -(-used // 8) * 8
    skip = first.shape[0]
    piece = jax.ShapeDtypeStruct((slots // FAN, total, LANES), jnp.float32)
    hbm = pl.BlockSpec(memory_space=pltpu.HBM)
    whole = pl.BlockSpec(memory_space=pltpu.VMEM)
    return pl.pallas_call(
        functools.partial(project_kernel, bits),
        out_shape=(piece,) * FAN,
        in_specs=[whole, whole, hbm, whole, whole, whole],
        out_specs=(whole,) * FAN,
        scratch_shapes=[
            pltpu.VMEM((max(depth - skip, 16), query_width), jnp.bfloat16),
            pltpu.VMEM((slots, depth), jnp.float32),
            pltpu.SemaphoreType.DMA((max(1, len(spread(depth, skip, CHUNK))), PIECES)),
        ],
        compiler_params=pltpu.CompilerParams(vmem_limit_bytes=32 * MIB),
        cost_estimate=pl.CostEstimate(
            flops=2 * slots * depth * (query_width + 2 * kv_width),
            bytes_accessed=2 * depth * (query_width + 2 * kv_width),
            transcendentals=0,
        ),
        name="project",
    )(rows, other, in_hbm(w_query), first, key_weight, value_weight)


def attend_kernel(
    query_heads, kv_heads, pieces, turn_ref, k_ref, v_ref, *refs
):
    heads_ref = refs[pieces]
    total = refs[0][0]
    for ref in refs[1:pieces]:
        total = total + ref[0]
    at = query_heads + 2 * kv_heads
    scale = lax.rsqrt(total[at : at + 1, :] / MODEL_WIDTH + 1e-05)
    turned = total[: query_heads + kv_heads] * scale
    half = HEAD_SIZE // 2
    swapped = jnp.concatenate([turned[:, half:], turned[:, :half]], axis=1)
    turned = (turned * turn_ref[0:1, :] + swapped * turn_ref[1:2, :]).astype(jnp.bfloat16)
    fresh_values = (total[query_heads + kv_heads : at] * scale).astype(jnp.bfloat16)
    group = query_heads // kv_heads
    factor = 1.0 / math.sqrt(HEAD_SIZE)
    length = turn_ref[2:3, 0:1].astype(jnp.int32)
    for head in range(kv_heads):
        queries = turned[head * group : (head + 1) * group]
        fresh_key = turned[query_heads + head : query_heads + head + 1].astype(jnp.float32)
        own = jnp.sum(queries.astype(jnp.float32) * fresh_key, axis=1, keepdims=True) * factor
        scores = (
            lax.dot_general(
                queries,
                k_ref[0, head],
                (((1,), (1,)), ((), ())),
                preferred_element_type=jnp.float32,
            )
            * factor
        )
        slot = lax.broadcasted_iota(jnp.int32, scores.shape, 1)
        scores = jnp.where(slot < length, scores, -jnp.inf)
        top = jnp.maximum(jnp.max(scores, axis=1, keepdims=True), own)
        exponent = jnp.exp(scores - top)
        own_exp = jnp.exp(own - top)
        share = 1.0 / (jnp.sum(exponent, axis=1, keepdims=True) + own_exp)
        weights = (exponent * share).astype(jnp.bfloat16)
        own_weight = (own_exp * share).astype(jnp.bfloat16)
        mixed = jnp.dot(weights, v_ref[0, head], preferred_element_type=jnp.float32)
        mixed = mixed + own_weight.astype(jnp.float32) * fresh_values[head : head + 1].astype(
            jnp.float32
        )
        heads_ref[0, pl.ds(head * group, group), :] = mixed.astype(jnp.bfloat16)


def attend(parts, turn, k_cache, value_cache, query_heads):
    kv_heads, cache_len = k_cache.shape[1:3]
    whole = pl.BlockSpec(memory_space=pltpu.VMEM)
    return pl.pallas_call(
        functools.partial(attend_kernel, query_heads, kv_heads, len(parts)),
        out_shape=jax.ShapeDtypeStruct((1, query_heads, HEAD_SIZE), jnp.bfloat16),
        in_specs=[whole] * (3 + len(parts)),
        out_specs=whole,
        compiler_params=pltpu.CompilerParams(vmem_limit_bytes=12 * MIB),
        cost_estimate=pl.CostEstimate(
            flops=4 * query_heads * cache_len * HEAD_SIZE,
            bytes_accessed=4 * kv_heads * cache_len * HEAD_SIZE,
            transcendentals=query_heads * cache_len,
        ),
        name="attend",
    )(turn, k_cache, value_cache, *parts)


def output_kernel(bits, pieces, staged, *refs):
    parts = refs[:pieces]
    ready = refs[pieces : pieces + staged]
    w_hbm, mine_ref, theirs_ref, rest, flat, left, sums, sems = refs[pieces + staged :]
    skip = sum(ref.shape[0] for ref in ready)
    ranges = spread(w_hbm.shape[0], skip, 2 * CHUNK)
    copies = [
        copies_in(w_hbm, rest, sems.at[i], start, size, start - skip)
        for i, (start, size) in enumerate(ranges)
    ]
    for group in copies:
        for copy in group:
            copy.start()
    slots = left.shape[0]
    heads = flat.shape[0] // slots
    at = 0
    for ref in parts:
        for i in range(ref.shape[0]):
            flat[at : at + heads, :] = ref[i].astype(jnp.float32)
            at += heads
    for head in range(heads):
        left[:, head * HEAD_SIZE : (head + 1) * HEAD_SIZE] = flat[
            pl.ds(head, slots, stride=heads), :
        ].astype(jnp.bfloat16)
    total = None
    at = 0
    for ref in ready:
        size = ref.shape[0]
        term = jnp.dot(left[:, at : at + size], ref[...], preferred_element_type=jnp.float32)
        total = term if total is None else total + term
        at += size
    for (start, size), group in zip(ranges, copies):
        for copy in group:
            copy.wait()
        term = jnp.dot(
            left[:, start : start + size],
            rest[start - skip : start - skip + size, :],
            preferred_element_type=jnp.float32,
        )
        total = term if total is None else total + term
    sums[...] = total
    half = slots // 2
    turn = bit_reverse(lax.axis_index("gx"), bits)
    gy = lax.axis_index("gy")
    for ref, side in ((mine_ref, gy), (theirs_ref, 1 - gy)):
        for t in range(half):
            slot = bit_reverse(t, bits) ^ turn ^ side
            ref[t : t + 1, :] = sums[pl.ds(slot, 1), :]


def output(parts, ready, w_out, slots):
    bits = slots.bit_length() - 1
    depth, width = w_out.shape
    heads = depth // HEAD_SIZE
    skip = sum(x.shape[0] for x in ready)
    whole = pl.BlockSpec(memory_space=pltpu.VMEM)
    piece = jax.ShapeDtypeStruct((slots // 2, width), jnp.float32)
    return pl.pallas_call(
        functools.partial(output_kernel, bits, len(parts), len(ready)),
        out_shape=(piece, piece),
        in_specs=[whole] * (len(parts) + len(ready)) + [pl.BlockSpec(memory_space=pltpu.HBM)],
        out_specs=(whole, whole),
        scratch_shapes=[
            pltpu.VMEM((max(depth - skip, 16), width), jnp.bfloat16),
            pltpu.VMEM((slots * heads, HEAD_SIZE), jnp.float32),
            pltpu.VMEM((slots, depth), jnp.bfloat16),
            pltpu.VMEM((slots, width), jnp.float32),
            pltpu.SemaphoreType.DMA((max(1, len(spread(depth, skip, 2 * CHUNK))), PIECES)),
        ],
        compiler_params=pltpu.CompilerParams(vmem_limit_bytes=24 * MIB),
        cost_estimate=pl.CostEstimate(
            flops=2 * slots * depth * width, bytes_accessed=2 * depth * width, transcendentals=0
        ),
        name="output",
    )(*parts, *ready, in_hbm(w_out))


def swap(block, axis, devices, mask):
    return lax.ppermute(block, axis, [(i, i ^ mask) for i in range(devices)])


def fan(pieces, devices):
    masks = [bit_reverse(q, 2) for q in range(FAN)]
    arrived = [None] * FAN
    for q in sorted(range(1, FAN), key=lambda q: (masks[q] + 1) % FAN):
        arrived[q] = swap(pieces[q], "gx", devices, masks[q])
    return arrived[1:]


def body(devices, activations, w_query, key_weight, value_weight, w_out, k_cache, value_cache, lengths):
    slots = devices
    query_heads = w_query.shape[1] // HEAD_SIZE
    other = swap(activations, "gy", 2, 1)
    depth = w_query.shape[0]
    first, key_weight, value_weight = stage(
        (w_query, key_weight, value_weight), ((0, min(CHUNK, depth)), (0, depth), (0, depth))
    )
    pieces = project(activations, other, w_query, first, key_weight, value_weight, slots)

    rows_out = w_out.shape[0]
    *pieces, w_out = lax.optimization_barrier((*pieces, w_out))
    few, most = rows_out // 8, rows_out // 4
    arrived = fan(pieces, devices)
    half = HEAD_SIZE // 2
    frequency = jnp.power(
        jnp.float32(500000.0), -2.0 * jnp.arange(half, dtype=jnp.float32) / HEAD_SIZE
    )
    frequency = jnp.concatenate([frequency, frequency])[None, :]
    turn, k_cache, value_cache, ready_one = stage(
        (k_cache, value_cache, w_out),
        ((0, k_cache.shape[0]), (0, value_cache.shape[0]), (0, few)),
        lengths,
        frequency,
    )
    total = pieces[0] + (arrived[2] + (arrived[1] + arrived[0]))
    mask = FAN
    while total.shape[0] > 2:
        rest = total.shape[0] // 2
        total = total[:rest] + swap(total[rest:], "gx", devices, mask)
        mask *= 2
    total, w_out, k_cache, value_cache, ready_one = lax.optimization_barrier(
        (total, w_out, k_cache, value_cache, ready_one)
    )
    (ready_two,) = stage((w_out,), ((few, most),))
    parts = [total[:1], swap(total[1:], "gx", devices, mask)]
    parts[1], ready_two = lax.optimization_barrier((parts[1], ready_two))
    heads = attend(parts, turn, k_cache, value_cache, query_heads)

    heads, w_out = lax.optimization_barrier((heads, w_out))
    (ready_three,) = stage((w_out,), ((few + most, most),))
    parts = [heads, swap(heads, "gx", devices, mask)]
    parts[1], ready_three = lax.optimization_barrier((parts[1], ready_three))
    while mask > FAN:
        mask //= 2
        parts.append(swap(jnp.concatenate(parts, axis=0), "gx", devices, mask))
    held = jnp.concatenate(parts, axis=0)
    parts += fan([held] * FAN, devices)
    mine, theirs = output(parts, (ready_one, ready_two, ready_three), w_out, slots)
    return (mine + swap(theirs, "gy", 2, 1)).astype(jnp.bfloat16)


def solution(mesh):
    placed = (
        P(("groups", "gy"), "gx"),
        P("gx", "gy"),
        P("gx", "gy"),
        P("gx", "gy"),
        P("gy", "gx"),
        P(("groups", "gx"), "gy", None, None),
        P(("groups", "gx"), "gy", None, None),
        P(("groups", "gx")),
    )
    return jax.shard_map(
        functools.partial(body, mesh.shape["gx"]),
        mesh=mesh,
        in_specs=placed,
        out_specs=P(("groups", "gy"), "gx"),
        check_vma=False,
    )
```

```python
import functools
import math

import jax
import jax.numpy as jnp
from jax import lax
from jax.experimental import pallas as pl
from jax.experimental.pallas import tpu as pltpu
from jax.sharding import PartitionSpec as P

MODEL_WIDTH = 16384
LANES = 128
HEAD_SIZE = 128
CHUNK = 256
FIRST = 256
PIECES = 4
FAN = 4
MIB = 2**20


def bit_reverse(value, bits):
    turned = 0
    for bit in range(bits):
        turned = turned | (((value >> bit) & 1) << (bits - 1 - bit))
    return turned


def in_hbm(array):
    return pltpu.with_memory_space_constraint(array, pltpu.HBM)


def cut(start, size):
    if size % (16 * PIECES):
        return [(start, size)]
    return [(start + i * (size // PIECES), size // PIECES) for i in range(PIECES)]


def copies_in(src, dst, sems, start, size, offset):
    return [
        pltpu.make_async_copy(
            src.at[pl.ds(at, rows)], dst.at[pl.ds(at - start + offset, rows)], sems.at[i]
        )
        for i, (at, rows) in enumerate(cut(start, size))
    ]


def stage_kernel(parts, *refs):
    count = len(parts)
    sems = refs[-1]
    copies = []
    for i, (start, size) in enumerate(parts):
        copies += copies_in(refs[i], refs[count + i], sems.at[i], start, size, 0)
    for copy in copies:
        copy.start()
    return copies


def plain_stage_kernel(parts, *refs):
    for copy in stage_kernel(parts, *refs):
        copy.wait()


def turning_stage_kernel(parts, length_ref, frequency_ref, turn_ref, *refs):
    copies = stage_kernel(parts, *refs)
    position = length_ref[0].astype(jnp.float32)
    angle = position * frequency_ref[...]
    lane = lax.broadcasted_iota(jnp.int32, angle.shape, 1)
    sine = jnp.sin(angle)
    turn_ref[0:1, :] = jnp.cos(angle)
    turn_ref[1:2, :] = jnp.where(lane < HEAD_SIZE // 2, -sine, sine)
    turn_ref[2:3, :] = jnp.full(angle.shape, position)
    for copy in copies:
        copy.wait()


def stage(arrays, parts, lengths=None, frequency=None):
    shapes = tuple(
        jax.ShapeDtypeStruct((part[1], *a.shape[1:]), a.dtype) for a, part in zip(arrays, parts)
    )
    vmem = pl.BlockSpec(memory_space=pltpu.VMEM)
    in_specs = [pl.BlockSpec(memory_space=pltpu.HBM)] * len(arrays)
    out_specs = [vmem] * len(arrays)
    kernel = functools.partial(plain_stage_kernel, parts)
    pinned = [in_hbm(a) for a in arrays]
    out_shape = shapes
    if lengths is not None:
        count = len(arrays)

        def kernel(length_ref, frequency_ref, *refs):
            turn_ref = refs[count]
            turning_stage_kernel(
                parts, length_ref, frequency_ref, turn_ref, *refs[:count], *refs[count + 1 :]
            )

        in_specs = [pl.BlockSpec(memory_space=pltpu.SMEM), vmem] + in_specs
        out_specs = [vmem] + out_specs
        out_shape = (jax.ShapeDtypeStruct((8, HEAD_SIZE), jnp.float32), *shapes)
        pinned = [lengths, frequency] + pinned
    return pl.pallas_call(
        kernel,
        out_shape=out_shape,
        in_specs=in_specs,
        out_specs=tuple(out_specs),
        scratch_shapes=[pltpu.SemaphoreType.DMA((len(arrays), PIECES))],
        compiler_params=pltpu.CompilerParams(vmem_limit_bytes=16 * MIB),
        cost_estimate=pl.CostEstimate(
            flops=0, bytes_accessed=sum(2 * math.prod(x.shape) for x in shapes), transcendentals=0
        ),
        name="stage",
    )(*pinned)


def spread(depth, skip, chunk):
    ranges = [(at, min(chunk, depth - at)) for at in range(skip, depth, chunk)]
    if ranges and ranges[-1][1] >= 2 * LANES:
        start, size = ranges.pop()
        ranges += [(start, size - LANES), (start + size - LANES, LANES)]
    return ranges


def project_kernel(
    bits, rows_ref, other_ref, wq_hbm, first, wk, wv, *refs
):
    pieces, (wq, rows, sems) = refs[:FAN], refs[FAN:]
    skip = first.shape[0]
    ranges = spread(wq_hbm.shape[0], skip, CHUNK)
    copies = [
        copies_in(wq_hbm, wq, sems.at[i], start, size, start - skip)
        for i, (start, size) in enumerate(ranges)
    ]
    for group in copies:
        for copy in group:
            copy.start()

    slots = rows.shape[0]
    half = slots // 2
    turn = bit_reverse(lax.axis_index("gx"), bits)
    gy = lax.axis_index("gy")
    for ref, side in ((rows_ref, gy), (other_ref, 1 - gy)):
        block = ref[...].astype(jnp.float32)
        for t in range(half):
            slot = bit_reverse(t, bits) ^ turn ^ side
            rows[pl.ds(slot, 1), :] = block[t : t + 1, :]
    wide = rows[...]
    squares = jnp.sum(wide * wide, axis=1, keepdims=True)
    narrow = wide.astype(jnp.bfloat16)

    fresh = [jnp.dot(narrow, w[...], preferred_element_type=jnp.float32) for w in (wk, wv)]
    sums = jnp.dot(narrow[:, :skip], first[...], preferred_element_type=jnp.float32)
    for (start, size), group in zip(ranges, copies):
        for copy in group:
            copy.wait()
        sums = sums + jnp.dot(
            narrow[:, start : start + size],
            wq[start - skip : start - skip + size, :],
            preferred_element_type=jnp.float32,
        )

    total = pieces[0].shape[1]
    blocks = []
    for part in (sums, *fresh):
        blocks += [part[:, i : i + LANES] for i in range(0, part.shape[1], LANES)]
    blocks.append(jnp.broadcast_to(squares, (slots, LANES)))
    blocks += [jnp.zeros((slots, LANES), jnp.float32)] * (total - len(blocks))
    size = slots // FAN
    for at, ref in enumerate(pieces):
        flat = ref.reshape(size * total, LANES)
        for i, block in enumerate(blocks):
            flat[pl.ds(i, size, stride=total), :] = block[at * size : (at + 1) * size]


def project(rows, other, w_query, first, key_weight, value_weight, slots):
    bits = slots.bit_length() - 1
    depth, query_width = w_query.shape
    kv_width = key_weight.shape[1]
    used = (query_width + 2 * kv_width) // LANES + 1
    total = -(-used // 8) * 8
    skip = first.shape[0]
    piece = jax.ShapeDtypeStruct((slots // FAN, total, LANES), jnp.float32)
    hbm = pl.BlockSpec(memory_space=pltpu.HBM)
    whole = pl.BlockSpec(memory_space=pltpu.VMEM)
    return pl.pallas_call(
        functools.partial(project_kernel, bits),
        out_shape=(piece,) * FAN,
        in_specs=[whole, whole, hbm, whole, whole, whole],
        out_specs=(whole,) * FAN,
        scratch_shapes=[
            pltpu.VMEM((max(depth - skip, 16), query_width), jnp.bfloat16),
            pltpu.VMEM((slots, depth), jnp.float32),
            pltpu.SemaphoreType.DMA((max(1, len(spread(depth, skip, CHUNK))), PIECES)),
        ],
        compiler_params=pltpu.CompilerParams(vmem_limit_bytes=32 * MIB),
        cost_estimate=pl.CostEstimate(
            flops=2 * slots * depth * (query_width + 2 * kv_width),
            bytes_accessed=2 * depth * (query_width + 2 * kv_width),
            transcendentals=0,
        ),
        name="project",
    )(rows, other, in_hbm(w_query), first, key_weight, value_weight)


def attend_kernel(
    query_heads, kv_heads, pieces, turn_ref, k_ref, v_ref, *refs
):
    heads_ref = refs[pieces]
    total = refs[0][0]
    for ref in refs[1:pieces]:
        total = total + ref[0]
    at = query_heads + 2 * kv_heads
    scale = lax.rsqrt(total[at : at + 1, :] / MODEL_WIDTH + 1e-05)
    turned = total[: query_heads + kv_heads] * scale
    half = HEAD_SIZE // 2
    swapped = jnp.concatenate([turned[:, half:], turned[:, :half]], axis=1)
    turned = (turned * turn_ref[0:1, :] + swapped * turn_ref[1:2, :]).astype(jnp.bfloat16)
    fresh_values = (total[query_heads + kv_heads : at] * scale).astype(jnp.bfloat16)
    group = query_heads // kv_heads
    factor = 1.0 / math.sqrt(HEAD_SIZE)
    length = turn_ref[2:3, 0:1].astype(jnp.int32)
    for head in range(kv_heads):
        queries = turned[head * group : (head + 1) * group]
        fresh_key = turned[query_heads + head : query_heads + head + 1].astype(jnp.float32)
        own = jnp.sum(queries.astype(jnp.float32) * fresh_key, axis=1, keepdims=True) * factor
        scores = (
            lax.dot_general(
                queries,
                k_ref[0, head],
                (((1,), (1,)), ((), ())),
                preferred_element_type=jnp.float32,
            )
            * factor
        )
        slot = lax.broadcasted_iota(jnp.int32, scores.shape, 1)
        scores = jnp.where(slot < length, scores, -jnp.inf)
        top = jnp.maximum(jnp.max(scores, axis=1, keepdims=True), own)
        exponent = jnp.exp(scores - top)
        own_exp = jnp.exp(own - top)
        share = 1.0 / (jnp.sum(exponent, axis=1, keepdims=True) + own_exp)
        weights = (exponent * share).astype(jnp.bfloat16)
        own_weight = (own_exp * share).astype(jnp.bfloat16)
        mixed = jnp.dot(weights, v_ref[0, head], preferred_element_type=jnp.float32)
        mixed = mixed + own_weight.astype(jnp.float32) * fresh_values[head : head + 1].astype(
            jnp.float32
        )
        heads_ref[0, pl.ds(head * group, group), :] = mixed.astype(jnp.bfloat16)


def attend(parts, turn, k_cache, value_cache, query_heads):
    kv_heads, cache_len = k_cache.shape[1:3]
    whole = pl.BlockSpec(memory_space=pltpu.VMEM)
    return pl.pallas_call(
        functools.partial(attend_kernel, query_heads, kv_heads, len(parts)),
        out_shape=jax.ShapeDtypeStruct((1, query_heads, HEAD_SIZE), jnp.bfloat16),
        in_specs=[whole] * (3 + len(parts)),
        out_specs=whole,
        compiler_params=pltpu.CompilerParams(vmem_limit_bytes=12 * MIB),
        cost_estimate=pl.CostEstimate(
            flops=4 * query_heads * cache_len * HEAD_SIZE,
            bytes_accessed=4 * kv_heads * cache_len * HEAD_SIZE,
            transcendentals=query_heads * cache_len,
        ),
        name="attend",
    )(turn, k_cache, value_cache, *parts)


def output_kernel(bits, pieces, staged, *refs):
    parts = refs[:pieces]
    ready = refs[pieces : pieces + staged]
    w_hbm, mine_ref, theirs_ref, rest, flat, left, sums, sems = refs[pieces + staged :]
    skip = sum(ref.shape[0] for ref in ready)
    ranges = spread(w_hbm.shape[0], skip, 2 * CHUNK)
    copies = [
        copies_in(w_hbm, rest, sems.at[i], start, size, start - skip)
        for i, (start, size) in enumerate(ranges)
    ]
    for group in copies:
        for copy in group:
            copy.start()
    slots = left.shape[0]
    heads = flat.shape[0] // slots
    at = 0
    for ref in parts:
        for i in range(ref.shape[0]):
            flat[at : at + heads, :] = ref[i].astype(jnp.float32)
            at += heads
    for head in range(heads):
        left[:, head * HEAD_SIZE : (head + 1) * HEAD_SIZE] = flat[
            pl.ds(head, slots, stride=heads), :
        ].astype(jnp.bfloat16)
    total = None
    at = 0
    for ref in ready:
        size = ref.shape[0]
        term = jnp.dot(left[:, at : at + size], ref[...], preferred_element_type=jnp.float32)
        total = term if total is None else total + term
        at += size
    for (start, size), group in zip(ranges, copies):
        for copy in group:
            copy.wait()
        term = jnp.dot(
            left[:, start : start + size],
            rest[start - skip : start - skip + size, :],
            preferred_element_type=jnp.float32,
        )
        total = term if total is None else total + term
    sums[...] = total
    half = slots // 2
    turn = bit_reverse(lax.axis_index("gx"), bits)
    gy = lax.axis_index("gy")
    for ref, side in ((mine_ref, gy), (theirs_ref, 1 - gy)):
        for t in range(half):
            slot = bit_reverse(t, bits) ^ turn ^ side
            ref[t : t + 1, :] = sums[pl.ds(slot, 1), :]


def output(parts, ready, w_out, slots):
    bits = slots.bit_length() - 1
    depth, width = w_out.shape
    heads = depth // HEAD_SIZE
    skip = sum(x.shape[0] for x in ready)
    whole = pl.BlockSpec(memory_space=pltpu.VMEM)
    piece = jax.ShapeDtypeStruct((slots // 2, width), jnp.float32)
    return pl.pallas_call(
        functools.partial(output_kernel, bits, len(parts), len(ready)),
        out_shape=(piece, piece),
        in_specs=[whole] * (len(parts) + len(ready)) + [pl.BlockSpec(memory_space=pltpu.HBM)],
        out_specs=(whole, whole),
        scratch_shapes=[
            pltpu.VMEM((max(depth - skip, 16), width), jnp.bfloat16),
            pltpu.VMEM((slots * heads, HEAD_SIZE), jnp.float32),
            pltpu.VMEM((slots, depth), jnp.bfloat16),
            pltpu.VMEM((slots, width), jnp.float32),
            pltpu.SemaphoreType.DMA((max(1, len(spread(depth, skip, 2 * CHUNK))), PIECES)),
        ],
        compiler_params=pltpu.CompilerParams(vmem_limit_bytes=24 * MIB),
        cost_estimate=pl.CostEstimate(
            flops=2 * slots * depth * width, bytes_accessed=2 * depth * width, transcendentals=0
        ),
        name="output",
    )(*parts, *ready, in_hbm(w_out))


def swap(block, axis, devices, mask):
    return lax.ppermute(block, axis, [(i, i ^ mask) for i in range(devices)])


def fan(pieces, devices):
    masks = [bit_reverse(q, 2) for q in range(FAN)]
    arrived = [None] * FAN
    for q in sorted(range(1, FAN), key=lambda q: (masks[q] + 1) % FAN):
        arrived[q] = swap(pieces[q], "gx", devices, masks[q])
    return arrived[1:]


def body(devices, activations, w_query, key_weight, value_weight, w_out, k_cache, value_cache, lengths):
    slots = devices
    query_heads = w_query.shape[1] // HEAD_SIZE
    other = swap(activations, "gy", 2, 1)
    depth = w_query.shape[0]
    (first,) = stage((w_query,), ((0, min(FIRST, depth)),))
    pieces = project(activations, other, w_query, first, key_weight, value_weight, slots)

    rows_out = w_out.shape[0]
    *pieces, w_out = lax.optimization_barrier((*pieces, w_out))
    few, most = rows_out // 8, rows_out // 4
    arrived = fan(pieces, devices)
    half = HEAD_SIZE // 2
    frequency = jnp.power(
        jnp.float32(500000.0), -2.0 * jnp.arange(half, dtype=jnp.float32) / HEAD_SIZE
    )
    frequency = jnp.concatenate([frequency, frequency])[None, :]
    turn, ready_one = stage((w_out,), ((0, few),), lengths, frequency)
    total = pieces[0] + (arrived[2] + (arrived[1] + arrived[0]))
    mask = FAN
    while total.shape[0] > 2:
        rest = total.shape[0] // 2
        total = total[:rest] + swap(total[rest:], "gx", devices, mask)
        mask *= 2
    total, w_out, ready_one = lax.optimization_barrier((total, w_out, ready_one))
    (ready_two,) = stage((w_out,), ((few, most),))
    parts = [total[:1], swap(total[1:], "gx", devices, mask)]
    parts[1], ready_two = lax.optimization_barrier((parts[1], ready_two))
    heads = attend(parts, turn, k_cache, value_cache, query_heads)

    heads, w_out = lax.optimization_barrier((heads, w_out))
    (ready_three,) = stage((w_out,), ((few + most, most),))
    parts = [heads, swap(heads, "gx", devices, mask)]
    parts[1], ready_three = lax.optimization_barrier((parts[1], ready_three))
    while mask > FAN:
        mask //= 2
        parts.append(swap(jnp.concatenate(parts, axis=0), "gx", devices, mask))
    held = jnp.concatenate(parts, axis=0)
    held, w_out = lax.optimization_barrier((held, w_out))
    (ready_four,) = stage((w_out,), ((few + 2 * most, most),))
    parts += fan([held] * FAN, devices)
    parts[-1], ready_four = lax.optimization_barrier((parts[-1], ready_four))
    ready = (ready_one, ready_two, ready_three, ready_four)
    mine, theirs = output(parts, ready, w_out, slots)
    return (mine + swap(theirs, "gy", 2, 1)).astype(jnp.bfloat16)


def solution(mesh):
    placed = (
        P(("groups", "gy"), "gx"),
        P("gx", "gy"),
        P("gx", "gy"),
        P("gx", "gy"),
        P("gy", "gx"),
        P(("groups", "gx"), "gy", None, None),
        P(("groups", "gx"), "gy", None, None),
        P(("groups", "gx")),
    )
    return jax.shard_map(
        functools.partial(body, mesh.shape["gx"]),
        mesh=mesh,
        in_specs=placed,
        out_specs=P(("groups", "gy"), "gx"),
        check_vma=False,
    )
```

```python
import functools
import math

import jax
import jax.numpy as jnp
from jax import lax
from jax.experimental import pallas as pl
from jax.experimental.pallas import tpu as pltpu
from jax.sharding import PartitionSpec as P

MODEL_WIDTH = 16384
LANES = 128
HEAD_SIZE = 128
CHUNK = 256
FIRST = 256
PIECES = 4
FAN = 4
MIB = 2**20


def bit_reverse(value, bits):
    turned = 0
    for bit in range(bits):
        turned = turned | (((value >> bit) & 1) << (bits - 1 - bit))
    return turned


def in_hbm(array):
    return pltpu.with_memory_space_constraint(array, pltpu.HBM)


def cut(start, size):
    if size % (16 * PIECES):
        return [(start, size)]
    return [(start + i * (size // PIECES), size // PIECES) for i in range(PIECES)]


def copies_in(src, dst, sems, start, size, offset):
    return [
        pltpu.make_async_copy(
            src.at[pl.ds(at, rows)], dst.at[pl.ds(at - start + offset, rows)], sems.at[i]
        )
        for i, (at, rows) in enumerate(cut(start, size))
    ]


def stage_kernel(rows, src, dst, sems):
    copies = copies_in(src, dst, sems, 0, rows, 0)
    for copy in copies:
        copy.start()
    for copy in copies:
        copy.wait()


def stage_rows(array, rows):
    vmem = pl.BlockSpec(memory_space=pltpu.VMEM)
    return pl.pallas_call(
        functools.partial(stage_kernel, rows),
        out_shape=jax.ShapeDtypeStruct((rows, array.shape[1]), array.dtype),
        in_specs=[pl.BlockSpec(memory_space=pltpu.HBM)],
        out_specs=vmem,
        scratch_shapes=[pltpu.SemaphoreType.DMA((PIECES,))],
        compiler_params=pltpu.CompilerParams(vmem_limit_bytes=16 * MIB),
        cost_estimate=pl.CostEstimate(
            flops=0, bytes_accessed=2 * rows * array.shape[1], transcendentals=0
        ),
        name="stage",
    )(in_hbm(array))


def turning_kernel(length_ref, frequency_ref, beside_ref, turn_ref):
    position = length_ref[0].astype(jnp.float32)
    angle = position * frequency_ref[...]
    lane = lax.broadcasted_iota(jnp.int32, angle.shape, 1)
    sine = jnp.sin(angle)
    turn_ref[0:1, :] = jnp.cos(angle)
    turn_ref[1:2, :] = jnp.where(lane < HEAD_SIZE // 2, -sine, sine)
    turn_ref[2:3, :] = jnp.full(angle.shape, position)


def turning(lengths, frequency, beside):
    vmem = pl.BlockSpec(memory_space=pltpu.VMEM)
    return pl.pallas_call(
        turning_kernel,
        out_shape=jax.ShapeDtypeStruct((8, HEAD_SIZE), jnp.float32),
        in_specs=[
            pl.BlockSpec(memory_space=pltpu.SMEM),
            vmem,
            pl.BlockSpec(memory_space=pltpu.HBM),
        ],
        out_specs=vmem,
        cost_estimate=pl.CostEstimate(flops=0, bytes_accessed=2 * beside.size, transcendentals=256),
        name="turning",
    )(lengths, frequency, in_hbm(beside))


def spread(depth, skip, chunk):
    ranges = [(at, min(chunk, depth - at)) for at in range(skip, depth, chunk)]
    if ranges and ranges[-1][1] >= 2 * LANES:
        start, size = ranges.pop()
        ranges += [(start, size - LANES), (start + size - LANES, LANES)]
    return ranges


def project_kernel(
    bits, rows_ref, other_ref, wq_hbm, first, wk, wv, *refs
):
    pieces, (wq, rows, sems) = refs[:FAN], refs[FAN:]
    skip = first.shape[0]
    ranges = spread(wq_hbm.shape[0], skip, CHUNK)
    copies = [
        copies_in(wq_hbm, wq, sems.at[i], start, size, start - skip)
        for i, (start, size) in enumerate(ranges)
    ]
    for group in copies:
        for copy in group:
            copy.start()

    slots = rows.shape[0]
    half = slots // 2
    turn = bit_reverse(lax.axis_index("gx"), bits)
    gy = lax.axis_index("gy")
    for ref, side in ((rows_ref, gy), (other_ref, 1 - gy)):
        block = ref[...].astype(jnp.float32)
        for t in range(half):
            slot = bit_reverse(t, bits) ^ turn ^ side
            rows[pl.ds(slot, 1), :] = block[t : t + 1, :]
    wide = rows[...]
    squares = jnp.sum(wide * wide, axis=1, keepdims=True)
    narrow = wide.astype(jnp.bfloat16)

    fresh = [jnp.dot(narrow, w[...], preferred_element_type=jnp.float32) for w in (wk, wv)]
    sums = jnp.dot(narrow[:, :skip], first[...], preferred_element_type=jnp.float32)
    for (start, size), group in zip(ranges, copies):
        for copy in group:
            copy.wait()
        sums = sums + jnp.dot(
            narrow[:, start : start + size],
            wq[start - skip : start - skip + size, :],
            preferred_element_type=jnp.float32,
        )

    total = pieces[0].shape[1]
    blocks = []
    for part in (sums, *fresh):
        blocks += [part[:, i : i + LANES] for i in range(0, part.shape[1], LANES)]
    blocks.append(jnp.broadcast_to(squares, (slots, LANES)))
    blocks += [jnp.zeros((slots, LANES), jnp.float32)] * (total - len(blocks))
    size = slots // FAN
    for at, ref in enumerate(pieces):
        flat = ref.reshape(size * total, LANES)
        for i, block in enumerate(blocks):
            flat[pl.ds(i, size, stride=total), :] = block[at * size : (at + 1) * size]


def project(rows, other, w_query, first, key_weight, value_weight, slots):
    bits = slots.bit_length() - 1
    depth, query_width = w_query.shape
    kv_width = key_weight.shape[1]
    used = (query_width + 2 * kv_width) // LANES + 1
    total = -(-used // 8) * 8
    skip = first.shape[0]
    piece = jax.ShapeDtypeStruct((slots // FAN, total, LANES), jnp.float32)
    hbm = pl.BlockSpec(memory_space=pltpu.HBM)
    whole = pl.BlockSpec(memory_space=pltpu.VMEM)
    return pl.pallas_call(
        functools.partial(project_kernel, bits),
        out_shape=(piece,) * FAN,
        in_specs=[whole, whole, hbm, whole, whole, whole],
        out_specs=(whole,) * FAN,
        scratch_shapes=[
            pltpu.VMEM((max(depth - skip, 16), query_width), jnp.bfloat16),
            pltpu.VMEM((slots, depth), jnp.float32),
            pltpu.SemaphoreType.DMA((max(1, len(spread(depth, skip, CHUNK))), PIECES)),
        ],
        compiler_params=pltpu.CompilerParams(vmem_limit_bytes=46 * MIB),
        cost_estimate=pl.CostEstimate(
            flops=2 * slots * depth * (query_width + 2 * kv_width),
            bytes_accessed=2 * depth * (query_width + 2 * kv_width),
            transcendentals=0,
        ),
        name="project",
    )(rows, other, in_hbm(w_query), first, key_weight, value_weight)


def attend_kernel(
    query_heads, kv_heads, pieces, beside_ref, turn_ref, k_ref, v_ref, *refs
):
    heads_ref = refs[pieces]
    total = refs[0][0]
    for ref in refs[1:pieces]:
        total = total + ref[0]
    at = query_heads + 2 * kv_heads
    scale = lax.rsqrt(total[at : at + 1, :] / MODEL_WIDTH + 1e-05)
    turned = total[: query_heads + kv_heads] * scale
    half = HEAD_SIZE // 2
    swapped = jnp.concatenate([turned[:, half:], turned[:, :half]], axis=1)
    turned = (turned * turn_ref[0:1, :] + swapped * turn_ref[1:2, :]).astype(jnp.bfloat16)
    fresh_values = (total[query_heads + kv_heads : at] * scale).astype(jnp.bfloat16)
    group = query_heads // kv_heads
    factor = 1.0 / math.sqrt(HEAD_SIZE)
    length = turn_ref[2:3, 0:1].astype(jnp.int32)
    for head in range(kv_heads):
        queries = turned[head * group : (head + 1) * group]
        fresh_key = turned[query_heads + head : query_heads + head + 1].astype(jnp.float32)
        own = jnp.sum(queries.astype(jnp.float32) * fresh_key, axis=1, keepdims=True) * factor
        scores = (
            lax.dot_general(
                queries,
                k_ref[0, head],
                (((1,), (1,)), ((), ())),
                preferred_element_type=jnp.float32,
            )
            * factor
        )
        slot = lax.broadcasted_iota(jnp.int32, scores.shape, 1)
        scores = jnp.where(slot < length, scores, -jnp.inf)
        top = jnp.maximum(jnp.max(scores, axis=1, keepdims=True), own)
        exponent = jnp.exp(scores - top)
        own_exp = jnp.exp(own - top)
        share = 1.0 / (jnp.sum(exponent, axis=1, keepdims=True) + own_exp)
        weights = (exponent * share).astype(jnp.bfloat16)
        own_weight = (own_exp * share).astype(jnp.bfloat16)
        mixed = jnp.dot(weights, v_ref[0, head], preferred_element_type=jnp.float32)
        mixed = mixed + own_weight.astype(jnp.float32) * fresh_values[head : head + 1].astype(
            jnp.float32
        )
        heads_ref[0, pl.ds(head * group, group), :] = mixed.astype(jnp.bfloat16)


def attend(parts, turn, k_cache, value_cache, query_heads, beside):
    kv_heads, cache_len = k_cache.shape[1:3]
    whole = pl.BlockSpec(memory_space=pltpu.VMEM)
    return pl.pallas_call(
        functools.partial(attend_kernel, query_heads, kv_heads, len(parts)),
        out_shape=jax.ShapeDtypeStruct((1, query_heads, HEAD_SIZE), jnp.bfloat16),
        in_specs=[pl.BlockSpec(memory_space=pltpu.HBM)] + [whole] * (3 + len(parts)),
        out_specs=whole,
        compiler_params=pltpu.CompilerParams(vmem_limit_bytes=12 * MIB),
        cost_estimate=pl.CostEstimate(
            flops=4 * query_heads * cache_len * HEAD_SIZE,
            bytes_accessed=4 * kv_heads * cache_len * HEAD_SIZE,
            transcendentals=query_heads * cache_len,
        ),
        name="attend",
    )(in_hbm(beside), turn, k_cache, value_cache, *parts)


def output_kernel(bits, pieces, *refs):
    parts = refs[:pieces]
    w_ref, mine_ref, theirs_ref, flat, left, sums = refs[pieces:]
    slots = left.shape[0]
    heads = flat.shape[0] // slots
    at = 0
    for ref in parts:
        for i in range(ref.shape[0]):
            flat[at : at + heads, :] = ref[i].astype(jnp.float32)
            at += heads
    for head in range(heads):
        left[:, head * HEAD_SIZE : (head + 1) * HEAD_SIZE] = flat[
            pl.ds(head, slots, stride=heads), :
        ].astype(jnp.bfloat16)
    total = None
    depth = w_ref.shape[0]
    chunk = min(2 * CHUNK, depth)
    for at in range(0, depth, chunk):
        part = slice(at, at + chunk)
        term = jnp.dot(left[:, part], w_ref[part, :], preferred_element_type=jnp.float32)
        total = term if total is None else total + term
    sums[...] = total
    half = slots // 2
    turn = bit_reverse(lax.axis_index("gx"), bits)
    gy = lax.axis_index("gy")
    for ref, side in ((mine_ref, gy), (theirs_ref, 1 - gy)):
        for t in range(half):
            slot = bit_reverse(t, bits) ^ turn ^ side
            ref[t : t + 1, :] = sums[pl.ds(slot, 1), :]


def output(parts, w_out, slots):
    bits = slots.bit_length() - 1
    depth, width = w_out.shape
    heads = depth // HEAD_SIZE
    whole = pl.BlockSpec(memory_space=pltpu.VMEM)
    piece = jax.ShapeDtypeStruct((slots // 2, width), jnp.float32)
    return pl.pallas_call(
        functools.partial(output_kernel, bits, len(parts)),
        out_shape=(piece, piece),
        in_specs=[whole] * (len(parts) + 1),
        out_specs=(whole, whole),
        scratch_shapes=[
            pltpu.VMEM((slots * heads, HEAD_SIZE), jnp.float32),
            pltpu.VMEM((slots, depth), jnp.bfloat16),
            pltpu.VMEM((slots, width), jnp.float32),
        ],
        compiler_params=pltpu.CompilerParams(vmem_limit_bytes=24 * MIB),
        cost_estimate=pl.CostEstimate(
            flops=2 * slots * depth * width, bytes_accessed=2 * depth * width, transcendentals=0
        ),
        name="output",
    )(*parts, w_out)


def swap(block, axis, devices, mask):
    return lax.ppermute(block, axis, [(i, i ^ mask) for i in range(devices)])


def fan(pieces, devices):
    masks = [bit_reverse(q, 2) for q in range(FAN)]
    arrived = [None] * FAN
    for q in sorted(range(1, FAN), key=lambda q: (masks[q] + 1) % FAN):
        arrived[q] = swap(pieces[q], "gx", devices, masks[q])
    return arrived[1:]


def body(devices, activations, w_query, key_weight, value_weight, w_out, k_cache, value_cache, lengths):
    slots = devices
    query_heads = w_query.shape[1] // HEAD_SIZE
    other = swap(activations, "gy", 2, 1)
    depth = w_query.shape[0]
    first = stage_rows(w_query, min(FIRST, depth))
    pieces = project(activations, other, w_query, first, key_weight, value_weight, slots)

    arrived = fan(pieces, devices)
    half = HEAD_SIZE // 2
    frequency = jnp.power(
        jnp.float32(500000.0), -2.0 * jnp.arange(half, dtype=jnp.float32) / HEAD_SIZE
    )
    frequency = jnp.concatenate([frequency, frequency])[None, :]
    turn = turning(lengths, frequency, w_out)
    total = pieces[0] + (arrived[2] + (arrived[1] + arrived[0]))
    mask = FAN
    while total.shape[0] > 2:
        rest = total.shape[0] // 2
        total = total[:rest] + swap(total[rest:], "gx", devices, mask)
        mask *= 2
    parts = [total[:1], swap(total[1:], "gx", devices, mask)]
    heads = attend(parts, turn, k_cache, value_cache, query_heads, w_out)

    parts = [heads, swap(heads, "gx", devices, mask)]
    while mask > FAN:
        mask //= 2
        parts.append(swap(jnp.concatenate(parts, axis=0), "gx", devices, mask))
    held = jnp.concatenate(parts, axis=0)
    parts += fan([held] * FAN, devices)
    mine, theirs = output(parts, w_out, slots)
    return (mine + swap(theirs, "gy", 2, 1)).astype(jnp.bfloat16)


def solution(mesh):
    placed = (
        P(("groups", "gy"), "gx"),
        P("gx", "gy"),
        P("gx", "gy"),
        P("gx", "gy"),
        P("gy", "gx"),
        P(("groups", "gx"), "gy", None, None),
        P(("groups", "gx"), "gy", None, None),
        P(("groups", "gx")),
    )
    return jax.shard_map(
        functools.partial(body, mesh.shape["gx"]),
        mesh=mesh,
        in_specs=placed,
        out_specs=P(("groups", "gy"), "gx"),
        check_vma=False,
    )
```

```python
import functools
import math

import jax
import jax.numpy as jnp
from jax import lax
from jax.experimental import pallas as pl
from jax.experimental.pallas import tpu as pltpu
from jax.sharding import PartitionSpec as P

MODEL_WIDTH = 16384
LANES = 128
HEAD_SIZE = 128
CHUNK = 256
FIRST = 256
PIECES = 4
FAN = 4
MIB = 2**20


def bit_reverse(value, bits):
    turned = 0
    for bit in range(bits):
        turned = turned | (((value >> bit) & 1) << (bits - 1 - bit))
    return turned


def in_hbm(array):
    return pltpu.with_memory_space_constraint(array, pltpu.HBM)


def cut(start, size):
    if size % (16 * PIECES):
        return [(start, size)]
    return [(start + i * (size // PIECES), size // PIECES) for i in range(PIECES)]


def copies_in(src, dst, sems, start, size, offset):
    return [
        pltpu.make_async_copy(
            src.at[pl.ds(at, rows)], dst.at[pl.ds(at - start + offset, rows)], sems.at[i]
        )
        for i, (at, rows) in enumerate(cut(start, size))
    ]


def stage_kernel(parts, *refs):
    count = len(parts)
    sems = refs[-1]
    copies = []
    for i, (start, size) in enumerate(parts):
        copies += copies_in(refs[i], refs[count + i], sems.at[i], start, size, 0)
    for copy in copies:
        copy.start()
    return copies


def plain_stage_kernel(parts, *refs):
    for copy in stage_kernel(parts, *refs):
        copy.wait()


def turning_stage_kernel(parts, length_ref, frequency_ref, turn_ref, *refs):
    copies = stage_kernel(parts, *refs)
    position = length_ref[0].astype(jnp.float32)
    angle = position * frequency_ref[...]
    lane = lax.broadcasted_iota(jnp.int32, angle.shape, 1)
    sine = jnp.sin(angle)
    turn_ref[0:1, :] = jnp.cos(angle)
    turn_ref[1:2, :] = jnp.where(lane < HEAD_SIZE // 2, -sine, sine)
    turn_ref[2:3, :] = jnp.full(angle.shape, position)
    for copy in copies:
        copy.wait()


def stage(arrays, parts, lengths=None, frequency=None):
    shapes = tuple(
        jax.ShapeDtypeStruct((part[1], *a.shape[1:]), a.dtype) for a, part in zip(arrays, parts)
    )
    vmem = pl.BlockSpec(memory_space=pltpu.VMEM)
    in_specs = [pl.BlockSpec(memory_space=pltpu.HBM)] * len(arrays)
    out_specs = [vmem] * len(arrays)
    kernel = functools.partial(plain_stage_kernel, parts)
    pinned = [in_hbm(a) for a in arrays]
    out_shape = shapes
    if lengths is not None:
        count = len(arrays)

        def kernel(length_ref, frequency_ref, *refs):
            turn_ref = refs[count]
            turning_stage_kernel(
                parts, length_ref, frequency_ref, turn_ref, *refs[:count], *refs[count + 1 :]
            )

        in_specs = [pl.BlockSpec(memory_space=pltpu.SMEM), vmem] + in_specs
        out_specs = [vmem] + out_specs
        out_shape = (jax.ShapeDtypeStruct((8, HEAD_SIZE), jnp.float32), *shapes)
        pinned = [lengths, frequency] + pinned
    return pl.pallas_call(
        kernel,
        out_shape=out_shape,
        in_specs=in_specs,
        out_specs=tuple(out_specs),
        scratch_shapes=[pltpu.SemaphoreType.DMA((len(arrays), PIECES))],
        compiler_params=pltpu.CompilerParams(vmem_limit_bytes=16 * MIB),
        cost_estimate=pl.CostEstimate(
            flops=0, bytes_accessed=sum(2 * math.prod(x.shape) for x in shapes), transcendentals=0
        ),
        name="stage",
    )(*pinned)


def spread(depth, skip, chunk):
    return [(at, min(chunk, depth - at)) for at in range(skip, depth, chunk)]


def tapered(ranges):
    *most, (start, size) = ranges
    if size < 2 * LANES:
        return ranges
    return most + [(start, size - LANES), (start + size - LANES, LANES)]


def feed(depth, skip):
    ranges = spread(depth, skip, CHUNK)
    return tapered(ranges) if ranges else ranges


def project_kernel(
    bits, rows_ref, other_ref, wq_hbm, first, wk, wv, *refs
):
    pieces, (wq, rows, sems) = refs[:FAN], refs[FAN:]
    skip = first.shape[0]
    ranges = feed(wq_hbm.shape[0], skip)
    copies = [
        copies_in(wq_hbm, wq, sems.at[i], start, size, start - skip)
        for i, (start, size) in enumerate(ranges)
    ]
    for group in copies:
        for copy in group:
            copy.start()

    slots = rows.shape[0]
    half = slots // 2
    turn = bit_reverse(lax.axis_index("gx"), bits)
    gy = lax.axis_index("gy")
    for ref, side in ((rows_ref, gy), (other_ref, 1 - gy)):
        block = ref[...].astype(jnp.float32)
        for t in range(half):
            slot = bit_reverse(t, bits) ^ turn ^ side
            rows[pl.ds(slot, 1), :] = block[t : t + 1, :]
    wide = rows[...]
    squares = jnp.sum(wide * wide, axis=1, keepdims=True)
    narrow = wide.astype(jnp.bfloat16)

    fresh = [jnp.dot(narrow, w[...], preferred_element_type=jnp.float32) for w in (wk, wv)]
    sums = jnp.dot(narrow[:, :skip], first[...], preferred_element_type=jnp.float32)
    for (start, size), group in zip(ranges, copies):
        for copy in group:
            copy.wait()
        sums = sums + jnp.dot(
            narrow[:, start : start + size],
            wq[start - skip : start - skip + size, :],
            preferred_element_type=jnp.float32,
        )

    total = pieces[0].shape[1]
    blocks = []
    for part in (sums, *fresh):
        blocks += [part[:, i : i + LANES] for i in range(0, part.shape[1], LANES)]
    blocks.append(jnp.broadcast_to(squares, (slots, LANES)))
    blocks += [jnp.zeros((slots, LANES), jnp.float32)] * (total - len(blocks))
    size = slots // FAN
    for at, ref in enumerate(pieces):
        flat = ref.reshape(size * total, LANES)
        for i, block in enumerate(blocks):
            flat[pl.ds(i, size, stride=total), :] = block[at * size : (at + 1) * size]


def project(rows, other, w_query, first, key_weight, value_weight, slots):
    bits = slots.bit_length() - 1
    depth, query_width = w_query.shape
    kv_width = key_weight.shape[1]
    used = (query_width + 2 * kv_width) // LANES + 1
    total = -(-used // 8) * 8
    skip = first.shape[0]
    piece = jax.ShapeDtypeStruct((slots // FAN, total, LANES), jnp.float32)
    hbm = pl.BlockSpec(memory_space=pltpu.HBM)
    whole = pl.BlockSpec(memory_space=pltpu.VMEM)
    return pl.pallas_call(
        functools.partial(project_kernel, bits),
        out_shape=(piece,) * FAN,
        in_specs=[whole, whole, hbm, whole, whole, whole],
        out_specs=(whole,) * FAN,
        scratch_shapes=[
            pltpu.VMEM((max(depth - skip, 16), query_width), jnp.bfloat16),
            pltpu.VMEM((slots, depth), jnp.float32),
            pltpu.SemaphoreType.DMA((max(1, len(feed(depth, skip))), PIECES)),
        ],
        compiler_params=pltpu.CompilerParams(vmem_limit_bytes=32 * MIB),
        cost_estimate=pl.CostEstimate(
            flops=2 * slots * depth * (query_width + 2 * kv_width),
            bytes_accessed=2 * depth * (query_width + 2 * kv_width),
            transcendentals=0,
        ),
        name="project",
    )(rows, other, in_hbm(w_query), first, key_weight, value_weight)


def attend_kernel(
    query_heads, kv_heads, pieces, part, w_hbm, turn_ref, k_ref, v_ref, *refs
):
    heads_ref, w_ref, sems = refs[pieces:]
    copies = copies_in(w_hbm, w_ref, sems, *part, 0)
    for copy in copies:
        copy.start()
    total = refs[0][0]
    for ref in refs[1:pieces]:
        total = total + ref[0]
    at = query_heads + 2 * kv_heads
    scale = lax.rsqrt(total[at : at + 1, :] / MODEL_WIDTH + 1e-05)
    turned = total[: query_heads + kv_heads] * scale
    half = HEAD_SIZE // 2
    swapped = jnp.concatenate([turned[:, half:], turned[:, :half]], axis=1)
    turned = (turned * turn_ref[0:1, :] + swapped * turn_ref[1:2, :]).astype(jnp.bfloat16)
    fresh_values = (total[query_heads + kv_heads : at] * scale).astype(jnp.bfloat16)
    group = query_heads // kv_heads
    factor = 1.0 / math.sqrt(HEAD_SIZE)
    length = turn_ref[2:3, 0:1].astype(jnp.int32)
    scores = []
    own = []
    for head in range(kv_heads):
        queries = turned[head * group : (head + 1) * group]
        scores.append(
            lax.dot_general(
                queries,
                k_ref[0, head],
                (((1,), (1,)), ((), ())),
                preferred_element_type=jnp.float32,
            )
        )
        fresh_key = turned[query_heads + head : query_heads + head + 1].astype(jnp.float32)
        own.append(jnp.sum(queries.astype(jnp.float32) * fresh_key, axis=1, keepdims=True) * factor)
    slot = lax.broadcasted_iota(jnp.int32, scores[0].shape, 1)
    for head in range(kv_heads):
        live = jnp.where(slot < length, scores[head] * factor, -jnp.inf)
        top = jnp.maximum(jnp.max(live, axis=1, keepdims=True), own[head])
        exponent = jnp.exp(live - top)
        own_exp = jnp.exp(own[head] - top)
        share = 1.0 / (jnp.sum(exponent, axis=1, keepdims=True) + own_exp)
        weights = (exponent * share).astype(jnp.bfloat16)
        own_weight = (own_exp * share).astype(jnp.bfloat16)
        mixed = jnp.dot(weights, v_ref[0, head], preferred_element_type=jnp.float32)
        mixed = mixed + own_weight.astype(jnp.float32) * fresh_values[head : head + 1].astype(
            jnp.float32
        )
        heads_ref[0, pl.ds(head * group, group), :] = mixed.astype(jnp.bfloat16)
    for copy in copies:
        copy.wait()


def attend(parts, turn, k_cache, value_cache, query_heads, w_out, part):
    kv_heads, cache_len = k_cache.shape[1:3]
    whole = pl.BlockSpec(memory_space=pltpu.VMEM)
    return pl.pallas_call(
        functools.partial(attend_kernel, query_heads, kv_heads, len(parts), part),
        out_shape=(
            jax.ShapeDtypeStruct((1, query_heads, HEAD_SIZE), jnp.bfloat16),
            jax.ShapeDtypeStruct((part[1], w_out.shape[1]), w_out.dtype),
        ),
        in_specs=[pl.BlockSpec(memory_space=pltpu.HBM)] + [whole] * (3 + len(parts)),
        out_specs=(whole, whole),
        scratch_shapes=[pltpu.SemaphoreType.DMA((PIECES,))],
        compiler_params=pltpu.CompilerParams(vmem_limit_bytes=12 * MIB),
        cost_estimate=pl.CostEstimate(
            flops=4 * query_heads * cache_len * HEAD_SIZE,
            bytes_accessed=4 * kv_heads * cache_len * HEAD_SIZE,
            transcendentals=query_heads * cache_len,
        ),
        name="attend",
    )(in_hbm(w_out), turn, k_cache, value_cache, *parts)


def output_kernel(bits, pieces, *refs):
    parts = refs[:pieces]
    ready = refs[pieces:-5]
    mine_ref, theirs_ref, flat, left, sums = refs[-5:]
    slots = left.shape[0]
    heads = flat.shape[0] // slots
    at = 0
    for ref in parts:
        for i in range(ref.shape[0]):
            flat[at : at + heads, :] = ref[i].astype(jnp.float32)
            at += heads
    for head in range(heads):
        left[:, head * HEAD_SIZE : (head + 1) * HEAD_SIZE] = flat[
            pl.ds(head, slots, stride=heads), :
        ].astype(jnp.bfloat16)
    total = None
    at = 0
    for ref in ready:
        size = ref.shape[0]
        for start, rows in spread(size, 0, 2 * CHUNK):
            term = jnp.dot(
                left[:, at + start : at + start + rows],
                ref[start : start + rows, :],
                preferred_element_type=jnp.float32,
            )
            total = term if total is None else total + term
        at += size
    sums[...] = total
    half = slots // 2
    turn = bit_reverse(lax.axis_index("gx"), bits)
    gy = lax.axis_index("gy")
    for ref, side in ((mine_ref, gy), (theirs_ref, 1 - gy)):
        for t in range(half):
            slot = bit_reverse(t, bits) ^ turn ^ side
            ref[t : t + 1, :] = sums[pl.ds(slot, 1), :]


def output(parts, ready, slots):
    bits = slots.bit_length() - 1
    depth, width = sum(x.shape[0] for x in ready), ready[0].shape[1]
    heads = depth // HEAD_SIZE
    whole = pl.BlockSpec(memory_space=pltpu.VMEM)
    piece = jax.ShapeDtypeStruct((slots // 2, width), jnp.float32)
    return pl.pallas_call(
        functools.partial(output_kernel, bits, len(parts)),
        out_shape=(piece, piece),
        in_specs=[whole] * (len(parts) + len(ready)),
        out_specs=(whole, whole),
        scratch_shapes=[
            pltpu.VMEM((slots * heads, HEAD_SIZE), jnp.float32),
            pltpu.VMEM((slots, depth), jnp.bfloat16),
            pltpu.VMEM((slots, width), jnp.float32),
        ],
        compiler_params=pltpu.CompilerParams(vmem_limit_bytes=24 * MIB),
        cost_estimate=pl.CostEstimate(
            flops=2 * slots * depth * width, bytes_accessed=2 * depth * width, transcendentals=0
        ),
        name="output",
    )(*parts, *ready)


def swap(block, axis, devices, mask):
    return lax.ppermute(block, axis, [(i, i ^ mask) for i in range(devices)])


def fan(pieces, devices):
    masks = [bit_reverse(q, 2) for q in range(FAN)]
    arrived = [None] * FAN
    for q in sorted(range(1, FAN), key=lambda q: (masks[q] + 1) % FAN):
        arrived[q] = swap(pieces[q], "gx", devices, masks[q])
    return arrived[1:]


def body(devices, activations, w_query, key_weight, value_weight, w_out, k_cache, value_cache, lengths):
    slots = devices
    query_heads = w_query.shape[1] // HEAD_SIZE
    other = swap(activations, "gy", 2, 1)
    depth = w_query.shape[0]
    (first,) = stage((w_query,), ((0, min(FIRST, depth)),))
    pieces = project(activations, other, w_query, first, key_weight, value_weight, slots)

    rows_out = w_out.shape[0]
    *pieces, w_out = lax.optimization_barrier((*pieces, w_out))
    few, most = rows_out // 8, rows_out // 4
    arrived = fan(pieces, devices)
    half = HEAD_SIZE // 2
    frequency = jnp.power(
        jnp.float32(500000.0), -2.0 * jnp.arange(half, dtype=jnp.float32) / HEAD_SIZE
    )
    frequency = jnp.concatenate([frequency, frequency])[None, :]
    turn, ready_one = stage((w_out,), ((0, few),), lengths, frequency)
    total = pieces[0] + (arrived[2] + (arrived[1] + arrived[0]))
    mask = FAN
    while total.shape[0] > 2:
        rest = total.shape[0] // 2
        total = total[:rest] + swap(total[rest:], "gx", devices, mask)
        mask *= 2
    total, w_out, ready_one = lax.optimization_barrier((total, w_out, ready_one))
    (ready_two,) = stage((w_out,), ((few, most),))
    parts = [total[:1], swap(total[1:], "gx", devices, mask)]
    parts[1], ready_two = lax.optimization_barrier((parts[1], ready_two))
    heads, ready_more = attend(
        parts, turn, k_cache, value_cache, query_heads, w_out, (few + most, few)
    )

    heads, w_out = lax.optimization_barrier((heads, w_out))
    (ready_three,) = stage((w_out,), ((2 * few + most, most),))
    parts = [heads, swap(heads, "gx", devices, mask)]
    parts[1], ready_three = lax.optimization_barrier((parts[1], ready_three))
    while mask > FAN:
        mask //= 2
        parts.append(swap(jnp.concatenate(parts, axis=0), "gx", devices, mask))
    held = jnp.concatenate(parts, axis=0)
    held, w_out = lax.optimization_barrier((held, w_out))
    (ready_four,) = stage((w_out,), ((2 * few + 2 * most, most),))
    parts += fan([held] * FAN, devices)
    parts[-1], ready_four = lax.optimization_barrier((parts[-1], ready_four))
    ready = (ready_one, ready_two, ready_more, ready_three, ready_four)
    mine, theirs = output(parts, ready, slots)
    return (mine + swap(theirs, "gy", 2, 1)).astype(jnp.bfloat16)


def solution(mesh):
    placed = (
        P(("groups", "gy"), "gx"),
        P("gx", "gy"),
        P("gx", "gy"),
        P("gx", "gy"),
        P("gy", "gx"),
        P(("groups", "gx"), "gy", None, None),
        P(("groups", "gx"), "gy", None, None),
        P(("groups", "gx")),
    )
    return jax.shard_map(
        functools.partial(body, mesh.shape["gx"]),
        mesh=mesh,
        in_specs=placed,
        out_specs=P(("groups", "gy"), "gx"),
        check_vma=False,
    )
```

```python
import functools
import math

import jax
import jax.numpy as jnp
from jax import lax
from jax.experimental import pallas as pl
from jax.experimental.pallas import tpu as pltpu
from jax.sharding import PartitionSpec as P

MODEL_WIDTH = 16384
LANES = 128
HEAD_SIZE = 128
CHUNK = 256
FIRST = 256
PIECES = 4
FAN = 4
MIB = 2**20


def bit_reverse(value, bits):
    turned = 0
    for bit in range(bits):
        turned = turned | (((value >> bit) & 1) << (bits - 1 - bit))
    return turned


def in_hbm(array):
    return pltpu.with_memory_space_constraint(array, pltpu.HBM)


def cut(start, size):
    if size % (16 * PIECES):
        return [(start, size)]
    return [(start + i * (size // PIECES), size // PIECES) for i in range(PIECES)]


def copies_in(src, dst, sems, start, size, offset):
    return [
        pltpu.make_async_copy(
            src.at[pl.ds(at, rows)], dst.at[pl.ds(at - start + offset, rows)], sems.at[i]
        )
        for i, (at, rows) in enumerate(cut(start, size))
    ]


def stage_kernel(parts, *refs):
    count = len(parts)
    sems = refs[-1]
    copies = []
    for i, (start, size) in enumerate(parts):
        copies += copies_in(refs[i], refs[count + i], sems.at[i], start, size, 0)
    for copy in copies:
        copy.start()
    return copies


def plain_stage_kernel(parts, *refs):
    for copy in stage_kernel(parts, *refs):
        copy.wait()


def turning_stage_kernel(parts, length_ref, frequency_ref, turn_ref, *refs):
    copies = stage_kernel(parts, *refs)
    position = length_ref[0].astype(jnp.float32)
    angle = position * frequency_ref[...]
    lane = lax.broadcasted_iota(jnp.int32, angle.shape, 1)
    sine = jnp.sin(angle)
    turn_ref[0:1, :] = jnp.cos(angle)
    turn_ref[1:2, :] = jnp.where(lane < HEAD_SIZE // 2, -sine, sine)
    turn_ref[2:3, :] = jnp.full(angle.shape, position)
    for copy in copies:
        copy.wait()


def stage(arrays, parts, lengths=None, frequency=None):
    shapes = tuple(
        jax.ShapeDtypeStruct((part[1], *a.shape[1:]), a.dtype) for a, part in zip(arrays, parts)
    )
    vmem = pl.BlockSpec(memory_space=pltpu.VMEM)
    in_specs = [pl.BlockSpec(memory_space=pltpu.HBM)] * len(arrays)
    out_specs = [vmem] * len(arrays)
    kernel = functools.partial(plain_stage_kernel, parts)
    pinned = [in_hbm(a) for a in arrays]
    out_shape = shapes
    if lengths is not None:
        count = len(arrays)

        def kernel(length_ref, frequency_ref, *refs):
            turn_ref = refs[count]
            turning_stage_kernel(
                parts, length_ref, frequency_ref, turn_ref, *refs[:count], *refs[count + 1 :]
            )

        in_specs = [pl.BlockSpec(memory_space=pltpu.SMEM), vmem] + in_specs
        out_specs = [vmem] + out_specs
        out_shape = (jax.ShapeDtypeStruct((8, HEAD_SIZE), jnp.float32), *shapes)
        pinned = [lengths, frequency] + pinned
    return pl.pallas_call(
        kernel,
        out_shape=out_shape,
        in_specs=in_specs,
        out_specs=tuple(out_specs),
        scratch_shapes=[pltpu.SemaphoreType.DMA((len(arrays), PIECES))],
        compiler_params=pltpu.CompilerParams(vmem_limit_bytes=16 * MIB),
        cost_estimate=pl.CostEstimate(
            flops=0, bytes_accessed=sum(2 * math.prod(x.shape) for x in shapes), transcendentals=0
        ),
        name="stage",
    )(*pinned)


def spread(depth, skip, chunk):
    return [(at, min(chunk, depth - at)) for at in range(skip, depth, chunk)]


def tapered(ranges):
    *most, (start, size) = ranges
    if size < 2 * LANES:
        return ranges
    return most + [(start, size - LANES), (start + size - LANES, LANES)]


def feed(depth, skip):
    ranges = spread(depth, skip, CHUNK)
    return tapered(ranges) if ranges else ranges


def project_kernel(
    bits, rows_ref, other_ref, wq_hbm, first, wk, wv, *refs
):
    pieces, (wq, rows, sems) = refs[:FAN], refs[FAN:]
    skip = first.shape[0]
    ranges = feed(wq_hbm.shape[0], skip)
    copies = [
        copies_in(wq_hbm, wq, sems.at[i], start, size, start - skip)
        for i, (start, size) in enumerate(ranges)
    ]
    for group in copies:
        for copy in group:
            copy.start()

    slots = rows.shape[0]
    half = slots // 2
    turn = bit_reverse(lax.axis_index("gx"), bits)
    gy = lax.axis_index("gy")
    for ref, side in ((rows_ref, gy), (other_ref, 1 - gy)):
        block = ref[...].astype(jnp.float32)
        for t in range(half):
            slot = bit_reverse(t, bits) ^ turn ^ side
            rows[pl.ds(slot, 1), :] = block[t : t + 1, :]
    wide = rows[...]
    squares = jnp.sum(wide * wide, axis=1, keepdims=True)
    narrow = wide.astype(jnp.bfloat16)

    fresh = [jnp.dot(narrow, w[...], preferred_element_type=jnp.float32) for w in (wk, wv)]
    sums = jnp.dot(narrow[:, :skip], first[...], preferred_element_type=jnp.float32)
    for (start, size), group in zip(ranges, copies):
        for copy in group:
            copy.wait()
        sums = sums + jnp.dot(
            narrow[:, start : start + size],
            wq[start - skip : start - skip + size, :],
            preferred_element_type=jnp.float32,
        )

    total = pieces[0].shape[1]
    blocks = []
    for part in (sums, *fresh):
        blocks += [part[:, i : i + LANES] for i in range(0, part.shape[1], LANES)]
    blocks.append(jnp.broadcast_to(squares, (slots, LANES)))
    blocks += [jnp.zeros((slots, LANES), jnp.float32)] * (total - len(blocks))
    size = slots // FAN
    for at, ref in enumerate(pieces):
        flat = ref.reshape(size * total, LANES)
        for i, block in enumerate(blocks):
            flat[pl.ds(i, size, stride=total), :] = block[at * size : (at + 1) * size]


def project(rows, other, w_query, first, key_weight, value_weight, slots):
    bits = slots.bit_length() - 1
    depth, query_width = w_query.shape
    kv_width = key_weight.shape[1]
    used = (query_width + 2 * kv_width) // LANES + 1
    total = -(-used // 8) * 8
    skip = first.shape[0]
    piece = jax.ShapeDtypeStruct((slots // FAN, total, LANES), jnp.float32)
    hbm = pl.BlockSpec(memory_space=pltpu.HBM)
    whole = pl.BlockSpec(memory_space=pltpu.VMEM)
    return pl.pallas_call(
        functools.partial(project_kernel, bits),
        out_shape=(piece,) * FAN,
        in_specs=[whole, whole, hbm, whole, whole, whole],
        out_specs=(whole,) * FAN,
        scratch_shapes=[
            pltpu.VMEM((max(depth - skip, 16), query_width), jnp.bfloat16),
            pltpu.VMEM((slots, depth), jnp.float32),
            pltpu.SemaphoreType.DMA((max(1, len(feed(depth, skip))), PIECES)),
        ],
        compiler_params=pltpu.CompilerParams(vmem_limit_bytes=32 * MIB),
        cost_estimate=pl.CostEstimate(
            flops=2 * slots * depth * (query_width + 2 * kv_width),
            bytes_accessed=2 * depth * (query_width + 2 * kv_width),
            transcendentals=0,
        ),
        name="project",
    )(rows, other, in_hbm(w_query), first, key_weight, value_weight)


def attend_kernel(query_heads, kv_heads, pieces, turn_ref, k_ref, v_ref, *refs):
    heads_ref = refs[pieces]
    total = refs[0][0]
    for ref in refs[1:pieces]:
        total = total + ref[0]
    at = query_heads + 2 * kv_heads
    scale = lax.rsqrt(total[at : at + 1, :] / MODEL_WIDTH + 1e-05)
    turned = total[: query_heads + kv_heads] * scale
    half = HEAD_SIZE // 2
    swapped = jnp.concatenate([turned[:, half:], turned[:, :half]], axis=1)
    turned = (turned * turn_ref[0:1, :] + swapped * turn_ref[1:2, :]).astype(jnp.bfloat16)
    fresh_values = (total[query_heads + kv_heads : at] * scale).astype(jnp.bfloat16)
    group = query_heads // kv_heads
    factor = 1.0 / math.sqrt(HEAD_SIZE)
    length = turn_ref[2:3, 0:1].astype(jnp.int32)
    side = 2 if kv_heads % 2 == 0 else 1
    for first in range(0, kv_heads, side):
        members = range(first, first + side)
        queries = [turned[head * group : (head + 1) * group] for head in members]
        empty = jnp.zeros((group, HEAD_SIZE), jnp.bfloat16)
        spread_out = jnp.concatenate(
            [
                jnp.concatenate([q if i == j else empty for j in range(side)], axis=1)
                for i, q in enumerate(queries)
            ],
            axis=0,
        )
        keys = jnp.concatenate([k_ref[0, head] for head in members], axis=1)
        values = jnp.concatenate([v_ref[0, head] for head in members], axis=1)
        scores = (
            lax.dot_general(
                spread_out, keys, (((1,), (1,)), ((), ())), preferred_element_type=jnp.float32
            )
            * factor
        )
        own = jnp.concatenate(
            [
                jnp.sum(
                    q.astype(jnp.float32)
                    * turned[query_heads + head : query_heads + head + 1].astype(jnp.float32),
                    axis=1,
                    keepdims=True,
                )
                for q, head in zip(queries, members)
            ],
            axis=0,
        ) * factor
        slot = lax.broadcasted_iota(jnp.int32, scores.shape, 1)
        scores = jnp.where(slot < length, scores, -jnp.inf)
        top = jnp.maximum(jnp.max(scores, axis=1, keepdims=True), own)
        exponent = jnp.exp(scores - top)
        own_exp = jnp.exp(own - top)
        share = 1.0 / (jnp.sum(exponent, axis=1, keepdims=True) + own_exp)
        weights = (exponent * share).astype(jnp.bfloat16)
        own_weight = (own_exp * share).astype(jnp.bfloat16).astype(jnp.float32)
        mixed = jnp.dot(weights, values, preferred_element_type=jnp.float32)
        for i, head in enumerate(members):
            block = mixed[i * group : (i + 1) * group, i * HEAD_SIZE : (i + 1) * HEAD_SIZE]
            block = block + own_weight[i * group : (i + 1) * group] * fresh_values[
                head : head + 1
            ].astype(jnp.float32)
            heads_ref[0, pl.ds(head * group, group), :] = block.astype(jnp.bfloat16)


def attend(parts, turn, k_cache, value_cache, query_heads):
    kv_heads, cache_len = k_cache.shape[1:3]
    whole = pl.BlockSpec(memory_space=pltpu.VMEM)
    return pl.pallas_call(
        functools.partial(attend_kernel, query_heads, kv_heads, len(parts)),
        out_shape=jax.ShapeDtypeStruct((1, query_heads, HEAD_SIZE), jnp.bfloat16),
        in_specs=[whole] * (3 + len(parts)),
        out_specs=whole,
        compiler_params=pltpu.CompilerParams(vmem_limit_bytes=12 * MIB),
        cost_estimate=pl.CostEstimate(
            flops=4 * query_heads * cache_len * HEAD_SIZE,
            bytes_accessed=4 * kv_heads * cache_len * HEAD_SIZE,
            transcendentals=query_heads * cache_len,
        ),
        name="attend",
    )(turn, k_cache, value_cache, *parts)


def output_kernel(bits, pieces, *refs):
    parts = refs[:pieces]
    ready = refs[pieces:-8]
    w_hbm, mine_ref, theirs_ref, rest, flat, left, sums, sems = refs[-8:]
    skip = w_hbm.shape[0] - rest.shape[0]
    copies = copies_in(w_hbm, rest, sems, skip, rest.shape[0], 0)
    for copy in copies:
        copy.start()
    slots = left.shape[0]
    heads = flat.shape[0] // slots
    at = 0
    for ref in parts:
        for i in range(ref.shape[0]):
            flat[at : at + heads, :] = ref[i].astype(jnp.float32)
            at += heads
    for head in range(heads):
        left[:, head * HEAD_SIZE : (head + 1) * HEAD_SIZE] = flat[
            pl.ds(head, slots, stride=heads), :
        ].astype(jnp.bfloat16)
    total = None
    at = 0
    for ref in (*ready, rest):
        if ref is rest:
            for copy in copies:
                copy.wait()
        size = ref.shape[0]
        for start, rows in spread(size, 0, 2 * CHUNK):
            term = jnp.dot(
                left[:, at + start : at + start + rows],
                ref[start : start + rows, :],
                preferred_element_type=jnp.float32,
            )
            total = term if total is None else total + term
        at += size
    sums[...] = total
    half = slots // 2
    turn = bit_reverse(lax.axis_index("gx"), bits)
    gy = lax.axis_index("gy")
    for ref, side in ((mine_ref, gy), (theirs_ref, 1 - gy)):
        for t in range(half):
            slot = bit_reverse(t, bits) ^ turn ^ side
            ref[t : t + 1, :] = sums[pl.ds(slot, 1), :]


def output(parts, ready, w_out, slots):
    bits = slots.bit_length() - 1
    depth, width = w_out.shape
    heads = depth // HEAD_SIZE
    rest = depth - sum(x.shape[0] for x in ready)
    whole = pl.BlockSpec(memory_space=pltpu.VMEM)
    piece = jax.ShapeDtypeStruct((slots // 2, width), jnp.float32)
    return pl.pallas_call(
        functools.partial(output_kernel, bits, len(parts)),
        out_shape=(piece, piece),
        in_specs=[whole] * (len(parts) + len(ready)) + [pl.BlockSpec(memory_space=pltpu.HBM)],
        out_specs=(whole, whole),
        scratch_shapes=[
            pltpu.VMEM((rest, width), jnp.bfloat16),
            pltpu.VMEM((slots * heads, HEAD_SIZE), jnp.float32),
            pltpu.VMEM((slots, depth), jnp.bfloat16),
            pltpu.VMEM((slots, width), jnp.float32),
            pltpu.SemaphoreType.DMA((PIECES,)),
        ],
        compiler_params=pltpu.CompilerParams(vmem_limit_bytes=24 * MIB),
        cost_estimate=pl.CostEstimate(
            flops=2 * slots * depth * width, bytes_accessed=2 * depth * width, transcendentals=0
        ),
        name="output",
    )(*parts, *ready, in_hbm(w_out))


def swap(block, axis, devices, mask):
    return lax.ppermute(block, axis, [(i, i ^ mask) for i in range(devices)])


def fan(pieces, devices):
    masks = [bit_reverse(q, 2) for q in range(FAN)]
    arrived = [None] * FAN
    for q in sorted(range(1, FAN), key=lambda q: (masks[q] + 1) % FAN):
        arrived[q] = swap(pieces[q], "gx", devices, masks[q])
    return arrived[1:]


def body(devices, activations, w_query, key_weight, value_weight, w_out, k_cache, value_cache, lengths):
    slots = devices
    query_heads = w_query.shape[1] // HEAD_SIZE
    other = swap(activations, "gy", 2, 1)
    depth = w_query.shape[0]
    (first,) = stage((w_query,), ((0, min(FIRST, depth)),))
    pieces = project(activations, other, w_query, first, key_weight, value_weight, slots)

    rows_out = w_out.shape[0]
    *pieces, w_out = lax.optimization_barrier((*pieces, w_out))
    few, most = rows_out // 8, rows_out // 4
    arrived = fan(pieces, devices)
    half = HEAD_SIZE // 2
    frequency = jnp.power(
        jnp.float32(500000.0), -2.0 * jnp.arange(half, dtype=jnp.float32) / HEAD_SIZE
    )
    frequency = jnp.concatenate([frequency, frequency])[None, :]
    turn, ready_one = stage((w_out,), ((0, few),), lengths, frequency)
    total = pieces[0] + (arrived[2] + (arrived[1] + arrived[0]))
    mask = FAN
    while total.shape[0] > 2:
        rest = total.shape[0] // 2
        total = total[:rest] + swap(total[rest:], "gx", devices, mask)
        mask *= 2
    total, w_out, ready_one = lax.optimization_barrier((total, w_out, ready_one))
    (ready_two,) = stage((w_out,), ((few, most),))
    parts = [total[:1], swap(total[1:], "gx", devices, mask)]
    parts[1], ready_two = lax.optimization_barrier((parts[1], ready_two))
    heads = attend(parts, turn, k_cache, value_cache, query_heads)

    heads, w_out = lax.optimization_barrier((heads, w_out))
    (ready_three,) = stage((w_out,), ((few + most, most),))
    parts = [heads, swap(heads, "gx", devices, mask)]
    parts[1], ready_three = lax.optimization_barrier((parts[1], ready_three))
    while mask > FAN:
        mask //= 2
        parts.append(swap(jnp.concatenate(parts, axis=0), "gx", devices, mask))
    held = jnp.concatenate(parts, axis=0)
    held, w_out = lax.optimization_barrier((held, w_out))
    (ready_four,) = stage((w_out,), ((few + 2 * most, most),))
    parts += fan([held] * FAN, devices)
    parts[-1], ready_four = lax.optimization_barrier((parts[-1], ready_four))
    ready = (ready_one, ready_two, ready_three, ready_four)
    mine, theirs = output(parts, ready, w_out, slots)
    return (mine + swap(theirs, "gy", 2, 1)).astype(jnp.bfloat16)


def solution(mesh):
    placed = (
        P(("groups", "gy"), "gx"),
        P("gx", "gy"),
        P("gx", "gy"),
        P("gx", "gy"),
        P("gy", "gx"),
        P(("groups", "gx"), "gy", None, None),
        P(("groups", "gx"), "gy", None, None),
        P(("groups", "gx")),
    )
    return jax.shard_map(
        functools.partial(body, mesh.shape["gx"]),
        mesh=mesh,
        in_specs=placed,
        out_specs=P(("groups", "gy"), "gx"),
        check_vma=False,
    )
```

```python
import functools
import math

import jax
import jax.numpy as jnp
from jax import lax
from jax.experimental import pallas as pl
from jax.experimental.pallas import tpu as pltpu
from jax.sharding import PartitionSpec as P

MODEL_WIDTH = 16384
LANES = 128
HEAD_SIZE = 128
CHUNK = 256
FIRST = 256
PIECES = 4
FAN = 4
MIB = 2**20


def bit_reverse(value, bits):
    turned = 0
    for bit in range(bits):
        turned = turned | (((value >> bit) & 1) << (bits - 1 - bit))
    return turned


def in_hbm(array):
    return pltpu.with_memory_space_constraint(array, pltpu.HBM)


def cut(start, size):
    if size % (16 * PIECES):
        return [(start, size)]
    return [(start + i * (size // PIECES), size // PIECES) for i in range(PIECES)]


def copies_in(src, dst, sems, start, size, offset):
    return [
        pltpu.make_async_copy(
            src.at[pl.ds(at, rows)], dst.at[pl.ds(at - start + offset, rows)], sems.at[i]
        )
        for i, (at, rows) in enumerate(cut(start, size))
    ]


def stage_kernel(parts, *refs):
    count = len(parts)
    sems = refs[-1]
    copies = []
    for i, (start, size) in enumerate(parts):
        copies += copies_in(refs[i], refs[count + i], sems.at[i], start, size, 0)
    for copy in copies:
        copy.start()
    return copies


def plain_stage_kernel(parts, *refs):
    for copy in stage_kernel(parts, *refs):
        copy.wait()


def turning_stage_kernel(parts, length_ref, frequency_ref, turn_ref, *refs):
    copies = stage_kernel(parts, *refs)
    position = length_ref[0].astype(jnp.float32)
    angle = position * frequency_ref[...]
    lane = lax.broadcasted_iota(jnp.int32, angle.shape, 1)
    sine = jnp.sin(angle)
    turn_ref[0:1, :] = jnp.cos(angle)
    turn_ref[1:2, :] = jnp.where(lane < HEAD_SIZE // 2, -sine, sine)
    turn_ref[2:3, :] = jnp.full(angle.shape, position)
    for copy in copies:
        copy.wait()


def stage(arrays, parts, lengths=None, frequency=None):
    shapes = tuple(
        jax.ShapeDtypeStruct((part[1], *a.shape[1:]), a.dtype) for a, part in zip(arrays, parts)
    )
    vmem = pl.BlockSpec(memory_space=pltpu.VMEM)
    in_specs = [pl.BlockSpec(memory_space=pltpu.HBM)] * len(arrays)
    out_specs = [vmem] * len(arrays)
    kernel = functools.partial(plain_stage_kernel, parts)
    pinned = [in_hbm(a) for a in arrays]
    out_shape = shapes
    if lengths is not None:
        count = len(arrays)

        def kernel(length_ref, frequency_ref, *refs):
            turn_ref = refs[count]
            turning_stage_kernel(
                parts, length_ref, frequency_ref, turn_ref, *refs[:count], *refs[count + 1 :]
            )

        in_specs = [pl.BlockSpec(memory_space=pltpu.SMEM), vmem] + in_specs
        out_specs = [vmem] + out_specs
        out_shape = (jax.ShapeDtypeStruct((8, HEAD_SIZE), jnp.float32), *shapes)
        pinned = [lengths, frequency] + pinned
    return pl.pallas_call(
        kernel,
        out_shape=out_shape,
        in_specs=in_specs,
        out_specs=tuple(out_specs),
        scratch_shapes=[pltpu.SemaphoreType.DMA((len(arrays), PIECES))],
        compiler_params=pltpu.CompilerParams(vmem_limit_bytes=16 * MIB),
        cost_estimate=pl.CostEstimate(
            flops=0, bytes_accessed=sum(2 * math.prod(x.shape) for x in shapes), transcendentals=0
        ),
        name="stage",
    )(*pinned)


def spread(depth, skip, chunk):
    return [(at, min(chunk, depth - at)) for at in range(skip, depth, chunk)]


def tapered(ranges):
    *most, (start, size) = ranges
    if size < 2 * LANES:
        return ranges
    return most + [(start, size - LANES), (start + size - LANES, LANES)]


def feed(depth, skip):
    ranges = spread(depth, skip, CHUNK)
    return tapered(ranges) if ranges else ranges


def project_kernel(
    bits, rows_ref, other_ref, wq_hbm, w_out_hbm, first, wk, wv, *refs
):
    pieces, (early, wq, rows, early_sems, sems) = refs[:FAN], refs[FAN:]
    skip = first.shape[0]
    ranges = feed(wq_hbm.shape[0], skip)
    copies = [
        copies_in(wq_hbm, wq, sems.at[i], start, size, start - skip)
        for i, (start, size) in enumerate(ranges)
    ]
    early_copies = copies_in(w_out_hbm, early, early_sems, 0, early.shape[0], 0)
    for group in (*copies, early_copies):
        for copy in group:
            copy.start()

    slots = rows.shape[0]
    half = slots // 2
    turn = bit_reverse(lax.axis_index("gx"), bits)
    gy = lax.axis_index("gy")
    for ref, side in ((rows_ref, gy), (other_ref, 1 - gy)):
        block = ref[...].astype(jnp.float32)
        for t in range(half):
            slot = bit_reverse(t, bits) ^ turn ^ side
            rows[pl.ds(slot, 1), :] = block[t : t + 1, :]
    wide = rows[...]
    squares = jnp.sum(wide * wide, axis=1, keepdims=True)
    narrow = wide.astype(jnp.bfloat16)

    fresh = [jnp.dot(narrow, w[...], preferred_element_type=jnp.float32) for w in (wk, wv)]
    sums = jnp.dot(narrow[:, :skip], first[...], preferred_element_type=jnp.float32)
    for (start, size), group in zip(ranges, copies):
        for copy in group:
            copy.wait()
        sums = sums + jnp.dot(
            narrow[:, start : start + size],
            wq[start - skip : start - skip + size, :],
            preferred_element_type=jnp.float32,
        )

    total = pieces[0].shape[1]
    blocks = []
    for part in (sums, *fresh):
        blocks += [part[:, i : i + LANES] for i in range(0, part.shape[1], LANES)]
    blocks.append(jnp.broadcast_to(squares, (slots, LANES)))
    blocks += [jnp.zeros((slots, LANES), jnp.float32)] * (total - len(blocks))
    size = slots // FAN
    for at, ref in enumerate(pieces):
        flat = ref.reshape(size * total, LANES)
        for i, block in enumerate(blocks):
            flat[pl.ds(i, size, stride=total), :] = block[at * size : (at + 1) * size]
    for copy in early_copies:
        copy.wait()


def project(rows, other, w_query, first, key_weight, value_weight, w_out, early, slots):
    bits = slots.bit_length() - 1
    depth, query_width = w_query.shape
    kv_width = key_weight.shape[1]
    used = (query_width + 2 * kv_width) // LANES + 1
    total = -(-used // 8) * 8
    skip = first.shape[0]
    piece = jax.ShapeDtypeStruct((slots // FAN, total, LANES), jnp.float32)
    hbm = pl.BlockSpec(memory_space=pltpu.HBM)
    whole = pl.BlockSpec(memory_space=pltpu.VMEM)
    return pl.pallas_call(
        functools.partial(project_kernel, bits),
        out_shape=(piece,) * FAN
        + (jax.ShapeDtypeStruct((early, w_out.shape[1]), w_out.dtype),),
        in_specs=[whole, whole, hbm, hbm, whole, whole, whole],
        out_specs=(whole,) * (FAN + 1),
        scratch_shapes=[
            pltpu.VMEM((max(depth - skip, 16), query_width), jnp.bfloat16),
            pltpu.VMEM((slots, depth), jnp.float32),
            pltpu.SemaphoreType.DMA((PIECES,)),
            pltpu.SemaphoreType.DMA((max(1, len(feed(depth, skip))), PIECES)),
        ],
        compiler_params=pltpu.CompilerParams(vmem_limit_bytes=32 * MIB),
        cost_estimate=pl.CostEstimate(
            flops=2 * slots * depth * (query_width + 2 * kv_width),
            bytes_accessed=2 * depth * (query_width + 2 * kv_width),
            transcendentals=0,
        ),
        name="project",
    )(rows, other, in_hbm(w_query), in_hbm(w_out), first, key_weight, value_weight)


def attend_kernel(query_heads, kv_heads, pieces, part, w_hbm, turn_ref, k_ref, v_ref, *refs):
    heads_ref, w_ref, sems = refs[pieces:]
    copies = copies_in(w_hbm, w_ref, sems, *part, 0)
    for copy in copies:
        copy.start()
    total = refs[0][0]
    for ref in refs[1:pieces]:
        total = total + ref[0]
    at = query_heads + 2 * kv_heads
    scale = lax.rsqrt(total[at : at + 1, :] / MODEL_WIDTH + 1e-05)
    turned = total[: query_heads + kv_heads] * scale
    half = HEAD_SIZE // 2
    swapped = jnp.concatenate([turned[:, half:], turned[:, :half]], axis=1)
    turned = (turned * turn_ref[0:1, :] + swapped * turn_ref[1:2, :]).astype(jnp.bfloat16)
    fresh_values = (total[query_heads + kv_heads : at] * scale).astype(jnp.bfloat16)
    group = query_heads // kv_heads
    factor = 1.0 / math.sqrt(HEAD_SIZE)
    length = turn_ref[2:3, 0:1].astype(jnp.int32)
    side = 2 if kv_heads % 2 == 0 else 1
    for first in range(0, kv_heads, side):
        members = range(first, first + side)
        queries = [turned[head * group : (head + 1) * group] for head in members]
        empty = jnp.zeros((group, HEAD_SIZE), jnp.bfloat16)
        spread_out = jnp.concatenate(
            [
                jnp.concatenate([q if i == j else empty for j in range(side)], axis=1)
                for i, q in enumerate(queries)
            ],
            axis=0,
        )
        keys = jnp.concatenate([k_ref[0, head] for head in members], axis=1)
        values = jnp.concatenate([v_ref[0, head] for head in members], axis=1)
        scores = (
            lax.dot_general(
                spread_out, keys, (((1,), (1,)), ((), ())), preferred_element_type=jnp.float32
            )
            * factor
        )
        own = jnp.concatenate(
            [
                jnp.sum(
                    q.astype(jnp.float32)
                    * turned[query_heads + head : query_heads + head + 1].astype(jnp.float32),
                    axis=1,
                    keepdims=True,
                )
                for q, head in zip(queries, members)
            ],
            axis=0,
        ) * factor
        slot = lax.broadcasted_iota(jnp.int32, scores.shape, 1)
        scores = jnp.where(slot < length, scores, -jnp.inf)
        top = jnp.maximum(jnp.max(scores, axis=1, keepdims=True), own)
        exponent = jnp.exp(scores - top)
        own_exp = jnp.exp(own - top)
        share = 1.0 / (jnp.sum(exponent, axis=1, keepdims=True) + own_exp)
        weights = (exponent * share).astype(jnp.bfloat16)
        own_weight = (own_exp * share).astype(jnp.bfloat16).astype(jnp.float32)
        mixed = jnp.dot(weights, values, preferred_element_type=jnp.float32)
        for i, head in enumerate(members):
            block = mixed[i * group : (i + 1) * group, i * HEAD_SIZE : (i + 1) * HEAD_SIZE]
            block = block + own_weight[i * group : (i + 1) * group] * fresh_values[
                head : head + 1
            ].astype(jnp.float32)
            heads_ref[0, pl.ds(head * group, group), :] = block.astype(jnp.bfloat16)
    for copy in copies:
        copy.wait()


def attend(parts, turn, k_cache, value_cache, query_heads, w_out, part):
    kv_heads, cache_len = k_cache.shape[1:3]
    whole = pl.BlockSpec(memory_space=pltpu.VMEM)
    return pl.pallas_call(
        functools.partial(attend_kernel, query_heads, kv_heads, len(parts), part),
        out_shape=(
            jax.ShapeDtypeStruct((1, query_heads, HEAD_SIZE), jnp.bfloat16),
            jax.ShapeDtypeStruct((part[1], w_out.shape[1]), w_out.dtype),
        ),
        in_specs=[pl.BlockSpec(memory_space=pltpu.HBM)] + [whole] * (3 + len(parts)),
        out_specs=(whole, whole),
        scratch_shapes=[pltpu.SemaphoreType.DMA((PIECES,))],
        compiler_params=pltpu.CompilerParams(vmem_limit_bytes=12 * MIB),
        cost_estimate=pl.CostEstimate(
            flops=4 * query_heads * cache_len * HEAD_SIZE,
            bytes_accessed=4 * kv_heads * cache_len * HEAD_SIZE,
            transcendentals=query_heads * cache_len,
        ),
        name="attend",
    )(in_hbm(w_out), turn, k_cache, value_cache, *parts)


def output_kernel(bits, pieces, *refs):
    parts = refs[:pieces]
    ready = refs[pieces:-5]
    mine_ref, theirs_ref, flat, left, sums = refs[-5:]
    slots = left.shape[0]
    heads = flat.shape[0] // slots
    at = 0
    for ref in parts:
        for i in range(ref.shape[0]):
            flat[at : at + heads, :] = ref[i].astype(jnp.float32)
            at += heads
    for head in range(heads):
        left[:, head * HEAD_SIZE : (head + 1) * HEAD_SIZE] = flat[
            pl.ds(head, slots, stride=heads), :
        ].astype(jnp.bfloat16)
    total = None
    at = 0
    for ref in ready:
        size = ref.shape[0]
        for start, rows in spread(size, 0, 2 * CHUNK):
            term = jnp.dot(
                left[:, at + start : at + start + rows],
                ref[start : start + rows, :],
                preferred_element_type=jnp.float32,
            )
            total = term if total is None else total + term
        at += size
    sums[...] = total
    half = slots // 2
    turn = bit_reverse(lax.axis_index("gx"), bits)
    gy = lax.axis_index("gy")
    for ref, side in ((mine_ref, gy), (theirs_ref, 1 - gy)):
        for t in range(half):
            slot = bit_reverse(t, bits) ^ turn ^ side
            ref[t : t + 1, :] = sums[pl.ds(slot, 1), :]


def output(parts, ready, slots):
    bits = slots.bit_length() - 1
    depth, width = sum(x.shape[0] for x in ready), ready[0].shape[1]
    heads = depth // HEAD_SIZE
    whole = pl.BlockSpec(memory_space=pltpu.VMEM)
    piece = jax.ShapeDtypeStruct((slots // 2, width), jnp.float32)
    return pl.pallas_call(
        functools.partial(output_kernel, bits, len(parts)),
        out_shape=(piece, piece),
        in_specs=[whole] * (len(parts) + len(ready)),
        out_specs=(whole, whole),
        scratch_shapes=[
            pltpu.VMEM((slots * heads, HEAD_SIZE), jnp.float32),
            pltpu.VMEM((slots, depth), jnp.bfloat16),
            pltpu.VMEM((slots, width), jnp.float32),
        ],
        compiler_params=pltpu.CompilerParams(vmem_limit_bytes=24 * MIB),
        cost_estimate=pl.CostEstimate(
            flops=2 * slots * depth * width, bytes_accessed=2 * depth * width, transcendentals=0
        ),
        name="output",
    )(*parts, *ready)


def swap(block, axis, devices, mask):
    return lax.ppermute(block, axis, [(i, i ^ mask) for i in range(devices)])


def fan(pieces, devices):
    masks = [bit_reverse(q, 2) for q in range(FAN)]
    arrived = [None] * FAN
    for q in sorted(range(1, FAN), key=lambda q: (masks[q] + 1) % FAN):
        arrived[q] = swap(pieces[q], "gx", devices, masks[q])
    return arrived[1:]


def body(devices, activations, w_query, key_weight, value_weight, w_out, k_cache, value_cache, lengths):
    slots = devices
    query_heads = w_query.shape[1] // HEAD_SIZE
    other = swap(activations, "gy", 2, 1)
    depth = w_query.shape[0]
    (first,) = stage((w_query,), ((0, min(FIRST, depth)),))
    rows_out = w_out.shape[0]
    fewest, few, most = rows_out // 16, rows_out // 8, rows_out // 4
    *pieces, ready_zero = project(
        activations, other, w_query, first, key_weight, value_weight, w_out, fewest, slots
    )

    *pieces, w_out = lax.optimization_barrier((*pieces, w_out))
    arrived = fan(pieces, devices)
    half = HEAD_SIZE // 2
    frequency = jnp.power(
        jnp.float32(500000.0), -2.0 * jnp.arange(half, dtype=jnp.float32) / HEAD_SIZE
    )
    frequency = jnp.concatenate([frequency, frequency])[None, :]
    turn, ready_one = stage((w_out,), ((fewest, few),), lengths, frequency)
    total = pieces[0] + (arrived[2] + (arrived[1] + arrived[0]))
    mask = FAN
    while total.shape[0] > 2:
        rest = total.shape[0] // 2
        total = total[:rest] + swap(total[rest:], "gx", devices, mask)
        mask *= 2
    total, w_out, ready_one = lax.optimization_barrier((total, w_out, ready_one))
    (ready_two,) = stage((w_out,), ((fewest + few, most),))
    parts = [total[:1], swap(total[1:], "gx", devices, mask)]
    parts[1], ready_two = lax.optimization_barrier((parts[1], ready_two))
    at = fewest + few + most
    heads, ready_more = attend(
        parts, turn, k_cache, value_cache, query_heads, w_out, (at, fewest)
    )

    heads, w_out = lax.optimization_barrier((heads, w_out))
    (ready_three,) = stage((w_out,), ((at + fewest, most),))
    parts = [heads, swap(heads, "gx", devices, mask)]
    parts[1], ready_three = lax.optimization_barrier((parts[1], ready_three))
    while mask > FAN:
        mask //= 2
        parts.append(swap(jnp.concatenate(parts, axis=0), "gx", devices, mask))
    held = jnp.concatenate(parts, axis=0)
    held, w_out = lax.optimization_barrier((held, w_out))
    (ready_four,) = stage((w_out,), ((at + fewest + most, most),))
    parts += fan([held] * FAN, devices)
    parts[-1], ready_four = lax.optimization_barrier((parts[-1], ready_four))
    ready = (ready_zero, ready_one, ready_two, ready_more, ready_three, ready_four)
    mine, theirs = output(parts, ready, slots)
    return (mine + swap(theirs, "gy", 2, 1)).astype(jnp.bfloat16)


def solution(mesh):
    placed = (
        P(("groups", "gy"), "gx"),
        P("gx", "gy"),
        P("gx", "gy"),
        P("gx", "gy"),
        P("gy", "gx"),
        P(("groups", "gx"), "gy", None, None),
        P(("groups", "gx"), "gy", None, None),
        P(("groups", "gx")),
    )
    return jax.shard_map(
        functools.partial(body, mesh.shape["gx"]),
        mesh=mesh,
        in_specs=placed,
        out_specs=P(("groups", "gy"), "gx"),
        check_vma=False,
    )
```

```python
import functools
import math

import jax
import jax.numpy as jnp
from jax import lax
from jax.experimental import pallas as pl
from jax.experimental.pallas import tpu as pltpu
from jax.sharding import PartitionSpec as P

MODEL_WIDTH = 16384
LANES = 128
HEAD_SIZE = 128
CHUNK = 256
FIRST = 256
PIECES = 4
FAN = 4
MIB = 2**20


def bit_reverse(value, bits):
    turned = 0
    for bit in range(bits):
        turned = turned | (((value >> bit) & 1) << (bits - 1 - bit))
    return turned


def in_hbm(array):
    return pltpu.with_memory_space_constraint(array, pltpu.HBM)


def cut(start, size):
    if size % (16 * PIECES):
        return [(start, size)]
    return [(start + i * (size // PIECES), size // PIECES) for i in range(PIECES)]


def copies_in(src, dst, sems, start, size, offset):
    return [
        pltpu.make_async_copy(
            src.at[pl.ds(at, rows)], dst.at[pl.ds(at - start + offset, rows)], sems.at[i]
        )
        for i, (at, rows) in enumerate(cut(start, size))
    ]


def stage_kernel(parts, *refs):
    count = len(parts)
    sems = refs[-1]
    copies = []
    for i, (start, size) in enumerate(parts):
        copies += copies_in(refs[i], refs[count + i], sems.at[i], start, size, 0)
    for copy in copies:
        copy.start()
    return copies


def plain_stage_kernel(parts, *refs):
    for copy in stage_kernel(parts, *refs):
        copy.wait()


def turning_stage_kernel(parts, length_ref, frequency_ref, turn_ref, *refs):
    copies = stage_kernel(parts, *refs)
    position = length_ref[0].astype(jnp.float32)
    angle = position * frequency_ref[...]
    lane = lax.broadcasted_iota(jnp.int32, angle.shape, 1)
    sine = jnp.sin(angle)
    turn_ref[0:1, :] = jnp.cos(angle)
    turn_ref[1:2, :] = jnp.where(lane < HEAD_SIZE // 2, -sine, sine)
    turn_ref[2:3, :] = jnp.full(angle.shape, position)
    for copy in copies:
        copy.wait()


def stage(arrays, parts, lengths=None, frequency=None):
    shapes = tuple(
        jax.ShapeDtypeStruct((part[1], *a.shape[1:]), a.dtype) for a, part in zip(arrays, parts)
    )
    vmem = pl.BlockSpec(memory_space=pltpu.VMEM)
    in_specs = [pl.BlockSpec(memory_space=pltpu.HBM)] * len(arrays)
    out_specs = [vmem] * len(arrays)
    kernel = functools.partial(plain_stage_kernel, parts)
    pinned = [in_hbm(a) for a in arrays]
    out_shape = shapes
    if lengths is not None:
        count = len(arrays)

        def kernel(length_ref, frequency_ref, *refs):
            turn_ref = refs[count]
            turning_stage_kernel(
                parts, length_ref, frequency_ref, turn_ref, *refs[:count], *refs[count + 1 :]
            )

        in_specs = [pl.BlockSpec(memory_space=pltpu.SMEM), vmem] + in_specs
        out_specs = [vmem] + out_specs
        out_shape = (jax.ShapeDtypeStruct((8, HEAD_SIZE), jnp.float32), *shapes)
        pinned = [lengths, frequency] + pinned
    return pl.pallas_call(
        kernel,
        out_shape=out_shape,
        in_specs=in_specs,
        out_specs=tuple(out_specs),
        scratch_shapes=[pltpu.SemaphoreType.DMA((len(arrays), PIECES))],
        compiler_params=pltpu.CompilerParams(vmem_limit_bytes=16 * MIB),
        cost_estimate=pl.CostEstimate(
            flops=0, bytes_accessed=sum(2 * math.prod(x.shape) for x in shapes), transcendentals=0
        ),
        name="stage",
    )(*pinned)


def spread(depth, skip, chunk):
    return [(at, min(chunk, depth - at)) for at in range(skip, depth, chunk)]


def tapered(ranges):
    *most, (start, size) = ranges
    if size < 2 * LANES:
        return ranges
    return most + [(start, size - LANES), (start + size - LANES, LANES)]


def feed(depth, skip):
    ranges = spread(depth, skip, CHUNK)
    return tapered(ranges) if ranges else ranges


def project_kernel(
    bits, rows_ref, other_ref, wq_hbm, first, wk, wv, *refs
):
    pieces, (wq, rows, sems) = refs[:FAN], refs[FAN:]
    skip = first.shape[0]
    ranges = feed(wq_hbm.shape[0], skip)
    copies = [
        copies_in(wq_hbm, wq, sems.at[i], start, size, start - skip)
        for i, (start, size) in enumerate(ranges)
    ]
    for group in copies:
        for copy in group:
            copy.start()

    slots = rows.shape[0]
    half = slots // 2
    turn = bit_reverse(lax.axis_index("gx"), bits)
    gy = lax.axis_index("gy")
    for ref, side in ((rows_ref, gy), (other_ref, 1 - gy)):
        block = ref[...].astype(jnp.float32)
        for t in range(half):
            slot = bit_reverse(t, bits) ^ turn ^ side
            rows[pl.ds(slot, 1), :] = block[t : t + 1, :]
    wide = rows[...]
    squares = jnp.sum(wide * wide, axis=1, keepdims=True)
    narrow = wide.astype(jnp.bfloat16)

    fresh = [jnp.dot(narrow, w[...], preferred_element_type=jnp.float32) for w in (wk, wv)]
    sums = jnp.dot(narrow[:, :skip], first[...], preferred_element_type=jnp.float32)
    for (start, size), group in zip(ranges, copies):
        for copy in group:
            copy.wait()
        sums = sums + jnp.dot(
            narrow[:, start : start + size],
            wq[start - skip : start - skip + size, :],
            preferred_element_type=jnp.float32,
        )

    total = pieces[0].shape[1]
    blocks = []
    for part in (sums, *fresh):
        blocks += [part[:, i : i + LANES] for i in range(0, part.shape[1], LANES)]
    blocks.append(jnp.broadcast_to(squares, (slots, LANES)))
    blocks += [jnp.zeros((slots, LANES), jnp.float32)] * (total - len(blocks))
    size = slots // FAN
    for at, ref in enumerate(pieces):
        flat = ref.reshape(size * total, LANES)
        for i, block in enumerate(blocks):
            flat[pl.ds(i, size, stride=total), :] = block[at * size : (at + 1) * size]


def project(rows, other, w_query, first, key_weight, value_weight, slots):
    bits = slots.bit_length() - 1
    depth, query_width = w_query.shape
    kv_width = key_weight.shape[1]
    used = (query_width + 2 * kv_width) // LANES + 1
    total = -(-used // 8) * 8
    skip = first.shape[0]
    piece = jax.ShapeDtypeStruct((slots // FAN, total, LANES), jnp.float32)
    hbm = pl.BlockSpec(memory_space=pltpu.HBM)
    whole = pl.BlockSpec(memory_space=pltpu.VMEM)
    return pl.pallas_call(
        functools.partial(project_kernel, bits),
        out_shape=(piece,) * FAN,
        in_specs=[whole, whole, hbm, whole, whole, whole],
        out_specs=(whole,) * FAN,
        scratch_shapes=[
            pltpu.VMEM((max(depth - skip, 16), query_width), jnp.bfloat16),
            pltpu.VMEM((slots, depth), jnp.float32),
            pltpu.SemaphoreType.DMA((max(1, len(feed(depth, skip))), PIECES)),
        ],
        compiler_params=pltpu.CompilerParams(vmem_limit_bytes=32 * MIB),
        cost_estimate=pl.CostEstimate(
            flops=2 * slots * depth * (query_width + 2 * kv_width),
            bytes_accessed=2 * depth * (query_width + 2 * kv_width),
            transcendentals=0,
        ),
        name="project",
    )(rows, other, in_hbm(w_query), first, key_weight, value_weight)


def attend_kernel(query_heads, kv_heads, pieces, turn_ref, k_ref, v_ref, *refs):
    heads_ref = refs[pieces]
    total = refs[0][0]
    for ref in refs[1:pieces]:
        total = total + ref[0]
    at = query_heads + 2 * kv_heads
    scale = lax.rsqrt(total[at : at + 1, :] / MODEL_WIDTH + 1e-05)
    turned = total[: query_heads + kv_heads] * scale
    half = HEAD_SIZE // 2
    swapped = jnp.concatenate([turned[:, half:], turned[:, :half]], axis=1)
    turned = (turned * turn_ref[0:1, :] + swapped * turn_ref[1:2, :]).astype(jnp.bfloat16)
    fresh_values = (total[query_heads + kv_heads : at] * scale).astype(jnp.bfloat16)
    group = query_heads // kv_heads
    factor = 1.0 / math.sqrt(HEAD_SIZE)
    length = turn_ref[2:3, 0:1].astype(jnp.int32)
    side = 2 if kv_heads % 2 == 0 else 1
    for first in range(0, kv_heads, side):
        members = range(first, first + side)
        queries = [turned[head * group : (head + 1) * group] for head in members]
        empty = jnp.zeros((group, HEAD_SIZE), jnp.bfloat16)
        spread_out = jnp.concatenate(
            [
                jnp.concatenate([q if i == j else empty for j in range(side)], axis=1)
                for i, q in enumerate(queries)
            ],
            axis=0,
        )
        keys = jnp.concatenate([k_ref[0, head] for head in members], axis=1)
        values = jnp.concatenate([v_ref[0, head] for head in members], axis=1)
        scores = (
            lax.dot_general(
                spread_out, keys, (((1,), (1,)), ((), ())), preferred_element_type=jnp.float32
            )
            * factor
        )
        own = jnp.concatenate(
            [
                jnp.sum(
                    q.astype(jnp.float32)
                    * turned[query_heads + head : query_heads + head + 1].astype(jnp.float32),
                    axis=1,
                    keepdims=True,
                )
                for q, head in zip(queries, members)
            ],
            axis=0,
        ) * factor
        slot = lax.broadcasted_iota(jnp.int32, scores.shape, 1)
        scores = jnp.where(slot < length, scores, -jnp.inf)
        top = jnp.maximum(jnp.max(scores, axis=1, keepdims=True), own)
        exponent = jnp.exp(scores - top)
        own_exp = jnp.exp(own - top)
        share = 1.0 / (jnp.sum(exponent, axis=1, keepdims=True) + own_exp)
        weights = (exponent * share).astype(jnp.bfloat16)
        own_weight = (own_exp * share).astype(jnp.bfloat16).astype(jnp.float32)
        mixed = jnp.dot(weights, values, preferred_element_type=jnp.float32)
        for i, head in enumerate(members):
            block = mixed[i * group : (i + 1) * group, i * HEAD_SIZE : (i + 1) * HEAD_SIZE]
            block = block + own_weight[i * group : (i + 1) * group] * fresh_values[
                head : head + 1
            ].astype(jnp.float32)
            block = block.astype(jnp.bfloat16)
            for i in range(heads_ref.shape[0]):
                heads_ref[i, pl.ds(head * group, group), :] = block


def attend(parts, turn, k_cache, value_cache, query_heads, copies):
    kv_heads, cache_len = k_cache.shape[1:3]
    whole = pl.BlockSpec(memory_space=pltpu.VMEM)
    return pl.pallas_call(
        functools.partial(attend_kernel, query_heads, kv_heads, len(parts)),
        out_shape=jax.ShapeDtypeStruct((copies, query_heads, HEAD_SIZE), jnp.bfloat16),
        in_specs=[whole] * (3 + len(parts)),
        out_specs=whole,
        compiler_params=pltpu.CompilerParams(vmem_limit_bytes=12 * MIB),
        cost_estimate=pl.CostEstimate(
            flops=4 * query_heads * cache_len * HEAD_SIZE,
            bytes_accessed=4 * kv_heads * cache_len * HEAD_SIZE,
            transcendentals=query_heads * cache_len,
        ),
        name="attend",
    )(turn, k_cache, value_cache, *parts)


def output_kernel(arrived_ref, *refs):
    ready = refs[:-5]
    mine_ref, theirs_ref, flat, left, sums = refs[-5:]
    slots, heads = arrived_ref.shape[:2]
    for i in range(slots):
        row = slots - 1 - i
        flat[row * heads : (row + 1) * heads, :] = arrived_ref[i].astype(jnp.float32)
    for head in range(heads):
        left[:, head * HEAD_SIZE : (head + 1) * HEAD_SIZE] = flat[
            pl.ds(head, slots, stride=heads), :
        ].astype(jnp.bfloat16)
    total = None
    at = 0
    for ref in ready:
        size = ref.shape[0]
        for start, rows in spread(size, 0, 2 * CHUNK):
            term = jnp.dot(
                left[:, at + start : at + start + rows],
                ref[start : start + rows, :],
                preferred_element_type=jnp.float32,
            )
            total = term if total is None else total + term
        at += size
    sums[...] = total
    half = slots // 2
    gy = lax.axis_index("gy")
    lower, upper = sums[:half], sums[half:]
    mine_ref[...] = jnp.where(gy == 0, lower, upper)
    theirs_ref[...] = jnp.where(gy == 0, upper, lower)


def output(arrived, ready):
    slots, heads = arrived.shape[:2]
    depth, width = sum(x.shape[0] for x in ready), ready[0].shape[1]
    whole = pl.BlockSpec(memory_space=pltpu.VMEM)
    piece = jax.ShapeDtypeStruct((slots // 2, width), jnp.float32)
    return pl.pallas_call(
        output_kernel,
        out_shape=(piece, piece),
        in_specs=[whole] * (1 + len(ready)),
        out_specs=(whole, whole),
        scratch_shapes=[
            pltpu.VMEM((slots * heads, HEAD_SIZE), jnp.float32),
            pltpu.VMEM((slots, depth), jnp.bfloat16),
            pltpu.VMEM((slots, width), jnp.float32),
        ],
        compiler_params=pltpu.CompilerParams(vmem_limit_bytes=24 * MIB),
        cost_estimate=pl.CostEstimate(
            flops=2 * slots * depth * width, bytes_accessed=2 * depth * width, transcendentals=0
        ),
        name="output",
    )(arrived, *ready)


def swap(block, axis, devices, mask):
    return lax.ppermute(block, axis, [(i, i ^ mask) for i in range(devices)])


def fan(pieces, devices):
    masks = [bit_reverse(q, 2) for q in range(FAN)]
    arrived = [None] * FAN
    for q in sorted(range(1, FAN), key=lambda q: (masks[q] + 1) % FAN):
        arrived[q] = swap(pieces[q], "gx", devices, masks[q])
    return arrived[1:]


def body(devices, activations, w_query, key_weight, value_weight, w_out, k_cache, value_cache, lengths):
    slots = devices
    query_heads = w_query.shape[1] // HEAD_SIZE
    other = swap(activations, "gy", 2, 1)
    depth = w_query.shape[0]
    (first,) = stage((w_query,), ((0, min(FIRST, depth)),))
    pieces = project(activations, other, w_query, first, key_weight, value_weight, slots)

    rows_out = w_out.shape[0]
    *pieces, w_out = lax.optimization_barrier((*pieces, w_out))
    few, most = rows_out // 8, rows_out // 4
    arrived = fan(pieces, devices)
    half = HEAD_SIZE // 2
    frequency = jnp.power(
        jnp.float32(500000.0), -2.0 * jnp.arange(half, dtype=jnp.float32) / HEAD_SIZE
    )
    frequency = jnp.concatenate([frequency, frequency])[None, :]
    turn, ready_one = stage((w_out,), ((0, few),), lengths, frequency)
    total = pieces[0] + (arrived[2] + (arrived[1] + arrived[0]))
    mask = FAN
    while total.shape[0] > 2:
        rest = total.shape[0] // 2
        total = total[:rest] + swap(total[rest:], "gx", devices, mask)
        mask *= 2
    total, w_out, ready_one = lax.optimization_barrier((total, w_out, ready_one))
    (ready_two,) = stage((w_out,), ((few, most),))
    parts = [total[:1], swap(total[1:], "gx", devices, mask)]
    parts[1], ready_two = lax.optimization_barrier((parts[1], ready_two))
    heads = attend(parts, turn, k_cache, value_cache, query_heads, devices)

    heads, w_out = lax.optimization_barrier((heads, w_out))
    ready_three, = stage((w_out,), ((few + most, most),))
    ready_four, = stage((w_out,), ((few + 2 * most, rows_out - few - 2 * most),))
    arrived = lax.all_to_all(
        heads, "gx", 0, 0, axis_index_groups=[list(range(devices))[::-1]], tiled=True
    )
    ready = (ready_one, ready_two, ready_three, ready_four)
    mine, theirs = output(arrived, ready)
    return (mine + swap(theirs, "gy", 2, 1)).astype(jnp.bfloat16)


def solution(mesh):
    placed = (
        P(("groups", "gy"), "gx"),
        P("gx", "gy"),
        P("gx", "gy"),
        P("gx", "gy"),
        P("gy", "gx"),
        P(("groups", "gx"), "gy", None, None),
        P(("groups", "gx"), "gy", None, None),
        P(("groups", "gx")),
    )
    return jax.shard_map(
        functools.partial(body, mesh.shape["gx"]),
        mesh=mesh,
        in_specs=placed,
        out_specs=P(("groups", "gy"), "gx"),
        check_vma=False,
    )
```

```python
import functools
import math

import jax
import jax.numpy as jnp
from jax import lax
from jax.experimental import pallas as pl
from jax.experimental.pallas import tpu as pltpu
from jax.sharding import PartitionSpec as P

MODEL_WIDTH = 16384
LANES = 128
HEAD_SIZE = 128
CHUNK = 256
FIRST = 256
PIECES = 4
FAN = 4
MIB = 2**20


def bit_reverse(value, bits):
    turned = 0
    for bit in range(bits):
        turned = turned | (((value >> bit) & 1) << (bits - 1 - bit))
    return turned


def in_hbm(array):
    return pltpu.with_memory_space_constraint(array, pltpu.HBM)


def cut(start, size):
    if size % (16 * PIECES):
        return [(start, size)]
    return [(start + i * (size // PIECES), size // PIECES) for i in range(PIECES)]


def copies_in(src, dst, sems, start, size, offset):
    return [
        pltpu.make_async_copy(
            src.at[pl.ds(at, rows)], dst.at[pl.ds(at - start + offset, rows)], sems.at[i]
        )
        for i, (at, rows) in enumerate(cut(start, size))
    ]


def stage_kernel(rows, src, dst, sems):
    copies = copies_in(src, dst, sems, 0, rows, 0)
    for copy in copies:
        copy.start()
    for copy in copies:
        copy.wait()


def stage_rows(array, rows):
    vmem = pl.BlockSpec(memory_space=pltpu.VMEM)
    return pl.pallas_call(
        functools.partial(stage_kernel, rows),
        out_shape=jax.ShapeDtypeStruct((rows, array.shape[1]), array.dtype),
        in_specs=[pl.BlockSpec(memory_space=pltpu.HBM)],
        out_specs=vmem,
        scratch_shapes=[pltpu.SemaphoreType.DMA((PIECES,))],
        compiler_params=pltpu.CompilerParams(vmem_limit_bytes=16 * MIB),
        cost_estimate=pl.CostEstimate(
            flops=0, bytes_accessed=2 * rows * array.shape[1], transcendentals=0
        ),
        name="stage",
    )(in_hbm(array))


def turning_kernel(length_ref, frequency_ref, beside_ref, turn_ref):
    position = length_ref[0].astype(jnp.float32)
    angle = position * frequency_ref[...]
    lane = lax.broadcasted_iota(jnp.int32, angle.shape, 1)
    sine = jnp.sin(angle)
    turn_ref[0:1, :] = jnp.cos(angle)
    turn_ref[1:2, :] = jnp.where(lane < HEAD_SIZE // 2, -sine, sine)
    turn_ref[2:3, :] = jnp.full(angle.shape, position)


def turning(lengths, frequency, beside):
    vmem = pl.BlockSpec(memory_space=pltpu.VMEM)
    return pl.pallas_call(
        turning_kernel,
        out_shape=jax.ShapeDtypeStruct((8, HEAD_SIZE), jnp.float32),
        in_specs=[
            pl.BlockSpec(memory_space=pltpu.SMEM),
            vmem,
            pl.BlockSpec(memory_space=pltpu.HBM),
        ],
        out_specs=vmem,
        compiler_params=pltpu.CompilerParams(vmem_limit_bytes=2 * MIB),
        cost_estimate=pl.CostEstimate(flops=0, bytes_accessed=2 * beside.size, transcendentals=256),
        name="turning",
    )(lengths, frequency, in_hbm(beside))


def spread(depth, skip, chunk):
    ranges = [(at, min(chunk, depth - at)) for at in range(skip, depth, chunk)]
    if ranges and ranges[-1][1] >= 2 * LANES:
        start, size = ranges.pop()
        ranges += [(start, size - LANES), (start + size - LANES, LANES)]
    return ranges


def project_kernel(
    bits, rows_ref, other_ref, wq_hbm, first, wk, wv, *refs
):
    pieces, (wq, rows, sems) = refs[:FAN], refs[FAN:]
    skip = first.shape[0]
    ranges = spread(wq_hbm.shape[0], skip, CHUNK)
    copies = [
        copies_in(wq_hbm, wq, sems.at[i], start, size, start - skip)
        for i, (start, size) in enumerate(ranges)
    ]
    for group in copies:
        for copy in group:
            copy.start()

    slots = rows.shape[0]
    half = slots // 2
    turn = bit_reverse(lax.axis_index("gx"), bits)
    gy = lax.axis_index("gy")
    for ref, side in ((rows_ref, gy), (other_ref, 1 - gy)):
        block = ref[...].astype(jnp.float32)
        for t in range(half):
            slot = bit_reverse(t, bits) ^ turn ^ side
            rows[pl.ds(slot, 1), :] = block[t : t + 1, :]
    wide = rows[...]
    squares = jnp.sum(wide * wide, axis=1, keepdims=True)
    narrow = wide.astype(jnp.bfloat16)

    fresh = [jnp.dot(narrow, w[...], preferred_element_type=jnp.float32) for w in (wk, wv)]
    sums = jnp.dot(narrow[:, :skip], first[...], preferred_element_type=jnp.float32)
    for (start, size), group in zip(ranges, copies):
        for copy in group:
            copy.wait()
        sums = sums + jnp.dot(
            narrow[:, start : start + size],
            wq[start - skip : start - skip + size, :],
            preferred_element_type=jnp.float32,
        )

    total = pieces[0].shape[1]
    blocks = []
    for part in (sums, *fresh):
        blocks += [part[:, i : i + LANES] for i in range(0, part.shape[1], LANES)]
    blocks.append(jnp.broadcast_to(squares, (slots, LANES)))
    blocks += [jnp.zeros((slots, LANES), jnp.float32)] * (total - len(blocks))
    size = slots // FAN
    for at, ref in enumerate(pieces):
        flat = ref.reshape(size * total, LANES)
        for i, block in enumerate(blocks):
            flat[pl.ds(i, size, stride=total), :] = block[at * size : (at + 1) * size]


def project(rows, other, w_query, first, key_weight, value_weight, slots):
    bits = slots.bit_length() - 1
    depth, query_width = w_query.shape
    kv_width = key_weight.shape[1]
    used = (query_width + 2 * kv_width) // LANES + 1
    total = -(-used // 8) * 8
    skip = first.shape[0]
    piece = jax.ShapeDtypeStruct((slots // FAN, total, LANES), jnp.float32)
    hbm = pl.BlockSpec(memory_space=pltpu.HBM)
    whole = pl.BlockSpec(memory_space=pltpu.VMEM)
    return pl.pallas_call(
        functools.partial(project_kernel, bits),
        out_shape=(piece,) * FAN,
        in_specs=[whole, whole, hbm, whole, whole, whole],
        out_specs=(whole,) * FAN,
        scratch_shapes=[
            pltpu.VMEM((max(depth - skip, 16), query_width), jnp.bfloat16),
            pltpu.VMEM((slots, depth), jnp.float32),
            pltpu.SemaphoreType.DMA((max(1, len(spread(depth, skip, CHUNK))), PIECES)),
        ],
        compiler_params=pltpu.CompilerParams(vmem_limit_bytes=46 * MIB),
        cost_estimate=pl.CostEstimate(
            flops=2 * slots * depth * (query_width + 2 * kv_width),
            bytes_accessed=2 * depth * (query_width + 2 * kv_width),
            transcendentals=0,
        ),
        name="project",
    )(rows, other, in_hbm(w_query), first, key_weight, value_weight)


def attend_kernel(
    query_heads, kv_heads, pieces, beside_ref, turn_ref, k_ref, v_ref, *refs
):
    heads_ref = refs[pieces]
    total = refs[0][0]
    for ref in refs[1:pieces]:
        total = total + ref[0]
    at = query_heads + 2 * kv_heads
    scale = lax.rsqrt(total[at : at + 1, :] / MODEL_WIDTH + 1e-05)
    turned = total[: query_heads + kv_heads] * scale
    half = HEAD_SIZE // 2
    swapped = jnp.concatenate([turned[:, half:], turned[:, :half]], axis=1)
    turned = (turned * turn_ref[0:1, :] + swapped * turn_ref[1:2, :]).astype(jnp.bfloat16)
    fresh_values = (total[query_heads + kv_heads : at] * scale).astype(jnp.bfloat16)
    group = query_heads // kv_heads
    factor = 1.0 / math.sqrt(HEAD_SIZE)
    length = turn_ref[2:3, 0:1].astype(jnp.int32)
    side = 2 if kv_heads % 2 == 0 else 1
    for first in range(0, kv_heads, side):
        members = range(first, first + side)
        queries = [turned[head * group : (head + 1) * group] for head in members]
        empty = jnp.zeros((group, HEAD_SIZE), jnp.bfloat16)
        spread_out = jnp.concatenate(
            [
                jnp.concatenate([q if i == j else empty for j in range(side)], axis=1)
                for i, q in enumerate(queries)
            ],
            axis=0,
        )
        keys = jnp.concatenate([k_ref[0, head] for head in members], axis=1)
        values = jnp.concatenate([v_ref[0, head] for head in members], axis=1)
        scores = (
            lax.dot_general(
                spread_out, keys, (((1,), (1,)), ((), ())), preferred_element_type=jnp.float32
            )
            * factor
        )
        own = jnp.concatenate(
            [
                jnp.sum(
                    q.astype(jnp.float32)
                    * turned[query_heads + head : query_heads + head + 1].astype(jnp.float32),
                    axis=1,
                    keepdims=True,
                )
                for q, head in zip(queries, members)
            ],
            axis=0,
        ) * factor
        slot = lax.broadcasted_iota(jnp.int32, scores.shape, 1)
        scores = jnp.where(slot < length, scores, -jnp.inf)
        top = jnp.maximum(jnp.max(scores, axis=1, keepdims=True), own)
        exponent = jnp.exp(scores - top)
        own_exp = jnp.exp(own - top)
        share = 1.0 / (jnp.sum(exponent, axis=1, keepdims=True) + own_exp)
        weights = (exponent * share).astype(jnp.bfloat16)
        own_weight = (own_exp * share).astype(jnp.bfloat16).astype(jnp.float32)
        mixed = jnp.dot(weights, values, preferred_element_type=jnp.float32)
        for i, head in enumerate(members):
            block = mixed[i * group : (i + 1) * group, i * HEAD_SIZE : (i + 1) * HEAD_SIZE]
            block = block + own_weight[i * group : (i + 1) * group] * fresh_values[
                head : head + 1
            ].astype(jnp.float32)
            heads_ref[0, pl.ds(head * group, group), :] = block.astype(jnp.bfloat16)


def attend(parts, turn, k_cache, value_cache, query_heads, beside):
    kv_heads, cache_len = k_cache.shape[1:3]
    whole = pl.BlockSpec(memory_space=pltpu.VMEM)
    return pl.pallas_call(
        functools.partial(attend_kernel, query_heads, kv_heads, len(parts)),
        out_shape=jax.ShapeDtypeStruct((1, query_heads, HEAD_SIZE), jnp.bfloat16),
        in_specs=[pl.BlockSpec(memory_space=pltpu.HBM)] + [whole] * (3 + len(parts)),
        out_specs=whole,
        compiler_params=pltpu.CompilerParams(vmem_limit_bytes=12 * MIB),
        cost_estimate=pl.CostEstimate(
            flops=4 * query_heads * cache_len * HEAD_SIZE,
            bytes_accessed=4 * kv_heads * cache_len * HEAD_SIZE,
            transcendentals=query_heads * cache_len,
        ),
        name="attend",
    )(in_hbm(beside), turn, k_cache, value_cache, *parts)


def output_kernel(bits, pieces, *refs):
    parts = refs[:pieces][::-1]
    w_ref, mine_ref, theirs_ref, flat, left, sums = refs[pieces:]
    slots = left.shape[0]
    heads = flat.shape[0] // slots
    at = 0
    for ref in parts:
        for i in range(ref.shape[0]):
            flat[at : at + heads, :] = ref[i].astype(jnp.float32)
            at += heads
    for head in range(heads):
        left[:, head * HEAD_SIZE : (head + 1) * HEAD_SIZE] = flat[
            pl.ds(head, slots, stride=heads), :
        ].astype(jnp.bfloat16)
    total = None
    depth = w_ref.shape[0]
    chunk = min(2 * CHUNK, depth)
    for at in range(0, depth, chunk):
        part = slice(at, at + chunk)
        term = jnp.dot(left[:, part], w_ref[part, :], preferred_element_type=jnp.float32)
        total = term if total is None else total + term
    sums[...] = total
    half = slots // 2
    turn = bit_reverse(lax.axis_index("gx"), bits)
    gy = lax.axis_index("gy")
    for ref, side in ((mine_ref, gy), (theirs_ref, 1 - gy)):
        for t in range(half):
            slot = bit_reverse(t, bits) ^ turn ^ side
            ref[t : t + 1, :] = sums[pl.ds(slot, 1), :]


def output(parts, w_out, slots):
    bits = slots.bit_length() - 1
    depth, width = w_out.shape
    heads = depth // HEAD_SIZE
    whole = pl.BlockSpec(memory_space=pltpu.VMEM)
    piece = jax.ShapeDtypeStruct((slots // 2, width), jnp.float32)
    return pl.pallas_call(
        functools.partial(output_kernel, bits, len(parts)),
        out_shape=(piece, piece),
        in_specs=[whole] * (len(parts) + 1),
        out_specs=(whole, whole),
        scratch_shapes=[
            pltpu.VMEM((slots * heads, HEAD_SIZE), jnp.float32),
            pltpu.VMEM((slots, depth), jnp.bfloat16),
            pltpu.VMEM((slots, width), jnp.float32),
        ],
        compiler_params=pltpu.CompilerParams(vmem_limit_bytes=12 * MIB),
        cost_estimate=pl.CostEstimate(
            flops=2 * slots * depth * width, bytes_accessed=2 * depth * width, transcendentals=0
        ),
        name="output",
    )(*parts, w_out)


def swap(block, axis, devices, mask):
    return lax.ppermute(block, axis, [(i, i ^ mask) for i in range(devices)])


def fan(pieces, devices):
    masks = [bit_reverse(q, 2) for q in range(FAN)]
    arrived = [None] * FAN
    for q in sorted(range(1, FAN), key=lambda q: (masks[q] + 1) % FAN):
        arrived[q] = swap(pieces[q], "gx", devices, masks[q])
    return arrived[1:]


def body(devices, activations, w_query, key_weight, value_weight, w_out, k_cache, value_cache, lengths):
    slots = devices
    query_heads = w_query.shape[1] // HEAD_SIZE
    other = swap(activations, "gy", 2, 1)
    depth = w_query.shape[0]
    first = stage_rows(w_query, min(FIRST, depth))
    pieces = project(activations, other, w_query, first, key_weight, value_weight, slots)

    arrived = fan(pieces, devices)
    half = HEAD_SIZE // 2
    frequency = jnp.power(
        jnp.float32(500000.0), -2.0 * jnp.arange(half, dtype=jnp.float32) / HEAD_SIZE
    )
    frequency = jnp.concatenate([frequency, frequency])[None, :]
    turn = turning(lengths, frequency, w_out)
    total = pieces[0] + (arrived[2] + (arrived[1] + arrived[0]))
    mask = FAN
    while total.shape[0] > 2:
        rest = total.shape[0] // 2
        total = total[:rest] + swap(total[rest:], "gx", devices, mask)
        mask *= 2
    total, turn = lax.optimization_barrier((total, turn))
    parts = [total[:1], swap(total[1:], "gx", devices, mask)]
    heads = attend(parts, turn, k_cache, value_cache, query_heads, w_out)

    parts = [heads, swap(heads, "gx", devices, mask)]
    while mask > FAN:
        mask //= 2
        parts.append(swap(jnp.concatenate(parts, axis=0), "gx", devices, mask))
    held = jnp.concatenate(parts, axis=0)
    parts += fan([held] * FAN, devices)
    mine, theirs = output(parts[::-1], w_out, slots)
    return (mine + swap(theirs, "gy", 2, 1)).astype(jnp.bfloat16)


def solution(mesh):
    placed = (
        P(("groups", "gy"), "gx"),
        P("gx", "gy"),
        P("gx", "gy"),
        P("gx", "gy"),
        P("gy", "gx"),
        P(("groups", "gx"), "gy", None, None),
        P(("groups", "gx"), "gy", None, None),
        P(("groups", "gx")),
    )
    return jax.shard_map(
        functools.partial(body, mesh.shape["gx"]),
        mesh=mesh,
        in_specs=placed,
        out_specs=P(("groups", "gy"), "gx"),
        check_vma=False,
    )
```

```python
import functools
import math

import jax
import jax.numpy as jnp
from jax import lax
from jax.experimental import pallas as pl
from jax.experimental.pallas import tpu as pltpu
from jax.sharding import PartitionSpec as P

MODEL_WIDTH = 16384
LANES = 128
HEAD_SIZE = 128
CHUNK = 256
FIRST = 256
PIECES = 4
FAN = 4
BLOCK = 8
TO_OWNERS = (
    "--016-54",
    "-210--75",
    "203-54--",
    "3---764-",
    "13-2-7-6",
)
TO_ALL = (
    "-0----45",
    "--0-54--",
    "32107654",
    "1-3267--",
    "23-1--76",
)
MIB = 2**20
LAST = 2


def pairs_of(order, devices):
    return [
        (block + g, block + int(to))
        for block in range(0, devices, BLOCK)
        for g, to in enumerate(order)
        if to != "-"
    ]


def sent_pieces(order):
    return [0 if to == "-" else bit_reverse(g ^ int(to), 2) for g, to in enumerate(order)]


def arriving_pieces(order):
    pieces = [FAN] * BLOCK
    for g, to in enumerate(order):
        if to != "-":
            pieces[int(to)] = bit_reverse(g ^ int(to), 2)
    return pieces


def look_up(table, device):
    packed = sum(entry << (4 * g) for g, entry in enumerate(table))
    return (jnp.int32(packed) >> (4 * (device % BLOCK))) & 7


def bit_reverse(value, bits):
    turned = 0
    for bit in range(bits):
        turned = turned | (((value >> bit) & 1) << (bits - 1 - bit))
    return turned


def in_hbm(array):
    return pltpu.with_memory_space_constraint(array, pltpu.HBM)


def cut(start, size):
    if size % (16 * PIECES):
        return [(start, size)]
    return [(start + i * (size // PIECES), size // PIECES) for i in range(PIECES)]


def copies_in(src, dst, sems, start, size, offset):
    return [
        pltpu.make_async_copy(
            src.at[pl.ds(at, rows)], dst.at[pl.ds(at - start + offset, rows)], sems.at[i]
        )
        for i, (at, rows) in enumerate(cut(start, size))
    ]


def stage_kernel(rows, src, dst, sems):
    copies = copies_in(src, dst, sems, 0, rows, 0)
    for copy in copies:
        copy.start()
    for copy in copies:
        copy.wait()


def stage_rows(array, rows):
    vmem = pl.BlockSpec(memory_space=pltpu.VMEM)
    return pl.pallas_call(
        functools.partial(stage_kernel, rows),
        out_shape=jax.ShapeDtypeStruct((rows, array.shape[1]), array.dtype),
        in_specs=[pl.BlockSpec(memory_space=pltpu.HBM)],
        out_specs=vmem,
        scratch_shapes=[pltpu.SemaphoreType.DMA((PIECES,))],
        compiler_params=pltpu.CompilerParams(vmem_limit_bytes=16 * MIB),
        cost_estimate=pl.CostEstimate(
            flops=0, bytes_accessed=2 * rows * array.shape[1], transcendentals=0
        ),
        name="stage",
    )(in_hbm(array))


def turning_kernel(length_ref, frequency_ref, beside_ref, turn_ref):
    position = length_ref[0].astype(jnp.float32)
    angle = position * frequency_ref[...]
    lane = lax.broadcasted_iota(jnp.int32, angle.shape, 1)
    sine = jnp.sin(angle)
    turn_ref[0:1, :] = jnp.cos(angle)
    turn_ref[1:2, :] = jnp.where(lane < HEAD_SIZE // 2, -sine, sine)
    turn_ref[2:3, :] = jnp.full(angle.shape, position)


def turning(lengths, frequency, beside):
    vmem = pl.BlockSpec(memory_space=pltpu.VMEM)
    return pl.pallas_call(
        turning_kernel,
        out_shape=jax.ShapeDtypeStruct((8, HEAD_SIZE), jnp.float32),
        in_specs=[
            pl.BlockSpec(memory_space=pltpu.SMEM),
            vmem,
            pl.BlockSpec(memory_space=pltpu.HBM),
        ],
        out_specs=vmem,
        compiler_params=pltpu.CompilerParams(vmem_limit_bytes=2 * MIB),
        cost_estimate=pl.CostEstimate(flops=0, bytes_accessed=2 * beside.size, transcendentals=256),
        name="turning",
    )(lengths, frequency, in_hbm(beside))


def spread(depth, skip, chunk):
    ranges = [(at, min(chunk, depth - at)) for at in range(skip, depth, chunk)]
    if ranges and ranges[-1][1] >= 2 * LANES:
        start, size = ranges.pop()
        ranges += [(start, size - LANES), (start + size - LANES, LANES)]
    return ranges


def project_kernel(
    bits, rows_ref, other_ref, wq_hbm, first, wk, wv, *refs
):
    count = len(TO_OWNERS)
    keep_ref, send_refs, (wq, rows, out, sems) = refs[0], refs[1 : 1 + count], refs[1 + count :]
    skip = first.shape[0]
    ranges = spread(wq_hbm.shape[0], skip, CHUNK)
    copies = [
        copies_in(wq_hbm, wq, sems.at[i], start, size, start - skip)
        for i, (start, size) in enumerate(ranges)
    ]
    for group in copies:
        for copy in group:
            copy.start()

    slots = rows.shape[0]
    half = slots // 2
    turn = bit_reverse(lax.axis_index("gx"), bits)
    gy = lax.axis_index("gy")
    for ref, side in ((rows_ref, gy), (other_ref, 1 - gy)):
        block = ref[...].astype(jnp.float32)
        for t in range(half):
            slot = bit_reverse(t, bits) ^ turn ^ side
            rows[pl.ds(slot, 1), :] = block[t : t + 1, :]
    wide = rows[...]
    squares = jnp.sum(wide * wide, axis=1, keepdims=True)
    narrow = wide.astype(jnp.bfloat16)

    fresh = [jnp.dot(narrow, w[...], preferred_element_type=jnp.float32) for w in (wk, wv)]
    sums = jnp.dot(narrow[:, :skip], first[...], preferred_element_type=jnp.float32)
    for (start, size), group in zip(ranges, copies):
        for copy in group:
            copy.wait()
        sums = sums + jnp.dot(
            narrow[:, start : start + size],
            wq[start - skip : start - skip + size, :],
            preferred_element_type=jnp.float32,
        )

    total = out.shape[2]
    blocks = []
    for part in (sums, *fresh):
        blocks += [part[:, i : i + LANES] for i in range(0, part.shape[1], LANES)]
    blocks.append(jnp.broadcast_to(squares, (slots, LANES)))
    blocks += [jnp.zeros((slots, LANES), jnp.float32)] * (total - len(blocks))
    flat = out.reshape(slots * total, LANES)
    for i, block in enumerate(blocks):
        flat[pl.ds(i, slots, stride=total), :] = block
    keep_ref[...] = out[0]
    for order, ref in zip(TO_OWNERS, send_refs):
        ref[...] = out[look_up(sent_pieces(order), lax.axis_index("gx"))]


def project(rows, other, w_query, first, key_weight, value_weight, slots):
    bits = slots.bit_length() - 1
    depth, query_width = w_query.shape
    kv_width = key_weight.shape[1]
    used = (query_width + 2 * kv_width) // LANES + 1
    total = -(-used // 8) * 8
    skip = first.shape[0]
    piece = jax.ShapeDtypeStruct((slots // FAN, total, LANES), jnp.float32)
    hbm = pl.BlockSpec(memory_space=pltpu.HBM)
    whole = pl.BlockSpec(memory_space=pltpu.VMEM)
    return pl.pallas_call(
        functools.partial(project_kernel, bits),
        out_shape=(piece,) * (1 + len(TO_OWNERS)),
        in_specs=[whole, whole, hbm, whole, whole, whole],
        out_specs=(whole,) * (1 + len(TO_OWNERS)),
        scratch_shapes=[
            pltpu.VMEM((max(depth - skip, 16), query_width), jnp.bfloat16),
            pltpu.VMEM((slots, depth), jnp.float32),
            pltpu.VMEM((FAN, slots // FAN, total, LANES), jnp.float32),
            pltpu.SemaphoreType.DMA((max(1, len(spread(depth, skip, CHUNK))), PIECES)),
        ],
        compiler_params=pltpu.CompilerParams(vmem_limit_bytes=46 * MIB),
        cost_estimate=pl.CostEstimate(
            flops=2 * slots * depth * (query_width + 2 * kv_width),
            bytes_accessed=2 * depth * (query_width + 2 * kv_width),
            transcendentals=0,
        ),
        name="project",
    )(rows, other, in_hbm(w_query), first, key_weight, value_weight)


def attend_kernel(
    query_heads, kv_heads, pieces, beside_ref, turn_ref, k_ref, v_ref, *refs
):
    heads_ref = refs[pieces]
    total = refs[0][0]
    for ref in refs[1:pieces]:
        total = total + ref[0]
    at = query_heads + 2 * kv_heads
    scale = lax.rsqrt(total[at : at + 1, :] / MODEL_WIDTH + 1e-05)
    turned = total[: query_heads + kv_heads] * scale
    half = HEAD_SIZE // 2
    swapped = jnp.concatenate([turned[:, half:], turned[:, :half]], axis=1)
    turned = (turned * turn_ref[0:1, :] + swapped * turn_ref[1:2, :]).astype(jnp.bfloat16)
    fresh_values = (total[query_heads + kv_heads : at] * scale).astype(jnp.bfloat16)
    group = query_heads // kv_heads
    factor = 1.0 / math.sqrt(HEAD_SIZE)
    length = turn_ref[2:3, 0:1].astype(jnp.int32)
    side = 2 if kv_heads % 2 == 0 else 1
    for first in range(0, kv_heads, side):
        members = range(first, first + side)
        queries = [turned[head * group : (head + 1) * group] for head in members]
        empty = jnp.zeros((group, HEAD_SIZE), jnp.bfloat16)
        spread_out = jnp.concatenate(
            [
                jnp.concatenate([q if i == j else empty for j in range(side)], axis=1)
                for i, q in enumerate(queries)
            ],
            axis=0,
        )
        keys = jnp.concatenate([k_ref[0, head] for head in members], axis=1)
        values = jnp.concatenate([v_ref[0, head] for head in members], axis=1)
        scores = (
            lax.dot_general(
                spread_out, keys, (((1,), (1,)), ((), ())), preferred_element_type=jnp.float32
            )
            * factor
        )
        own = jnp.concatenate(
            [
                jnp.sum(
                    q.astype(jnp.float32)
                    * turned[query_heads + head : query_heads + head + 1].astype(jnp.float32),
                    axis=1,
                    keepdims=True,
                )
                for q, head in zip(queries, members)
            ],
            axis=0,
        ) * factor
        slot = lax.broadcasted_iota(jnp.int32, scores.shape, 1)
        scores = jnp.where(slot < length, scores, -jnp.inf)
        top = jnp.maximum(jnp.max(scores, axis=1, keepdims=True), own)
        exponent = jnp.exp(scores - top)
        own_exp = jnp.exp(own - top)
        share = 1.0 / (jnp.sum(exponent, axis=1, keepdims=True) + own_exp)
        weights = (exponent * share).astype(jnp.bfloat16)
        own_weight = (own_exp * share).astype(jnp.bfloat16).astype(jnp.float32)
        mixed = jnp.dot(weights, values, preferred_element_type=jnp.float32)
        for i, head in enumerate(members):
            block = mixed[i * group : (i + 1) * group, i * HEAD_SIZE : (i + 1) * HEAD_SIZE]
            block = block + own_weight[i * group : (i + 1) * group] * fresh_values[
                head : head + 1
            ].astype(jnp.float32)
            heads_ref[0, pl.ds(head * group, group), :] = block.astype(jnp.bfloat16)


def attend(parts, turn, k_cache, value_cache, query_heads, beside):
    kv_heads, cache_len = k_cache.shape[1:3]
    whole = pl.BlockSpec(memory_space=pltpu.VMEM)
    return pl.pallas_call(
        functools.partial(attend_kernel, query_heads, kv_heads, len(parts)),
        out_shape=jax.ShapeDtypeStruct((1, query_heads, HEAD_SIZE), jnp.bfloat16),
        in_specs=[pl.BlockSpec(memory_space=pltpu.HBM)] + [whole] * (3 + len(parts)),
        out_specs=whole,
        compiler_params=pltpu.CompilerParams(vmem_limit_bytes=12 * MIB),
        cost_estimate=pl.CostEstimate(
            flops=4 * query_heads * cache_len * HEAD_SIZE,
            bytes_accessed=4 * kv_heads * cache_len * HEAD_SIZE,
            transcendentals=query_heads * cache_len,
        ),
        name="attend",
    )(in_hbm(beside), turn, k_cache, value_cache, *parts)


def output_kernel(bits, held_ref, *refs):
    count = len(TO_ALL)
    arrived, (w_ref, mine_ref, theirs_ref, flat, left, sums) = refs[:count], refs[count:]
    slots = left.shape[0]
    size, heads = held_ref.shape[:2]
    rows = size * heads
    flat[:rows, :] = held_ref[...].reshape(rows, HEAD_SIZE).astype(jnp.float32)
    for order, ref in zip(TO_ALL[-LAST:] + TO_ALL[:-LAST], arrived):
        piece = look_up(arriving_pieces(order), lax.axis_index("gx"))
        flat[pl.ds(pl.multiple_of(piece * rows, rows), rows), :] = (
            ref[...].reshape(rows, HEAD_SIZE).astype(jnp.float32)
        )
    for head in range(heads):
        left[:, head * HEAD_SIZE : (head + 1) * HEAD_SIZE] = flat[
            pl.ds(head, slots, stride=heads), :
        ].astype(jnp.bfloat16)
    total = None
    depth = w_ref.shape[0]
    chunk = min(2 * CHUNK, depth)
    for at in range(0, depth, chunk):
        part = slice(at, at + chunk)
        term = jnp.dot(left[:, part], w_ref[part, :], preferred_element_type=jnp.float32)
        total = term if total is None else total + term
    sums[...] = total
    half = slots // 2
    turn = bit_reverse(lax.axis_index("gx"), bits)
    gy = lax.axis_index("gy")
    for ref, side in ((mine_ref, gy), (theirs_ref, 1 - gy)):
        for t in range(half):
            slot = bit_reverse(t, bits) ^ turn ^ side
            ref[t : t + 1, :] = sums[pl.ds(slot, 1), :]


def output(held, arrived, w_out, slots):
    bits = slots.bit_length() - 1
    depth, width = w_out.shape
    heads = depth // HEAD_SIZE
    whole = pl.BlockSpec(memory_space=pltpu.VMEM)
    piece = jax.ShapeDtypeStruct((slots // 2, width), jnp.float32)
    return pl.pallas_call(
        functools.partial(output_kernel, bits),
        out_shape=(piece, piece),
        in_specs=[whole] * (2 + len(arrived)),
        out_specs=(whole, whole),
        scratch_shapes=[
            pltpu.VMEM((slots // FAN * (FAN + 1) * heads, HEAD_SIZE), jnp.float32),
            pltpu.VMEM((slots, depth), jnp.bfloat16),
            pltpu.VMEM((slots, width), jnp.float32),
        ],
        compiler_params=pltpu.CompilerParams(vmem_limit_bytes=12 * MIB),
        cost_estimate=pl.CostEstimate(
            flops=2 * slots * depth * width, bytes_accessed=2 * depth * width, transcendentals=0
        ),
        name="output",
    )(held, *arrived, w_out)


def swap(block, axis, devices, mask):
    return lax.ppermute(block, axis, [(i, i ^ mask) for i in range(devices)])


def body(devices, activations, w_query, key_weight, value_weight, w_out, k_cache, value_cache, lengths):
    slots = devices
    query_heads = w_query.shape[1] // HEAD_SIZE
    other = swap(activations, "gy", 2, 1)
    depth = w_query.shape[0]
    first = stage_rows(w_query, min(FIRST, depth))
    keep, *sends = project(activations, other, w_query, first, key_weight, value_weight, slots)

    arrived = [
        lax.ppermute(send, "gx", pairs_of(order, devices)) for order, send in zip(TO_OWNERS, sends)
    ]
    half = HEAD_SIZE // 2
    frequency = jnp.power(
        jnp.float32(500000.0), -2.0 * jnp.arange(half, dtype=jnp.float32) / HEAD_SIZE
    )
    frequency = jnp.concatenate([frequency, frequency])[None, :]
    turn = turning(lengths, frequency, w_out)
    total = keep + functools.reduce(lambda later, earlier: earlier + later, arrived[::-1])
    mask = FAN
    while total.shape[0] > 2:
        rest = total.shape[0] // 2
        total = total[:rest] + swap(total[rest:], "gx", devices, mask)
        mask *= 2
    total, turn = lax.optimization_barrier((total, turn))
    parts = [total[:1], swap(total[1:], "gx", devices, mask)]
    heads = attend(parts, turn, k_cache, value_cache, query_heads, w_out)

    parts = [heads, swap(heads, "gx", devices, mask)]
    while mask > FAN:
        mask //= 2
        parts.append(swap(jnp.concatenate(parts, axis=0), "gx", devices, mask))
    held = jnp.concatenate(parts, axis=0)
    arrived = [lax.ppermute(held, "gx", pairs_of(order, devices)) for order in TO_ALL]
    arrived = arrived[-LAST:] + arrived[:-LAST]
    mine, theirs = output(held, arrived, w_out, slots)
    return (mine + swap(theirs, "gy", 2, 1)).astype(jnp.bfloat16)


def solution(mesh):
    placed = (
        P(("groups", "gy"), "gx"),
        P("gx", "gy"),
        P("gx", "gy"),
        P("gx", "gy"),
        P("gy", "gx"),
        P(("groups", "gx"), "gy", None, None),
        P(("groups", "gx"), "gy", None, None),
        P(("groups", "gx")),
    )
    return jax.shard_map(
        functools.partial(body, mesh.shape["gx"]),
        mesh=mesh,
        in_specs=placed,
        out_specs=P(("groups", "gy"), "gx"),
        check_vma=False,
    )
```

```python
import functools
import math

import jax
import jax.numpy as jnp
from jax import lax
from jax.experimental import pallas as pl
from jax.experimental.pallas import tpu as pltpu
from jax.sharding import PartitionSpec as P

MODEL_WIDTH = 16384
LANES = 128
HEAD_SIZE = 128
CHUNK = 256
FIRST = 256
PIECES = 4
FAN = 4
MIB = 2**20

BLOCK = 8
TO_OWNERS = (
    "32014756",
    "01325674",
    "13207465",
    "20136547",
)
TO_ALL = (
    "31206754",
    "20135467",
    "13027645",
    "02314576",
)
LAST = 3


def pairs_of(order, devices):
    return [
        (block + g, block + int(to))
        for block in range(0, devices, BLOCK)
        for g, to in enumerate(order)
    ]


def sent_pieces(order):
    return [bit_reverse(g ^ int(to), 2) or FAN for g, to in enumerate(order)]


def arriving_pieces(order):
    pieces = [FAN] * BLOCK
    for g, to in enumerate(order):
        pieces[int(to)] = bit_reverse(g ^ int(to), 2) or FAN
    return pieces


def look_up(table, device):
    packed = sum(entry << (4 * g) for g, entry in enumerate(table))
    return (jnp.int32(packed) >> (4 * (device % BLOCK))) & 7


def bit_reverse(value, bits):
    turned = 0
    for bit in range(bits):
        turned = turned | (((value >> bit) & 1) << (bits - 1 - bit))
    return turned


def in_hbm(array):
    return pltpu.with_memory_space_constraint(array, pltpu.HBM)


def cut(start, size):
    if size % (16 * PIECES):
        return [(start, size)]
    return [(start + i * (size // PIECES), size // PIECES) for i in range(PIECES)]


def copies_in(src, dst, sems, start, size, offset):
    return [
        pltpu.make_async_copy(
            src.at[pl.ds(at, rows)], dst.at[pl.ds(at - start + offset, rows)], sems.at[i]
        )
        for i, (at, rows) in enumerate(cut(start, size))
    ]


def stage_kernel(rows, src, dst, sems):
    copies = copies_in(src, dst, sems, 0, rows, 0)
    for copy in copies:
        copy.start()
    for copy in copies:
        copy.wait()


def stage_rows(array, rows):
    vmem = pl.BlockSpec(memory_space=pltpu.VMEM)
    return pl.pallas_call(
        functools.partial(stage_kernel, rows),
        out_shape=jax.ShapeDtypeStruct((rows, array.shape[1]), array.dtype),
        in_specs=[pl.BlockSpec(memory_space=pltpu.HBM)],
        out_specs=vmem,
        scratch_shapes=[pltpu.SemaphoreType.DMA((PIECES,))],
        compiler_params=pltpu.CompilerParams(vmem_limit_bytes=16 * MIB),
        cost_estimate=pl.CostEstimate(
            flops=0, bytes_accessed=2 * rows * array.shape[1], transcendentals=0
        ),
        name="stage",
    )(in_hbm(array))


def turning_kernel(length_ref, frequency_ref, beside_ref, turn_ref):
    position = length_ref[0].astype(jnp.float32)
    angle = position * frequency_ref[...]
    lane = lax.broadcasted_iota(jnp.int32, angle.shape, 1)
    sine = jnp.sin(angle)
    turn_ref[0:1, :] = jnp.cos(angle)
    turn_ref[1:2, :] = jnp.where(lane < HEAD_SIZE // 2, -sine, sine)
    turn_ref[2:3, :] = jnp.full(angle.shape, position)


def turning(lengths, frequency, beside):
    vmem = pl.BlockSpec(memory_space=pltpu.VMEM)
    return pl.pallas_call(
        turning_kernel,
        out_shape=jax.ShapeDtypeStruct((8, HEAD_SIZE), jnp.float32),
        in_specs=[
            pl.BlockSpec(memory_space=pltpu.SMEM),
            vmem,
            pl.BlockSpec(memory_space=pltpu.HBM),
        ],
        out_specs=vmem,
        compiler_params=pltpu.CompilerParams(vmem_limit_bytes=2 * MIB),
        cost_estimate=pl.CostEstimate(flops=0, bytes_accessed=2 * beside.size, transcendentals=256),
        name="turning",
    )(lengths, frequency, in_hbm(beside))


def spread(depth, skip, chunk):
    ranges = [(at, min(chunk, depth - at)) for at in range(skip, depth, chunk)]
    if ranges and ranges[-1][1] >= 2 * LANES:
        start, size = ranges.pop()
        ranges += [(start, size - LANES), (start + size - LANES, LANES)]
    return ranges


def project_kernel(
    bits, rows_ref, other_ref, wq_hbm, first, wk, wv, *refs
):
    count = len(TO_OWNERS)
    keep_ref, send_refs, (wq, rows, out, sems) = refs[0], refs[1 : 1 + count], refs[1 + count :]
    skip = first.shape[0]
    ranges = spread(wq_hbm.shape[0], skip, CHUNK)
    copies = [
        copies_in(wq_hbm, wq, sems.at[i], start, size, start - skip)
        for i, (start, size) in enumerate(ranges)
    ]
    for group in copies:
        for copy in group:
            copy.start()

    slots = rows.shape[0]
    half = slots // 2
    turn = bit_reverse(lax.axis_index("gx"), bits)
    gy = lax.axis_index("gy")
    for ref, side in ((rows_ref, gy), (other_ref, 1 - gy)):
        block = ref[...].astype(jnp.float32)
        for t in range(half):
            slot = bit_reverse(t, bits) ^ turn ^ side
            rows[pl.ds(slot, 1), :] = block[t : t + 1, :]
    wide = rows[...]
    squares = jnp.sum(wide * wide, axis=1, keepdims=True)
    narrow = wide.astype(jnp.bfloat16)

    fresh = [jnp.dot(narrow, w[...], preferred_element_type=jnp.float32) for w in (wk, wv)]
    sums = jnp.dot(narrow[:, :skip], first[...], preferred_element_type=jnp.float32)
    for (start, size), group in zip(ranges, copies):
        for copy in group:
            copy.wait()
        sums = sums + jnp.dot(
            narrow[:, start : start + size],
            wq[start - skip : start - skip + size, :],
            preferred_element_type=jnp.float32,
        )

    total = out.shape[2]
    blocks = []
    for part in (sums, *fresh):
        blocks += [part[:, i : i + LANES] for i in range(0, part.shape[1], LANES)]
    blocks.append(jnp.broadcast_to(squares, (slots, LANES)))
    blocks += [jnp.zeros((slots, LANES), jnp.float32)] * (total - len(blocks))
    out[FAN] = jnp.zeros(out.shape[1:], jnp.float32)
    flat = out.reshape((FAN + 1) * slots // FAN * total, LANES)
    for i, block in enumerate(blocks):
        flat[pl.ds(i, slots, stride=total), :] = block
    keep_ref[...] = out[0]
    for order, ref in zip(TO_OWNERS, send_refs):
        ref[...] = out[look_up(sent_pieces(order), lax.axis_index("gx"))]


def project(rows, other, w_query, first, key_weight, value_weight, slots):
    bits = slots.bit_length() - 1
    depth, query_width = w_query.shape
    kv_width = key_weight.shape[1]
    used = (query_width + 2 * kv_width) // LANES + 1
    total = -(-used // 8) * 8
    skip = first.shape[0]
    piece = jax.ShapeDtypeStruct((slots // FAN, total, LANES), jnp.float32)
    hbm = pl.BlockSpec(memory_space=pltpu.HBM)
    whole = pl.BlockSpec(memory_space=pltpu.VMEM)
    return pl.pallas_call(
        functools.partial(project_kernel, bits),
        out_shape=(piece,) * (1 + len(TO_OWNERS)),
        in_specs=[whole, whole, hbm, whole, whole, whole],
        out_specs=(whole,) * (1 + len(TO_OWNERS)),
        scratch_shapes=[
            pltpu.VMEM((max(depth - skip, 16), query_width), jnp.bfloat16),
            pltpu.VMEM((slots, depth), jnp.float32),
            pltpu.VMEM((FAN + 1, slots // FAN, total, LANES), jnp.float32),
            pltpu.SemaphoreType.DMA((max(1, len(spread(depth, skip, CHUNK))), PIECES)),
        ],
        compiler_params=pltpu.CompilerParams(vmem_limit_bytes=46 * MIB),
        cost_estimate=pl.CostEstimate(
            flops=2 * slots * depth * (query_width + 2 * kv_width),
            bytes_accessed=2 * depth * (query_width + 2 * kv_width),
            transcendentals=0,
        ),
        name="project",
    )(rows, other, in_hbm(w_query), first, key_weight, value_weight)


def attend_kernel(
    query_heads, kv_heads, pieces, beside_ref, turn_ref, k_ref, v_ref, *refs
):
    heads_ref = refs[pieces]
    total = refs[0][0]
    for ref in refs[1:pieces]:
        total = total + ref[0]
    at = query_heads + 2 * kv_heads
    scale = lax.rsqrt(total[at : at + 1, :] / MODEL_WIDTH + 1e-05)
    turned = total[: query_heads + kv_heads] * scale
    half = HEAD_SIZE // 2
    swapped = jnp.concatenate([turned[:, half:], turned[:, :half]], axis=1)
    turned = (turned * turn_ref[0:1, :] + swapped * turn_ref[1:2, :]).astype(jnp.bfloat16)
    fresh_values = (total[query_heads + kv_heads : at] * scale).astype(jnp.bfloat16)
    group = query_heads // kv_heads
    factor = 1.0 / math.sqrt(HEAD_SIZE)
    length = turn_ref[2:3, 0:1].astype(jnp.int32)
    side = 2 if kv_heads % 2 == 0 else 1
    for first in range(0, kv_heads, side):
        members = range(first, first + side)
        queries = [turned[head * group : (head + 1) * group] for head in members]
        empty = jnp.zeros((group, HEAD_SIZE), jnp.bfloat16)
        spread_out = jnp.concatenate(
            [
                jnp.concatenate([q if i == j else empty for j in range(side)], axis=1)
                for i, q in enumerate(queries)
            ],
            axis=0,
        )
        keys = jnp.concatenate([k_ref[0, head] for head in members], axis=1)
        values = jnp.concatenate([v_ref[0, head] for head in members], axis=1)
        scores = (
            lax.dot_general(
                spread_out, keys, (((1,), (1,)), ((), ())), preferred_element_type=jnp.float32
            )
            * factor
        )
        own = jnp.concatenate(
            [
                jnp.sum(
                    q.astype(jnp.float32)
                    * turned[query_heads + head : query_heads + head + 1].astype(jnp.float32),
                    axis=1,
                    keepdims=True,
                )
                for q, head in zip(queries, members)
            ],
            axis=0,
        ) * factor
        slot = lax.broadcasted_iota(jnp.int32, scores.shape, 1)
        scores = jnp.where(slot < length, scores, -jnp.inf)
        top = jnp.maximum(jnp.max(scores, axis=1, keepdims=True), own)
        exponent = jnp.exp(scores - top)
        own_exp = jnp.exp(own - top)
        share = 1.0 / (jnp.sum(exponent, axis=1, keepdims=True) + own_exp)
        weights = (exponent * share).astype(jnp.bfloat16)
        own_weight = (own_exp * share).astype(jnp.bfloat16).astype(jnp.float32)
        mixed = jnp.dot(weights, values, preferred_element_type=jnp.float32)
        for i, head in enumerate(members):
            block = mixed[i * group : (i + 1) * group, i * HEAD_SIZE : (i + 1) * HEAD_SIZE]
            block = block + own_weight[i * group : (i + 1) * group] * fresh_values[
                head : head + 1
            ].astype(jnp.float32)
            heads_ref[0, pl.ds(head * group, group), :] = block.astype(jnp.bfloat16)


def attend(parts, turn, k_cache, value_cache, query_heads, beside):
    kv_heads, cache_len = k_cache.shape[1:3]
    whole = pl.BlockSpec(memory_space=pltpu.VMEM)
    return pl.pallas_call(
        functools.partial(attend_kernel, query_heads, kv_heads, len(parts)),
        out_shape=jax.ShapeDtypeStruct((1, query_heads, HEAD_SIZE), jnp.bfloat16),
        in_specs=[pl.BlockSpec(memory_space=pltpu.HBM)] + [whole] * (3 + len(parts)),
        out_specs=whole,
        compiler_params=pltpu.CompilerParams(vmem_limit_bytes=12 * MIB),
        cost_estimate=pl.CostEstimate(
            flops=4 * query_heads * cache_len * HEAD_SIZE,
            bytes_accessed=4 * kv_heads * cache_len * HEAD_SIZE,
            transcendentals=query_heads * cache_len,
        ),
        name="attend",
    )(in_hbm(beside), turn, k_cache, value_cache, *parts)


def output_kernel(bits, held_ref, *refs):
    count = len(TO_ALL)
    arrived, (w_ref, mine_ref, theirs_ref, flat, left, sums) = refs[:count], refs[count:]
    slots = left.shape[0]
    size, heads = held_ref.shape[:2]
    rows = size * heads
    flat[:rows, :] = held_ref[...].reshape(rows, HEAD_SIZE).astype(jnp.float32)
    for order, ref in zip(TO_ALL[-LAST:] + TO_ALL[:-LAST], arrived):
        piece = look_up(arriving_pieces(order), lax.axis_index("gx"))
        flat[pl.ds(pl.multiple_of(piece * rows, rows), rows), :] = (
            ref[...].reshape(rows, HEAD_SIZE).astype(jnp.float32)
        )
    for head in range(heads):
        left[:, head * HEAD_SIZE : (head + 1) * HEAD_SIZE] = flat[
            pl.ds(head, slots, stride=heads), :
        ].astype(jnp.bfloat16)
    total = None
    depth = w_ref.shape[0]
    chunk = min(2 * CHUNK, depth)
    for at in range(0, depth, chunk):
        part = slice(at, at + chunk)
        term = jnp.dot(left[:, part], w_ref[part, :], preferred_element_type=jnp.float32)
        total = term if total is None else total + term
    sums[...] = total
    half = slots // 2
    turn = bit_reverse(lax.axis_index("gx"), bits)
    gy = lax.axis_index("gy")
    for ref, side in ((mine_ref, gy), (theirs_ref, 1 - gy)):
        for t in range(half):
            slot = bit_reverse(t, bits) ^ turn ^ side
            ref[t : t + 1, :] = sums[pl.ds(slot, 1), :]


def output(held, arrived, w_out, slots):
    bits = slots.bit_length() - 1
    depth, width = w_out.shape
    heads = depth // HEAD_SIZE
    whole = pl.BlockSpec(memory_space=pltpu.VMEM)
    piece = jax.ShapeDtypeStruct((slots // 2, width), jnp.float32)
    return pl.pallas_call(
        functools.partial(output_kernel, bits),
        out_shape=(piece, piece),
        in_specs=[whole] * (2 + len(arrived)),
        out_specs=(whole, whole),
        scratch_shapes=[
            pltpu.VMEM((slots // FAN * (FAN + 1) * heads, HEAD_SIZE), jnp.float32),
            pltpu.VMEM((slots, depth), jnp.bfloat16),
            pltpu.VMEM((slots, width), jnp.float32),
        ],
        compiler_params=pltpu.CompilerParams(vmem_limit_bytes=12 * MIB),
        cost_estimate=pl.CostEstimate(
            flops=2 * slots * depth * width, bytes_accessed=2 * depth * width, transcendentals=0
        ),
        name="output",
    )(held, *arrived, w_out)


def swap(block, axis, devices, mask):
    return lax.ppermute(block, axis, [(i, i ^ mask) for i in range(devices)])


def body(devices, activations, w_query, key_weight, value_weight, w_out, k_cache, value_cache, lengths):
    slots = devices
    query_heads = w_query.shape[1] // HEAD_SIZE
    other = swap(activations, "gy", 2, 1)
    depth = w_query.shape[0]
    first = stage_rows(w_query, min(FIRST, depth))
    keep, *sends = project(activations, other, w_query, first, key_weight, value_weight, slots)

    arrived = [
        lax.ppermute(send, "gx", pairs_of(order, devices)) for order, send in zip(TO_OWNERS, sends)
    ]
    half = HEAD_SIZE // 2
    frequency = jnp.power(
        jnp.float32(500000.0), -2.0 * jnp.arange(half, dtype=jnp.float32) / HEAD_SIZE
    )
    frequency = jnp.concatenate([frequency, frequency])[None, :]
    turn = turning(lengths, frequency, w_out)
    total = keep + functools.reduce(lambda later, earlier: earlier + later, arrived[::-1])
    mask = FAN
    while total.shape[0] > 2:
        rest = total.shape[0] // 2
        total = total[:rest] + swap(total[rest:], "gx", devices, mask)
        mask *= 2
    total, turn = lax.optimization_barrier((total, turn))
    parts = [total[:1], swap(total[1:], "gx", devices, mask)]
    heads = attend(parts, turn, k_cache, value_cache, query_heads, w_out)

    parts = [heads, swap(heads, "gx", devices, mask)]
    while mask > FAN:
        mask //= 2
        parts.append(swap(jnp.concatenate(parts, axis=0), "gx", devices, mask))
    held = jnp.concatenate(parts, axis=0)
    arrived = [lax.ppermute(held, "gx", pairs_of(order, devices)) for order in TO_ALL]
    arrived = arrived[-LAST:] + arrived[:-LAST]
    mine, theirs = output(held, arrived, w_out, slots)
    return (mine + swap(theirs, "gy", 2, 1)).astype(jnp.bfloat16)


def solution(mesh):
    placed = (
        P(("groups", "gy"), "gx"),
        P("gx", "gy"),
        P("gx", "gy"),
        P("gx", "gy"),
        P("gy", "gx"),
        P(("groups", "gx"), "gy", None, None),
        P(("groups", "gx"), "gy", None, None),
        P(("groups", "gx")),
    )
    return jax.shard_map(
        functools.partial(body, mesh.shape["gx"]),
        mesh=mesh,
        in_specs=placed,
        out_specs=P(("groups", "gy"), "gx"),
        check_vma=False,
    )
```

```python
import functools
import math

import jax
import jax.numpy as jnp
from jax import lax
from jax.experimental import pallas as pl
from jax.experimental.pallas import tpu as pltpu
from jax.sharding import PartitionSpec as P

MODEL_WIDTH = 16384
LANES = 128
HEAD_SIZE = 128
CHUNK = 256
FIRST = 256
PIECES = 4
FAN = 4
MIB = 2**20


def bit_reverse(value, bits):
    turned = 0
    for bit in range(bits):
        turned = turned | (((value >> bit) & 1) << (bits - 1 - bit))
    return turned


def in_hbm(array):
    return pltpu.with_memory_space_constraint(array, pltpu.HBM)


def cut(start, size):
    if size % (16 * PIECES):
        return [(start, size)]
    return [(start + i * (size // PIECES), size // PIECES) for i in range(PIECES)]


def copies_in(src, dst, sems, start, size, offset):
    return [
        pltpu.make_async_copy(
            src.at[pl.ds(at, rows)], dst.at[pl.ds(at - start + offset, rows)], sems.at[i]
        )
        for i, (at, rows) in enumerate(cut(start, size))
    ]


def stage_kernel(rows, src, dst, sems):
    copies = copies_in(src, dst, sems, 0, rows, 0)
    for copy in copies:
        copy.start()
    for copy in copies:
        copy.wait()


def stage_rows(array, rows):
    vmem = pl.BlockSpec(memory_space=pltpu.VMEM)
    return pl.pallas_call(
        functools.partial(stage_kernel, rows),
        out_shape=jax.ShapeDtypeStruct((rows, array.shape[1]), array.dtype),
        in_specs=[pl.BlockSpec(memory_space=pltpu.HBM)],
        out_specs=vmem,
        scratch_shapes=[pltpu.SemaphoreType.DMA((PIECES,))],
        compiler_params=pltpu.CompilerParams(vmem_limit_bytes=16 * MIB),
        cost_estimate=pl.CostEstimate(
            flops=0, bytes_accessed=2 * rows * array.shape[1], transcendentals=0
        ),
        name="stage",
    )(in_hbm(array))


def turning_kernel(length_ref, frequency_ref, beside_ref, after_ref, turn_ref):
    position = length_ref[0].astype(jnp.float32)
    angle = position * frequency_ref[...]
    lane = lax.broadcasted_iota(jnp.int32, angle.shape, 1)
    sine = jnp.sin(angle)
    turn_ref[0:1, :] = jnp.cos(angle)
    turn_ref[1:2, :] = jnp.where(lane < HEAD_SIZE // 2, -sine, sine)
    turn_ref[2:3, :] = jnp.full(angle.shape, position)


def turning(lengths, frequency, beside, after):
    vmem = pl.BlockSpec(memory_space=pltpu.VMEM)
    return pl.pallas_call(
        turning_kernel,
        out_shape=jax.ShapeDtypeStruct((8, HEAD_SIZE), jnp.float32),
        in_specs=[
            pl.BlockSpec(memory_space=pltpu.SMEM),
            vmem,
            pl.BlockSpec(memory_space=pltpu.HBM),
            vmem,
        ],
        out_specs=vmem,
        compiler_params=pltpu.CompilerParams(vmem_limit_bytes=2 * MIB),
        cost_estimate=pl.CostEstimate(flops=0, bytes_accessed=2 * beside.size, transcendentals=256),
        name="turning",
    )(lengths, frequency, in_hbm(beside), after)


def spread(depth, skip, chunk):
    ranges = [(at, min(chunk, depth - at)) for at in range(skip, depth, chunk)]
    if ranges and ranges[-1][1] >= 2 * LANES:
        start, size = ranges.pop()
        ranges += [(start, size - LANES), (start + size - LANES, LANES)]
    return ranges


def project_kernel(
    bits, rows_ref, other_ref, wq_hbm, first, wk, wv, *refs
):
    pieces, (wq, rows, sems) = refs[:FAN], refs[FAN:]
    skip = first.shape[0]
    ranges = spread(wq_hbm.shape[0], skip, CHUNK)
    copies = [
        copies_in(wq_hbm, wq, sems.at[i], start, size, start - skip)
        for i, (start, size) in enumerate(ranges)
    ]
    for group in copies:
        for copy in group:
            copy.start()

    slots = rows.shape[0]
    half = slots // 2
    turn = bit_reverse(lax.axis_index("gx"), bits)
    gy = lax.axis_index("gy")
    for ref, side in ((rows_ref, gy), (other_ref, 1 - gy)):
        block = ref[...].astype(jnp.float32)
        for t in range(half):
            slot = bit_reverse(t, bits) ^ turn ^ side
            rows[pl.ds(slot, 1), :] = block[t : t + 1, :]
    wide = rows[...]
    squares = jnp.sum(wide * wide, axis=1, keepdims=True)
    narrow = wide.astype(jnp.bfloat16)

    fresh = [jnp.dot(narrow, w[...], preferred_element_type=jnp.float32) for w in (wk, wv)]
    sums = jnp.dot(narrow[:, :skip], first[...], preferred_element_type=jnp.float32)
    for (start, size), group in zip(ranges, copies):
        for copy in group:
            copy.wait()
        sums = sums + jnp.dot(
            narrow[:, start : start + size],
            wq[start - skip : start - skip + size, :],
            preferred_element_type=jnp.float32,
        )

    total = pieces[0].shape[1]
    blocks = []
    for part in (sums, *fresh):
        blocks += [part[:, i : i + LANES] for i in range(0, part.shape[1], LANES)]
    blocks.append(jnp.broadcast_to(squares, (slots, LANES)))
    blocks += [jnp.zeros((slots, LANES), jnp.float32)] * (total - len(blocks))
    size = slots // FAN
    for at, ref in enumerate(pieces):
        flat = ref.reshape(size * total, LANES)
        for i, block in enumerate(blocks):
            flat[pl.ds(i, size, stride=total), :] = block[at * size : (at + 1) * size]


def project(rows, other, w_query, first, key_weight, value_weight, slots):
    bits = slots.bit_length() - 1
    depth, query_width = w_query.shape
    kv_width = key_weight.shape[1]
    used = (query_width + 2 * kv_width) // LANES + 1
    total = -(-used // 8) * 8
    skip = first.shape[0]
    piece = jax.ShapeDtypeStruct((slots // FAN, total, LANES), jnp.float32)
    hbm = pl.BlockSpec(memory_space=pltpu.HBM)
    whole = pl.BlockSpec(memory_space=pltpu.VMEM)
    return pl.pallas_call(
        functools.partial(project_kernel, bits),
        out_shape=(piece,) * FAN,
        in_specs=[whole, whole, hbm, whole, whole, whole],
        out_specs=(whole,) * FAN,
        scratch_shapes=[
            pltpu.VMEM((max(depth - skip, 16), query_width), jnp.bfloat16),
            pltpu.VMEM((slots, depth), jnp.float32),
            pltpu.SemaphoreType.DMA((max(1, len(spread(depth, skip, CHUNK))), PIECES)),
        ],
        compiler_params=pltpu.CompilerParams(vmem_limit_bytes=46 * MIB),
        cost_estimate=pl.CostEstimate(
            flops=2 * slots * depth * (query_width + 2 * kv_width),
            bytes_accessed=2 * depth * (query_width + 2 * kv_width),
            transcendentals=0,
        ),
        name="project",
    )(rows, other, in_hbm(w_query), first, key_weight, value_weight)


def attend_kernel(
    query_heads, kv_heads, pieces, beside_ref, turn_ref, k_ref, v_ref, *refs
):
    heads_ref = refs[pieces]
    total = refs[0][0]
    for ref in refs[1:pieces]:
        total = total + ref[0]
    at = query_heads + 2 * kv_heads
    scale = lax.rsqrt(total[at : at + 1, :] / MODEL_WIDTH + 1e-05)
    turned = total[: query_heads + kv_heads] * scale
    half = HEAD_SIZE // 2
    swapped = jnp.concatenate([turned[:, half:], turned[:, :half]], axis=1)
    turned = (turned * turn_ref[0:1, :] + swapped * turn_ref[1:2, :]).astype(jnp.bfloat16)
    fresh_values = (total[query_heads + kv_heads : at] * scale).astype(jnp.bfloat16)
    group = query_heads // kv_heads
    factor = 1.0 / math.sqrt(HEAD_SIZE)
    length = turn_ref[2:3, 0:1].astype(jnp.int32)
    side = 2 if kv_heads % 2 == 0 else 1
    for first in range(0, kv_heads, side):
        members = range(first, first + side)
        queries = [turned[head * group : (head + 1) * group] for head in members]
        empty = jnp.zeros((group, HEAD_SIZE), jnp.bfloat16)
        spread_out = jnp.concatenate(
            [
                jnp.concatenate([q if i == j else empty for j in range(side)], axis=1)
                for i, q in enumerate(queries)
            ],
            axis=0,
        )
        keys = jnp.concatenate([k_ref[0, head] for head in members], axis=1)
        values = jnp.concatenate([v_ref[0, head] for head in members], axis=1)
        scores = (
            lax.dot_general(
                spread_out, keys, (((1,), (1,)), ((), ())), preferred_element_type=jnp.float32
            )
            * factor
        )
        own = jnp.concatenate(
            [
                jnp.sum(
                    q.astype(jnp.float32)
                    * turned[query_heads + head : query_heads + head + 1].astype(jnp.float32),
                    axis=1,
                    keepdims=True,
                )
                for q, head in zip(queries, members)
            ],
            axis=0,
        ) * factor
        slot = lax.broadcasted_iota(jnp.int32, scores.shape, 1)
        scores = jnp.where(slot < length, scores, -jnp.inf)
        top = jnp.maximum(jnp.max(scores, axis=1, keepdims=True), own)
        exponent = jnp.exp(scores - top)
        own_exp = jnp.exp(own - top)
        share = 1.0 / (jnp.sum(exponent, axis=1, keepdims=True) + own_exp)
        weights = (exponent * share).astype(jnp.bfloat16)
        own_weight = (own_exp * share).astype(jnp.bfloat16).astype(jnp.float32)
        mixed = jnp.dot(weights, values, preferred_element_type=jnp.float32)
        for i, head in enumerate(members):
            block = mixed[i * group : (i + 1) * group, i * HEAD_SIZE : (i + 1) * HEAD_SIZE]
            block = block + own_weight[i * group : (i + 1) * group] * fresh_values[
                head : head + 1
            ].astype(jnp.float32)
            heads_ref[0, pl.ds(head * group, group), :] = block.astype(jnp.bfloat16)


def attend(parts, turn, k_cache, value_cache, query_heads, beside):
    kv_heads, cache_len = k_cache.shape[1:3]
    whole = pl.BlockSpec(memory_space=pltpu.VMEM)
    return pl.pallas_call(
        functools.partial(attend_kernel, query_heads, kv_heads, len(parts)),
        out_shape=jax.ShapeDtypeStruct((1, query_heads, HEAD_SIZE), jnp.bfloat16),
        in_specs=[pl.BlockSpec(memory_space=pltpu.HBM)] + [whole] * (3 + len(parts)),
        out_specs=whole,
        compiler_params=pltpu.CompilerParams(vmem_limit_bytes=12 * MIB),
        cost_estimate=pl.CostEstimate(
            flops=4 * query_heads * cache_len * HEAD_SIZE,
            bytes_accessed=4 * kv_heads * cache_len * HEAD_SIZE,
            transcendentals=query_heads * cache_len,
        ),
        name="attend",
    )(in_hbm(beside), turn, k_cache, value_cache, *parts)


def output_kernel(bits, places, turned, *refs):
    pieces = len(places)
    parts = refs[:pieces]
    w_ref, mine_ref, theirs_ref, flat, left, sums = refs[pieces:]
    slots = left.shape[0]
    heads = flat.shape[0] // slots
    for slot, ref in zip(places, parts):
        for i, row in enumerate(range(ref.shape[0])[::turned]):
            at = (slot + i) * heads
            flat[at : at + heads, :] = ref[row].astype(jnp.float32)
    for head in range(heads):
        left[:, head * HEAD_SIZE : (head + 1) * HEAD_SIZE] = flat[
            pl.ds(head, slots, stride=heads), :
        ].astype(jnp.bfloat16)
    total = None
    depth = w_ref.shape[0]
    chunk = min(2 * CHUNK, depth)
    for at in range(0, depth, chunk):
        part = slice(at, at + chunk)
        term = jnp.dot(left[:, part], w_ref[part, :], preferred_element_type=jnp.float32)
        total = term if total is None else total + term
    sums[...] = total
    half = slots // 2
    turn = bit_reverse(lax.axis_index("gx"), bits)
    gy = lax.axis_index("gy")
    for ref, side in ((mine_ref, gy), (theirs_ref, 1 - gy)):
        for t in range(half):
            slot = bit_reverse(t, bits) ^ turn ^ side
            ref[t : t + 1, :] = sums[pl.ds(slot, 1), :]


def output(parts, order, w_out, slots, turned=1):
    bits = slots.bit_length() - 1
    depth, width = w_out.shape
    heads = depth // HEAD_SIZE
    starts = [sum(x.shape[0] for x in parts[:i]) for i in range(len(parts))]
    places = tuple(starts[i] for i in order)
    parts = [parts[i] for i in order]
    whole = pl.BlockSpec(memory_space=pltpu.VMEM)
    piece = jax.ShapeDtypeStruct((slots // 2, width), jnp.float32)
    return pl.pallas_call(
        functools.partial(output_kernel, bits, places, turned),
        out_shape=(piece, piece),
        in_specs=[whole] * (len(parts) + 1),
        out_specs=(whole, whole),
        scratch_shapes=[
            pltpu.VMEM((slots * heads, HEAD_SIZE), jnp.float32),
            pltpu.VMEM((slots, depth), jnp.bfloat16),
            pltpu.VMEM((slots, width), jnp.float32),
        ],
        compiler_params=pltpu.CompilerParams(vmem_limit_bytes=12 * MIB),
        cost_estimate=pl.CostEstimate(
            flops=2 * slots * depth * width, bytes_accessed=2 * depth * width, transcendentals=0
        ),
        name="output",
    )(*parts, w_out)


def swap(block, axis, devices, mask):
    return lax.ppermute(block, axis, [(i, i ^ mask) for i in range(devices)])


def cross(block, devices, mask):
    pairs = [(i, i ^ (2 * mask + 1)) for i in range(2 * devices)]
    return lax.ppermute(block, ("gx", "gy"), pairs)


def fan(pieces, trade):
    masks = [bit_reverse(q, 2) for q in range(FAN)]
    arrived = [None] * FAN
    for q in sorted(range(1, FAN), key=lambda q: (masks[q] + 1) % FAN):
        arrived[q] = trade(pieces[q], masks[q])
    return arrived[1:]


def body(devices, activations, w_query, key_weight, value_weight, w_out, k_cache, value_cache, lengths):
    slots = devices
    query_heads = w_query.shape[1] // HEAD_SIZE
    other = swap(activations, "gy", 2, 1)
    depth = w_query.shape[0]
    first = stage_rows(w_query, min(FIRST, depth))
    pieces = project(activations, other, w_query, first, key_weight, value_weight, slots)
    half = HEAD_SIZE // 2
    frequency = jnp.power(
        jnp.float32(500000.0), -2.0 * jnp.arange(half, dtype=jnp.float32) / HEAD_SIZE
    )
    frequency = jnp.concatenate([frequency, frequency])[None, :]

    if devices == 2 * FAN:
        far = FAN
        arrived = fan(pieces, lambda block, mask: cross(block, devices, mask))
        early = swap(pieces[0][1:], "gx", devices, far)
        turn = turning(lengths, frequency, w_out, pieces[0])
        total = arrived[2] + (arrived[1] + arrived[0])
        total, turn = lax.optimization_barrier((total, turn))
        crossed = cross(total[1:], devices, far)
        beside = swap(total[:1], "gy", 2, 1)
        parts = [pieces[0][:1], early, crossed, beside]
        heads = attend(parts, turn, k_cache, value_cache, query_heads, w_out)
        crossed = cross(heads, devices, far)
        beside = swap(heads, "gy", 2, 1)
        held = jnp.concatenate([crossed, beside], axis=0)
        arrived = fan([held] * FAN, lambda block, mask: cross(block, devices, mask))
        parts = [heads, swap(crossed, "gy", 2, 1)] + arrived
        order, turned = (2, 4, 3, 1, 0), -1
    else:
        arrived = fan(pieces, lambda block, mask: swap(block, "gx", devices, mask))
        turn = turning(lengths, frequency, w_out, pieces[0])
        total = pieces[0] + (arrived[2] + (arrived[1] + arrived[0]))
        mask = FAN
        while total.shape[0] > 2:
            rest = total.shape[0] // 2
            total = total[:rest] + swap(total[rest:], "gx", devices, mask)
            mask *= 2
        parts = [total[:1], swap(total[1:], "gx", devices, mask)]
        heads = attend(parts, turn, k_cache, value_cache, query_heads, w_out)

        parts = [heads, swap(heads, "gx", devices, mask)]
        while mask > FAN:
            mask //= 2
            parts.append(swap(jnp.concatenate(parts, axis=0), "gx", devices, mask))
        held = jnp.concatenate(parts, axis=0)
        parts += fan([held] * FAN, lambda block, mask: swap(block, "gx", devices, mask))
        order, turned = range(len(parts))[::-1], 1
    mine, theirs = output(parts, order, w_out, slots, turned)
    return (mine + swap(theirs, "gy", 2, 1)).astype(jnp.bfloat16)


def solution(mesh):
    placed = (
        P(("groups", "gy"), "gx"),
        P("gx", "gy"),
        P("gx", "gy"),
        P("gx", "gy"),
        P("gy", "gx"),
        P(("groups", "gx"), "gy", None, None),
        P(("groups", "gx"), "gy", None, None),
        P(("groups", "gx")),
    )
    return jax.shard_map(
        functools.partial(body, mesh.shape["gx"]),
        mesh=mesh,
        in_specs=placed,
        out_specs=P(("groups", "gy"), "gx"),
        check_vma=False,
    )
```

```python
import functools
import math

import jax
import jax.numpy as jnp
from jax import lax
from jax.experimental import pallas as pl
from jax.experimental.pallas import tpu as pltpu
from jax.sharding import PartitionSpec as P

MODEL_WIDTH = 16384
LANES = 128
HEAD_SIZE = 128
CHUNK = 256
FIRST = 256
PIECES = 4
FAN = 4
MIB = 2**20


def bit_reverse(value, bits):
    turned = 0
    for bit in range(bits):
        turned = turned | (((value >> bit) & 1) << (bits - 1 - bit))
    return turned


def in_hbm(array):
    return pltpu.with_memory_space_constraint(array, pltpu.HBM)


def cut(start, size):
    if size % (16 * PIECES):
        return [(start, size)]
    return [(start + i * (size // PIECES), size // PIECES) for i in range(PIECES)]


def copies_in(src, dst, sems, start, size, offset):
    return [
        pltpu.make_async_copy(
            src.at[pl.ds(at, rows)], dst.at[pl.ds(at - start + offset, rows)], sems.at[i]
        )
        for i, (at, rows) in enumerate(cut(start, size))
    ]


def stage_kernel(rows, src, dst, sems):
    copies = copies_in(src, dst, sems, 0, rows, 0)
    for copy in copies:
        copy.start()
    for copy in copies:
        copy.wait()


def stage_rows(array, rows):
    vmem = pl.BlockSpec(memory_space=pltpu.VMEM)
    return pl.pallas_call(
        functools.partial(stage_kernel, rows),
        out_shape=jax.ShapeDtypeStruct((rows, array.shape[1]), array.dtype),
        in_specs=[pl.BlockSpec(memory_space=pltpu.HBM)],
        out_specs=vmem,
        scratch_shapes=[pltpu.SemaphoreType.DMA((PIECES,))],
        compiler_params=pltpu.CompilerParams(vmem_limit_bytes=16 * MIB),
        cost_estimate=pl.CostEstimate(
            flops=0, bytes_accessed=2 * rows * array.shape[1], transcendentals=0
        ),
        name="stage",
    )(in_hbm(array))


def turning_kernel(length_ref, frequency_ref, beside_ref, after_ref, turn_ref):
    position = length_ref[0].astype(jnp.float32)
    angle = position * frequency_ref[...]
    lane = lax.broadcasted_iota(jnp.int32, angle.shape, 1)
    sine = jnp.sin(angle)
    turn_ref[0:1, :] = jnp.cos(angle)
    turn_ref[1:2, :] = jnp.where(lane < HEAD_SIZE // 2, -sine, sine)
    turn_ref[2:3, :] = jnp.full(angle.shape, position)


def turning(lengths, frequency, beside, after):
    vmem = pl.BlockSpec(memory_space=pltpu.VMEM)
    return pl.pallas_call(
        turning_kernel,
        out_shape=jax.ShapeDtypeStruct((8, HEAD_SIZE), jnp.float32),
        in_specs=[
            pl.BlockSpec(memory_space=pltpu.SMEM),
            vmem,
            pl.BlockSpec(memory_space=pltpu.HBM),
            vmem,
        ],
        out_specs=vmem,
        compiler_params=pltpu.CompilerParams(vmem_limit_bytes=2 * MIB),
        cost_estimate=pl.CostEstimate(flops=0, bytes_accessed=2 * beside.size, transcendentals=256),
        name="turning",
    )(lengths, frequency, in_hbm(beside), after)


def spread(depth, skip, chunk):
    ranges = [(at, min(chunk, depth - at)) for at in range(skip, depth, chunk)]
    if ranges and ranges[-1][1] >= 2 * LANES:
        start, size = ranges.pop()
        ranges += [(start, size - LANES), (start + size - LANES, LANES)]
    return ranges


def project_kernel(
    bits, rows_ref, other_ref, wq_hbm, first, wk, wv, *refs
):
    pieces, (wq, rows, sems) = refs[:FAN], refs[FAN:]
    skip = first.shape[0]
    ranges = spread(wq_hbm.shape[0], skip, CHUNK)
    copies = [
        copies_in(wq_hbm, wq, sems.at[i], start, size, start - skip)
        for i, (start, size) in enumerate(ranges)
    ]
    for group in copies:
        for copy in group:
            copy.start()

    slots = rows.shape[0]
    half = slots // 2
    turn = bit_reverse(lax.axis_index("gx"), bits)
    gy = lax.axis_index("gy")
    for ref, side in ((rows_ref, gy), (other_ref, 1 - gy)):
        block = ref[...].astype(jnp.float32)
        for t in range(half):
            slot = bit_reverse(t, bits) ^ turn ^ side
            rows[pl.ds(slot, 1), :] = block[t : t + 1, :]
    wide = rows[...]
    squares = jnp.sum(wide * wide, axis=1, keepdims=True)
    narrow = wide.astype(jnp.bfloat16)

    fresh = [jnp.dot(narrow, w[...], preferred_element_type=jnp.float32) for w in (wk, wv)]
    sums = jnp.dot(narrow[:, :skip], first[...], preferred_element_type=jnp.float32)
    for (start, size), group in zip(ranges, copies):
        for copy in group:
            copy.wait()
        sums = sums + jnp.dot(
            narrow[:, start : start + size],
            wq[start - skip : start - skip + size, :],
            preferred_element_type=jnp.float32,
        )

    total = pieces[0].shape[1]
    blocks = []
    for part in (sums, *fresh):
        blocks += [part[:, i : i + LANES] for i in range(0, part.shape[1], LANES)]
    blocks.append(jnp.broadcast_to(squares, (slots, LANES)))
    blocks += [jnp.zeros((slots, LANES), jnp.float32)] * (total - len(blocks))
    size = slots // FAN
    for at, ref in enumerate(pieces):
        flat = ref.reshape(size * total, LANES)
        for i, block in enumerate(blocks):
            flat[pl.ds(i, size, stride=total), :] = block[at * size : (at + 1) * size]


def project(rows, other, w_query, first, key_weight, value_weight, slots):
    bits = slots.bit_length() - 1
    depth, query_width = w_query.shape
    kv_width = key_weight.shape[1]
    used = (query_width + 2 * kv_width) // LANES + 1
    total = -(-used // 8) * 8
    skip = first.shape[0]
    piece = jax.ShapeDtypeStruct((slots // FAN, total, LANES), jnp.float32)
    hbm = pl.BlockSpec(memory_space=pltpu.HBM)
    whole = pl.BlockSpec(memory_space=pltpu.VMEM)
    return pl.pallas_call(
        functools.partial(project_kernel, bits),
        out_shape=(piece,) * FAN,
        in_specs=[whole, whole, hbm, whole, whole, whole],
        out_specs=(whole,) * FAN,
        scratch_shapes=[
            pltpu.VMEM((max(depth - skip, 16), query_width), jnp.bfloat16),
            pltpu.VMEM((slots, depth), jnp.float32),
            pltpu.SemaphoreType.DMA((max(1, len(spread(depth, skip, CHUNK))), PIECES)),
        ],
        compiler_params=pltpu.CompilerParams(vmem_limit_bytes=46 * MIB),
        cost_estimate=pl.CostEstimate(
            flops=2 * slots * depth * (query_width + 2 * kv_width),
            bytes_accessed=2 * depth * (query_width + 2 * kv_width),
            transcendentals=0,
        ),
        name="project",
    )(rows, other, in_hbm(w_query), first, key_weight, value_weight)


def attend_kernel(
    query_heads, kv_heads, pieces, beside_ref, turn_ref, k_ref, v_ref, *refs
):
    heads_ref = refs[pieces]
    total = refs[0][0]
    for ref in refs[1:pieces]:
        total = total + ref[0]
    at = query_heads + 2 * kv_heads
    scale = lax.rsqrt(total[at : at + 1, :] / MODEL_WIDTH + 1e-05)
    turned = total[: query_heads + kv_heads] * scale
    half = HEAD_SIZE // 2
    swapped = jnp.concatenate([turned[:, half:], turned[:, :half]], axis=1)
    turned = (turned * turn_ref[0:1, :] + swapped * turn_ref[1:2, :]).astype(jnp.bfloat16)
    fresh_values = (total[query_heads + kv_heads : at] * scale).astype(jnp.bfloat16)
    group = query_heads // kv_heads
    factor = 1.0 / math.sqrt(HEAD_SIZE)
    length = turn_ref[2:3, 0:1].astype(jnp.int32)
    side = 2 if kv_heads % 2 == 0 else 1
    for first in range(0, kv_heads, side):
        members = range(first, first + side)
        queries = [turned[head * group : (head + 1) * group] for head in members]
        empty = jnp.zeros((group, HEAD_SIZE), jnp.bfloat16)
        spread_out = jnp.concatenate(
            [
                jnp.concatenate([q if i == j else empty for j in range(side)], axis=1)
                for i, q in enumerate(queries)
            ],
            axis=0,
        )
        keys = jnp.concatenate([k_ref[0, head] for head in members], axis=1)
        values = jnp.concatenate([v_ref[0, head] for head in members], axis=1)
        scores = (
            lax.dot_general(
                spread_out, keys, (((1,), (1,)), ((), ())), preferred_element_type=jnp.float32
            )
            * factor
        )
        own = jnp.concatenate(
            [
                jnp.sum(
                    q.astype(jnp.float32)
                    * turned[query_heads + head : query_heads + head + 1].astype(jnp.float32),
                    axis=1,
                    keepdims=True,
                )
                for q, head in zip(queries, members)
            ],
            axis=0,
        ) * factor
        slot = lax.broadcasted_iota(jnp.int32, scores.shape, 1)
        scores = jnp.where(slot < length, scores, -jnp.inf)
        top = jnp.maximum(jnp.max(scores, axis=1, keepdims=True), own)
        exponent = jnp.exp(scores - top)
        own_exp = jnp.exp(own - top)
        share = 1.0 / (jnp.sum(exponent, axis=1, keepdims=True) + own_exp)
        weights = (exponent * share).astype(jnp.bfloat16)
        own_weight = (own_exp * share).astype(jnp.bfloat16).astype(jnp.float32)
        mixed = jnp.dot(weights, values, preferred_element_type=jnp.float32)
        for i, head in enumerate(members):
            block = mixed[i * group : (i + 1) * group, i * HEAD_SIZE : (i + 1) * HEAD_SIZE]
            block = block + own_weight[i * group : (i + 1) * group] * fresh_values[
                head : head + 1
            ].astype(jnp.float32)
            heads_ref[0, pl.ds(head * group, group), :] = block.astype(jnp.bfloat16)


def attend(parts, turn, k_cache, value_cache, query_heads, beside):
    kv_heads, cache_len = k_cache.shape[1:3]
    whole = pl.BlockSpec(memory_space=pltpu.VMEM)
    return pl.pallas_call(
        functools.partial(attend_kernel, query_heads, kv_heads, len(parts)),
        out_shape=jax.ShapeDtypeStruct((1, query_heads, HEAD_SIZE), jnp.bfloat16),
        in_specs=[pl.BlockSpec(memory_space=pltpu.HBM)] + [whole] * (3 + len(parts)),
        out_specs=whole,
        compiler_params=pltpu.CompilerParams(vmem_limit_bytes=12 * MIB),
        cost_estimate=pl.CostEstimate(
            flops=4 * query_heads * cache_len * HEAD_SIZE,
            bytes_accessed=4 * kv_heads * cache_len * HEAD_SIZE,
            transcendentals=query_heads * cache_len,
        ),
        name="attend",
    )(in_hbm(beside), turn, k_cache, value_cache, *parts)


def output_kernel(bits, places, turned, *refs):
    pieces = len(places)
    parts = refs[:pieces]
    w_ref, mine_ref, theirs_ref, flat, left, sums = refs[pieces:]
    slots = left.shape[0]
    heads = flat.shape[0] // slots
    for slot, ref in zip(places, parts):
        for i, row in enumerate(range(ref.shape[0])[::turned]):
            at = (slot + i) * heads
            flat[at : at + heads, :] = ref[row].astype(jnp.float32)
    for head in range(heads):
        left[:, head * HEAD_SIZE : (head + 1) * HEAD_SIZE] = flat[
            pl.ds(head, slots, stride=heads), :
        ].astype(jnp.bfloat16)
    total = None
    depth = w_ref.shape[0]
    chunk = min(2 * CHUNK, depth)
    for at in range(0, depth, chunk):
        part = slice(at, at + chunk)
        term = jnp.dot(left[:, part], w_ref[part, :], preferred_element_type=jnp.float32)
        total = term if total is None else total + term
    sums[...] = total
    half = slots // 2
    turn = bit_reverse(lax.axis_index("gx"), bits)
    gy = lax.axis_index("gy")
    for ref, side in ((mine_ref, gy), (theirs_ref, 1 - gy)):
        for t in range(half):
            slot = bit_reverse(t, bits) ^ turn ^ side
            ref[t : t + 1, :] = sums[pl.ds(slot, 1), :]


def output(parts, order, w_out, slots, turned=1):
    bits = slots.bit_length() - 1
    depth, width = w_out.shape
    heads = depth // HEAD_SIZE
    starts = [sum(x.shape[0] for x in parts[:i]) for i in range(len(parts))]
    places = tuple(starts[i] for i in order)
    parts = [parts[i] for i in order]
    whole = pl.BlockSpec(memory_space=pltpu.VMEM)
    piece = jax.ShapeDtypeStruct((slots // 2, width), jnp.float32)
    return pl.pallas_call(
        functools.partial(output_kernel, bits, places, turned),
        out_shape=(piece, piece),
        in_specs=[whole] * (len(parts) + 1),
        out_specs=(whole, whole),
        scratch_shapes=[
            pltpu.VMEM((slots * heads, HEAD_SIZE), jnp.float32),
            pltpu.VMEM((slots, depth), jnp.bfloat16),
            pltpu.VMEM((slots, width), jnp.float32),
        ],
        compiler_params=pltpu.CompilerParams(vmem_limit_bytes=12 * MIB),
        cost_estimate=pl.CostEstimate(
            flops=2 * slots * depth * width, bytes_accessed=2 * depth * width, transcendentals=0
        ),
        name="output",
    )(*parts, w_out)


def swap(block, axis, devices, mask):
    return lax.ppermute(block, axis, [(i, i ^ mask) for i in range(devices)])


def cross(block, devices, mask):
    pairs = [(i, i ^ (2 * mask + 1)) for i in range(2 * devices)]
    return lax.ppermute(block, ("gx", "gy"), pairs)


def fan(pieces, trade):
    masks = [bit_reverse(q, 2) for q in range(FAN)]
    arrived = [None] * FAN
    for q in sorted(range(1, FAN), key=lambda q: (masks[q] + 1) % FAN):
        arrived[q] = trade(pieces[q], masks[q])
    return arrived[1:]


def body(devices, activations, w_query, key_weight, value_weight, w_out, k_cache, value_cache, lengths):
    slots = devices
    query_heads = w_query.shape[1] // HEAD_SIZE
    other = swap(activations, "gy", 2, 1)
    depth = w_query.shape[0]
    first = stage_rows(w_query, min(FIRST, depth))
    pieces = project(activations, other, w_query, first, key_weight, value_weight, slots)
    half = HEAD_SIZE // 2
    frequency = jnp.power(
        jnp.float32(500000.0), -2.0 * jnp.arange(half, dtype=jnp.float32) / HEAD_SIZE
    )
    frequency = jnp.concatenate([frequency, frequency])[None, :]

    if devices == 2 * FAN:
        far = FAN
        arrived = fan(pieces, lambda block, mask: cross(block, devices, mask))
        beside = swap(pieces[0], "gy", 2, 1)
        turn = turning(lengths, frequency, w_out, pieces[3])
        total = arrived[2] + (arrived[1] + (arrived[0] + beside))
        total, turn = lax.optimization_barrier((total, turn))
        crossed = cross(total[1:], devices, far)
        beside = swap(total[:1], "gy", 2, 1)
        parts = [crossed, beside]
        heads = attend(parts, turn, k_cache, value_cache, query_heads, w_out)
        crossed = cross(heads, devices, far)
        beside = swap(heads, "gy", 2, 1)
        held = jnp.concatenate([crossed, beside], axis=0)
        arrived = fan([held] * FAN, lambda block, mask: cross(block, devices, mask))
        parts = [heads, swap(crossed, "gy", 2, 1)] + arrived
        order, turned = (2, 4, 3, 1, 0), -1
    else:
        arrived = fan(pieces, lambda block, mask: swap(block, "gx", devices, mask))
        turn = turning(lengths, frequency, w_out, pieces[3])
        total = pieces[0] + (arrived[2] + (arrived[1] + arrived[0]))
        mask = FAN
        while total.shape[0] > 2:
            rest = total.shape[0] // 2
            total = total[:rest] + swap(total[rest:], "gx", devices, mask)
            mask *= 2
        parts = [total[:1], swap(total[1:], "gx", devices, mask)]
        heads = attend(parts, turn, k_cache, value_cache, query_heads, w_out)

        parts = [heads, swap(heads, "gx", devices, mask)]
        while mask > FAN:
            mask //= 2
            parts.append(swap(jnp.concatenate(parts, axis=0), "gx", devices, mask))
        held = jnp.concatenate(parts, axis=0)
        parts += fan([held] * FAN, lambda block, mask: swap(block, "gx", devices, mask))
        order, turned = range(len(parts))[::-1], 1
    mine, theirs = output(parts, order, w_out, slots, turned)
    return (mine + swap(theirs, "gy", 2, 1)).astype(jnp.bfloat16)


def solution(mesh):
    placed = (
        P(("groups", "gy"), "gx"),
        P("gx", "gy"),
        P("gx", "gy"),
        P("gx", "gy"),
        P("gy", "gx"),
        P(("groups", "gx"), "gy", None, None),
        P(("groups", "gx"), "gy", None, None),
        P(("groups", "gx")),
    )
    return jax.shard_map(
        functools.partial(body, mesh.shape["gx"]),
        mesh=mesh,
        in_specs=placed,
        out_specs=P(("groups", "gy"), "gx"),
        check_vma=False,
    )
```

```python
import functools
import math

import jax
import jax.numpy as jnp
from jax import lax
from jax.experimental import pallas as pl
from jax.experimental.pallas import tpu as pltpu
from jax.sharding import PartitionSpec as P

MODEL_WIDTH = 16384
LANES = 128
HEAD_SIZE = 128
CHUNK = 256
FIRST = 256
PIECES = 4
FAN = 4
MIB = 2**20


def bit_reverse(value, bits):
    turned = 0
    for bit in range(bits):
        turned = turned | (((value >> bit) & 1) << (bits - 1 - bit))
    return turned


def in_hbm(array):
    return pltpu.with_memory_space_constraint(array, pltpu.HBM)


def cut(start, size):
    if size % (16 * PIECES):
        return [(start, size)]
    return [(start + i * (size // PIECES), size // PIECES) for i in range(PIECES)]


def copies_in(src, dst, sems, start, size, offset):
    return [
        pltpu.make_async_copy(
            src.at[pl.ds(at, rows)], dst.at[pl.ds(at - start + offset, rows)], sems.at[i]
        )
        for i, (at, rows) in enumerate(cut(start, size))
    ]


def stage_kernel(rows, src, dst, sems):
    copies = copies_in(src, dst, sems, 0, rows, 0)
    for copy in copies:
        copy.start()
    for copy in copies:
        copy.wait()


def stage_rows(array, rows):
    vmem = pl.BlockSpec(memory_space=pltpu.VMEM)
    return pl.pallas_call(
        functools.partial(stage_kernel, rows),
        out_shape=jax.ShapeDtypeStruct((rows, array.shape[1]), array.dtype),
        in_specs=[pl.BlockSpec(memory_space=pltpu.HBM)],
        out_specs=vmem,
        scratch_shapes=[pltpu.SemaphoreType.DMA((PIECES,))],
        compiler_params=pltpu.CompilerParams(vmem_limit_bytes=16 * MIB),
        cost_estimate=pl.CostEstimate(
            flops=0, bytes_accessed=2 * rows * array.shape[1], transcendentals=0
        ),
        name="stage",
    )(in_hbm(array))


def turning_kernel(length_ref, frequency_ref, beside_ref, after_ref, turn_ref, mask_ref):
    position = length_ref[0].astype(jnp.float32)
    angle = position * frequency_ref[...]
    lane = lax.broadcasted_iota(jnp.int32, angle.shape, 1)
    sine = jnp.sin(angle)
    turn_ref[0:1, :] = jnp.cos(angle)
    turn_ref[1:2, :] = jnp.where(lane < HEAD_SIZE // 2, -sine, sine)
    slot = lax.broadcasted_iota(jnp.int32, mask_ref.shape, 1)
    mask_ref[...] = jnp.where(slot < length_ref[0], 0.0, -jnp.inf)


def turning(lengths, frequency, beside, after, cache_len):
    vmem = pl.BlockSpec(memory_space=pltpu.VMEM)
    return pl.pallas_call(
        turning_kernel,
        out_shape=(
            jax.ShapeDtypeStruct((8, HEAD_SIZE), jnp.float32),
            jax.ShapeDtypeStruct((1, cache_len), jnp.float32),
        ),
        in_specs=[
            pl.BlockSpec(memory_space=pltpu.SMEM),
            vmem,
            pl.BlockSpec(memory_space=pltpu.HBM),
            vmem,
        ],
        out_specs=(vmem, vmem),
        compiler_params=pltpu.CompilerParams(vmem_limit_bytes=2 * MIB),
        cost_estimate=pl.CostEstimate(flops=0, bytes_accessed=2 * beside.size, transcendentals=256),
        name="turning",
    )(lengths, frequency, in_hbm(beside), after)


def spread(depth, skip, chunk):
    ranges = [(at, min(chunk, depth - at)) for at in range(skip, depth, chunk)]
    if ranges and ranges[-1][1] >= 2 * LANES:
        start, size = ranges.pop()
        ranges += [(start, size - LANES), (start + size - LANES, LANES)]
    return ranges


def project_kernel(
    bits, rows_ref, other_ref, wq_hbm, first, wk, wv, *refs
):
    pieces, (wq, rows, sems) = refs[:FAN], refs[FAN:]
    skip = first.shape[0]
    ranges = spread(wq_hbm.shape[0], skip, CHUNK)
    copies = [
        copies_in(wq_hbm, wq, sems.at[i], start, size, start - skip)
        for i, (start, size) in enumerate(ranges)
    ]
    for group in copies:
        for copy in group:
            copy.start()

    slots = rows.shape[0]
    half = slots // 2
    turn = bit_reverse(lax.axis_index("gx"), bits)
    gy = lax.axis_index("gy")
    for ref, side in ((rows_ref, gy), (other_ref, 1 - gy)):
        block = ref[...].astype(jnp.float32)
        for t in range(half):
            slot = bit_reverse(t, bits) ^ turn ^ side
            rows[pl.ds(slot, 1), :] = block[t : t + 1, :]
    wide = rows[...]
    squares = jnp.sum(wide * wide, axis=1, keepdims=True)
    narrow = wide.astype(jnp.bfloat16)

    total = pieces[0].shape[1]
    each = slots // FAN
    flats = [ref.reshape(each * total, LANES) for ref in pieces]

    def put(first_block, part):
        for i in range(0, part.shape[1], LANES):
            for at, flat in enumerate(flats):
                flat[pl.ds(first_block + i // LANES, each, stride=total), :] = part[
                    at * each : (at + 1) * each, i : i + LANES
                ]

    at = wq.shape[1] // LANES
    for w in (wk, wv):
        put(at, jnp.dot(narrow, w[...], preferred_element_type=jnp.float32))
        at += w.shape[1] // LANES
    put(at, jnp.broadcast_to(squares, (slots, LANES)))
    put(at + 1, jnp.zeros((slots, (total - at - 1) * LANES), jnp.float32))

    sums = jnp.dot(narrow[:, :skip], first[...], preferred_element_type=jnp.float32)
    for (start, size), group in zip(ranges, copies):
        for copy in group:
            copy.wait()
        sums = sums + jnp.dot(
            narrow[:, start : start + size],
            wq[start - skip : start - skip + size, :],
            preferred_element_type=jnp.float32,
        )

    put(0, sums)


def project(rows, other, w_query, first, key_weight, value_weight, slots):
    bits = slots.bit_length() - 1
    depth, query_width = w_query.shape
    kv_width = key_weight.shape[1]
    used = (query_width + 2 * kv_width) // LANES + 1
    total = -(-used // 8) * 8
    skip = first.shape[0]
    piece = jax.ShapeDtypeStruct((slots // FAN, total, LANES), jnp.float32)
    hbm = pl.BlockSpec(memory_space=pltpu.HBM)
    whole = pl.BlockSpec(memory_space=pltpu.VMEM)
    return pl.pallas_call(
        functools.partial(project_kernel, bits),
        out_shape=(piece,) * FAN,
        in_specs=[whole, whole, hbm, whole, whole, whole],
        out_specs=(whole,) * FAN,
        scratch_shapes=[
            pltpu.VMEM((max(depth - skip, 16), query_width), jnp.bfloat16),
            pltpu.VMEM((slots, depth), jnp.float32),
            pltpu.SemaphoreType.DMA((max(1, len(spread(depth, skip, CHUNK))), PIECES)),
        ],
        compiler_params=pltpu.CompilerParams(vmem_limit_bytes=46 * MIB),
        cost_estimate=pl.CostEstimate(
            flops=2 * slots * depth * (query_width + 2 * kv_width),
            bytes_accessed=2 * depth * (query_width + 2 * kv_width),
            transcendentals=0,
        ),
        name="project",
    )(rows, other, in_hbm(w_query), first, key_weight, value_weight)


def attend_kernel(
    query_heads, kv_heads, pieces, beside_ref, turn_ref, live_ref, k_ref, v_ref, *refs
):
    heads_ref = refs[pieces]
    total = refs[0][0]
    for ref in refs[1:pieces]:
        total = total + ref[0]
    at = query_heads + 2 * kv_heads
    scale = lax.rsqrt(total[at : at + 1, :] / MODEL_WIDTH + 1e-05)
    turned = total[: query_heads + kv_heads] * scale
    half = HEAD_SIZE // 2
    swapped = jnp.concatenate([turned[:, half:], turned[:, :half]], axis=1)
    turned = (turned * turn_ref[0:1, :] + swapped * turn_ref[1:2, :]).astype(jnp.bfloat16)
    fresh_values = (total[query_heads + kv_heads : at] * scale).astype(jnp.bfloat16)
    group = query_heads // kv_heads
    factor = 1.0 / math.sqrt(HEAD_SIZE)
    side = 2 if kv_heads % 2 == 0 else 1
    for first in range(0, kv_heads, side):
        members = range(first, first + side)
        queries = [turned[head * group : (head + 1) * group] for head in members]
        empty = jnp.zeros((group, HEAD_SIZE), jnp.bfloat16)
        spread_out = jnp.concatenate(
            [
                jnp.concatenate([q if i == j else empty for j in range(side)], axis=1)
                for i, q in enumerate(queries)
            ],
            axis=0,
        )
        keys = jnp.concatenate([k_ref[0, head] for head in members], axis=1)
        values = jnp.concatenate([v_ref[0, head] for head in members], axis=1)
        scores = (
            lax.dot_general(
                spread_out, keys, (((1,), (1,)), ((), ())), preferred_element_type=jnp.float32
            )
            * factor
            + live_ref[...]
        )
        own = jnp.concatenate(
            [
                jnp.sum(
                    q.astype(jnp.float32)
                    * turned[query_heads + head : query_heads + head + 1].astype(jnp.float32),
                    axis=1,
                    keepdims=True,
                )
                for q, head in zip(queries, members)
            ],
            axis=0,
        ) * factor
        top = jnp.maximum(jnp.max(scores, axis=1, keepdims=True), own)
        exponent = jnp.exp(scores - top)
        own_exp = jnp.exp(own - top)
        mixed = jnp.dot(
            exponent.astype(jnp.bfloat16), values, preferred_element_type=jnp.float32
        )
        share = 1.0 / (jnp.sum(exponent, axis=1, keepdims=True) + own_exp)
        for i, head in enumerate(members):
            part = slice(i * group, (i + 1) * group)
            block = mixed[part, i * HEAD_SIZE : (i + 1) * HEAD_SIZE]
            block = block + own_exp[part] * fresh_values[head : head + 1].astype(jnp.float32)
            block = block * share[part]
            heads_ref[0, pl.ds(head * group, group), :] = block.astype(jnp.bfloat16)


def attend(parts, turn, live, k_cache, value_cache, query_heads, beside):
    kv_heads, cache_len = k_cache.shape[1:3]
    whole = pl.BlockSpec(memory_space=pltpu.VMEM)
    return pl.pallas_call(
        functools.partial(attend_kernel, query_heads, kv_heads, len(parts)),
        out_shape=jax.ShapeDtypeStruct((1, query_heads, HEAD_SIZE), jnp.bfloat16),
        in_specs=[pl.BlockSpec(memory_space=pltpu.HBM)] + [whole] * (4 + len(parts)),
        out_specs=whole,
        compiler_params=pltpu.CompilerParams(vmem_limit_bytes=12 * MIB),
        cost_estimate=pl.CostEstimate(
            flops=4 * query_heads * cache_len * HEAD_SIZE,
            bytes_accessed=4 * kv_heads * cache_len * HEAD_SIZE,
            transcendentals=query_heads * cache_len,
        ),
        name="attend",
    )(in_hbm(beside), turn, live, k_cache, value_cache, *parts)


def output_kernel(bits, places, turned, *refs):
    pieces = len(places)
    parts = refs[:pieces]
    w_ref, mine_ref, theirs_ref, flat, left, sums = refs[pieces:]
    slots = left.shape[0]
    heads = flat.shape[0] // slots
    for slot, ref in zip(places, parts):
        for i, row in enumerate(range(ref.shape[0])[::turned]):
            at = (slot + i) * heads
            flat[at : at + heads, :] = ref[row].astype(jnp.float32)
    for head in range(heads):
        left[:, head * HEAD_SIZE : (head + 1) * HEAD_SIZE] = flat[
            pl.ds(head, slots, stride=heads), :
        ].astype(jnp.bfloat16)
    total = None
    depth = w_ref.shape[0]
    chunk = min(2 * CHUNK, depth)
    for at in range(0, depth, chunk):
        part = slice(at, at + chunk)
        term = jnp.dot(left[:, part], w_ref[part, :], preferred_element_type=jnp.float32)
        total = term if total is None else total + term
    sums[...] = total
    half = slots // 2
    turn = bit_reverse(lax.axis_index("gx"), bits)
    gy = lax.axis_index("gy")
    for ref, side in ((mine_ref, gy), (theirs_ref, 1 - gy)):
        for t in range(half):
            slot = bit_reverse(t, bits) ^ turn ^ side
            ref[t : t + 1, :] = sums[pl.ds(slot, 1), :]


def output(parts, order, w_out, slots, turned=1):
    bits = slots.bit_length() - 1
    depth, width = w_out.shape
    heads = depth // HEAD_SIZE
    starts = [sum(x.shape[0] for x in parts[:i]) for i in range(len(parts))]
    places = tuple(starts[i] for i in order)
    parts = [parts[i] for i in order]
    whole = pl.BlockSpec(memory_space=pltpu.VMEM)
    piece = jax.ShapeDtypeStruct((slots // 2, width), jnp.float32)
    return pl.pallas_call(
        functools.partial(output_kernel, bits, places, turned),
        out_shape=(piece, piece),
        in_specs=[whole] * (len(parts) + 1),
        out_specs=(whole, whole),
        scratch_shapes=[
            pltpu.VMEM((slots * heads, HEAD_SIZE), jnp.float32),
            pltpu.VMEM((slots, depth), jnp.bfloat16),
            pltpu.VMEM((slots, width), jnp.float32),
        ],
        compiler_params=pltpu.CompilerParams(vmem_limit_bytes=12 * MIB),
        cost_estimate=pl.CostEstimate(
            flops=2 * slots * depth * width, bytes_accessed=2 * depth * width, transcendentals=0
        ),
        name="output",
    )(*parts, w_out)


def swap(block, axis, devices, mask):
    return lax.ppermute(block, axis, [(i, i ^ mask) for i in range(devices)])


def cross(block, devices, mask):
    pairs = [(i, i ^ (2 * mask + 1)) for i in range(2 * devices)]
    return lax.ppermute(block, ("gx", "gy"), pairs)


def fan(pieces, trade):
    masks = [bit_reverse(q, 2) for q in range(FAN)]
    arrived = [None] * FAN
    for q in sorted(range(1, FAN), key=lambda q: (masks[q] + 1) % FAN):
        arrived[q] = trade(pieces[q], masks[q])
    return arrived[1:]


def body(devices, activations, w_query, key_weight, value_weight, w_out, k_cache, value_cache, lengths):
    slots = devices
    query_heads = w_query.shape[1] // HEAD_SIZE
    other = swap(activations, "gy", 2, 1)
    depth = w_query.shape[0]
    first = stage_rows(w_query, min(FIRST, depth))
    pieces = project(activations, other, w_query, first, key_weight, value_weight, slots)
    half = HEAD_SIZE // 2
    frequency = jnp.power(
        jnp.float32(500000.0), -2.0 * jnp.arange(half, dtype=jnp.float32) / HEAD_SIZE
    )
    frequency = jnp.concatenate([frequency, frequency])[None, :]

    if devices == 2 * FAN:
        far = FAN
        arrived = fan(pieces, lambda block, mask: cross(block, devices, mask))
        beside = swap(pieces[0], "gy", 2, 1)
        turn, live = turning(lengths, frequency, w_out, pieces[3], k_cache.shape[2])
        leaving = [x[1:] for x in (*arrived, beside)]
        staying = [x[:1] for x in (*arrived, beside)]
        total = leaving[2] + (leaving[1] + (leaving[0] + leaving[3]))
        total, turn = lax.optimization_barrier((total, turn))
        crossed = cross(total, devices, far)
        beside = swap(staying[2] + (staying[1] + (staying[0] + staying[3])), "gy", 2, 1)
        parts = [crossed, beside]
        heads = attend(parts, turn, live, k_cache, value_cache, query_heads, w_out)
        crossed = cross(heads, devices, far)
        beside = swap(heads, "gy", 2, 1)
        held = jnp.concatenate([crossed, beside], axis=0)
        arrived = fan([held] * FAN, lambda block, mask: cross(block, devices, mask))
        parts = [heads, swap(crossed, "gy", 2, 1)] + arrived
        order, turned = (2, 4, 3, 1, 0), -1
    else:
        arrived = fan(pieces, lambda block, mask: swap(block, "gx", devices, mask))
        turn, live = turning(lengths, frequency, w_out, pieces[3], k_cache.shape[2])
        total = pieces[0] + (arrived[2] + (arrived[1] + arrived[0]))
        mask = FAN
        while total.shape[0] > 2:
            rest = total.shape[0] // 2
            total = total[:rest] + swap(total[rest:], "gx", devices, mask)
            mask *= 2
        parts = [total[:1], swap(total[1:], "gx", devices, mask)]
        heads = attend(parts, turn, live, k_cache, value_cache, query_heads, w_out)

        parts = [heads, swap(heads, "gx", devices, mask)]
        while mask > FAN:
            mask //= 2
            parts.append(swap(jnp.concatenate(parts, axis=0), "gx", devices, mask))
        held = jnp.concatenate(parts, axis=0)
        parts += fan([held] * FAN, lambda block, mask: swap(block, "gx", devices, mask))
        order, turned = range(len(parts))[::-1], 1
    mine, theirs = output(parts, order, w_out, slots, turned)
    return (mine + swap(theirs, "gy", 2, 1)).astype(jnp.bfloat16)


def solution(mesh):
    placed = (
        P(("groups", "gy"), "gx"),
        P("gx", "gy"),
        P("gx", "gy"),
        P("gx", "gy"),
        P("gy", "gx"),
        P(("groups", "gx"), "gy", None, None),
        P(("groups", "gx"), "gy", None, None),
        P(("groups", "gx")),
    )
    return jax.shard_map(
        functools.partial(body, mesh.shape["gx"]),
        mesh=mesh,
        in_specs=placed,
        out_specs=P(("groups", "gy"), "gx"),
        check_vma=False,
    )
```

```python
import functools
import math

import jax
import jax.numpy as jnp
from jax import lax
from jax.experimental import pallas as pl
from jax.experimental.pallas import tpu as pltpu
from jax.sharding import PartitionSpec as P

MODEL_WIDTH = 16384
LANES = 128
HEAD_SIZE = 128
CHUNK = 256
FIRST = 384
PIECES = 4
FAN = 4
MIB = 2**20


def bit_reverse(value, bits):
    turned = 0
    for bit in range(bits):
        turned = turned | (((value >> bit) & 1) << (bits - 1 - bit))
    return turned


def in_hbm(array):
    return pltpu.with_memory_space_constraint(array, pltpu.HBM)


def cut(start, size):
    if size % (16 * PIECES):
        return [(start, size)]
    return [(start + i * (size // PIECES), size // PIECES) for i in range(PIECES)]


def copies_in(src, dst, sems, start, size, offset):
    return [
        pltpu.make_async_copy(
            src.at[pl.ds(at, rows)], dst.at[pl.ds(at - start + offset, rows)], sems.at[i]
        )
        for i, (at, rows) in enumerate(cut(start, size))
    ]


def stage_kernel(rows, src, dst, sems):
    copies = copies_in(src, dst, sems, 0, rows, 0)
    for copy in copies:
        copy.start()
    for copy in copies:
        copy.wait()


def stage_rows(array, rows):
    vmem = pl.BlockSpec(memory_space=pltpu.VMEM)
    return pl.pallas_call(
        functools.partial(stage_kernel, rows),
        out_shape=jax.ShapeDtypeStruct((rows, array.shape[1]), array.dtype),
        in_specs=[pl.BlockSpec(memory_space=pltpu.HBM)],
        out_specs=vmem,
        scratch_shapes=[pltpu.SemaphoreType.DMA((PIECES,))],
        compiler_params=pltpu.CompilerParams(vmem_limit_bytes=16 * MIB),
        cost_estimate=pl.CostEstimate(
            flops=0, bytes_accessed=2 * rows * array.shape[1], transcendentals=0
        ),
        name="stage",
    )(in_hbm(array))


def turning_kernel(length_ref, frequency_ref, beside_ref, after_ref, turn_ref, mask_ref):
    position = length_ref[0].astype(jnp.float32)
    angle = position * frequency_ref[...]
    lane = lax.broadcasted_iota(jnp.int32, angle.shape, 1)
    sine = jnp.sin(angle)
    turn_ref[0:1, :] = jnp.cos(angle)
    turn_ref[1:2, :] = jnp.where(lane < HEAD_SIZE // 2, -sine, sine)
    slot = lax.broadcasted_iota(jnp.int32, mask_ref.shape, 1)
    mask_ref[...] = jnp.where(slot < length_ref[0], 0.0, -jnp.inf)


def turning(lengths, frequency, beside, after, cache_len):
    vmem = pl.BlockSpec(memory_space=pltpu.VMEM)
    return pl.pallas_call(
        turning_kernel,
        out_shape=(
            jax.ShapeDtypeStruct((8, HEAD_SIZE), jnp.float32),
            jax.ShapeDtypeStruct((1, cache_len), jnp.float32),
        ),
        in_specs=[
            pl.BlockSpec(memory_space=pltpu.SMEM),
            vmem,
            pl.BlockSpec(memory_space=pltpu.HBM),
            vmem,
        ],
        out_specs=(vmem, vmem),
        compiler_params=pltpu.CompilerParams(vmem_limit_bytes=2 * MIB),
        cost_estimate=pl.CostEstimate(flops=0, bytes_accessed=2 * beside.size, transcendentals=256),
        name="turning",
    )(lengths, frequency, in_hbm(beside), after)


def spread(depth, skip, chunk):
    ranges = [(at, min(chunk, depth - at)) for at in range(skip, depth, chunk)]
    if ranges and ranges[-1][1] >= 2 * LANES:
        start, size = ranges.pop()
        ranges += [(start, size - LANES), (start + size - LANES, LANES)]
    return ranges


def project_kernel(
    bits, rows_ref, other_ref, wq_hbm, first, wk, wv, *refs
):
    pieces, (wq, rows, sems) = refs[:FAN], refs[FAN:]
    skip = first.shape[0]
    ranges = spread(wq_hbm.shape[0], skip, CHUNK)
    copies = [
        copies_in(wq_hbm, wq, sems.at[i], start, size, start - skip)
        for i, (start, size) in enumerate(ranges)
    ]
    for group in copies:
        for copy in group:
            copy.start()

    slots = rows.shape[0]
    half = slots // 2
    turn = bit_reverse(lax.axis_index("gx"), bits)
    gy = lax.axis_index("gy")
    for ref, side in ((rows_ref, gy), (other_ref, 1 - gy)):
        block = ref[...].astype(jnp.float32)
        for t in range(half):
            slot = bit_reverse(t, bits) ^ turn ^ side
            rows[pl.ds(slot, 1), :] = block[t : t + 1, :]
    wide = rows[...]
    squares = jnp.sum(wide * wide, axis=1, keepdims=True)
    narrow = wide.astype(jnp.bfloat16)

    total = pieces[0].shape[1]
    each = slots // FAN
    flats = [ref.reshape(each * total, LANES) for ref in pieces]

    def put(first_block, part):
        for i in range(0, part.shape[1], LANES):
            for at, flat in enumerate(flats):
                flat[pl.ds(first_block + i // LANES, each, stride=total), :] = part[
                    at * each : (at + 1) * each, i : i + LANES
                ]

    at = wq.shape[1] // LANES
    for w in (wk, wv):
        put(at, jnp.dot(narrow, w[...], preferred_element_type=jnp.float32))
        at += w.shape[1] // LANES
    put(at, jnp.broadcast_to(squares, (slots, LANES)))
    put(at + 1, jnp.zeros((slots, (total - at - 1) * LANES), jnp.float32))

    sums = jnp.dot(narrow[:, :skip], first[...], preferred_element_type=jnp.float32)
    for (start, size), group in zip(ranges, copies):
        for copy in group:
            copy.wait()
        sums = sums + jnp.dot(
            narrow[:, start : start + size],
            wq[start - skip : start - skip + size, :],
            preferred_element_type=jnp.float32,
        )

    put(0, sums)


def project(rows, other, w_query, first, key_weight, value_weight, slots):
    bits = slots.bit_length() - 1
    depth, query_width = w_query.shape
    kv_width = key_weight.shape[1]
    used = (query_width + 2 * kv_width) // LANES + 1
    total = -(-used // 8) * 8
    skip = first.shape[0]
    piece = jax.ShapeDtypeStruct((slots // FAN, total, LANES), jnp.float32)
    hbm = pl.BlockSpec(memory_space=pltpu.HBM)
    whole = pl.BlockSpec(memory_space=pltpu.VMEM)
    return pl.pallas_call(
        functools.partial(project_kernel, bits),
        out_shape=(piece,) * FAN,
        in_specs=[whole, whole, hbm, whole, whole, whole],
        out_specs=(whole,) * FAN,
        scratch_shapes=[
            pltpu.VMEM((max(depth - skip, 16), query_width), jnp.bfloat16),
            pltpu.VMEM((slots, depth), jnp.float32),
            pltpu.SemaphoreType.DMA((max(1, len(spread(depth, skip, CHUNK))), PIECES)),
        ],
        compiler_params=pltpu.CompilerParams(vmem_limit_bytes=46 * MIB),
        cost_estimate=pl.CostEstimate(
            flops=2 * slots * depth * (query_width + 2 * kv_width),
            bytes_accessed=2 * depth * (query_width + 2 * kv_width),
            transcendentals=0,
        ),
        name="project",
    )(rows, other, in_hbm(w_query), first, key_weight, value_weight)


def attend_kernel(
    query_heads, kv_heads, pieces, beside_ref, turn_ref, live_ref, k_ref, v_ref, *refs
):
    heads_ref = refs[pieces]
    total = refs[0][0]
    for ref in refs[1:pieces]:
        total = total + ref[0]
    at = query_heads + 2 * kv_heads
    scale = lax.rsqrt(total[at : at + 1, :] / MODEL_WIDTH + 1e-05)
    turned = total[: query_heads + kv_heads] * scale
    half = HEAD_SIZE // 2
    swapped = jnp.concatenate([turned[:, half:], turned[:, :half]], axis=1)
    turned = (turned * turn_ref[0:1, :] + swapped * turn_ref[1:2, :]).astype(jnp.bfloat16)
    fresh_values = (total[query_heads + kv_heads : at] * scale).astype(jnp.bfloat16)
    group = query_heads // kv_heads
    factor = 1.0 / math.sqrt(HEAD_SIZE)
    side = 2 if kv_heads % 2 == 0 else 1
    for first in range(0, kv_heads, side):
        members = range(first, first + side)
        queries = [turned[head * group : (head + 1) * group] for head in members]
        empty = jnp.zeros((group, HEAD_SIZE), jnp.bfloat16)
        spread_out = jnp.concatenate(
            [
                jnp.concatenate([q if i == j else empty for j in range(side)], axis=1)
                for i, q in enumerate(queries)
            ],
            axis=0,
        )
        keys = jnp.concatenate([k_ref[0, head] for head in members], axis=1)
        values = jnp.concatenate([v_ref[0, head] for head in members], axis=1)
        scores = (
            lax.dot_general(
                spread_out, keys, (((1,), (1,)), ((), ())), preferred_element_type=jnp.float32
            )
            * factor
            + live_ref[...]
        )
        own = jnp.concatenate(
            [
                jnp.sum(
                    q.astype(jnp.float32)
                    * turned[query_heads + head : query_heads + head + 1].astype(jnp.float32),
                    axis=1,
                    keepdims=True,
                )
                for q, head in zip(queries, members)
            ],
            axis=0,
        ) * factor
        top = jnp.maximum(jnp.max(scores, axis=1, keepdims=True), own)
        exponent = jnp.exp(scores - top)
        own_exp = jnp.exp(own - top)
        mixed = jnp.dot(
            exponent.astype(jnp.bfloat16), values, preferred_element_type=jnp.float32
        )
        share = 1.0 / (jnp.sum(exponent, axis=1, keepdims=True) + own_exp)
        for i, head in enumerate(members):
            part = slice(i * group, (i + 1) * group)
            block = mixed[part, i * HEAD_SIZE : (i + 1) * HEAD_SIZE]
            block = block + own_exp[part] * fresh_values[head : head + 1].astype(jnp.float32)
            block = block * share[part]
            heads_ref[0, pl.ds(head * group, group), :] = block.astype(jnp.bfloat16)


def attend(parts, turn, live, k_cache, value_cache, query_heads, beside):
    kv_heads, cache_len = k_cache.shape[1:3]
    whole = pl.BlockSpec(memory_space=pltpu.VMEM)
    return pl.pallas_call(
        functools.partial(attend_kernel, query_heads, kv_heads, len(parts)),
        out_shape=jax.ShapeDtypeStruct((1, query_heads, HEAD_SIZE), jnp.bfloat16),
        in_specs=[pl.BlockSpec(memory_space=pltpu.HBM)] + [whole] * (4 + len(parts)),
        out_specs=whole,
        compiler_params=pltpu.CompilerParams(vmem_limit_bytes=12 * MIB),
        cost_estimate=pl.CostEstimate(
            flops=4 * query_heads * cache_len * HEAD_SIZE,
            bytes_accessed=4 * kv_heads * cache_len * HEAD_SIZE,
            transcendentals=query_heads * cache_len,
        ),
        name="attend",
    )(in_hbm(beside), turn, live, k_cache, value_cache, *parts)


def output_kernel(bits, places, turned, *refs):
    pieces = len(places)
    parts = refs[:pieces]
    w_ref, mine_ref, theirs_ref, flat, left, sums = refs[pieces:]
    slots = left.shape[0]
    heads = flat.shape[0] // slots
    for slot, ref in zip(places, parts):
        for i, row in enumerate(range(ref.shape[0])[::turned]):
            at = (slot + i) * heads
            flat[at : at + heads, :] = ref[row].astype(jnp.float32)
    for head in range(heads):
        left[:, head * HEAD_SIZE : (head + 1) * HEAD_SIZE] = flat[
            pl.ds(head, slots, stride=heads), :
        ].astype(jnp.bfloat16)
    total = None
    depth = w_ref.shape[0]
    chunk = min(2 * CHUNK, depth)
    for at in range(0, depth, chunk):
        part = slice(at, at + chunk)
        term = jnp.dot(left[:, part], w_ref[part, :], preferred_element_type=jnp.float32)
        total = term if total is None else total + term
    sums[...] = total
    half = slots // 2
    turn = bit_reverse(lax.axis_index("gx"), bits)
    gy = lax.axis_index("gy")
    for ref, side in ((mine_ref, gy), (theirs_ref, 1 - gy)):
        for t in range(half):
            slot = bit_reverse(t, bits) ^ turn ^ side
            ref[t : t + 1, :] = sums[pl.ds(slot, 1), :]


def output(parts, order, w_out, slots, turned=1):
    bits = slots.bit_length() - 1
    depth, width = w_out.shape
    heads = depth // HEAD_SIZE
    starts = [sum(x.shape[0] for x in parts[:i]) for i in range(len(parts))]
    places = tuple(starts[i] for i in order)
    parts = [parts[i] for i in order]
    whole = pl.BlockSpec(memory_space=pltpu.VMEM)
    piece = jax.ShapeDtypeStruct((slots // 2, width), jnp.float32)
    return pl.pallas_call(
        functools.partial(output_kernel, bits, places, turned),
        out_shape=(piece, piece),
        in_specs=[whole] * (len(parts) + 1),
        out_specs=(whole, whole),
        scratch_shapes=[
            pltpu.VMEM((slots * heads, HEAD_SIZE), jnp.float32),
            pltpu.VMEM((slots, depth), jnp.bfloat16),
            pltpu.VMEM((slots, width), jnp.float32),
        ],
        compiler_params=pltpu.CompilerParams(vmem_limit_bytes=12 * MIB),
        cost_estimate=pl.CostEstimate(
            flops=2 * slots * depth * width, bytes_accessed=2 * depth * width, transcendentals=0
        ),
        name="output",
    )(*parts, w_out)


def swap(block, axis, devices, mask):
    return lax.ppermute(block, axis, [(i, i ^ mask) for i in range(devices)])


def cross(block, devices, mask):
    pairs = [(i, i ^ (2 * mask + 1)) for i in range(2 * devices)]
    return lax.ppermute(block, ("gx", "gy"), pairs)


def fan(pieces, trade):
    masks = [bit_reverse(q, 2) for q in range(FAN)]
    arrived = [None] * FAN
    for q in sorted(range(1, FAN), key=lambda q: (masks[q] + 1) % FAN):
        arrived[q] = trade(pieces[q], masks[q])
    return arrived[1:]


def body(devices, activations, w_query, key_weight, value_weight, w_out, k_cache, value_cache, lengths):
    slots = devices
    query_heads = w_query.shape[1] // HEAD_SIZE
    other = swap(activations, "gy", 2, 1)
    depth = w_query.shape[0]
    first = stage_rows(w_query, min(FIRST, depth))
    pieces = project(activations, other, w_query, first, key_weight, value_weight, slots)
    half = HEAD_SIZE // 2
    frequency = jnp.power(
        jnp.float32(500000.0), -2.0 * jnp.arange(half, dtype=jnp.float32) / HEAD_SIZE
    )
    frequency = jnp.concatenate([frequency, frequency])[None, :]

    if devices == 2 * FAN:
        far = FAN
        arrived = fan(pieces, lambda block, mask: cross(block, devices, mask))
        beside = swap(pieces[0], "gy", 2, 1)
        turn, live = turning(lengths, frequency, w_out, pieces[3], k_cache.shape[2])
        leaving = [x[1:] for x in (*arrived, beside)]
        staying = [x[:1] for x in (*arrived, beside)]
        total = leaving[2] + (leaving[1] + (leaving[0] + leaving[3]))
        total, turn = lax.optimization_barrier((total, turn))
        crossed = cross(total, devices, far)
        beside = swap(staying[2] + (staying[1] + (staying[0] + staying[3])), "gy", 2, 1)
        parts = [crossed, beside]
        heads = attend(parts, turn, live, k_cache, value_cache, query_heads, w_out)
        crossed = cross(heads, devices, far)
        beside = swap(heads, "gy", 2, 1)
        held = jnp.concatenate([crossed, beside], axis=0)
        arrived = fan([held] * FAN, lambda block, mask: cross(block, devices, mask))
        parts = [heads, swap(crossed, "gy", 2, 1)] + arrived
        order, turned = (2, 4, 3, 1, 0), -1
    else:
        arrived = fan(pieces, lambda block, mask: swap(block, "gx", devices, mask))
        turn, live = turning(lengths, frequency, w_out, pieces[3], k_cache.shape[2])
        total = pieces[0] + (arrived[2] + (arrived[1] + arrived[0]))
        mask = FAN
        while total.shape[0] > 2:
            rest = total.shape[0] // 2
            total = total[:rest] + swap(total[rest:], "gx", devices, mask)
            mask *= 2
        parts = [total[:1], swap(total[1:], "gx", devices, mask)]
        heads = attend(parts, turn, live, k_cache, value_cache, query_heads, w_out)

        parts = [heads, swap(heads, "gx", devices, mask)]
        while mask > FAN:
            mask //= 2
            parts.append(swap(jnp.concatenate(parts, axis=0), "gx", devices, mask))
        held = jnp.concatenate(parts, axis=0)
        parts += fan([held] * FAN, lambda block, mask: swap(block, "gx", devices, mask))
        order, turned = range(len(parts))[::-1], 1
    mine, theirs = output(parts, order, w_out, slots, turned)
    return (mine + swap(theirs, "gy", 2, 1)).astype(jnp.bfloat16)


def solution(mesh):
    placed = (
        P(("groups", "gy"), "gx"),
        P("gx", "gy"),
        P("gx", "gy"),
        P("gx", "gy"),
        P("gy", "gx"),
        P(("groups", "gx"), "gy", None, None),
        P(("groups", "gx"), "gy", None, None),
        P(("groups", "gx")),
    )
    return jax.shard_map(
        functools.partial(body, mesh.shape["gx"]),
        mesh=mesh,
        in_specs=placed,
        out_specs=P(("groups", "gy"), "gx"),
        check_vma=False,
    )
```

```python
import functools
import math

import jax
import jax.numpy as jnp
from jax import lax
from jax.experimental import pallas as pl
from jax.experimental.pallas import tpu as pltpu
from jax.sharding import PartitionSpec as P

MODEL_WIDTH = 16384
LANES = 128
HEAD_SIZE = 128
CHUNK = 256
FIRST = 384
PIECES = 4
FAN = 4
MIB = 2**20


def bit_reverse(value, bits):
    turned = 0
    for bit in range(bits):
        turned = turned | (((value >> bit) & 1) << (bits - 1 - bit))
    return turned


def in_hbm(array):
    return pltpu.with_memory_space_constraint(array, pltpu.HBM)


def cut(start, size):
    if size % (16 * PIECES):
        return [(start, size)]
    return [(start + i * (size // PIECES), size // PIECES) for i in range(PIECES)]


def copies_in(src, dst, sems, start, size, offset):
    return [
        pltpu.make_async_copy(
            src.at[pl.ds(at, rows)], dst.at[pl.ds(at - start + offset, rows)], sems.at[i]
        )
        for i, (at, rows) in enumerate(cut(start, size))
    ]


def stage_kernel(rows, src, dst, sems):
    copies = copies_in(src, dst, sems, 0, rows, 0)
    for copy in copies:
        copy.start()
    for copy in copies:
        copy.wait()


def stage_rows(array, rows):
    vmem = pl.BlockSpec(memory_space=pltpu.VMEM)
    return pl.pallas_call(
        functools.partial(stage_kernel, rows),
        out_shape=jax.ShapeDtypeStruct((rows, array.shape[1]), array.dtype),
        in_specs=[pl.BlockSpec(memory_space=pltpu.HBM)],
        out_specs=vmem,
        scratch_shapes=[pltpu.SemaphoreType.DMA((PIECES,))],
        compiler_params=pltpu.CompilerParams(vmem_limit_bytes=16 * MIB),
        cost_estimate=pl.CostEstimate(
            flops=0, bytes_accessed=2 * rows * array.shape[1], transcendentals=0
        ),
        name="stage",
    )(in_hbm(array))


def turning_kernel(length_ref, frequency_ref, beside_ref, after_ref, turn_ref, mask_ref):
    position = length_ref[0].astype(jnp.float32)
    angle = position * frequency_ref[...]
    lane = lax.broadcasted_iota(jnp.int32, angle.shape, 1)
    sine = jnp.sin(angle)
    turn_ref[0:1, :] = jnp.cos(angle)
    turn_ref[1:2, :] = jnp.where(lane < HEAD_SIZE // 2, -sine, sine)
    slot = lax.broadcasted_iota(jnp.int32, mask_ref.shape, 1)
    mask_ref[...] = jnp.where(slot < length_ref[0], 0.0, -jnp.inf)


def turning(lengths, frequency, beside, after, cache_len):
    vmem = pl.BlockSpec(memory_space=pltpu.VMEM)
    return pl.pallas_call(
        turning_kernel,
        out_shape=(
            jax.ShapeDtypeStruct((8, HEAD_SIZE), jnp.float32),
            jax.ShapeDtypeStruct((1, cache_len), jnp.float32),
        ),
        in_specs=[
            pl.BlockSpec(memory_space=pltpu.SMEM),
            vmem,
            pl.BlockSpec(memory_space=pltpu.HBM),
            vmem,
        ],
        out_specs=(vmem, vmem),
        compiler_params=pltpu.CompilerParams(vmem_limit_bytes=2 * MIB),
        cost_estimate=pl.CostEstimate(flops=0, bytes_accessed=2 * beside.size, transcendentals=256),
        name="turning",
    )(lengths, frequency, in_hbm(beside), after)


def spread(depth, skip, chunk):
    ranges = [(at, min(chunk, depth - at)) for at in range(skip, depth, chunk)]
    if ranges and ranges[-1][1] >= 2 * LANES:
        start, size = ranges.pop()
        ranges += [(start, size - LANES), (start + size - LANES, LANES)]
    return ranges


def project_kernel(
    bits, rows_ref, other_ref, wq_hbm, first, wk, wv, *refs
):
    pieces, (wq, rows, out, sems) = refs[:FAN], refs[FAN:]
    skip = first.shape[0]
    ranges = spread(wq_hbm.shape[0], skip, CHUNK)
    copies = [
        copies_in(wq_hbm, wq, sems.at[i], start, size, start - skip)
        for i, (start, size) in enumerate(ranges)
    ]
    for group in copies:
        for copy in group:
            copy.start()

    slots = rows.shape[0]
    half = slots // 2
    turn = bit_reverse(lax.axis_index("gx"), bits)
    gy = lax.axis_index("gy")
    for ref, side in ((rows_ref, gy), (other_ref, 1 - gy)):
        block = ref[...].astype(jnp.float32)
        for t in range(half):
            slot = bit_reverse(t, bits) ^ turn ^ side
            rows[pl.ds(slot, 1), :] = block[t : t + 1, :]
    wide = rows[...]
    squares = jnp.sum(wide * wide, axis=1, keepdims=True)
    narrow = wide.astype(jnp.bfloat16)

    total = pieces[0].shape[1]
    flat = out.reshape(slots * total, LANES)

    def put(first_block, part):
        for i in range(0, part.shape[1], LANES):
            flat[pl.ds(first_block + i // LANES, slots, stride=total), :] = part[:, i : i + LANES]

    at = wq.shape[1] // LANES
    for w in (wk, wv):
        put(at, jnp.dot(narrow, w[...], preferred_element_type=jnp.float32))
        at += w.shape[1] // LANES
    put(at, jnp.broadcast_to(squares, (slots, LANES)))
    put(at + 1, jnp.zeros((slots, (total - at - 1) * LANES), jnp.float32))

    sums = jnp.dot(narrow[:, :skip], first[...], preferred_element_type=jnp.float32)
    for (start, size), group in zip(ranges, copies):
        for copy in group:
            copy.wait()
        sums = sums + jnp.dot(
            narrow[:, start : start + size],
            wq[start - skip : start - skip + size, :],
            preferred_element_type=jnp.float32,
        )

    put(0, sums)
    for at, ref in enumerate(pieces):
        ref[...] = out[at]


def project(rows, other, w_query, first, key_weight, value_weight, slots):
    bits = slots.bit_length() - 1
    depth, query_width = w_query.shape
    kv_width = key_weight.shape[1]
    used = (query_width + 2 * kv_width) // LANES + 1
    total = -(-used // 8) * 8
    skip = first.shape[0]
    piece = jax.ShapeDtypeStruct((slots // FAN, total, LANES), jnp.float32)
    hbm = pl.BlockSpec(memory_space=pltpu.HBM)
    whole = pl.BlockSpec(memory_space=pltpu.VMEM)
    return pl.pallas_call(
        functools.partial(project_kernel, bits),
        out_shape=(piece,) * FAN,
        in_specs=[whole, whole, hbm, whole, whole, whole],
        out_specs=(whole,) * FAN,
        scratch_shapes=[
            pltpu.VMEM((max(depth - skip, 16), query_width), jnp.bfloat16),
            pltpu.VMEM((slots, depth), jnp.float32),
            pltpu.VMEM((FAN, slots // FAN, total, LANES), jnp.float32),
            pltpu.SemaphoreType.DMA((max(1, len(spread(depth, skip, CHUNK))), PIECES)),
        ],
        compiler_params=pltpu.CompilerParams(vmem_limit_bytes=46 * MIB),
        cost_estimate=pl.CostEstimate(
            flops=2 * slots * depth * (query_width + 2 * kv_width),
            bytes_accessed=2 * depth * (query_width + 2 * kv_width),
            transcendentals=0,
        ),
        name="project",
    )(rows, other, in_hbm(w_query), first, key_weight, value_weight)


def attend_kernel(
    query_heads, kv_heads, pieces, beside_ref, turn_ref, live_ref, k_ref, v_ref, *refs
):
    heads_ref = refs[pieces]
    total = refs[0][0]
    for ref in refs[1:pieces]:
        total = total + ref[0]
    at = query_heads + 2 * kv_heads
    scale = lax.rsqrt(total[at : at + 1, :] / MODEL_WIDTH + 1e-05)
    turned = total[: query_heads + kv_heads] * scale
    half = HEAD_SIZE // 2
    swapped = jnp.concatenate([turned[:, half:], turned[:, :half]], axis=1)
    turned = (turned * turn_ref[0:1, :] + swapped * turn_ref[1:2, :]).astype(jnp.bfloat16)
    fresh_values = (total[query_heads + kv_heads : at] * scale).astype(jnp.bfloat16)
    group = query_heads // kv_heads
    factor = 1.0 / math.sqrt(HEAD_SIZE)
    side = 2 if kv_heads % 2 == 0 else 1
    for first in range(0, kv_heads, side):
        members = range(first, first + side)
        queries = [turned[head * group : (head + 1) * group] for head in members]
        empty = jnp.zeros((group, HEAD_SIZE), jnp.bfloat16)
        spread_out = jnp.concatenate(
            [
                jnp.concatenate([q if i == j else empty for j in range(side)], axis=1)
                for i, q in enumerate(queries)
            ],
            axis=0,
        )
        keys = jnp.concatenate([k_ref[0, head] for head in members], axis=1)
        values = jnp.concatenate([v_ref[0, head] for head in members], axis=1)
        scores = (
            lax.dot_general(
                spread_out, keys, (((1,), (1,)), ((), ())), preferred_element_type=jnp.float32
            )
            * factor
            + live_ref[...]
        )
        own = jnp.concatenate(
            [
                jnp.sum(
                    q.astype(jnp.float32)
                    * turned[query_heads + head : query_heads + head + 1].astype(jnp.float32),
                    axis=1,
                    keepdims=True,
                )
                for q, head in zip(queries, members)
            ],
            axis=0,
        ) * factor
        top = jnp.maximum(jnp.max(scores, axis=1, keepdims=True), own)
        exponent = jnp.exp(scores - top)
        own_exp = jnp.exp(own - top)
        mixed = jnp.dot(
            exponent.astype(jnp.bfloat16), values, preferred_element_type=jnp.float32
        )
        share = 1.0 / (jnp.sum(exponent, axis=1, keepdims=True) + own_exp)
        for i, head in enumerate(members):
            part = slice(i * group, (i + 1) * group)
            block = mixed[part, i * HEAD_SIZE : (i + 1) * HEAD_SIZE]
            block = block + own_exp[part] * fresh_values[head : head + 1].astype(jnp.float32)
            block = block * share[part]
            heads_ref[0, pl.ds(head * group, group), :] = block.astype(jnp.bfloat16)


def attend(parts, turn, live, k_cache, value_cache, query_heads, beside):
    kv_heads, cache_len = k_cache.shape[1:3]
    whole = pl.BlockSpec(memory_space=pltpu.VMEM)
    return pl.pallas_call(
        functools.partial(attend_kernel, query_heads, kv_heads, len(parts)),
        out_shape=jax.ShapeDtypeStruct((1, query_heads, HEAD_SIZE), jnp.bfloat16),
        in_specs=[pl.BlockSpec(memory_space=pltpu.HBM)] + [whole] * (4 + len(parts)),
        out_specs=whole,
        compiler_params=pltpu.CompilerParams(vmem_limit_bytes=12 * MIB),
        cost_estimate=pl.CostEstimate(
            flops=4 * query_heads * cache_len * HEAD_SIZE,
            bytes_accessed=4 * kv_heads * cache_len * HEAD_SIZE,
            transcendentals=query_heads * cache_len,
        ),
        name="attend",
    )(in_hbm(beside), turn, live, k_cache, value_cache, *parts)


def output_kernel(bits, places, turned, *refs):
    pieces = len(places)
    parts = refs[:pieces]
    w_ref, mine_ref, theirs_ref, flat, sums = refs[pieces:]
    slots = sums.shape[0]
    heads = flat.shape[0] // slots
    for slot, ref in zip(places, parts):
        for i, row in enumerate(range(ref.shape[0])[::turned]):
            at = (slot + i) * heads
            flat[at : at + heads, :] = ref[row].astype(jnp.float32)
    total = None
    depth = w_ref.shape[0]
    chunk = min(2 * CHUNK, depth)
    for at in range(0, depth, chunk):
        left = jnp.concatenate(
            [
                flat[pl.ds(head, slots, stride=heads), :]
                for head in range(at // HEAD_SIZE, (at + chunk) // HEAD_SIZE)
            ],
            axis=1,
        ).astype(jnp.bfloat16)
        term = jnp.dot(left, w_ref[at : at + chunk, :], preferred_element_type=jnp.float32)
        total = term if total is None else total + term
    sums[...] = total
    half = slots // 2
    turn = bit_reverse(lax.axis_index("gx"), bits)
    gy = lax.axis_index("gy")
    for ref, side in ((mine_ref, gy), (theirs_ref, 1 - gy)):
        for t in range(half):
            slot = bit_reverse(t, bits) ^ turn ^ side
            ref[t : t + 1, :] = sums[pl.ds(slot, 1), :]


def output(parts, order, w_out, slots, turned=1):
    bits = slots.bit_length() - 1
    depth, width = w_out.shape
    heads = depth // HEAD_SIZE
    starts = [sum(x.shape[0] for x in parts[:i]) for i in range(len(parts))]
    places = tuple(starts[i] for i in order)
    parts = [parts[i] for i in order]
    whole = pl.BlockSpec(memory_space=pltpu.VMEM)
    piece = jax.ShapeDtypeStruct((slots // 2, width), jnp.float32)
    return pl.pallas_call(
        functools.partial(output_kernel, bits, places, turned),
        out_shape=(piece, piece),
        in_specs=[whole] * (len(parts) + 1),
        out_specs=(whole, whole),
        scratch_shapes=[
            pltpu.VMEM((slots * heads, HEAD_SIZE), jnp.float32),
            pltpu.VMEM((slots, width), jnp.float32),
        ],
        compiler_params=pltpu.CompilerParams(vmem_limit_bytes=12 * MIB),
        cost_estimate=pl.CostEstimate(
            flops=2 * slots * depth * width, bytes_accessed=2 * depth * width, transcendentals=0
        ),
        name="output",
    )(*parts, w_out)


def swap(block, axis, devices, mask):
    return lax.ppermute(block, axis, [(i, i ^ mask) for i in range(devices)])


def cross(block, devices, mask):
    pairs = [(i, i ^ (2 * mask + 1)) for i in range(2 * devices)]
    return lax.ppermute(block, ("gx", "gy"), pairs)


def fan(pieces, trade):
    masks = [bit_reverse(q, 2) for q in range(FAN)]
    arrived = [None] * FAN
    for q in sorted(range(1, FAN), key=lambda q: (masks[q] + 1) % FAN):
        arrived[q] = trade(pieces[q], masks[q])
    return arrived[1:]


def body(devices, activations, w_query, key_weight, value_weight, w_out, k_cache, value_cache, lengths):
    slots = devices
    query_heads = w_query.shape[1] // HEAD_SIZE
    other = swap(activations, "gy", 2, 1)
    depth = w_query.shape[0]
    first = stage_rows(w_query, min(FIRST, depth))
    pieces = project(activations, other, w_query, first, key_weight, value_weight, slots)
    half = HEAD_SIZE // 2
    frequency = jnp.power(
        jnp.float32(500000.0), -2.0 * jnp.arange(half, dtype=jnp.float32) / HEAD_SIZE
    )
    frequency = jnp.concatenate([frequency, frequency])[None, :]

    if devices == 2 * FAN:
        far = FAN
        arrived = fan(pieces, lambda block, mask: cross(block, devices, mask))
        beside = swap(pieces[0], "gy", 2, 1)
        turn, live = turning(lengths, frequency, w_out, pieces[3], k_cache.shape[2])
        leaving = [x[1:] for x in (*arrived, beside)]
        staying = [x[:1] for x in (*arrived, beside)]
        total = leaving[2] + (leaving[1] + (leaving[0] + leaving[3]))
        total, turn = lax.optimization_barrier((total, turn))
        crossed = cross(total, devices, far)
        beside = swap(staying[2] + (staying[1] + (staying[0] + staying[3])), "gy", 2, 1)
        parts = [crossed, beside]
        heads = attend(parts, turn, live, k_cache, value_cache, query_heads, w_out)
        crossed = cross(heads, devices, far)
        beside = swap(heads, "gy", 2, 1)
        held = jnp.concatenate([crossed, beside], axis=0)
        arrived = fan([held] * FAN, lambda block, mask: cross(block, devices, mask))
        parts = [heads, swap(crossed, "gy", 2, 1)] + arrived
        order, turned = (2, 4, 3, 1, 0), -1
    else:
        arrived = fan(pieces, lambda block, mask: swap(block, "gx", devices, mask))
        turn, live = turning(lengths, frequency, w_out, pieces[3], k_cache.shape[2])
        total = pieces[0] + (arrived[2] + (arrived[1] + arrived[0]))
        mask = FAN
        while total.shape[0] > 2:
            rest = total.shape[0] // 2
            total = total[:rest] + swap(total[rest:], "gx", devices, mask)
            mask *= 2
        parts = [total[:1], swap(total[1:], "gx", devices, mask)]
        heads = attend(parts, turn, live, k_cache, value_cache, query_heads, w_out)

        parts = [heads, swap(heads, "gx", devices, mask)]
        while mask > FAN:
            mask //= 2
            parts.append(swap(jnp.concatenate(parts, axis=0), "gx", devices, mask))
        held = jnp.concatenate(parts, axis=0)
        parts += fan([held] * FAN, lambda block, mask: swap(block, "gx", devices, mask))
        order, turned = range(len(parts))[::-1], 1
    mine, theirs = output(parts, order, w_out, slots, turned)
    return (mine + swap(theirs, "gy", 2, 1)).astype(jnp.bfloat16)


def solution(mesh):
    placed = (
        P(("groups", "gy"), "gx"),
        P("gx", "gy"),
        P("gx", "gy"),
        P("gx", "gy"),
        P("gy", "gx"),
        P(("groups", "gx"), "gy", None, None),
        P(("groups", "gx"), "gy", None, None),
        P(("groups", "gx")),
    )
    return jax.shard_map(
        functools.partial(body, mesh.shape["gx"]),
        mesh=mesh,
        in_specs=placed,
        out_specs=P(("groups", "gy"), "gx"),
        check_vma=False,
    )
```

```python
import functools
import math

import jax
import jax.numpy as jnp
from jax import lax
from jax.experimental import pallas as pl
from jax.experimental.pallas import tpu as pltpu
from jax.sharding import PartitionSpec as P

MODEL_WIDTH = 16384
LANES = 128
HEAD_SIZE = 128
CHUNK = 256
FIRST = 384
PIECES = 4
FAN = 4
MIB = 2**20


def bit_reverse(value, bits):
    turned = 0
    for bit in range(bits):
        turned = turned | (((value >> bit) & 1) << (bits - 1 - bit))
    return turned


def in_hbm(array):
    return pltpu.with_memory_space_constraint(array, pltpu.HBM)


def cut(start, size):
    if size % (16 * PIECES):
        return [(start, size)]
    return [(start + i * (size // PIECES), size // PIECES) for i in range(PIECES)]


def copies_in(src, dst, sems, start, size, offset):
    return [
        pltpu.make_async_copy(
            src.at[pl.ds(at, rows)], dst.at[pl.ds(at - start + offset, rows)], sems.at[i]
        )
        for i, (at, rows) in enumerate(cut(start, size))
    ]


def stage_kernel(rows, src, dst, sems):
    copies = copies_in(src, dst, sems, 0, rows, 0)
    for copy in copies:
        copy.start()
    for copy in copies:
        copy.wait()


def stage_rows(array, rows):
    vmem = pl.BlockSpec(memory_space=pltpu.VMEM)
    return pl.pallas_call(
        functools.partial(stage_kernel, rows),
        out_shape=jax.ShapeDtypeStruct((rows, array.shape[1]), array.dtype),
        in_specs=[pl.BlockSpec(memory_space=pltpu.HBM)],
        out_specs=vmem,
        scratch_shapes=[pltpu.SemaphoreType.DMA((PIECES,))],
        compiler_params=pltpu.CompilerParams(vmem_limit_bytes=16 * MIB),
        cost_estimate=pl.CostEstimate(
            flops=0, bytes_accessed=2 * rows * array.shape[1], transcendentals=0
        ),
        name="stage",
    )(in_hbm(array))


def caches_kernel(k_hbm, v_hbm, after_ref, k_ref, v_ref, sems):
    copies = [
        pltpu.make_async_copy(src, dst, sems.at[i])
        for i, (src, dst) in enumerate(((k_hbm, k_ref), (v_hbm, v_ref)))
    ]
    for copy in copies:
        copy.start()
    for copy in copies:
        copy.wait()


def stage_caches(k_cache, value_cache, after):
    vmem = pl.BlockSpec(memory_space=pltpu.VMEM)
    hbm = pl.BlockSpec(memory_space=pltpu.HBM)
    return pl.pallas_call(
        caches_kernel,
        out_shape=tuple(jax.ShapeDtypeStruct(a.shape, a.dtype) for a in (k_cache, value_cache)),
        in_specs=[hbm, hbm, vmem],
        out_specs=(vmem, vmem),
        scratch_shapes=[pltpu.SemaphoreType.DMA((2,))],
        compiler_params=pltpu.CompilerParams(vmem_limit_bytes=4 * MIB),
        cost_estimate=pl.CostEstimate(
            flops=0, bytes_accessed=4 * k_cache.size, transcendentals=0
        ),
        name="caches",
    )(in_hbm(k_cache), in_hbm(value_cache), after)


def turning_kernel(length_ref, frequency_ref, beside_ref, after_ref, turn_ref, mask_ref):
    position = length_ref[0].astype(jnp.float32)
    angle = position * frequency_ref[...]
    lane = lax.broadcasted_iota(jnp.int32, angle.shape, 1)
    sine = jnp.sin(angle)
    turn_ref[0:1, :] = jnp.cos(angle)
    turn_ref[1:2, :] = jnp.where(lane < HEAD_SIZE // 2, -sine, sine)
    slot = lax.broadcasted_iota(jnp.int32, mask_ref.shape, 1)
    mask_ref[...] = jnp.where(slot < length_ref[0], 0.0, -jnp.inf)


def turning(lengths, frequency, beside, after, cache_len):
    vmem = pl.BlockSpec(memory_space=pltpu.VMEM)
    return pl.pallas_call(
        turning_kernel,
        out_shape=(
            jax.ShapeDtypeStruct((8, HEAD_SIZE), jnp.float32),
            jax.ShapeDtypeStruct((1, cache_len), jnp.float32),
        ),
        in_specs=[
            pl.BlockSpec(memory_space=pltpu.SMEM),
            vmem,
            pl.BlockSpec(memory_space=pltpu.HBM),
            vmem,
        ],
        out_specs=(vmem, vmem),
        compiler_params=pltpu.CompilerParams(vmem_limit_bytes=4 * MIB),
        cost_estimate=pl.CostEstimate(flops=0, bytes_accessed=2 * beside.size, transcendentals=256),
        name="turning",
    )(lengths, frequency, in_hbm(beside), after)


def spread(depth, skip, chunk):
    ranges = [(at, min(chunk, depth - at)) for at in range(skip, depth, chunk)]
    if ranges and ranges[-1][1] >= 2 * LANES:
        start, size = ranges.pop()
        ranges += [(start, size - LANES), (start + size - LANES, LANES)]
    return ranges


def project_kernel(
    bits, rows_ref, other_ref, wq_hbm, first, wk, wv, *refs
):
    pieces, (wq, rows, sems) = refs[:FAN], refs[FAN:]
    skip = first.shape[0]
    ranges = spread(wq_hbm.shape[0], skip, CHUNK)
    copies = [
        copies_in(wq_hbm, wq, sems.at[i], start, size, start - skip)
        for i, (start, size) in enumerate(ranges)
    ]
    for group in copies:
        for copy in group:
            copy.start()

    slots = rows.shape[0]
    half = slots // 2
    turn = bit_reverse(lax.axis_index("gx"), bits)
    gy = lax.axis_index("gy")
    for ref, side in ((rows_ref, gy), (other_ref, 1 - gy)):
        block = ref[...].astype(jnp.float32)
        for t in range(half):
            slot = bit_reverse(t, bits) ^ turn ^ side
            rows[pl.ds(slot, 1), :] = block[t : t + 1, :]
    wide = rows[...]
    squares = jnp.sum(wide * wide, axis=1, keepdims=True)
    narrow = wide.astype(jnp.bfloat16)

    total = pieces[0].shape[1]
    each = slots // FAN
    flats = [ref.reshape(each * total, LANES) for ref in pieces]

    def put(first_block, part):
        for i in range(0, part.shape[1], LANES):
            for at, flat in enumerate(flats):
                flat[pl.ds(first_block + i // LANES, each, stride=total), :] = part[
                    at * each : (at + 1) * each, i : i + LANES
                ]

    at = wq.shape[1] // LANES
    for w in (wk, wv):
        put(at, jnp.dot(narrow, w[...], preferred_element_type=jnp.float32))
        at += w.shape[1] // LANES
    put(at, jnp.broadcast_to(squares, (slots, LANES)))
    put(at + 1, jnp.zeros((slots, (total - at - 1) * LANES), jnp.float32))

    sums = jnp.dot(narrow[:, :skip], first[...], preferred_element_type=jnp.float32)
    for (start, size), group in zip(ranges, copies):
        for copy in group:
            copy.wait()
        sums = sums + jnp.dot(
            narrow[:, start : start + size],
            wq[start - skip : start - skip + size, :],
            preferred_element_type=jnp.float32,
        )

    put(0, sums)


def project(rows, other, w_query, first, key_weight, value_weight, slots):
    bits = slots.bit_length() - 1
    depth, query_width = w_query.shape
    kv_width = key_weight.shape[1]
    used = (query_width + 2 * kv_width) // LANES + 1
    total = -(-used // 8) * 8
    skip = first.shape[0]
    piece = jax.ShapeDtypeStruct((slots // FAN, total, LANES), jnp.float32)
    hbm = pl.BlockSpec(memory_space=pltpu.HBM)
    whole = pl.BlockSpec(memory_space=pltpu.VMEM)
    return pl.pallas_call(
        functools.partial(project_kernel, bits),
        out_shape=(piece,) * FAN,
        in_specs=[whole, whole, hbm, whole, whole, whole],
        out_specs=(whole,) * FAN,
        scratch_shapes=[
            pltpu.VMEM((max(depth - skip, 16), query_width), jnp.bfloat16),
            pltpu.VMEM((slots, depth), jnp.float32),
            pltpu.SemaphoreType.DMA((max(1, len(spread(depth, skip, CHUNK))), PIECES)),
        ],
        compiler_params=pltpu.CompilerParams(vmem_limit_bytes=46 * MIB),
        cost_estimate=pl.CostEstimate(
            flops=2 * slots * depth * (query_width + 2 * kv_width),
            bytes_accessed=2 * depth * (query_width + 2 * kv_width),
            transcendentals=0,
        ),
        name="project",
    )(rows, other, in_hbm(w_query), first, key_weight, value_weight)


def attend_kernel(
    query_heads, kv_heads, pieces, beside_ref, turn_ref, live_ref, k_ref, v_ref, *refs
):
    heads_ref = refs[pieces]
    total = refs[0][0]
    for ref in refs[1:pieces]:
        total = total + ref[0]
    at = query_heads + 2 * kv_heads
    scale = lax.rsqrt(total[at : at + 1, :] / MODEL_WIDTH + 1e-05)
    turned = total[: query_heads + kv_heads] * scale
    half = HEAD_SIZE // 2
    swapped = jnp.concatenate([turned[:, half:], turned[:, :half]], axis=1)
    turned = (turned * turn_ref[0:1, :] + swapped * turn_ref[1:2, :]).astype(jnp.bfloat16)
    fresh_values = (total[query_heads + kv_heads : at] * scale).astype(jnp.bfloat16)
    group = query_heads // kv_heads
    factor = 1.0 / math.sqrt(HEAD_SIZE)
    side = 2 if kv_heads % 2 == 0 else 1
    for first in range(0, kv_heads, side):
        members = range(first, first + side)
        queries = [turned[head * group : (head + 1) * group] for head in members]
        empty = jnp.zeros((group, HEAD_SIZE), jnp.bfloat16)
        spread_out = jnp.concatenate(
            [
                jnp.concatenate([q if i == j else empty for j in range(side)], axis=1)
                for i, q in enumerate(queries)
            ],
            axis=0,
        )
        keys = jnp.concatenate([k_ref[0, head] for head in members], axis=1)
        values = jnp.concatenate([v_ref[0, head] for head in members], axis=1)
        scores = (
            lax.dot_general(
                spread_out, keys, (((1,), (1,)), ((), ())), preferred_element_type=jnp.float32
            )
            * factor
            + live_ref[...]
        )
        own = jnp.concatenate(
            [
                jnp.sum(
                    q.astype(jnp.float32)
                    * turned[query_heads + head : query_heads + head + 1].astype(jnp.float32),
                    axis=1,
                    keepdims=True,
                )
                for q, head in zip(queries, members)
            ],
            axis=0,
        ) * factor
        top = jnp.maximum(jnp.max(scores, axis=1, keepdims=True), own)
        exponent = jnp.exp(scores - top)
        own_exp = jnp.exp(own - top)
        mixed = jnp.dot(
            exponent.astype(jnp.bfloat16), values, preferred_element_type=jnp.float32
        )
        share = 1.0 / (jnp.sum(exponent, axis=1, keepdims=True) + own_exp)
        for i, head in enumerate(members):
            part = slice(i * group, (i + 1) * group)
            block = mixed[part, i * HEAD_SIZE : (i + 1) * HEAD_SIZE]
            block = block + own_exp[part] * fresh_values[head : head + 1].astype(jnp.float32)
            block = block * share[part]
            heads_ref[0, pl.ds(head * group, group), :] = block.astype(jnp.bfloat16)


def attend(parts, turn, live, k_cache, value_cache, query_heads, beside):
    kv_heads, cache_len = k_cache.shape[1:3]
    whole = pl.BlockSpec(memory_space=pltpu.VMEM)
    return pl.pallas_call(
        functools.partial(attend_kernel, query_heads, kv_heads, len(parts)),
        out_shape=jax.ShapeDtypeStruct((1, query_heads, HEAD_SIZE), jnp.bfloat16),
        in_specs=[pl.BlockSpec(memory_space=pltpu.HBM)] + [whole] * (4 + len(parts)),
        out_specs=whole,
        compiler_params=pltpu.CompilerParams(vmem_limit_bytes=12 * MIB),
        cost_estimate=pl.CostEstimate(
            flops=4 * query_heads * cache_len * HEAD_SIZE,
            bytes_accessed=4 * kv_heads * cache_len * HEAD_SIZE,
            transcendentals=query_heads * cache_len,
        ),
        name="attend",
    )(in_hbm(beside), turn, live, k_cache, value_cache, *parts)


def output_kernel(bits, places, turned, *refs):
    pieces = len(places)
    parts = refs[:pieces]
    w_ref, mine_ref, theirs_ref, flat, left, sums = refs[pieces:]
    slots = left.shape[0]
    heads = flat.shape[0] // slots
    for slot, ref in zip(places, parts):
        for i, row in enumerate(range(ref.shape[0])[::turned]):
            at = (slot + i) * heads
            flat[at : at + heads, :] = ref[row].astype(jnp.float32)
    for head in range(heads):
        left[:, head * HEAD_SIZE : (head + 1) * HEAD_SIZE] = flat[
            pl.ds(head, slots, stride=heads), :
        ].astype(jnp.bfloat16)
    total = None
    depth = w_ref.shape[0]
    chunk = min(2 * CHUNK, depth)
    for at in range(0, depth, chunk):
        part = slice(at, at + chunk)
        term = jnp.dot(left[:, part], w_ref[part, :], preferred_element_type=jnp.float32)
        total = term if total is None else total + term
    sums[...] = total
    half = slots // 2
    turn = bit_reverse(lax.axis_index("gx"), bits)
    gy = lax.axis_index("gy")
    for ref, side in ((mine_ref, gy), (theirs_ref, 1 - gy)):
        for t in range(half):
            slot = bit_reverse(t, bits) ^ turn ^ side
            ref[t : t + 1, :] = sums[pl.ds(slot, 1), :]


def output(parts, order, w_out, slots, turned=1):
    bits = slots.bit_length() - 1
    depth, width = w_out.shape
    heads = depth // HEAD_SIZE
    starts = [sum(x.shape[0] for x in parts[:i]) for i in range(len(parts))]
    places = tuple(starts[i] for i in order)
    parts = [parts[i] for i in order]
    whole = pl.BlockSpec(memory_space=pltpu.VMEM)
    piece = jax.ShapeDtypeStruct((slots // 2, width), jnp.float32)
    return pl.pallas_call(
        functools.partial(output_kernel, bits, places, turned),
        out_shape=(piece, piece),
        in_specs=[whole] * (len(parts) + 1),
        out_specs=(whole, whole),
        scratch_shapes=[
            pltpu.VMEM((slots * heads, HEAD_SIZE), jnp.float32),
            pltpu.VMEM((slots, depth), jnp.bfloat16),
            pltpu.VMEM((slots, width), jnp.float32),
        ],
        compiler_params=pltpu.CompilerParams(vmem_limit_bytes=12 * MIB),
        cost_estimate=pl.CostEstimate(
            flops=2 * slots * depth * width, bytes_accessed=2 * depth * width, transcendentals=0
        ),
        name="output",
    )(*parts, w_out)


def swap(block, axis, devices, mask):
    return lax.ppermute(block, axis, [(i, i ^ mask) for i in range(devices)])


def cross(block, devices, mask):
    pairs = [(i, i ^ (2 * mask + 1)) for i in range(2 * devices)]
    return lax.ppermute(block, ("gx", "gy"), pairs)


def fan(pieces, trade):
    masks = [bit_reverse(q, 2) for q in range(FAN)]
    arrived = [None] * FAN
    for q in sorted(range(1, FAN), key=lambda q: (masks[q] + 1) % FAN):
        arrived[q] = trade(pieces[q], masks[q])
    return arrived[1:]


def body(devices, activations, w_query, key_weight, value_weight, w_out, k_cache, value_cache, lengths):
    slots = devices
    query_heads = w_query.shape[1] // HEAD_SIZE
    other = swap(activations, "gy", 2, 1)
    depth = w_query.shape[0]
    first = stage_rows(w_query, min(FIRST, depth))
    pieces = project(activations, other, w_query, first, key_weight, value_weight, slots)
    half = HEAD_SIZE // 2
    frequency = jnp.power(
        jnp.float32(500000.0), -2.0 * jnp.arange(half, dtype=jnp.float32) / HEAD_SIZE
    )
    frequency = jnp.concatenate([frequency, frequency])[None, :]

    if devices == 2 * FAN:
        far = FAN
        arrived = fan(pieces, lambda block, mask: cross(block, devices, mask))
        beside = swap(pieces[0], "gy", 2, 1)
        k_cache, value_cache = stage_caches(k_cache, value_cache, pieces[3])
        turn, live = turning(lengths, frequency, w_out, k_cache, k_cache.shape[2])
        leaving = [x[1:] for x in (*arrived, beside)]
        staying = [x[:1] for x in (*arrived, beside)]
        total = leaving[2] + (leaving[1] + (leaving[0] + leaving[3]))
        total, turn = lax.optimization_barrier((total, turn))
        crossed = cross(total, devices, far)
        beside = swap(staying[2] + (staying[1] + (staying[0] + staying[3])), "gy", 2, 1)
        parts = [crossed, beside]
        heads = attend(parts, turn, live, k_cache, value_cache, query_heads, w_out)
        crossed = cross(heads, devices, far)
        beside = swap(heads, "gy", 2, 1)
        held = jnp.concatenate([crossed, beside], axis=0)
        arrived = fan([held] * FAN, lambda block, mask: cross(block, devices, mask))
        parts = [heads, swap(crossed, "gy", 2, 1)] + arrived
        order, turned = (2, 4, 3, 1, 0), -1
    else:
        arrived = fan(pieces, lambda block, mask: swap(block, "gx", devices, mask))
        k_cache, value_cache = stage_caches(k_cache, value_cache, pieces[3])
        turn, live = turning(lengths, frequency, w_out, k_cache, k_cache.shape[2])
        total = pieces[0] + (arrived[2] + (arrived[1] + arrived[0]))
        mask = FAN
        while total.shape[0] > 2:
            rest = total.shape[0] // 2
            total = total[:rest] + swap(total[rest:], "gx", devices, mask)
            mask *= 2
        parts = [total[:1], swap(total[1:], "gx", devices, mask)]
        heads = attend(parts, turn, live, k_cache, value_cache, query_heads, w_out)

        parts = [heads, swap(heads, "gx", devices, mask)]
        while mask > FAN:
            mask //= 2
            parts.append(swap(jnp.concatenate(parts, axis=0), "gx", devices, mask))
        held = jnp.concatenate(parts, axis=0)
        parts += fan([held] * FAN, lambda block, mask: swap(block, "gx", devices, mask))
        order, turned = range(len(parts))[::-1], 1
    mine, theirs = output(parts, order, w_out, slots, turned)
    return (mine + swap(theirs, "gy", 2, 1)).astype(jnp.bfloat16)


def solution(mesh):
    placed = (
        P(("groups", "gy"), "gx"),
        P("gx", "gy"),
        P("gx", "gy"),
        P("gx", "gy"),
        P("gy", "gx"),
        P(("groups", "gx"), "gy", None, None),
        P(("groups", "gx"), "gy", None, None),
        P(("groups", "gx")),
    )
    return jax.shard_map(
        functools.partial(body, mesh.shape["gx"]),
        mesh=mesh,
        in_specs=placed,
        out_specs=P(("groups", "gy"), "gx"),
        check_vma=False,
    )
```

```python
import functools
import math

import jax
import jax.numpy as jnp
from jax import lax
from jax.experimental import pallas as pl
from jax.experimental.pallas import tpu as pltpu
from jax.sharding import PartitionSpec as P

MODEL_WIDTH = 16384
LANES = 128
HEAD_SIZE = 128
CHUNK = 256
FIRST = 384
PIECES = 4
FAN = 4
MIB = 2**20


def bit_reverse(value, bits):
    turned = 0
    for bit in range(bits):
        turned = turned | (((value >> bit) & 1) << (bits - 1 - bit))
    return turned


def in_hbm(array):
    return pltpu.with_memory_space_constraint(array, pltpu.HBM)


def cut(start, size):
    if size % (16 * PIECES):
        return [(start, size)]
    return [(start + i * (size // PIECES), size // PIECES) for i in range(PIECES)]


def copies_in(src, dst, sems, start, size, offset):
    return [
        pltpu.make_async_copy(
            src.at[pl.ds(at, rows)], dst.at[pl.ds(at - start + offset, rows)], sems.at[i]
        )
        for i, (at, rows) in enumerate(cut(start, size))
    ]


def stage_kernel(rows, src, dst, sems):
    copies = copies_in(src, dst, sems, 0, rows, 0)
    for copy in copies:
        copy.start()
    for copy in copies:
        copy.wait()


def stage_rows(array, rows):
    vmem = pl.BlockSpec(memory_space=pltpu.VMEM)
    return pl.pallas_call(
        functools.partial(stage_kernel, rows),
        out_shape=jax.ShapeDtypeStruct((rows, array.shape[1]), array.dtype),
        in_specs=[pl.BlockSpec(memory_space=pltpu.HBM)],
        out_specs=vmem,
        scratch_shapes=[pltpu.SemaphoreType.DMA((PIECES,))],
        compiler_params=pltpu.CompilerParams(vmem_limit_bytes=16 * MIB),
        cost_estimate=pl.CostEstimate(
            flops=0, bytes_accessed=2 * rows * array.shape[1], transcendentals=0
        ),
        name="stage",
    )(in_hbm(array))


def turning_kernel(length_ref, frequency_ref, beside_ref, after_ref, turn_ref, mask_ref):
    position = length_ref[0].astype(jnp.float32)
    angle = position * frequency_ref[...]
    lane = lax.broadcasted_iota(jnp.int32, angle.shape, 1)
    sine = jnp.sin(angle)
    turn_ref[0:1, :] = jnp.cos(angle)
    turn_ref[1:2, :] = jnp.where(lane < HEAD_SIZE // 2, -sine, sine)
    slot = lax.broadcasted_iota(jnp.int32, mask_ref.shape, 1)
    mask_ref[...] = jnp.where(slot < length_ref[0], 0.0, -jnp.inf)


def turning(lengths, frequency, beside, after, cache_len):
    vmem = pl.BlockSpec(memory_space=pltpu.VMEM)
    return pl.pallas_call(
        turning_kernel,
        out_shape=(
            jax.ShapeDtypeStruct((8, HEAD_SIZE), jnp.float32),
            jax.ShapeDtypeStruct((1, cache_len), jnp.float32),
        ),
        in_specs=[
            pl.BlockSpec(memory_space=pltpu.SMEM),
            vmem,
            pl.BlockSpec(memory_space=pltpu.HBM),
            vmem,
        ],
        out_specs=(vmem, vmem),
        compiler_params=pltpu.CompilerParams(vmem_limit_bytes=2 * MIB),
        cost_estimate=pl.CostEstimate(flops=0, bytes_accessed=2 * beside.size, transcendentals=256),
        name="turning",
    )(lengths, frequency, in_hbm(beside), after)


def spread(depth, skip, chunk):
    ranges = [(at, min(chunk, depth - at)) for at in range(skip, depth, chunk)]
    if ranges and ranges[-1][1] >= 2 * LANES:
        start, size = ranges.pop()
        ranges += [(start, size - LANES), (start + size - LANES, LANES)]
    return ranges


def project_kernel(
    bits, rows_ref, other_ref, wq_hbm, first, wk, wv, *refs
):
    pieces, (wq, rows, sems) = refs[:FAN], refs[FAN:]
    skip = first.shape[0]
    ranges = spread(wq_hbm.shape[0], skip, CHUNK)
    copies = [
        copies_in(wq_hbm, wq, sems.at[i], start, size, start - skip)
        for i, (start, size) in enumerate(ranges)
    ]
    for group in copies:
        for copy in group:
            copy.start()

    slots = rows.shape[0]
    half = slots // 2
    turn = bit_reverse(lax.axis_index("gx"), bits)
    gy = lax.axis_index("gy")
    for ref, side in ((rows_ref, gy), (other_ref, 1 - gy)):
        block = ref[...].astype(jnp.float32)
        for t in range(half):
            slot = bit_reverse(t, bits) ^ turn ^ side
            rows[pl.ds(slot, 1), :] = block[t : t + 1, :]
    wide = rows[...]
    squares = jnp.sum(wide * wide, axis=1, keepdims=True)
    narrow = wide.astype(jnp.bfloat16)

    total = pieces[0].shape[1]
    each = slots // FAN
    flats = [ref.reshape(each * total, LANES) for ref in pieces]

    def put(first_block, part):
        for i in range(0, part.shape[1], LANES):
            for at, flat in enumerate(flats):
                flat[pl.ds(first_block + i // LANES, each, stride=total), :] = part[
                    at * each : (at + 1) * each, i : i + LANES
                ]

    at = wq.shape[1] // LANES
    for w in (wk, wv):
        put(at, jnp.dot(narrow, w[...], preferred_element_type=jnp.float32))
        at += w.shape[1] // LANES
    put(at, jnp.broadcast_to(squares, (slots, LANES)))
    put(at + 1, jnp.zeros((slots, (total - at - 1) * LANES), jnp.float32))

    sums = jnp.dot(narrow[:, :skip], first[...], preferred_element_type=jnp.float32)
    for (start, size), group in zip(ranges, copies):
        for copy in group:
            copy.wait()
        sums = sums + jnp.dot(
            narrow[:, start : start + size],
            wq[start - skip : start - skip + size, :],
            preferred_element_type=jnp.float32,
        )

    put(0, sums)


def project(rows, other, w_query, first, key_weight, value_weight, slots):
    bits = slots.bit_length() - 1
    depth, query_width = w_query.shape
    kv_width = key_weight.shape[1]
    used = (query_width + 2 * kv_width) // LANES + 1
    total = -(-used // 8) * 8
    skip = first.shape[0]
    piece = jax.ShapeDtypeStruct((slots // FAN, total, LANES), jnp.float32)
    hbm = pl.BlockSpec(memory_space=pltpu.HBM)
    whole = pl.BlockSpec(memory_space=pltpu.VMEM)
    return pl.pallas_call(
        functools.partial(project_kernel, bits),
        out_shape=(piece,) * FAN,
        in_specs=[whole, whole, hbm, whole, whole, whole],
        out_specs=(whole,) * FAN,
        scratch_shapes=[
            pltpu.VMEM((max(depth - skip, 16), query_width), jnp.bfloat16),
            pltpu.VMEM((slots, depth), jnp.float32),
            pltpu.SemaphoreType.DMA((max(1, len(spread(depth, skip, CHUNK))), PIECES)),
        ],
        compiler_params=pltpu.CompilerParams(vmem_limit_bytes=46 * MIB),
        cost_estimate=pl.CostEstimate(
            flops=2 * slots * depth * (query_width + 2 * kv_width),
            bytes_accessed=2 * depth * (query_width + 2 * kv_width),
            transcendentals=0,
        ),
        name="project",
    )(rows, other, in_hbm(w_query), first, key_weight, value_weight)


def attend_kernel(
    query_heads, kv_heads, pieces, beside_ref, turn_ref, live_ref, k_ref, v_ref, *refs
):
    heads_ref = refs[pieces]
    total = refs[0][0]
    for ref in refs[1:pieces]:
        total = total + ref[0]
    at = query_heads + 2 * kv_heads
    scale = lax.rsqrt(total[at : at + 1, :] / MODEL_WIDTH + 1e-05)
    turned = total[: query_heads + kv_heads] * scale
    half = HEAD_SIZE // 2
    swapped = jnp.concatenate([turned[:, half:], turned[:, :half]], axis=1)
    turned = (turned * turn_ref[0:1, :] + swapped * turn_ref[1:2, :]).astype(jnp.bfloat16)
    fresh_values = (total[query_heads + kv_heads : at] * scale).astype(jnp.bfloat16)
    group = query_heads // kv_heads
    factor = 1.0 / math.sqrt(HEAD_SIZE)
    side = 2 if kv_heads % 2 == 0 else 1
    for first in range(0, kv_heads, side):
        members = range(first, first + side)
        queries = [turned[head * group : (head + 1) * group] for head in members]
        empty = jnp.zeros((group, HEAD_SIZE), jnp.bfloat16)
        spread_out = jnp.concatenate(
            [
                jnp.concatenate([q if i == j else empty for j in range(side)], axis=1)
                for i, q in enumerate(queries)
            ],
            axis=0,
        )
        keys = jnp.concatenate([k_ref[0, head] for head in members], axis=1)
        values = jnp.concatenate([v_ref[0, head] for head in members], axis=1)
        scores = (
            lax.dot_general(
                spread_out, keys, (((1,), (1,)), ((), ())), preferred_element_type=jnp.float32
            )
            * factor
            + live_ref[...]
        )
        own = jnp.concatenate(
            [
                jnp.sum(
                    q.astype(jnp.float32)
                    * turned[query_heads + head : query_heads + head + 1].astype(jnp.float32),
                    axis=1,
                    keepdims=True,
                )
                for q, head in zip(queries, members)
            ],
            axis=0,
        ) * factor
        top = jnp.maximum(jnp.max(scores, axis=1, keepdims=True), own)
        exponent = jnp.exp(scores - top)
        own_exp = jnp.exp(own - top)
        mixed = jnp.dot(
            exponent.astype(jnp.bfloat16), values, preferred_element_type=jnp.float32
        )
        share = 1.0 / (jnp.sum(exponent, axis=1, keepdims=True) + own_exp)
        for i, head in enumerate(members):
            part = slice(i * group, (i + 1) * group)
            block = mixed[part, i * HEAD_SIZE : (i + 1) * HEAD_SIZE]
            block = block + own_exp[part] * fresh_values[head : head + 1].astype(jnp.float32)
            block = block * share[part]
            heads_ref[0, pl.ds(head * group, group), :] = block.astype(jnp.bfloat16)


def attend(parts, turn, live, k_cache, value_cache, query_heads, beside):
    kv_heads, cache_len = k_cache.shape[1:3]
    whole = pl.BlockSpec(memory_space=pltpu.VMEM)
    return pl.pallas_call(
        functools.partial(attend_kernel, query_heads, kv_heads, len(parts)),
        out_shape=jax.ShapeDtypeStruct((1, query_heads, HEAD_SIZE), jnp.bfloat16),
        in_specs=[pl.BlockSpec(memory_space=pltpu.HBM)] + [whole] * (4 + len(parts)),
        out_specs=whole,
        compiler_params=pltpu.CompilerParams(vmem_limit_bytes=12 * MIB),
        cost_estimate=pl.CostEstimate(
            flops=4 * query_heads * cache_len * HEAD_SIZE,
            bytes_accessed=4 * kv_heads * cache_len * HEAD_SIZE,
            transcendentals=query_heads * cache_len,
        ),
        name="attend",
    )(in_hbm(beside), turn, live, k_cache, value_cache, *parts)


def output_kernel(bits, places, turned, *refs):
    pieces = len(places)
    parts = refs[:pieces]
    w_ref, mine_ref, theirs_ref, flat, left = refs[pieces:]
    slots = left.shape[0]
    heads = flat.shape[0] // slots
    here = lax.axis_index("gx")
    for slot, ref in zip(places, parts):
        for i, row in enumerate(range(ref.shape[0])[::turned]):
            at = pl.multiple_of((here ^ bit_reverse(slot + i, bits)) * heads, heads)
            flat[pl.ds(at, heads), :] = ref[row].astype(jnp.float32)
    for head in range(heads):
        left[:, head * HEAD_SIZE : (head + 1) * HEAD_SIZE] = flat[
            pl.ds(head, slots, stride=heads), :
        ].astype(jnp.bfloat16)
    total = None
    depth = w_ref.shape[0]
    chunk = min(2 * CHUNK, depth)
    for at in range(0, depth, chunk):
        part = slice(at, at + chunk)
        term = jnp.dot(left[:, part], w_ref[part, :], preferred_element_type=jnp.float32)
        total = term if total is None else total + term
    half = slots // 2
    gy = lax.axis_index("gy")
    lower, upper = total[:half], total[half:]
    mine_ref[...] = jnp.where(gy == 0, lower, upper)
    theirs_ref[...] = jnp.where(gy == 0, upper, lower)


def output(parts, order, w_out, slots, turned=1):
    bits = slots.bit_length() - 1
    depth, width = w_out.shape
    heads = depth // HEAD_SIZE
    starts = [sum(x.shape[0] for x in parts[:i]) for i in range(len(parts))]
    places = tuple(starts[i] for i in order)
    parts = [parts[i] for i in order]
    whole = pl.BlockSpec(memory_space=pltpu.VMEM)
    piece = jax.ShapeDtypeStruct((slots // 2, width), jnp.float32)
    return pl.pallas_call(
        functools.partial(output_kernel, bits, places, turned),
        out_shape=(piece, piece),
        in_specs=[whole] * (len(parts) + 1),
        out_specs=(whole, whole),
        scratch_shapes=[
            pltpu.VMEM((slots * heads, HEAD_SIZE), jnp.float32),
            pltpu.VMEM((slots, depth), jnp.bfloat16),
        ],
        compiler_params=pltpu.CompilerParams(vmem_limit_bytes=12 * MIB),
        cost_estimate=pl.CostEstimate(
            flops=2 * slots * depth * width, bytes_accessed=2 * depth * width, transcendentals=0
        ),
        name="output",
    )(*parts, w_out)


def swap(block, axis, devices, mask):
    return lax.ppermute(block, axis, [(i, i ^ mask) for i in range(devices)])


def cross(block, devices, mask):
    pairs = [(i, i ^ (2 * mask + 1)) for i in range(2 * devices)]
    return lax.ppermute(block, ("gx", "gy"), pairs)


def fan(pieces, trade):
    masks = [bit_reverse(q, 2) for q in range(FAN)]
    arrived = [None] * FAN
    for q in sorted(range(1, FAN), key=lambda q: (masks[q] + 1) % FAN):
        arrived[q] = trade(pieces[q], masks[q])
    return arrived[1:]


def body(devices, activations, w_query, key_weight, value_weight, w_out, k_cache, value_cache, lengths):
    slots = devices
    query_heads = w_query.shape[1] // HEAD_SIZE
    other = swap(activations, "gy", 2, 1)
    depth = w_query.shape[0]
    first = stage_rows(w_query, min(FIRST, depth))
    pieces = project(activations, other, w_query, first, key_weight, value_weight, slots)
    half = HEAD_SIZE // 2
    frequency = jnp.power(
        jnp.float32(500000.0), -2.0 * jnp.arange(half, dtype=jnp.float32) / HEAD_SIZE
    )
    frequency = jnp.concatenate([frequency, frequency])[None, :]

    if devices == 2 * FAN:
        far = FAN
        arrived = fan(pieces, lambda block, mask: cross(block, devices, mask))
        beside = swap(pieces[0], "gy", 2, 1)
        turn, live = turning(lengths, frequency, w_out, pieces[3], k_cache.shape[2])
        leaving = [x[1:] for x in (*arrived, beside)]
        staying = [x[:1] for x in (*arrived, beside)]
        total = leaving[2] + (leaving[1] + (leaving[0] + leaving[3]))
        total, turn = lax.optimization_barrier((total, turn))
        crossed = cross(total, devices, far)
        beside = swap(staying[2] + (staying[1] + (staying[0] + staying[3])), "gy", 2, 1)
        parts = [crossed, beside]
        heads = attend(parts, turn, live, k_cache, value_cache, query_heads, w_out)
        crossed = cross(heads, devices, far)
        beside = swap(heads, "gy", 2, 1)
        held = jnp.concatenate([crossed, beside], axis=0)
        arrived = fan([held] * FAN, lambda block, mask: cross(block, devices, mask))
        parts = [heads, swap(crossed, "gy", 2, 1)] + arrived
        order, turned = (2, 4, 3, 1, 0), -1
    else:
        arrived = fan(pieces, lambda block, mask: swap(block, "gx", devices, mask))
        turn, live = turning(lengths, frequency, w_out, pieces[3], k_cache.shape[2])
        total = pieces[0] + (arrived[2] + (arrived[1] + arrived[0]))
        mask = FAN
        while total.shape[0] > 2:
            rest = total.shape[0] // 2
            total = total[:rest] + swap(total[rest:], "gx", devices, mask)
            mask *= 2
        parts = [total[:1], swap(total[1:], "gx", devices, mask)]
        heads = attend(parts, turn, live, k_cache, value_cache, query_heads, w_out)

        parts = [heads, swap(heads, "gx", devices, mask)]
        while mask > FAN:
            mask //= 2
            parts.append(swap(jnp.concatenate(parts, axis=0), "gx", devices, mask))
        held = jnp.concatenate(parts, axis=0)
        parts += fan([held] * FAN, lambda block, mask: swap(block, "gx", devices, mask))
        order, turned = range(len(parts))[::-1], 1
    mine, theirs = output(parts, order, w_out, slots, turned)
    return (mine + swap(theirs, "gy", 2, 1)).astype(jnp.bfloat16)


def solution(mesh):
    placed = (
        P(("groups", "gy"), "gx"),
        P("gx", "gy"),
        P("gx", "gy"),
        P("gx", "gy"),
        P("gy", "gx"),
        P(("groups", "gx"), "gy", None, None),
        P(("groups", "gx"), "gy", None, None),
        P(("groups", "gx")),
    )
    return jax.shard_map(
        functools.partial(body, mesh.shape["gx"]),
        mesh=mesh,
        in_specs=placed,
        out_specs=P(("groups", "gy"), "gx"),
        check_vma=False,
    )
```

```python
import functools
import math

import jax
import jax.numpy as jnp
from jax import lax
from jax.experimental import pallas as pl
from jax.experimental.pallas import tpu as pltpu
from jax.sharding import PartitionSpec as P

MODEL_WIDTH = 16384
LANES = 128
HEAD_SIZE = 128
CHUNK = 256
FIRST = 384
PIECES = 1
FAN = 4
MIB = 2**20


def bit_reverse(value, bits):
    turned = 0
    for bit in range(bits):
        turned = turned | (((value >> bit) & 1) << (bits - 1 - bit))
    return turned


def in_hbm(array):
    return pltpu.with_memory_space_constraint(array, pltpu.HBM)


def cut(start, size):
    if size % (16 * PIECES):
        return [(start, size)]
    return [(start + i * (size // PIECES), size // PIECES) for i in range(PIECES)]


def copies_in(src, dst, sems, start, size, offset):
    return [
        pltpu.make_async_copy(
            src.at[pl.ds(at, rows)], dst.at[pl.ds(at - start + offset, rows)], sems.at[i]
        )
        for i, (at, rows) in enumerate(cut(start, size))
    ]


def stage_kernel(rows, src, dst, sems):
    copies = copies_in(src, dst, sems, 0, rows, 0)
    for copy in copies:
        copy.start()
    for copy in copies:
        copy.wait()


def stage_rows(array, rows):
    vmem = pl.BlockSpec(memory_space=pltpu.VMEM)
    return pl.pallas_call(
        functools.partial(stage_kernel, rows),
        out_shape=jax.ShapeDtypeStruct((rows, array.shape[1]), array.dtype),
        in_specs=[pl.BlockSpec(memory_space=pltpu.HBM)],
        out_specs=vmem,
        scratch_shapes=[pltpu.SemaphoreType.DMA((PIECES,))],
        compiler_params=pltpu.CompilerParams(vmem_limit_bytes=16 * MIB),
        cost_estimate=pl.CostEstimate(
            flops=0, bytes_accessed=2 * rows * array.shape[1], transcendentals=0
        ),
        name="stage",
    )(in_hbm(array))


def turning_kernel(length_ref, frequency_ref, beside_ref, after_ref, turn_ref, mask_ref):
    position = length_ref[0].astype(jnp.float32)
    angle = position * frequency_ref[...]
    lane = lax.broadcasted_iota(jnp.int32, angle.shape, 1)
    sine = jnp.sin(angle)
    turn_ref[0:1, :] = jnp.cos(angle)
    turn_ref[1:2, :] = jnp.where(lane < HEAD_SIZE // 2, -sine, sine)
    slot = lax.broadcasted_iota(jnp.int32, mask_ref.shape, 1)
    mask_ref[...] = jnp.where(slot < length_ref[0], 0.0, -jnp.inf)


def turning(lengths, frequency, beside, after, cache_len):
    vmem = pl.BlockSpec(memory_space=pltpu.VMEM)
    return pl.pallas_call(
        turning_kernel,
        out_shape=(
            jax.ShapeDtypeStruct((8, HEAD_SIZE), jnp.float32),
            jax.ShapeDtypeStruct((1, cache_len), jnp.float32),
        ),
        in_specs=[
            pl.BlockSpec(memory_space=pltpu.SMEM),
            vmem,
            pl.BlockSpec(memory_space=pltpu.HBM),
            vmem,
        ],
        out_specs=(vmem, vmem),
        compiler_params=pltpu.CompilerParams(vmem_limit_bytes=2 * MIB),
        cost_estimate=pl.CostEstimate(flops=0, bytes_accessed=2 * beside.size, transcendentals=256),
        name="turning",
    )(lengths, frequency, in_hbm(beside), after)


def spread(depth, skip, chunk):
    ranges = [(at, min(chunk, depth - at)) for at in range(skip, depth, chunk)]
    if ranges and ranges[-1][1] >= 2 * LANES:
        start, size = ranges.pop()
        ranges += [(start, size - LANES), (start + size - LANES, LANES)]
    return ranges


def project_kernel(
    bits, rows_ref, other_ref, wq_hbm, first, wk, wv, *refs
):
    pieces, (wq, rows, sems) = refs[:FAN], refs[FAN:]
    skip = first.shape[0]
    ranges = spread(wq_hbm.shape[0], skip, CHUNK)
    copies = [
        copies_in(wq_hbm, wq, sems.at[i], start, size, start - skip)
        for i, (start, size) in enumerate(ranges)
    ]
    for group in copies:
        for copy in group:
            copy.start()

    slots = rows.shape[0]
    half = slots // 2
    turn = bit_reverse(lax.axis_index("gx"), bits)
    gy = lax.axis_index("gy")
    for ref, side in ((rows_ref, gy), (other_ref, 1 - gy)):
        block = ref[...].astype(jnp.float32)
        for t in range(half):
            slot = bit_reverse(t, bits) ^ turn ^ side
            rows[pl.ds(slot, 1), :] = block[t : t + 1, :]
    wide = rows[...]
    squares = jnp.sum(wide * wide, axis=1, keepdims=True)
    narrow = wide.astype(jnp.bfloat16)

    total = pieces[0].shape[1]
    each = slots // FAN
    flats = [ref.reshape(each * total, LANES) for ref in pieces]

    def put(first_block, part):
        for i in range(0, part.shape[1], LANES):
            for at, flat in enumerate(flats):
                flat[pl.ds(first_block + i // LANES, each, stride=total), :] = part[
                    at * each : (at + 1) * each, i : i + LANES
                ]

    at = wq.shape[1] // LANES
    for w in (wk, wv):
        put(at, jnp.dot(narrow, w[...], preferred_element_type=jnp.float32))
        at += w.shape[1] // LANES
    put(at, jnp.broadcast_to(squares, (slots, LANES)))
    put(at + 1, jnp.zeros((slots, (total - at - 1) * LANES), jnp.float32))

    sums = jnp.dot(narrow[:, :skip], first[...], preferred_element_type=jnp.float32)
    for (start, size), group in zip(ranges, copies):
        for copy in group:
            copy.wait()
        sums = sums + jnp.dot(
            narrow[:, start : start + size],
            wq[start - skip : start - skip + size, :],
            preferred_element_type=jnp.float32,
        )

    put(0, sums)


def project(rows, other, w_query, first, key_weight, value_weight, slots):
    bits = slots.bit_length() - 1
    depth, query_width = w_query.shape
    kv_width = key_weight.shape[1]
    used = (query_width + 2 * kv_width) // LANES + 1
    total = -(-used // 8) * 8
    skip = first.shape[0]
    piece = jax.ShapeDtypeStruct((slots // FAN, total, LANES), jnp.float32)
    hbm = pl.BlockSpec(memory_space=pltpu.HBM)
    whole = pl.BlockSpec(memory_space=pltpu.VMEM)
    return pl.pallas_call(
        functools.partial(project_kernel, bits),
        out_shape=(piece,) * FAN,
        in_specs=[whole, whole, hbm, whole, whole, whole],
        out_specs=(whole,) * FAN,
        scratch_shapes=[
            pltpu.VMEM((max(depth - skip, 16), query_width), jnp.bfloat16),
            pltpu.VMEM((slots, depth), jnp.float32),
            pltpu.SemaphoreType.DMA((max(1, len(spread(depth, skip, CHUNK))), PIECES)),
        ],
        compiler_params=pltpu.CompilerParams(vmem_limit_bytes=46 * MIB),
        cost_estimate=pl.CostEstimate(
            flops=2 * slots * depth * (query_width + 2 * kv_width),
            bytes_accessed=2 * depth * (query_width + 2 * kv_width),
            transcendentals=0,
        ),
        name="project",
    )(rows, other, in_hbm(w_query), first, key_weight, value_weight)


def attend_kernel(
    query_heads, kv_heads, pieces, beside_ref, turn_ref, live_ref, k_ref, v_ref, *refs
):
    heads_ref = refs[pieces]
    total = refs[0][0]
    for ref in refs[1:pieces]:
        total = total + ref[0]
    at = query_heads + 2 * kv_heads
    scale = lax.rsqrt(total[at : at + 1, :] / MODEL_WIDTH + 1e-05)
    turned = total[: query_heads + kv_heads] * scale
    half = HEAD_SIZE // 2
    swapped = jnp.concatenate([turned[:, half:], turned[:, :half]], axis=1)
    turned = (turned * turn_ref[0:1, :] + swapped * turn_ref[1:2, :]).astype(jnp.bfloat16)
    fresh_values = (total[query_heads + kv_heads : at] * scale).astype(jnp.bfloat16)
    group = query_heads // kv_heads
    factor = 1.0 / math.sqrt(HEAD_SIZE)
    side = 2 if kv_heads % 2 == 0 else 1
    for first in range(0, kv_heads, side):
        members = range(first, first + side)
        queries = [turned[head * group : (head + 1) * group] for head in members]
        empty = jnp.zeros((group, HEAD_SIZE), jnp.bfloat16)
        spread_out = jnp.concatenate(
            [
                jnp.concatenate([q if i == j else empty for j in range(side)], axis=1)
                for i, q in enumerate(queries)
            ],
            axis=0,
        )
        keys = jnp.concatenate([k_ref[0, head] for head in members], axis=1)
        values = jnp.concatenate([v_ref[0, head] for head in members], axis=1)
        scores = (
            lax.dot_general(
                spread_out, keys, (((1,), (1,)), ((), ())), preferred_element_type=jnp.float32
            )
            * factor
            + live_ref[...]
        )
        own = jnp.concatenate(
            [
                jnp.sum(
                    q.astype(jnp.float32)
                    * turned[query_heads + head : query_heads + head + 1].astype(jnp.float32),
                    axis=1,
                    keepdims=True,
                )
                for q, head in zip(queries, members)
            ],
            axis=0,
        ) * factor
        top = jnp.maximum(jnp.max(scores, axis=1, keepdims=True), own)
        exponent = jnp.exp(scores - top)
        own_exp = jnp.exp(own - top)
        mixed = jnp.dot(
            exponent.astype(jnp.bfloat16), values, preferred_element_type=jnp.float32
        )
        share = 1.0 / (jnp.sum(exponent, axis=1, keepdims=True) + own_exp)
        for i, head in enumerate(members):
            part = slice(i * group, (i + 1) * group)
            block = mixed[part, i * HEAD_SIZE : (i + 1) * HEAD_SIZE]
            block = block + own_exp[part] * fresh_values[head : head + 1].astype(jnp.float32)
            block = block * share[part]
            heads_ref[0, pl.ds(head * group, group), :] = block.astype(jnp.bfloat16)


def attend(parts, turn, live, k_cache, value_cache, query_heads, beside):
    kv_heads, cache_len = k_cache.shape[1:3]
    whole = pl.BlockSpec(memory_space=pltpu.VMEM)
    return pl.pallas_call(
        functools.partial(attend_kernel, query_heads, kv_heads, len(parts)),
        out_shape=jax.ShapeDtypeStruct((1, query_heads, HEAD_SIZE), jnp.bfloat16),
        in_specs=[pl.BlockSpec(memory_space=pltpu.HBM)] + [whole] * (4 + len(parts)),
        out_specs=whole,
        compiler_params=pltpu.CompilerParams(vmem_limit_bytes=12 * MIB),
        cost_estimate=pl.CostEstimate(
            flops=4 * query_heads * cache_len * HEAD_SIZE,
            bytes_accessed=4 * kv_heads * cache_len * HEAD_SIZE,
            transcendentals=query_heads * cache_len,
        ),
        name="attend",
    )(in_hbm(beside), turn, live, k_cache, value_cache, *parts)


def output_kernel(bits, places, turned, *refs):
    pieces = len(places)
    parts = refs[:pieces]
    w_ref, mine_ref, theirs_ref, flat, left = refs[pieces:]
    slots = left.shape[0]
    heads = flat.shape[0] // slots
    here = lax.axis_index("gx")
    for slot, ref in zip(places, parts):
        for i, row in enumerate(range(ref.shape[0])[::turned]):
            at = pl.multiple_of((here ^ bit_reverse(slot + i, bits)) * heads, heads)
            flat[pl.ds(at, heads), :] = ref[row].astype(jnp.float32)
    for head in range(heads):
        left[:, head * HEAD_SIZE : (head + 1) * HEAD_SIZE] = flat[
            pl.ds(head, slots, stride=heads), :
        ].astype(jnp.bfloat16)
    total = None
    depth = w_ref.shape[0]
    chunk = min(2 * CHUNK, depth)
    for at in range(0, depth, chunk):
        part = slice(at, at + chunk)
        term = jnp.dot(left[:, part], w_ref[part, :], preferred_element_type=jnp.float32)
        total = term if total is None else total + term
    half = slots // 2
    gy = lax.axis_index("gy")
    lower, upper = total[:half], total[half:]
    mine_ref[...] = jnp.where(gy == 0, lower, upper)
    theirs_ref[...] = jnp.where(gy == 0, upper, lower)


def output(parts, order, w_out, slots, turned=1):
    bits = slots.bit_length() - 1
    depth, width = w_out.shape
    heads = depth // HEAD_SIZE
    starts = [sum(x.shape[0] for x in parts[:i]) for i in range(len(parts))]
    places = tuple(starts[i] for i in order)
    parts = [parts[i] for i in order]
    whole = pl.BlockSpec(memory_space=pltpu.VMEM)
    piece = jax.ShapeDtypeStruct((slots // 2, width), jnp.float32)
    return pl.pallas_call(
        functools.partial(output_kernel, bits, places, turned),
        out_shape=(piece, piece),
        in_specs=[whole] * (len(parts) + 1),
        out_specs=(whole, whole),
        scratch_shapes=[
            pltpu.VMEM((slots * heads, HEAD_SIZE), jnp.float32),
            pltpu.VMEM((slots, depth), jnp.bfloat16),
        ],
        compiler_params=pltpu.CompilerParams(vmem_limit_bytes=12 * MIB),
        cost_estimate=pl.CostEstimate(
            flops=2 * slots * depth * width, bytes_accessed=2 * depth * width, transcendentals=0
        ),
        name="output",
    )(*parts, w_out)


def swap(block, axis, devices, mask):
    return lax.ppermute(block, axis, [(i, i ^ mask) for i in range(devices)])


def cross(block, devices, mask):
    pairs = [(i, i ^ (2 * mask + 1)) for i in range(2 * devices)]
    return lax.ppermute(block, ("gx", "gy"), pairs)


def fan(pieces, trade):
    masks = [bit_reverse(q, 2) for q in range(FAN)]
    arrived = [None] * FAN
    for q in sorted(range(1, FAN), key=lambda q: (masks[q] + 1) % FAN):
        arrived[q] = trade(pieces[q], masks[q])
    return arrived[1:]


def body(devices, activations, w_query, key_weight, value_weight, w_out, k_cache, value_cache, lengths):
    slots = devices
    query_heads = w_query.shape[1] // HEAD_SIZE
    other = swap(activations, "gy", 2, 1)
    depth = w_query.shape[0]
    first = stage_rows(w_query, min(FIRST, depth))
    pieces = project(activations, other, w_query, first, key_weight, value_weight, slots)
    half = HEAD_SIZE // 2
    frequency = jnp.power(
        jnp.float32(500000.0), -2.0 * jnp.arange(half, dtype=jnp.float32) / HEAD_SIZE
    )
    frequency = jnp.concatenate([frequency, frequency])[None, :]

    if devices == 2 * FAN:
        far = FAN
        arrived = fan(pieces, lambda block, mask: cross(block, devices, mask))
        beside = swap(pieces[0], "gy", 2, 1)
        turn, live = turning(lengths, frequency, w_out, pieces[3], k_cache.shape[2])
        leaving = [x[1:] for x in (*arrived, beside)]
        staying = [x[:1] for x in (*arrived, beside)]
        total = leaving[2] + (leaving[1] + (leaving[0] + leaving[3]))
        total, turn = lax.optimization_barrier((total, turn))
        crossed = cross(total, devices, far)
        beside = swap(staying[2] + (staying[1] + (staying[0] + staying[3])), "gy", 2, 1)
        parts = [crossed, beside]
        heads = attend(parts, turn, live, k_cache, value_cache, query_heads, w_out)
        crossed = cross(heads, devices, far)
        beside = swap(heads, "gy", 2, 1)
        held = jnp.concatenate([crossed, beside], axis=0)
        arrived = fan([held] * FAN, lambda block, mask: cross(block, devices, mask))
        parts = [heads, swap(crossed, "gy", 2, 1)] + arrived
        order, turned = (2, 4, 3, 1, 0), -1
    else:
        arrived = fan(pieces, lambda block, mask: swap(block, "gx", devices, mask))
        turn, live = turning(lengths, frequency, w_out, pieces[3], k_cache.shape[2])
        total = pieces[0] + (arrived[2] + (arrived[1] + arrived[0]))
        mask = FAN
        while total.shape[0] > 2:
            rest = total.shape[0] // 2
            total = total[:rest] + swap(total[rest:], "gx", devices, mask)
            mask *= 2
        parts = [total[:1], swap(total[1:], "gx", devices, mask)]
        heads = attend(parts, turn, live, k_cache, value_cache, query_heads, w_out)

        parts = [heads, swap(heads, "gx", devices, mask)]
        while mask > FAN:
            mask //= 2
            parts.append(swap(jnp.concatenate(parts, axis=0), "gx", devices, mask))
        held = jnp.concatenate(parts, axis=0)
        parts += fan([held] * FAN, lambda block, mask: swap(block, "gx", devices, mask))
        order, turned = range(len(parts))[::-1], 1
    mine, theirs = output(parts, order, w_out, slots, turned)
    return (mine + swap(theirs, "gy", 2, 1)).astype(jnp.bfloat16)


def solution(mesh):
    placed = (
        P(("groups", "gy"), "gx"),
        P("gx", "gy"),
        P("gx", "gy"),
        P("gx", "gy"),
        P("gy", "gx"),
        P(("groups", "gx"), "gy", None, None),
        P(("groups", "gx"), "gy", None, None),
        P(("groups", "gx")),
    )
    return jax.shard_map(
        functools.partial(body, mesh.shape["gx"]),
        mesh=mesh,
        in_specs=placed,
        out_specs=P(("groups", "gy"), "gx"),
        check_vma=False,
    )
```

```python
import functools
import math

import jax
import jax.numpy as jnp
from jax import lax
from jax.experimental import pallas as pl
from jax.experimental.pallas import tpu as pltpu
from jax.sharding import PartitionSpec as P

MODEL_WIDTH = 16384
LANES = 128
HEAD_SIZE = 128
CHUNK = 256
FIRST = 384
PIECES = 1
FAN = 4
MIB = 2**20


def bit_reverse(value, bits):
    turned = 0
    for bit in range(bits):
        turned = turned | (((value >> bit) & 1) << (bits - 1 - bit))
    return turned


def in_hbm(array):
    return pltpu.with_memory_space_constraint(array, pltpu.HBM)


def cut(start, size):
    if size % (16 * PIECES):
        return [(start, size)]
    return [(start + i * (size // PIECES), size // PIECES) for i in range(PIECES)]


def copies_in(src, dst, sems, start, size, offset):
    return [
        pltpu.make_async_copy(
            src.at[pl.ds(at, rows)], dst.at[pl.ds(at - start + offset, rows)], sems.at[i]
        )
        for i, (at, rows) in enumerate(cut(start, size))
    ]


def stage_kernel(rows, src, dst, sems):
    copies = copies_in(src, dst, sems, 0, rows, 0)
    for copy in copies:
        copy.start()
    for copy in copies:
        copy.wait()


def stage_rows(array, rows):
    vmem = pl.BlockSpec(memory_space=pltpu.VMEM)
    return pl.pallas_call(
        functools.partial(stage_kernel, rows),
        out_shape=jax.ShapeDtypeStruct((rows, array.shape[1]), array.dtype),
        in_specs=[pl.BlockSpec(memory_space=pltpu.HBM)],
        out_specs=vmem,
        scratch_shapes=[pltpu.SemaphoreType.DMA((PIECES,))],
        compiler_params=pltpu.CompilerParams(vmem_limit_bytes=16 * MIB),
        cost_estimate=pl.CostEstimate(
            flops=0, bytes_accessed=2 * rows * array.shape[1], transcendentals=0
        ),
        name="stage",
    )(in_hbm(array))


def turning_kernel(length_ref, frequency_ref, beside_ref, after_ref, turn_ref, mask_ref):
    position = length_ref[0].astype(jnp.float32)
    angle = position * frequency_ref[...]
    lane = lax.broadcasted_iota(jnp.int32, angle.shape, 1)
    sine = jnp.sin(angle)
    turn_ref[0:1, :] = jnp.cos(angle)
    turn_ref[1:2, :] = jnp.where(lane < HEAD_SIZE // 2, -sine, sine)
    slot = lax.broadcasted_iota(jnp.int32, mask_ref.shape, 1)
    mask_ref[...] = jnp.where(slot < length_ref[0], 0.0, -jnp.inf)


def turning(lengths, frequency, beside, after, cache_len):
    vmem = pl.BlockSpec(memory_space=pltpu.VMEM)
    return pl.pallas_call(
        turning_kernel,
        out_shape=(
            jax.ShapeDtypeStruct((8, HEAD_SIZE), jnp.float32),
            jax.ShapeDtypeStruct((1, cache_len), jnp.float32),
        ),
        in_specs=[
            pl.BlockSpec(memory_space=pltpu.SMEM),
            vmem,
            pl.BlockSpec(memory_space=pltpu.HBM),
            vmem,
        ],
        out_specs=(vmem, vmem),
        compiler_params=pltpu.CompilerParams(vmem_limit_bytes=2 * MIB),
        cost_estimate=pl.CostEstimate(flops=0, bytes_accessed=2 * beside.size, transcendentals=256),
        name="turning",
    )(lengths, frequency, in_hbm(beside), after)


def spread(depth, skip, chunk):
    ranges = [(at, min(chunk, depth - at)) for at in range(skip, depth, chunk)]
    if ranges and ranges[-1][1] >= 2 * LANES:
        start, size = ranges.pop()
        ranges += [(start, size - LANES), (start + size - LANES, LANES)]
    return ranges


def project_kernel(
    bits, rows_ref, other_ref, wq_hbm, first, wk, wv, *refs
):
    pieces, (wq, rows, sems) = refs[:FAN], refs[FAN:]
    skip = first.shape[0]
    ranges = spread(wq_hbm.shape[0], skip, CHUNK)
    copies = [
        copies_in(wq_hbm, wq, sems.at[i], start, size, start - skip)
        for i, (start, size) in enumerate(ranges)
    ]
    for group in copies:
        for copy in group:
            copy.start()

    slots = rows.shape[0]
    half = slots // 2
    turn = bit_reverse(lax.axis_index("gx"), bits)
    gy = lax.axis_index("gy")
    for ref, side in ((rows_ref, gy), (other_ref, 1 - gy)):
        block = ref[...].astype(jnp.float32)
        for t in range(half):
            slot = bit_reverse(t, bits) ^ turn ^ side
            rows[pl.ds(slot, 1), :] = block[t : t + 1, :]
    wide = rows[...]
    squares = jnp.sum(wide * wide, axis=1, keepdims=True)
    narrow = wide.astype(jnp.bfloat16)

    total = pieces[0].shape[1]
    each = slots // FAN
    flats = [ref.reshape(each * total, LANES) for ref in pieces]

    def put(first_block, part):
        for i in range(0, part.shape[1], LANES):
            for at, flat in enumerate(flats):
                flat[pl.ds(first_block + i // LANES, each, stride=total), :] = part[
                    at * each : (at + 1) * each, i : i + LANES
                ]

    at = wq.shape[1] // LANES
    for w in (wk, wv):
        put(at, jnp.dot(narrow, w[...], preferred_element_type=jnp.float32))
        at += w.shape[1] // LANES
    put(at, jnp.broadcast_to(squares, (slots, LANES)))
    put(at + 1, jnp.zeros((slots, (total - at - 1) * LANES), jnp.float32))

    sums = jnp.dot(narrow[:, :skip], first[...], preferred_element_type=jnp.float32)
    for (start, size), group in zip(ranges, copies):
        for copy in group:
            copy.wait()
        sums = sums + jnp.dot(
            narrow[:, start : start + size],
            wq[start - skip : start - skip + size, :],
            preferred_element_type=jnp.float32,
        )

    put(0, sums)


def project(rows, other, w_query, first, key_weight, value_weight, slots):
    bits = slots.bit_length() - 1
    depth, query_width = w_query.shape
    kv_width = key_weight.shape[1]
    used = (query_width + 2 * kv_width) // LANES + 1
    total = -(-used // 8) * 8
    skip = first.shape[0]
    piece = jax.ShapeDtypeStruct((slots // FAN, total, LANES), jnp.float32)
    hbm = pl.BlockSpec(memory_space=pltpu.HBM)
    whole = pl.BlockSpec(memory_space=pltpu.VMEM)
    return pl.pallas_call(
        functools.partial(project_kernel, bits),
        out_shape=(piece,) * FAN,
        in_specs=[whole, whole, hbm, whole, whole, whole],
        out_specs=(whole,) * FAN,
        scratch_shapes=[
            pltpu.VMEM((max(depth - skip, 16), query_width), jnp.bfloat16),
            pltpu.VMEM((slots, depth), jnp.float32),
            pltpu.SemaphoreType.DMA((max(1, len(spread(depth, skip, CHUNK))), PIECES)),
        ],
        compiler_params=pltpu.CompilerParams(vmem_limit_bytes=46 * MIB),
        cost_estimate=pl.CostEstimate(
            flops=2 * slots * depth * (query_width + 2 * kv_width),
            bytes_accessed=2 * depth * (query_width + 2 * kv_width),
            transcendentals=0,
        ),
        name="project",
    )(rows, other, in_hbm(w_query), first, key_weight, value_weight)


def attend_kernel(
    query_heads, kv_heads, pieces, beside_ref, turn_ref, live_ref, k_ref, v_ref, *refs
):
    heads_ref = refs[pieces]
    total = refs[0][0]
    for ref in refs[1:pieces]:
        total = total + ref[0]
    at = query_heads + 2 * kv_heads
    scale = lax.rsqrt(total[at : at + 1, :] / MODEL_WIDTH + 1e-05)
    turned = total[: query_heads + kv_heads] * scale
    half = HEAD_SIZE // 2
    swapped = jnp.concatenate([turned[:, half:], turned[:, :half]], axis=1)
    turned = (turned * turn_ref[0:1, :] + swapped * turn_ref[1:2, :]).astype(jnp.bfloat16)
    fresh_values = (total[query_heads + kv_heads : at] * scale).astype(jnp.bfloat16)
    group = query_heads // kv_heads
    factor = 1.0 / math.sqrt(HEAD_SIZE)
    side = 2 if kv_heads % 2 == 0 else 1
    for first in range(0, kv_heads, side):
        members = range(first, first + side)
        queries = [turned[head * group : (head + 1) * group] for head in members]
        empty = jnp.zeros((group, HEAD_SIZE), jnp.bfloat16)
        spread_out = jnp.concatenate(
            [
                jnp.concatenate([q if i == j else empty for j in range(side)], axis=1)
                for i, q in enumerate(queries)
            ],
            axis=0,
        )
        keys = jnp.concatenate([k_ref[0, head] for head in members], axis=1)
        values = jnp.concatenate([v_ref[0, head] for head in members], axis=1)
        scores = (
            lax.dot_general(
                spread_out, keys, (((1,), (1,)), ((), ())), preferred_element_type=jnp.float32
            )
            * factor
            + live_ref[...]
        )
        own = jnp.concatenate(
            [
                jnp.sum(
                    q.astype(jnp.float32)
                    * turned[query_heads + head : query_heads + head + 1].astype(jnp.float32),
                    axis=1,
                    keepdims=True,
                )
                for q, head in zip(queries, members)
            ],
            axis=0,
        ) * factor
        top = jnp.maximum(jnp.max(scores, axis=1, keepdims=True), own)
        exponent = jnp.exp(scores - top)
        own_exp = jnp.exp(own - top)
        mixed = jnp.dot(
            exponent.astype(jnp.bfloat16), values, preferred_element_type=jnp.float32
        )
        share = 1.0 / (jnp.sum(exponent, axis=1, keepdims=True) + own_exp)
        for i, head in enumerate(members):
            part = slice(i * group, (i + 1) * group)
            block = mixed[part, i * HEAD_SIZE : (i + 1) * HEAD_SIZE]
            block = block + own_exp[part] * fresh_values[head : head + 1].astype(jnp.float32)
            block = block * share[part]
            heads_ref[0, pl.ds(head * group, group), :] = block.astype(jnp.bfloat16)


def attend(parts, turn, live, k_cache, value_cache, query_heads, beside):
    kv_heads, cache_len = k_cache.shape[1:3]
    whole = pl.BlockSpec(memory_space=pltpu.VMEM)
    return pl.pallas_call(
        functools.partial(attend_kernel, query_heads, kv_heads, len(parts)),
        out_shape=jax.ShapeDtypeStruct((1, query_heads, HEAD_SIZE), jnp.bfloat16),
        in_specs=[pl.BlockSpec(memory_space=pltpu.HBM)] + [whole] * (4 + len(parts)),
        out_specs=whole,
        compiler_params=pltpu.CompilerParams(vmem_limit_bytes=12 * MIB),
        cost_estimate=pl.CostEstimate(
            flops=4 * query_heads * cache_len * HEAD_SIZE,
            bytes_accessed=4 * kv_heads * cache_len * HEAD_SIZE,
            transcendentals=query_heads * cache_len,
        ),
        name="attend",
    )(in_hbm(beside), turn, live, k_cache, value_cache, *parts)


def output_kernel(bits, places, turned, *refs):
    pieces = len(places)
    parts = refs[:pieces]
    w_ref, mine_ref, theirs_ref, flat, left = refs[pieces:]
    slots = left.shape[0]
    heads = flat.shape[0] // slots
    here = lax.axis_index("gx")
    for slot, ref in zip(places, parts):
        for i, row in enumerate(range(ref.shape[0])[::turned]):
            at = pl.multiple_of((here ^ bit_reverse(slot + i, bits)) * heads, heads)
            flat[pl.ds(at, heads), :] = ref[row].astype(jnp.float32)
    for head in range(heads):
        left[:, head * HEAD_SIZE : (head + 1) * HEAD_SIZE] = flat[
            pl.ds(head, slots, stride=heads), :
        ].astype(jnp.bfloat16)
    total = jnp.dot(left[...], w_ref[...], preferred_element_type=jnp.float32)
    half = slots // 2
    gy = lax.axis_index("gy")
    lower, upper = total[:half], total[half:]
    mine_ref[...] = jnp.where(gy == 0, lower, upper)
    theirs_ref[...] = jnp.where(gy == 0, upper, lower)


def output(parts, order, w_out, slots, turned=1):
    bits = slots.bit_length() - 1
    depth, width = w_out.shape
    heads = depth // HEAD_SIZE
    starts = [sum(x.shape[0] for x in parts[:i]) for i in range(len(parts))]
    places = tuple(starts[i] for i in order)
    parts = [parts[i] for i in order]
    whole = pl.BlockSpec(memory_space=pltpu.VMEM)
    piece = jax.ShapeDtypeStruct((slots // 2, width), jnp.float32)
    return pl.pallas_call(
        functools.partial(output_kernel, bits, places, turned),
        out_shape=(piece, piece),
        in_specs=[whole] * (len(parts) + 1),
        out_specs=(whole, whole),
        scratch_shapes=[
            pltpu.VMEM((slots * heads, HEAD_SIZE), jnp.float32),
            pltpu.VMEM((slots, depth), jnp.bfloat16),
        ],
        compiler_params=pltpu.CompilerParams(vmem_limit_bytes=12 * MIB),
        cost_estimate=pl.CostEstimate(
            flops=2 * slots * depth * width, bytes_accessed=2 * depth * width, transcendentals=0
        ),
        name="output",
    )(*parts, w_out)


def swap(block, axis, devices, mask):
    return lax.ppermute(block, axis, [(i, i ^ mask) for i in range(devices)])


def cross(block, devices, mask):
    pairs = [(i, i ^ (2 * mask + 1)) for i in range(2 * devices)]
    return lax.ppermute(block, ("gx", "gy"), pairs)


def fan(pieces, trade):
    masks = [bit_reverse(q, 2) for q in range(FAN)]
    arrived = [None] * FAN
    for q in sorted(range(1, FAN), key=lambda q: (masks[q] + 1) % FAN):
        arrived[q] = trade(pieces[q], masks[q])
    return arrived[1:]


def body(devices, activations, w_query, key_weight, value_weight, w_out, k_cache, value_cache, lengths):
    slots = devices
    query_heads = w_query.shape[1] // HEAD_SIZE
    other = swap(activations, "gy", 2, 1)
    depth = w_query.shape[0]
    first = stage_rows(w_query, min(FIRST, depth))
    pieces = project(activations, other, w_query, first, key_weight, value_weight, slots)
    half = HEAD_SIZE // 2
    frequency = jnp.power(
        jnp.float32(500000.0), -2.0 * jnp.arange(half, dtype=jnp.float32) / HEAD_SIZE
    )
    frequency = jnp.concatenate([frequency, frequency])[None, :]

    if devices == 2 * FAN:
        far = FAN
        arrived = fan(pieces, lambda block, mask: cross(block, devices, mask))
        beside = swap(pieces[0], "gy", 2, 1)
        turn, live = turning(lengths, frequency, w_out, pieces[3], k_cache.shape[2])
        leaving = [x[1:] for x in (*arrived, beside)]
        staying = [x[:1] for x in (*arrived, beside)]
        total = leaving[2] + (leaving[1] + (leaving[0] + leaving[3]))
        total, turn = lax.optimization_barrier((total, turn))
        crossed = cross(total, devices, far)
        beside = swap(staying[2] + (staying[1] + (staying[0] + staying[3])), "gy", 2, 1)
        parts = [crossed, beside]
        heads = attend(parts, turn, live, k_cache, value_cache, query_heads, w_out)
        crossed = cross(heads, devices, far)
        beside = swap(heads, "gy", 2, 1)
        held = jnp.concatenate([crossed, beside], axis=0)
        arrived = fan([held] * FAN, lambda block, mask: cross(block, devices, mask))
        parts = [heads, swap(crossed, "gy", 2, 1)] + arrived
        order, turned = (2, 4, 3, 1, 0), -1
    else:
        arrived = fan(pieces, lambda block, mask: swap(block, "gx", devices, mask))
        turn, live = turning(lengths, frequency, w_out, pieces[3], k_cache.shape[2])
        total = pieces[0] + (arrived[2] + (arrived[1] + arrived[0]))
        mask = FAN
        while total.shape[0] > 2:
            rest = total.shape[0] // 2
            total = total[:rest] + swap(total[rest:], "gx", devices, mask)
            mask *= 2
        parts = [total[:1], swap(total[1:], "gx", devices, mask)]
        heads = attend(parts, turn, live, k_cache, value_cache, query_heads, w_out)

        parts = [heads, swap(heads, "gx", devices, mask)]
        while mask > FAN:
            mask //= 2
            parts.append(swap(jnp.concatenate(parts, axis=0), "gx", devices, mask))
        held = jnp.concatenate(parts, axis=0)
        parts += fan([held] * FAN, lambda block, mask: swap(block, "gx", devices, mask))
        order, turned = range(len(parts))[::-1], 1
    mine, theirs = output(parts, order, w_out, slots, turned)
    return (mine + swap(theirs, "gy", 2, 1)).astype(jnp.bfloat16)


def solution(mesh):
    placed = (
        P(("groups", "gy"), "gx"),
        P("gx", "gy"),
        P("gx", "gy"),
        P("gx", "gy"),
        P("gy", "gx"),
        P(("groups", "gx"), "gy", None, None),
        P(("groups", "gx"), "gy", None, None),
        P(("groups", "gx")),
    )
    return jax.shard_map(
        functools.partial(body, mesh.shape["gx"]),
        mesh=mesh,
        in_specs=placed,
        out_specs=P(("groups", "gy"), "gx"),
        check_vma=False,
    )
```

```python
import functools
import math

import jax
import jax.numpy as jnp
from jax import lax
from jax.experimental import pallas as pl
from jax.experimental.pallas import tpu as pltpu
from jax.sharding import PartitionSpec as P

MODEL_WIDTH = 16384
LANES = 128
HEAD_SIZE = 128
CHUNK = 512
FIRST = 384
PIECES = 1
FAN = 4
MIB = 2**20


def bit_reverse(value, bits):
    turned = 0
    for bit in range(bits):
        turned = turned | (((value >> bit) & 1) << (bits - 1 - bit))
    return turned


def in_hbm(array):
    return pltpu.with_memory_space_constraint(array, pltpu.HBM)


def cut(start, size):
    if size % (16 * PIECES):
        return [(start, size)]
    return [(start + i * (size // PIECES), size // PIECES) for i in range(PIECES)]


def copies_in(src, dst, sems, start, size, offset):
    return [
        pltpu.make_async_copy(
            src.at[pl.ds(at, rows)], dst.at[pl.ds(at - start + offset, rows)], sems.at[i]
        )
        for i, (at, rows) in enumerate(cut(start, size))
    ]


def stage_kernel(rows, src, dst, sems):
    copies = copies_in(src, dst, sems, 0, rows, 0)
    for copy in copies:
        copy.start()
    for copy in copies:
        copy.wait()


def stage_rows(array, rows):
    vmem = pl.BlockSpec(memory_space=pltpu.VMEM)
    return pl.pallas_call(
        functools.partial(stage_kernel, rows),
        out_shape=jax.ShapeDtypeStruct((rows, array.shape[1]), array.dtype),
        in_specs=[pl.BlockSpec(memory_space=pltpu.HBM)],
        out_specs=vmem,
        scratch_shapes=[pltpu.SemaphoreType.DMA((PIECES,))],
        compiler_params=pltpu.CompilerParams(vmem_limit_bytes=16 * MIB),
        cost_estimate=pl.CostEstimate(
            flops=0, bytes_accessed=2 * rows * array.shape[1], transcendentals=0
        ),
        name="stage",
    )(in_hbm(array))


def turning_kernel(length_ref, frequency_ref, beside_ref, after_ref, turn_ref, mask_ref):
    position = length_ref[0].astype(jnp.float32)
    angle = position * frequency_ref[...]
    lane = lax.broadcasted_iota(jnp.int32, angle.shape, 1)
    sine = jnp.sin(angle)
    turn_ref[0:1, :] = jnp.cos(angle)
    turn_ref[1:2, :] = jnp.where(lane < HEAD_SIZE // 2, -sine, sine)
    slot = lax.broadcasted_iota(jnp.int32, mask_ref.shape, 1)
    mask_ref[...] = jnp.where(slot < length_ref[0], 0.0, -jnp.inf)


def turning(lengths, frequency, beside, after, cache_len):
    vmem = pl.BlockSpec(memory_space=pltpu.VMEM)
    return pl.pallas_call(
        turning_kernel,
        out_shape=(
            jax.ShapeDtypeStruct((8, HEAD_SIZE), jnp.float32),
            jax.ShapeDtypeStruct((1, cache_len), jnp.float32),
        ),
        in_specs=[
            pl.BlockSpec(memory_space=pltpu.SMEM),
            vmem,
            pl.BlockSpec(memory_space=pltpu.HBM),
            vmem,
        ],
        out_specs=(vmem, vmem),
        compiler_params=pltpu.CompilerParams(vmem_limit_bytes=2 * MIB),
        cost_estimate=pl.CostEstimate(flops=0, bytes_accessed=2 * beside.size, transcendentals=256),
        name="turning",
    )(lengths, frequency, in_hbm(beside), after)


def spread(depth, skip, chunk):
    ranges = [(at, min(chunk, depth - at)) for at in range(skip, depth, chunk)]
    if ranges and ranges[-1][1] >= 2 * LANES:
        start, size = ranges.pop()
        ranges += [(start, size - LANES), (start + size - LANES, LANES)]
    return ranges


def project_kernel(
    bits, rows_ref, other_ref, wq_hbm, first, wk, wv, *refs
):
    pieces, (wq, rows, sems) = refs[:FAN], refs[FAN:]
    skip = first.shape[0]
    ranges = spread(wq_hbm.shape[0], skip, CHUNK)
    copies = [
        copies_in(wq_hbm, wq, sems.at[i], start, size, start - skip)
        for i, (start, size) in enumerate(ranges)
    ]
    for group in copies:
        for copy in group:
            copy.start()

    slots = rows.shape[0]
    half = slots // 2
    turn = bit_reverse(lax.axis_index("gx"), bits)
    gy = lax.axis_index("gy")
    for ref, side in ((rows_ref, gy), (other_ref, 1 - gy)):
        block = ref[...].astype(jnp.float32)
        for t in range(half):
            slot = bit_reverse(t, bits) ^ turn ^ side
            rows[pl.ds(slot, 1), :] = block[t : t + 1, :]
    wide = rows[...]
    squares = jnp.sum(wide * wide, axis=1, keepdims=True)
    narrow = wide.astype(jnp.bfloat16)

    total = pieces[0].shape[1]
    each = slots // FAN
    flats = [ref.reshape(each * total, LANES) for ref in pieces]

    def put(first_block, part):
        for i in range(0, part.shape[1], LANES):
            for at, flat in enumerate(flats):
                flat[pl.ds(first_block + i // LANES, each, stride=total), :] = part[
                    at * each : (at + 1) * each, i : i + LANES
                ]

    at = wq.shape[1] // LANES
    for w in (wk, wv):
        put(at, jnp.dot(narrow, w[...], preferred_element_type=jnp.float32))
        at += w.shape[1] // LANES
    put(at, jnp.broadcast_to(squares, (slots, LANES)))
    put(at + 1, jnp.zeros((slots, (total - at - 1) * LANES), jnp.float32))

    sums = jnp.dot(narrow[:, :skip], first[...], preferred_element_type=jnp.float32)
    for (start, size), group in zip(ranges, copies):
        for copy in group:
            copy.wait()
        sums = sums + jnp.dot(
            narrow[:, start : start + size],
            wq[start - skip : start - skip + size, :],
            preferred_element_type=jnp.float32,
        )

    put(0, sums)


def project(rows, other, w_query, first, key_weight, value_weight, slots):
    bits = slots.bit_length() - 1
    depth, query_width = w_query.shape
    kv_width = key_weight.shape[1]
    used = (query_width + 2 * kv_width) // LANES + 1
    total = -(-used // 8) * 8
    skip = first.shape[0]
    piece = jax.ShapeDtypeStruct((slots // FAN, total, LANES), jnp.float32)
    hbm = pl.BlockSpec(memory_space=pltpu.HBM)
    whole = pl.BlockSpec(memory_space=pltpu.VMEM)
    return pl.pallas_call(
        functools.partial(project_kernel, bits),
        out_shape=(piece,) * FAN,
        in_specs=[whole, whole, hbm, whole, whole, whole],
        out_specs=(whole,) * FAN,
        scratch_shapes=[
            pltpu.VMEM((max(depth - skip, 16), query_width), jnp.bfloat16),
            pltpu.VMEM((slots, depth), jnp.float32),
            pltpu.SemaphoreType.DMA((max(1, len(spread(depth, skip, CHUNK))), PIECES)),
        ],
        compiler_params=pltpu.CompilerParams(vmem_limit_bytes=46 * MIB),
        cost_estimate=pl.CostEstimate(
            flops=2 * slots * depth * (query_width + 2 * kv_width),
            bytes_accessed=2 * depth * (query_width + 2 * kv_width),
            transcendentals=0,
        ),
        name="project",
    )(rows, other, in_hbm(w_query), first, key_weight, value_weight)


def attend_kernel(
    query_heads, kv_heads, pieces, beside_ref, turn_ref, live_ref, k_ref, v_ref, *refs
):
    heads_ref = refs[pieces]
    total = refs[0][0]
    for ref in refs[1:pieces]:
        total = total + ref[0]
    at = query_heads + 2 * kv_heads
    scale = lax.rsqrt(total[at : at + 1, :] / MODEL_WIDTH + 1e-05)
    turned = total[: query_heads + kv_heads] * scale
    half = HEAD_SIZE // 2
    swapped = jnp.concatenate([turned[:, half:], turned[:, :half]], axis=1)
    turned = (turned * turn_ref[0:1, :] + swapped * turn_ref[1:2, :]).astype(jnp.bfloat16)
    fresh_values = (total[query_heads + kv_heads : at] * scale).astype(jnp.bfloat16)
    group = query_heads // kv_heads
    factor = 1.0 / math.sqrt(HEAD_SIZE)
    side = 2 if kv_heads % 2 == 0 else 1
    for first in range(0, kv_heads, side):
        members = range(first, first + side)
        queries = [turned[head * group : (head + 1) * group] for head in members]
        empty = jnp.zeros((group, HEAD_SIZE), jnp.bfloat16)
        spread_out = jnp.concatenate(
            [
                jnp.concatenate([q if i == j else empty for j in range(side)], axis=1)
                for i, q in enumerate(queries)
            ],
            axis=0,
        )
        keys = jnp.concatenate([k_ref[0, head] for head in members], axis=1)
        values = jnp.concatenate([v_ref[0, head] for head in members], axis=1)
        scores = (
            lax.dot_general(
                spread_out, keys, (((1,), (1,)), ((), ())), preferred_element_type=jnp.float32
            )
            * factor
            + live_ref[...]
        )
        own = jnp.concatenate(
            [
                jnp.sum(
                    q.astype(jnp.float32)
                    * turned[query_heads + head : query_heads + head + 1].astype(jnp.float32),
                    axis=1,
                    keepdims=True,
                )
                for q, head in zip(queries, members)
            ],
            axis=0,
        ) * factor
        top = jnp.maximum(jnp.max(scores, axis=1, keepdims=True), own)
        exponent = jnp.exp(scores - top)
        own_exp = jnp.exp(own - top)
        mixed = jnp.dot(
            exponent.astype(jnp.bfloat16), values, preferred_element_type=jnp.float32
        )
        share = 1.0 / (jnp.sum(exponent, axis=1, keepdims=True) + own_exp)
        for i, head in enumerate(members):
            part = slice(i * group, (i + 1) * group)
            block = mixed[part, i * HEAD_SIZE : (i + 1) * HEAD_SIZE]
            block = block + own_exp[part] * fresh_values[head : head + 1].astype(jnp.float32)
            block = block * share[part]
            heads_ref[0, pl.ds(head * group, group), :] = block.astype(jnp.bfloat16)


def attend(parts, turn, live, k_cache, value_cache, query_heads, beside):
    kv_heads, cache_len = k_cache.shape[1:3]
    whole = pl.BlockSpec(memory_space=pltpu.VMEM)
    return pl.pallas_call(
        functools.partial(attend_kernel, query_heads, kv_heads, len(parts)),
        out_shape=jax.ShapeDtypeStruct((1, query_heads, HEAD_SIZE), jnp.bfloat16),
        in_specs=[pl.BlockSpec(memory_space=pltpu.HBM)] + [whole] * (4 + len(parts)),
        out_specs=whole,
        compiler_params=pltpu.CompilerParams(vmem_limit_bytes=12 * MIB),
        cost_estimate=pl.CostEstimate(
            flops=4 * query_heads * cache_len * HEAD_SIZE,
            bytes_accessed=4 * kv_heads * cache_len * HEAD_SIZE,
            transcendentals=query_heads * cache_len,
        ),
        name="attend",
    )(in_hbm(beside), turn, live, k_cache, value_cache, *parts)


def output_kernel(bits, places, turned, *refs):
    pieces = len(places)
    parts = refs[:pieces]
    w_ref, mine_ref, theirs_ref, flat, left = refs[pieces:]
    slots = left.shape[0]
    heads = flat.shape[0] // slots
    here = lax.axis_index("gx")
    for slot, ref in zip(places, parts):
        for i, row in enumerate(range(ref.shape[0])[::turned]):
            at = pl.multiple_of((here ^ bit_reverse(slot + i, bits)) * heads, heads)
            flat[pl.ds(at, heads), :] = ref[row].astype(jnp.float32)
    for head in range(heads):
        left[:, head * HEAD_SIZE : (head + 1) * HEAD_SIZE] = flat[
            pl.ds(head, slots, stride=heads), :
        ].astype(jnp.bfloat16)
    total = jnp.dot(left[...], w_ref[...], preferred_element_type=jnp.float32)
    half = slots // 2
    gy = lax.axis_index("gy")
    lower, upper = total[:half], total[half:]
    mine_ref[...] = jnp.where(gy == 0, lower, upper)
    theirs_ref[...] = jnp.where(gy == 0, upper, lower)


def output(parts, order, w_out, slots, turned=1):
    bits = slots.bit_length() - 1
    depth, width = w_out.shape
    heads = depth // HEAD_SIZE
    starts = [sum(x.shape[0] for x in parts[:i]) for i in range(len(parts))]
    places = tuple(starts[i] for i in order)
    parts = [parts[i] for i in order]
    whole = pl.BlockSpec(memory_space=pltpu.VMEM)
    piece = jax.ShapeDtypeStruct((slots // 2, width), jnp.float32)
    return pl.pallas_call(
        functools.partial(output_kernel, bits, places, turned),
        out_shape=(piece, piece),
        in_specs=[whole] * (len(parts) + 1),
        out_specs=(whole, whole),
        scratch_shapes=[
            pltpu.VMEM((slots * heads, HEAD_SIZE), jnp.float32),
            pltpu.VMEM((slots, depth), jnp.bfloat16),
        ],
        compiler_params=pltpu.CompilerParams(vmem_limit_bytes=12 * MIB),
        cost_estimate=pl.CostEstimate(
            flops=2 * slots * depth * width, bytes_accessed=2 * depth * width, transcendentals=0
        ),
        name="output",
    )(*parts, w_out)


def swap(block, axis, devices, mask):
    return lax.ppermute(block, axis, [(i, i ^ mask) for i in range(devices)])


def cross(block, devices, mask):
    pairs = [(i, i ^ (2 * mask + 1)) for i in range(2 * devices)]
    return lax.ppermute(block, ("gx", "gy"), pairs)


def fan(pieces, trade):
    masks = [bit_reverse(q, 2) for q in range(FAN)]
    arrived = [None] * FAN
    for q in sorted(range(1, FAN), key=lambda q: (masks[q] + 1) % FAN):
        arrived[q] = trade(pieces[q], masks[q])
    return arrived[1:]


def body(devices, activations, w_query, key_weight, value_weight, w_out, k_cache, value_cache, lengths):
    slots = devices
    query_heads = w_query.shape[1] // HEAD_SIZE
    other = swap(activations, "gy", 2, 1)
    depth = w_query.shape[0]
    first = stage_rows(w_query, min(FIRST, depth))
    pieces = project(activations, other, w_query, first, key_weight, value_weight, slots)
    half = HEAD_SIZE // 2
    frequency = jnp.power(
        jnp.float32(500000.0), -2.0 * jnp.arange(half, dtype=jnp.float32) / HEAD_SIZE
    )
    frequency = jnp.concatenate([frequency, frequency])[None, :]

    if devices == 2 * FAN:
        far = FAN
        arrived = fan(pieces, lambda block, mask: cross(block, devices, mask))
        beside = swap(pieces[0], "gy", 2, 1)
        turn, live = turning(lengths, frequency, w_out, pieces[3], k_cache.shape[2])
        leaving = [x[1:] for x in (*arrived, beside)]
        staying = [x[:1] for x in (*arrived, beside)]
        total = leaving[2] + (leaving[1] + (leaving[0] + leaving[3]))
        total, turn = lax.optimization_barrier((total, turn))
        crossed = cross(total, devices, far)
        beside = swap(staying[2] + (staying[1] + (staying[0] + staying[3])), "gy", 2, 1)
        parts = [crossed, beside]
        heads = attend(parts, turn, live, k_cache, value_cache, query_heads, w_out)
        crossed = cross(heads, devices, far)
        beside = swap(heads, "gy", 2, 1)
        held = jnp.concatenate([crossed, beside], axis=0)
        arrived = fan([held] * FAN, lambda block, mask: cross(block, devices, mask))
        parts = [heads, swap(crossed, "gy", 2, 1)] + arrived
        order, turned = (2, 4, 3, 1, 0), -1
    else:
        arrived = fan(pieces, lambda block, mask: swap(block, "gx", devices, mask))
        turn, live = turning(lengths, frequency, w_out, pieces[3], k_cache.shape[2])
        total = pieces[0] + (arrived[2] + (arrived[1] + arrived[0]))
        mask = FAN
        while total.shape[0] > 2:
            rest = total.shape[0] // 2
            total = total[:rest] + swap(total[rest:], "gx", devices, mask)
            mask *= 2
        parts = [total[:1], swap(total[1:], "gx", devices, mask)]
        heads = attend(parts, turn, live, k_cache, value_cache, query_heads, w_out)

        parts = [heads, swap(heads, "gx", devices, mask)]
        while mask > FAN:
            mask //= 2
            parts.append(swap(jnp.concatenate(parts, axis=0), "gx", devices, mask))
        held = jnp.concatenate(parts, axis=0)
        parts += fan([held] * FAN, lambda block, mask: swap(block, "gx", devices, mask))
        order, turned = range(len(parts))[::-1], 1
    mine, theirs = output(parts, order, w_out, slots, turned)
    return (mine + swap(theirs, "gy", 2, 1)).astype(jnp.bfloat16)


def solution(mesh):
    placed = (
        P(("groups", "gy"), "gx"),
        P("gx", "gy"),
        P("gx", "gy"),
        P("gx", "gy"),
        P("gy", "gx"),
        P(("groups", "gx"), "gy", None, None),
        P(("groups", "gx"), "gy", None, None),
        P(("groups", "gx")),
    )
    return jax.shard_map(
        functools.partial(body, mesh.shape["gx"]),
        mesh=mesh,
        in_specs=placed,
        out_specs=P(("groups", "gy"), "gx"),
        check_vma=False,
    )
```

```python
import functools
import math

import jax
import jax.numpy as jnp
from jax import lax
from jax.experimental import pallas as pl
from jax.experimental.pallas import tpu as pltpu
from jax.sharding import PartitionSpec as P

MODEL_WIDTH = 16384
LANES = 128
HEAD_SIZE = 128
CHUNK = 256
FIRST = 384
PIECES = 1
FAN = 4
MIB = 2**20


def bit_reverse(value, bits):
    turned = 0
    for bit in range(bits):
        turned = turned | (((value >> bit) & 1) << (bits - 1 - bit))
    return turned


def in_hbm(array):
    return pltpu.with_memory_space_constraint(array, pltpu.HBM)


def cut(start, size):
    if size % (16 * PIECES):
        return [(start, size)]
    return [(start + i * (size // PIECES), size // PIECES) for i in range(PIECES)]


def copies_in(src, dst, sems, start, size, offset):
    return [
        pltpu.make_async_copy(
            src.at[pl.ds(at, rows)], dst.at[pl.ds(at - start + offset, rows)], sems.at[i]
        )
        for i, (at, rows) in enumerate(cut(start, size))
    ]


def stage_kernel(rows, src, dst, sems):
    copies = copies_in(src, dst, sems, 0, rows, 0)
    for copy in copies:
        copy.start()
    for copy in copies:
        copy.wait()


def stage_rows(array, rows):
    vmem = pl.BlockSpec(memory_space=pltpu.VMEM)
    return pl.pallas_call(
        functools.partial(stage_kernel, rows),
        out_shape=jax.ShapeDtypeStruct((rows, array.shape[1]), array.dtype),
        in_specs=[pl.BlockSpec(memory_space=pltpu.HBM)],
        out_specs=vmem,
        scratch_shapes=[pltpu.SemaphoreType.DMA((PIECES,))],
        compiler_params=pltpu.CompilerParams(vmem_limit_bytes=16 * MIB),
        cost_estimate=pl.CostEstimate(
            flops=0, bytes_accessed=2 * rows * array.shape[1], transcendentals=0
        ),
        name="stage",
    )(in_hbm(array))


def turning_kernel(length_ref, frequency_ref, beside_ref, after_ref, turn_ref, mask_ref):
    position = length_ref[0].astype(jnp.float32)
    angle = position * frequency_ref[...]
    lane = lax.broadcasted_iota(jnp.int32, angle.shape, 1)
    sine = jnp.sin(angle)
    turn_ref[0:1, :] = jnp.cos(angle)
    turn_ref[1:2, :] = jnp.where(lane < HEAD_SIZE // 2, -sine, sine)
    slot = lax.broadcasted_iota(jnp.int32, mask_ref.shape, 1)
    mask_ref[...] = jnp.where(slot < length_ref[0], 0.0, -jnp.inf)


def turning(lengths, frequency, beside, after, cache_len):
    vmem = pl.BlockSpec(memory_space=pltpu.VMEM)
    return pl.pallas_call(
        turning_kernel,
        out_shape=(
            jax.ShapeDtypeStruct((8, HEAD_SIZE), jnp.float32),
            jax.ShapeDtypeStruct((1, cache_len), jnp.float32),
        ),
        in_specs=[
            pl.BlockSpec(memory_space=pltpu.SMEM),
            vmem,
            pl.BlockSpec(memory_space=pltpu.HBM),
            vmem,
        ],
        out_specs=(vmem, vmem),
        compiler_params=pltpu.CompilerParams(vmem_limit_bytes=2 * MIB),
        cost_estimate=pl.CostEstimate(flops=0, bytes_accessed=2 * beside.size, transcendentals=256),
        name="turning",
    )(lengths, frequency, in_hbm(beside), after)


def spread(depth, skip, chunk):
    ranges = [(at, min(chunk, depth - at)) for at in range(skip, depth, chunk)]
    if ranges and ranges[-1][1] >= 2 * LANES:
        start, size = ranges.pop()
        ranges += [(start, size - LANES), (start + size - LANES, LANES)]
    return ranges


def project_kernel(
    bits, rows_ref, other_ref, wq_hbm, first, wk, wv, *refs
):
    pieces, (wq, rows, sems) = refs[:FAN], refs[FAN:]
    skip = first.shape[0]
    ranges = spread(wq_hbm.shape[0], skip, CHUNK)
    copies = [
        copies_in(wq_hbm, wq, sems.at[i], start, size, start - skip)
        for i, (start, size) in enumerate(ranges)
    ]
    for group in copies:
        for copy in group:
            copy.start()

    slots = rows.shape[0]
    half = slots // 2
    turn = bit_reverse(lax.axis_index("gx"), bits)
    gy = lax.axis_index("gy")
    for ref, side in ((rows_ref, gy), (other_ref, 1 - gy)):
        block = ref[...].astype(jnp.float32)
        for t in range(half):
            slot = bit_reverse(t, bits) ^ turn ^ side
            rows[pl.ds(slot, 1), :] = block[t : t + 1, :]
    wide = rows[...]
    squares = jnp.sum(wide * wide, axis=1, keepdims=True)
    narrow = wide.astype(jnp.bfloat16)

    total = pieces[0].shape[1]
    each = slots // FAN
    flats = [ref.reshape(each * total, LANES) for ref in pieces]

    def put(first_block, part):
        for i in range(0, part.shape[1], LANES):
            for at, flat in enumerate(flats):
                flat[pl.ds(first_block + i // LANES, each, stride=total), :] = part[
                    at * each : (at + 1) * each, i : i + LANES
                ]

    at = wq.shape[1] // LANES
    for w in (wk, wv):
        put(at, jnp.dot(narrow, w[...], preferred_element_type=jnp.float32))
        at += w.shape[1] // LANES
    put(at, jnp.broadcast_to(squares, (slots, LANES)))
    put(at + 1, jnp.zeros((slots, (total - at - 1) * LANES), jnp.float32))

    sums = jnp.dot(narrow[:, :skip], first[...], preferred_element_type=jnp.float32)
    for (start, size), group in zip(ranges, copies):
        for copy in group:
            copy.wait()
        sums = sums + jnp.dot(
            narrow[:, start : start + size],
            wq[start - skip : start - skip + size, :],
            preferred_element_type=jnp.float32,
        )

    put(0, sums)


def project(rows, other, w_query, first, key_weight, value_weight, slots):
    bits = slots.bit_length() - 1
    depth, query_width = w_query.shape
    kv_width = key_weight.shape[1]
    used = (query_width + 2 * kv_width) // LANES + 1
    total = -(-used // 8) * 8
    skip = first.shape[0]
    piece = jax.ShapeDtypeStruct((slots // FAN, total, LANES), jnp.float32)
    hbm = pl.BlockSpec(memory_space=pltpu.HBM)
    whole = pl.BlockSpec(memory_space=pltpu.VMEM)
    return pl.pallas_call(
        functools.partial(project_kernel, bits),
        out_shape=(piece,) * FAN,
        in_specs=[whole, whole, hbm, whole, whole, whole],
        out_specs=(whole,) * FAN,
        scratch_shapes=[
            pltpu.VMEM((max(depth - skip, 16), query_width), jnp.bfloat16),
            pltpu.VMEM((slots, depth), jnp.float32),
            pltpu.SemaphoreType.DMA((max(1, len(spread(depth, skip, CHUNK))), PIECES)),
        ],
        compiler_params=pltpu.CompilerParams(vmem_limit_bytes=46 * MIB),
        cost_estimate=pl.CostEstimate(
            flops=2 * slots * depth * (query_width + 2 * kv_width),
            bytes_accessed=2 * depth * (query_width + 2 * kv_width),
            transcendentals=0,
        ),
        name="project",
    )(rows, other, in_hbm(w_query), first, key_weight, value_weight)


def attend_kernel(
    query_heads, kv_heads, pieces, beside_ref, turn_ref, live_ref, k_ref, v_ref, *refs
):
    heads_ref = refs[pieces]
    total = refs[0][0]
    for ref in refs[1:pieces]:
        total = total + ref[0]
    at = query_heads + 2 * kv_heads
    scale = lax.rsqrt(total[at : at + 1, :] / MODEL_WIDTH + 1e-05)
    turned = total[: query_heads + kv_heads] * scale
    half = HEAD_SIZE // 2
    swapped = jnp.concatenate([turned[:, half:], turned[:, :half]], axis=1)
    turned = (turned * turn_ref[0:1, :] + swapped * turn_ref[1:2, :]).astype(jnp.bfloat16)
    fresh_values = (total[query_heads + kv_heads : at] * scale).astype(jnp.bfloat16)
    group = query_heads // kv_heads
    factor = 1.0 / math.sqrt(HEAD_SIZE)
    side = 2 if kv_heads % 2 == 0 else 1
    for first in range(0, kv_heads, side):
        members = range(first, first + side)
        queries = [turned[head * group : (head + 1) * group] for head in members]
        empty = jnp.zeros((group, HEAD_SIZE), jnp.bfloat16)
        spread_out = jnp.concatenate(
            [
                jnp.concatenate([q if i == j else empty for j in range(side)], axis=1)
                for i, q in enumerate(queries)
            ],
            axis=0,
        )
        keys = jnp.concatenate([k_ref[0, head] for head in members], axis=1)
        values = jnp.concatenate([v_ref[0, head] for head in members], axis=1)
        scores = (
            lax.dot_general(
                spread_out, keys, (((1,), (1,)), ((), ())), preferred_element_type=jnp.float32
            )
            * factor
            + live_ref[...]
        )
        own = jnp.concatenate(
            [
                jnp.sum(
                    q.astype(jnp.float32)
                    * turned[query_heads + head : query_heads + head + 1].astype(jnp.float32),
                    axis=1,
                    keepdims=True,
                )
                for q, head in zip(queries, members)
            ],
            axis=0,
        ) * factor
        top = jnp.maximum(jnp.max(scores, axis=1, keepdims=True), own)
        exponent = jnp.exp(scores - top)
        own_exp = jnp.exp(own - top)
        mixed = jnp.dot(
            exponent.astype(jnp.bfloat16), values, preferred_element_type=jnp.float32
        )
        share = 1.0 / (jnp.sum(exponent, axis=1, keepdims=True) + own_exp)
        for i, head in enumerate(members):
            part = slice(i * group, (i + 1) * group)
            block = mixed[part, i * HEAD_SIZE : (i + 1) * HEAD_SIZE]
            block = block + own_exp[part] * fresh_values[head : head + 1].astype(jnp.float32)
            block = block * share[part]
            heads_ref[0, pl.ds(head * group, group), :] = block.astype(jnp.bfloat16)


def attend(parts, turn, live, k_cache, value_cache, query_heads, beside):
    kv_heads, cache_len = k_cache.shape[1:3]
    whole = pl.BlockSpec(memory_space=pltpu.VMEM)
    return pl.pallas_call(
        functools.partial(attend_kernel, query_heads, kv_heads, len(parts)),
        out_shape=jax.ShapeDtypeStruct((1, query_heads, HEAD_SIZE), jnp.bfloat16),
        in_specs=[pl.BlockSpec(memory_space=pltpu.HBM)] + [whole] * (4 + len(parts)),
        out_specs=whole,
        compiler_params=pltpu.CompilerParams(vmem_limit_bytes=12 * MIB),
        cost_estimate=pl.CostEstimate(
            flops=4 * query_heads * cache_len * HEAD_SIZE,
            bytes_accessed=4 * kv_heads * cache_len * HEAD_SIZE,
            transcendentals=query_heads * cache_len,
        ),
        name="attend",
    )(in_hbm(beside), turn, live, k_cache, value_cache, *parts)


def output_kernel(bits, places, turned, *refs):
    pieces = len(places)
    parts = refs[:pieces]
    w_ref, mine_ref, theirs_ref, flat, left = refs[pieces:]
    slots = left.shape[0]
    heads = flat.shape[0] // slots
    here = lax.axis_index("gx")
    for slot, ref in zip(places, parts):
        for i, row in enumerate(range(ref.shape[0])[::turned]):
            at = pl.multiple_of((here ^ bit_reverse(slot + i, bits)) * heads, heads)
            flat[pl.ds(at, heads), :] = ref[row].astype(jnp.float32)
    for head in range(heads):
        left[:, head * HEAD_SIZE : (head + 1) * HEAD_SIZE] = flat[
            pl.ds(head, slots, stride=heads), :
        ].astype(jnp.bfloat16)
    total = jnp.dot(left[...], w_ref[...], preferred_element_type=jnp.float32)
    half = slots // 2
    gy = lax.axis_index("gy")
    lower, upper = total[:half], total[half:]
    mine_ref[...] = jnp.where(gy == 0, lower, upper)
    theirs_ref[...] = jnp.where(gy == 0, upper, lower)


def output(parts, order, w_out, slots, turned=1):
    bits = slots.bit_length() - 1
    depth, width = w_out.shape
    heads = depth // HEAD_SIZE
    starts = [sum(x.shape[0] for x in parts[:i]) for i in range(len(parts))]
    places = tuple(starts[i] for i in order)
    parts = [parts[i] for i in order]
    whole = pl.BlockSpec(memory_space=pltpu.VMEM)
    piece = jax.ShapeDtypeStruct((slots // 2, width), jnp.float32)
    return pl.pallas_call(
        functools.partial(output_kernel, bits, places, turned),
        out_shape=(piece, piece),
        in_specs=[whole] * (len(parts) + 1),
        out_specs=(whole, whole),
        scratch_shapes=[
            pltpu.VMEM((slots * heads, HEAD_SIZE), jnp.float32),
            pltpu.VMEM((slots, depth), jnp.bfloat16),
        ],
        compiler_params=pltpu.CompilerParams(vmem_limit_bytes=12 * MIB),
        cost_estimate=pl.CostEstimate(
            flops=2 * slots * depth * width, bytes_accessed=2 * depth * width, transcendentals=0
        ),
        name="output",
    )(*parts, w_out)


def swap(block, axis, devices, mask):
    return lax.ppermute(block, axis, [(i, i ^ mask) for i in range(devices)])


def cross(block, devices, mask):
    pairs = [(i, i ^ (2 * mask + 1)) for i in range(2 * devices)]
    return lax.ppermute(block, ("gx", "gy"), pairs)


def fan(pieces, trade):
    masks = [bit_reverse(q, 2) for q in range(FAN)]
    arrived = [None] * FAN
    for q in sorted(range(1, FAN), key=lambda q: -masks[q]):
        arrived[q] = trade(pieces[q], masks[q])
    return arrived[1:]


def body(devices, activations, w_query, key_weight, value_weight, w_out, k_cache, value_cache, lengths):
    slots = devices
    query_heads = w_query.shape[1] // HEAD_SIZE
    other = swap(activations, "gy", 2, 1)
    depth = w_query.shape[0]
    first = stage_rows(w_query, min(FIRST, depth))
    pieces = project(activations, other, w_query, first, key_weight, value_weight, slots)
    half = HEAD_SIZE // 2
    frequency = jnp.power(
        jnp.float32(500000.0), -2.0 * jnp.arange(half, dtype=jnp.float32) / HEAD_SIZE
    )
    frequency = jnp.concatenate([frequency, frequency])[None, :]

    if devices == 2 * FAN:
        far = FAN
        arrived = fan(pieces, lambda block, mask: cross(block, devices, mask))
        beside = swap(pieces[0], "gy", 2, 1)
        turn, live = turning(lengths, frequency, w_out, pieces[3], k_cache.shape[2])
        leaving = [x[1:] for x in (*arrived, beside)]
        staying = [x[:1] for x in (*arrived, beside)]
        total = leaving[2] + (leaving[0] + (leaving[1] + leaving[3]))
        total, turn = lax.optimization_barrier((total, turn))
        crossed = cross(total, devices, far)
        beside = swap(staying[2] + (staying[0] + (staying[1] + staying[3])), "gy", 2, 1)
        parts = [crossed, beside]
        heads = attend(parts, turn, live, k_cache, value_cache, query_heads, w_out)
        crossed = cross(heads, devices, far)
        beside = swap(heads, "gy", 2, 1)
        held = jnp.concatenate([crossed, beside], axis=0)
        arrived = fan([held] * FAN, lambda block, mask: cross(block, devices, mask))
        parts = [heads, swap(crossed, "gy", 2, 1)] + arrived
        order, turned = (3, 4, 2, 1, 0), -1
    else:
        arrived = fan(pieces, lambda block, mask: swap(block, "gx", devices, mask))
        turn, live = turning(lengths, frequency, w_out, pieces[3], k_cache.shape[2])
        total = pieces[0] + (arrived[2] + (arrived[1] + arrived[0]))
        mask = FAN
        while total.shape[0] > 2:
            rest = total.shape[0] // 2
            total = total[:rest] + swap(total[rest:], "gx", devices, mask)
            mask *= 2
        parts = [total[:1], swap(total[1:], "gx", devices, mask)]
        heads = attend(parts, turn, live, k_cache, value_cache, query_heads, w_out)

        parts = [heads, swap(heads, "gx", devices, mask)]
        while mask > FAN:
            mask //= 2
            parts.append(swap(jnp.concatenate(parts, axis=0), "gx", devices, mask))
        held = jnp.concatenate(parts, axis=0)
        parts += fan([held] * FAN, lambda block, mask: swap(block, "gx", devices, mask))
        order, turned = range(len(parts))[::-1], 1
    mine, theirs = output(parts, order, w_out, slots, turned)
    return (mine + swap(theirs, "gy", 2, 1)).astype(jnp.bfloat16)


def solution(mesh):
    placed = (
        P(("groups", "gy"), "gx"),
        P("gx", "gy"),
        P("gx", "gy"),
        P("gx", "gy"),
        P("gy", "gx"),
        P(("groups", "gx"), "gy", None, None),
        P(("groups", "gx"), "gy", None, None),
        P(("groups", "gx")),
    )
    return jax.shard_map(
        functools.partial(body, mesh.shape["gx"]),
        mesh=mesh,
        in_specs=placed,
        out_specs=P(("groups", "gy"), "gx"),
        check_vma=False,
    )
```

```python
import functools
import math

import jax
import jax.numpy as jnp
from jax import lax
from jax.experimental import pallas as pl
from jax.experimental.pallas import tpu as pltpu
from jax.sharding import PartitionSpec as P

MODEL_WIDTH = 16384
LANES = 128
HEAD_SIZE = 128
CHUNK = 256
FIRST = 384
PIECES = 1
FAN = 4
MIB = 2**20


def bit_reverse(value, bits):
    turned = 0
    for bit in range(bits):
        turned = turned | (((value >> bit) & 1) << (bits - 1 - bit))
    return turned


def in_hbm(array):
    return pltpu.with_memory_space_constraint(array, pltpu.HBM)


def cut(start, size):
    if size % (16 * PIECES):
        return [(start, size)]
    return [(start + i * (size // PIECES), size // PIECES) for i in range(PIECES)]


def copies_in(src, dst, sems, start, size, offset):
    return [
        pltpu.make_async_copy(
            src.at[pl.ds(at, rows)], dst.at[pl.ds(at - start + offset, rows)], sems.at[i]
        )
        for i, (at, rows) in enumerate(cut(start, size))
    ]


def stage_kernel(rows, src, dst, sems):
    copies = copies_in(src, dst, sems, 0, rows, 0)
    for copy in copies:
        copy.start()
    for copy in copies:
        copy.wait()


def stage_rows(array, rows):
    vmem = pl.BlockSpec(memory_space=pltpu.VMEM)
    return pl.pallas_call(
        functools.partial(stage_kernel, rows),
        out_shape=jax.ShapeDtypeStruct((rows, array.shape[1]), array.dtype),
        in_specs=[pl.BlockSpec(memory_space=pltpu.HBM)],
        out_specs=vmem,
        scratch_shapes=[pltpu.SemaphoreType.DMA((PIECES,))],
        compiler_params=pltpu.CompilerParams(vmem_limit_bytes=16 * MIB),
        cost_estimate=pl.CostEstimate(
            flops=0, bytes_accessed=2 * rows * array.shape[1], transcendentals=0
        ),
        name="stage",
    )(in_hbm(array))


def turning_kernel(
    length_ref, frequency_ref, beside_ref, more_ref, after_ref, turn_ref, mask_ref
):
    position = length_ref[0].astype(jnp.float32)
    angle = position * frequency_ref[...]
    lane = lax.broadcasted_iota(jnp.int32, angle.shape, 1)
    sine = jnp.sin(angle)
    turn_ref[0:1, :] = jnp.cos(angle)
    turn_ref[1:2, :] = jnp.where(lane < HEAD_SIZE // 2, -sine, sine)
    slot = lax.broadcasted_iota(jnp.int32, mask_ref.shape, 1)
    mask_ref[...] = jnp.where(slot < length_ref[0], 0.0, -jnp.inf)


def turning(lengths, frequency, beside, more, after, cache_len):
    vmem = pl.BlockSpec(memory_space=pltpu.VMEM)
    return pl.pallas_call(
        turning_kernel,
        out_shape=(
            jax.ShapeDtypeStruct((8, HEAD_SIZE), jnp.float32),
            jax.ShapeDtypeStruct((1, cache_len), jnp.float32),
        ),
        in_specs=[
            pl.BlockSpec(memory_space=pltpu.SMEM),
            vmem,
            pl.BlockSpec(memory_space=pltpu.HBM),
            pl.BlockSpec(memory_space=pltpu.HBM),
            vmem,
        ],
        out_specs=(vmem, vmem),
        compiler_params=pltpu.CompilerParams(vmem_limit_bytes=2 * MIB),
        cost_estimate=pl.CostEstimate(flops=0, bytes_accessed=2 * beside.size, transcendentals=256),
        name="turning",
    )(lengths, frequency, in_hbm(beside), in_hbm(more), after)


def spread(depth, skip, chunk):
    ranges = [(at, min(chunk, depth - at)) for at in range(skip, depth, chunk)]
    if ranges and ranges[-1][1] >= 2 * LANES:
        start, size = ranges.pop()
        ranges += [(start, size - LANES), (start + size - LANES, LANES)]
    return ranges


def project_kernel(
    bits, rows_ref, other_ref, wq_hbm, first, wk, wv, *refs
):
    pieces, (wq, rows, sems) = refs[:FAN], refs[FAN:]
    skip = first.shape[0]
    ranges = spread(wq_hbm.shape[0], skip, CHUNK)
    copies = [
        copies_in(wq_hbm, wq, sems.at[i], start, size, start - skip)
        for i, (start, size) in enumerate(ranges)
    ]
    for group in copies:
        for copy in group:
            copy.start()

    slots = rows.shape[0]
    half = slots // 2
    turn = bit_reverse(lax.axis_index("gx"), bits)
    gy = lax.axis_index("gy")
    for ref, side in ((rows_ref, gy), (other_ref, 1 - gy)):
        block = ref[...].astype(jnp.float32)
        for t in range(half):
            slot = bit_reverse(t, bits) ^ turn ^ side
            rows[pl.ds(slot, 1), :] = block[t : t + 1, :]
    wide = rows[...]
    squares = jnp.sum(wide * wide, axis=1, keepdims=True)
    narrow = wide.astype(jnp.bfloat16)

    total = pieces[0].shape[1]
    each = slots // FAN
    flats = [ref.reshape(each * total, LANES) for ref in pieces]

    def put(first_block, part):
        for i in range(0, part.shape[1], LANES):
            for at, flat in enumerate(flats):
                flat[pl.ds(first_block + i // LANES, each, stride=total), :] = part[
                    at * each : (at + 1) * each, i : i + LANES
                ]

    at = wq.shape[1] // LANES
    for w in (wk, wv):
        put(at, jnp.dot(narrow, w[...], preferred_element_type=jnp.float32))
        at += w.shape[1] // LANES
    put(at, jnp.broadcast_to(squares, (slots, LANES)))
    put(at + 1, jnp.zeros((slots, (total - at - 1) * LANES), jnp.float32))

    sums = jnp.dot(narrow[:, :skip], first[...], preferred_element_type=jnp.float32)
    for (start, size), group in zip(ranges, copies):
        for copy in group:
            copy.wait()
        sums = sums + jnp.dot(
            narrow[:, start : start + size],
            wq[start - skip : start - skip + size, :],
            preferred_element_type=jnp.float32,
        )

    put(0, sums)


def project(rows, other, w_query, first, key_weight, value_weight, slots):
    bits = slots.bit_length() - 1
    depth, query_width = w_query.shape
    kv_width = key_weight.shape[1]
    used = (query_width + 2 * kv_width) // LANES + 1
    total = -(-used // 8) * 8
    skip = first.shape[0]
    piece = jax.ShapeDtypeStruct((slots // FAN, total, LANES), jnp.float32)
    hbm = pl.BlockSpec(memory_space=pltpu.HBM)
    whole = pl.BlockSpec(memory_space=pltpu.VMEM)
    return pl.pallas_call(
        functools.partial(project_kernel, bits),
        out_shape=(piece,) * FAN,
        in_specs=[whole, whole, hbm, whole, whole, whole],
        out_specs=(whole,) * FAN,
        scratch_shapes=[
            pltpu.VMEM((max(depth - skip, 16), query_width), jnp.bfloat16),
            pltpu.VMEM((slots, depth), jnp.float32),
            pltpu.SemaphoreType.DMA((max(1, len(spread(depth, skip, CHUNK))), PIECES)),
        ],
        compiler_params=pltpu.CompilerParams(vmem_limit_bytes=46 * MIB),
        cost_estimate=pl.CostEstimate(
            flops=2 * slots * depth * (query_width + 2 * kv_width),
            bytes_accessed=2 * depth * (query_width + 2 * kv_width),
            transcendentals=0,
        ),
        name="project",
    )(rows, other, in_hbm(w_query), first, key_weight, value_weight)


def attend_kernel(
    query_heads, kv_heads, pieces, beside_ref, turn_ref, live_ref, k_ref, v_ref, *refs
):
    heads_ref = refs[pieces]
    total = refs[0][0]
    for ref in refs[1:pieces]:
        total = total + ref[0]
    at = query_heads + 2 * kv_heads
    scale = lax.rsqrt(total[at : at + 1, :] / MODEL_WIDTH + 1e-05)
    turned = total[: query_heads + kv_heads] * scale
    half = HEAD_SIZE // 2
    swapped = jnp.concatenate([turned[:, half:], turned[:, :half]], axis=1)
    turned = (turned * turn_ref[0:1, :] + swapped * turn_ref[1:2, :]).astype(jnp.bfloat16)
    fresh_values = (total[query_heads + kv_heads : at] * scale).astype(jnp.bfloat16)
    group = query_heads // kv_heads
    factor = 1.0 / math.sqrt(HEAD_SIZE)
    side = 2 if kv_heads % 2 == 0 else 1
    for first in range(0, kv_heads, side):
        members = range(first, first + side)
        queries = [turned[head * group : (head + 1) * group] for head in members]
        empty = jnp.zeros((group, HEAD_SIZE), jnp.bfloat16)
        spread_out = jnp.concatenate(
            [
                jnp.concatenate([q if i == j else empty for j in range(side)], axis=1)
                for i, q in enumerate(queries)
            ],
            axis=0,
        )
        keys = jnp.concatenate([k_ref[0, head] for head in members], axis=1)
        values = jnp.concatenate([v_ref[0, head] for head in members], axis=1)
        scores = (
            lax.dot_general(
                spread_out, keys, (((1,), (1,)), ((), ())), preferred_element_type=jnp.float32
            )
            * factor
            + live_ref[...]
        )
        own = jnp.concatenate(
            [
                jnp.sum(
                    q.astype(jnp.float32)
                    * turned[query_heads + head : query_heads + head + 1].astype(jnp.float32),
                    axis=1,
                    keepdims=True,
                )
                for q, head in zip(queries, members)
            ],
            axis=0,
        ) * factor
        top = jnp.maximum(jnp.max(scores, axis=1, keepdims=True), own)
        exponent = jnp.exp(scores - top)
        own_exp = jnp.exp(own - top)
        mixed = jnp.dot(
            exponent.astype(jnp.bfloat16), values, preferred_element_type=jnp.float32
        )
        share = 1.0 / (jnp.sum(exponent, axis=1, keepdims=True) + own_exp)
        for i, head in enumerate(members):
            part = slice(i * group, (i + 1) * group)
            block = mixed[part, i * HEAD_SIZE : (i + 1) * HEAD_SIZE]
            block = block + own_exp[part] * fresh_values[head : head + 1].astype(jnp.float32)
            block = block * share[part]
            heads_ref[0, pl.ds(head * group, group), :] = block.astype(jnp.bfloat16)


def attend(parts, turn, live, k_cache, value_cache, query_heads, beside):
    kv_heads, cache_len = k_cache.shape[1:3]
    whole = pl.BlockSpec(memory_space=pltpu.VMEM)
    return pl.pallas_call(
        functools.partial(attend_kernel, query_heads, kv_heads, len(parts)),
        out_shape=jax.ShapeDtypeStruct((1, query_heads, HEAD_SIZE), jnp.bfloat16),
        in_specs=[pl.BlockSpec(memory_space=pltpu.HBM)] + [whole] * (4 + len(parts)),
        out_specs=whole,
        compiler_params=pltpu.CompilerParams(vmem_limit_bytes=12 * MIB),
        cost_estimate=pl.CostEstimate(
            flops=4 * query_heads * cache_len * HEAD_SIZE,
            bytes_accessed=4 * kv_heads * cache_len * HEAD_SIZE,
            transcendentals=query_heads * cache_len,
        ),
        name="attend",
    )(in_hbm(beside), turn, live, k_cache, value_cache, *parts)


def output_kernel(bits, places, turned, *refs):
    pieces = len(places)
    parts = refs[:pieces]
    w_ref, mine_ref, theirs_ref, flat, left = refs[pieces:]
    slots = left.shape[0]
    heads = flat.shape[0] // slots
    here = lax.axis_index("gx")
    for slot, ref in zip(places, parts):
        for i, row in enumerate(range(ref.shape[0])[::turned]):
            at = pl.multiple_of((here ^ bit_reverse(slot + i, bits)) * heads, heads)
            flat[pl.ds(at, heads), :] = ref[row].astype(jnp.float32)
    for head in range(heads):
        left[:, head * HEAD_SIZE : (head + 1) * HEAD_SIZE] = flat[
            pl.ds(head, slots, stride=heads), :
        ].astype(jnp.bfloat16)
    total = jnp.dot(left[...], w_ref[...], preferred_element_type=jnp.float32)
    half = slots // 2
    gy = lax.axis_index("gy")
    lower, upper = total[:half], total[half:]
    mine_ref[...] = jnp.where(gy == 0, lower, upper)
    theirs_ref[...] = jnp.where(gy == 0, upper, lower)


def output(parts, order, w_out, slots, turned=1):
    bits = slots.bit_length() - 1
    depth, width = w_out.shape
    heads = depth // HEAD_SIZE
    starts = [sum(x.shape[0] for x in parts[:i]) for i in range(len(parts))]
    places = tuple(starts[i] for i in order)
    parts = [parts[i] for i in order]
    whole = pl.BlockSpec(memory_space=pltpu.VMEM)
    piece = jax.ShapeDtypeStruct((slots // 2, width), jnp.float32)
    return pl.pallas_call(
        functools.partial(output_kernel, bits, places, turned),
        out_shape=(piece, piece),
        in_specs=[whole] * (len(parts) + 1),
        out_specs=(whole, whole),
        scratch_shapes=[
            pltpu.VMEM((slots * heads, HEAD_SIZE), jnp.float32),
            pltpu.VMEM((slots, depth), jnp.bfloat16),
        ],
        compiler_params=pltpu.CompilerParams(vmem_limit_bytes=12 * MIB),
        cost_estimate=pl.CostEstimate(
            flops=2 * slots * depth * width, bytes_accessed=2 * depth * width, transcendentals=0
        ),
        name="output",
    )(*parts, w_out)


def swap(block, axis, devices, mask):
    return lax.ppermute(block, axis, [(i, i ^ mask) for i in range(devices)])


def cross(block, devices, mask):
    pairs = [(i, i ^ (2 * mask + 1)) for i in range(2 * devices)]
    return lax.ppermute(block, ("gx", "gy"), pairs)


def fan(pieces, trade):
    masks = [bit_reverse(q, 2) for q in range(FAN)]
    arrived = [None] * FAN
    for q in sorted(range(1, FAN), key=lambda q: -masks[q]):
        arrived[q] = trade(pieces[q], masks[q])
    return arrived[1:]


def body(devices, activations, w_query, key_weight, value_weight, w_out, k_cache, value_cache, lengths):
    slots = devices
    query_heads = w_query.shape[1] // HEAD_SIZE
    other = swap(activations, "gy", 2, 1)
    depth = w_query.shape[0]
    first = stage_rows(w_query, min(FIRST, depth))
    pieces = project(activations, other, w_query, first, key_weight, value_weight, slots)
    half = HEAD_SIZE // 2
    frequency = jnp.power(
        jnp.float32(500000.0), -2.0 * jnp.arange(half, dtype=jnp.float32) / HEAD_SIZE
    )
    frequency = jnp.concatenate([frequency, frequency])[None, :]

    if devices == 2 * FAN:
        far = FAN
        arrived = fan(pieces, lambda block, mask: cross(block, devices, mask))
        beside = swap(pieces[0], "gy", 2, 1)
        turn, live = turning(lengths, frequency, w_out, w_query, pieces[3], k_cache.shape[2])
        leaving = [x[1:] for x in (*arrived, beside)]
        staying = [x[:1] for x in (*arrived, beside)]
        total = leaving[2] + (leaving[0] + (leaving[1] + leaving[3]))
        total, turn = lax.optimization_barrier((total, turn))
        crossed = cross(total, devices, far)
        beside = swap(staying[2] + (staying[0] + (staying[1] + staying[3])), "gy", 2, 1)
        parts = [crossed, beside]
        heads = attend(parts, turn, live, k_cache, value_cache, query_heads, w_out)
        crossed = cross(heads, devices, far)
        beside = swap(heads, "gy", 2, 1)
        held = jnp.concatenate([crossed, beside], axis=0)
        arrived = fan([held] * FAN, lambda block, mask: cross(block, devices, mask))
        parts = [heads, swap(crossed, "gy", 2, 1)] + arrived
        order, turned = (3, 4, 2, 1, 0), -1
    else:
        arrived = fan(pieces, lambda block, mask: swap(block, "gx", devices, mask))
        turn, live = turning(lengths, frequency, w_out, w_query, pieces[3], k_cache.shape[2])
        total = pieces[0] + (arrived[2] + (arrived[1] + arrived[0]))
        mask = FAN
        while total.shape[0] > 2:
            rest = total.shape[0] // 2
            total = total[:rest] + swap(total[rest:], "gx", devices, mask)
            mask *= 2
        parts = [total[:1], swap(total[1:], "gx", devices, mask)]
        heads = attend(parts, turn, live, k_cache, value_cache, query_heads, w_out)

        parts = [heads, swap(heads, "gx", devices, mask)]
        while mask > FAN:
            mask //= 2
            parts.append(swap(jnp.concatenate(parts, axis=0), "gx", devices, mask))
        held = jnp.concatenate(parts, axis=0)
        parts += fan([held] * FAN, lambda block, mask: swap(block, "gx", devices, mask))
        order, turned = range(len(parts))[::-1], 1
    mine, theirs = output(parts, order, w_out, slots, turned)
    return (mine + swap(theirs, "gy", 2, 1)).astype(jnp.bfloat16)


def solution(mesh):
    placed = (
        P(("groups", "gy"), "gx"),
        P("gx", "gy"),
        P("gx", "gy"),
        P("gx", "gy"),
        P("gy", "gx"),
        P(("groups", "gx"), "gy", None, None),
        P(("groups", "gx"), "gy", None, None),
        P(("groups", "gx")),
    )
    return jax.shard_map(
        functools.partial(body, mesh.shape["gx"]),
        mesh=mesh,
        in_specs=placed,
        out_specs=P(("groups", "gy"), "gx"),
        check_vma=False,
    )
```

```python
import functools
import math

import jax
import jax.numpy as jnp
from jax import lax
from jax.experimental import pallas as pl
from jax.experimental.pallas import tpu as pltpu
from jax.sharding import PartitionSpec as P

MODEL_WIDTH = 16384
LANES = 128
HEAD_SIZE = 128
CHUNK = 256
FIRST = 512
PIECES = 1
FAN = 4
MIB = 2**20


def bit_reverse(value, bits):
    turned = 0
    for bit in range(bits):
        turned = turned | (((value >> bit) & 1) << (bits - 1 - bit))
    return turned


def in_hbm(array):
    return pltpu.with_memory_space_constraint(array, pltpu.HBM)


def cut(start, size):
    if size % (16 * PIECES):
        return [(start, size)]
    return [(start + i * (size // PIECES), size // PIECES) for i in range(PIECES)]


def copies_in(src, dst, sems, start, size, offset):
    return [
        pltpu.make_async_copy(
            src.at[pl.ds(at, rows)], dst.at[pl.ds(at - start + offset, rows)], sems.at[i]
        )
        for i, (at, rows) in enumerate(cut(start, size))
    ]


def stage_kernel(rows, src, dst, sems):
    copies = copies_in(src, dst, sems, 0, rows, 0)
    for copy in copies:
        copy.start()
    for copy in copies:
        copy.wait()


def stage_rows(array, rows):
    vmem = pl.BlockSpec(memory_space=pltpu.VMEM)
    return pl.pallas_call(
        functools.partial(stage_kernel, rows),
        out_shape=jax.ShapeDtypeStruct((rows, array.shape[1]), array.dtype),
        in_specs=[pl.BlockSpec(memory_space=pltpu.HBM)],
        out_specs=vmem,
        scratch_shapes=[pltpu.SemaphoreType.DMA((PIECES,))],
        compiler_params=pltpu.CompilerParams(vmem_limit_bytes=16 * MIB),
        cost_estimate=pl.CostEstimate(
            flops=0, bytes_accessed=2 * rows * array.shape[1], transcendentals=0
        ),
        name="stage",
    )(in_hbm(array))


def turning_kernel(
    length_ref, frequency_ref, beside_ref, more_ref, after_ref, turn_ref, mask_ref
):
    position = length_ref[0].astype(jnp.float32)
    angle = position * frequency_ref[...]
    lane = lax.broadcasted_iota(jnp.int32, angle.shape, 1)
    sine = jnp.sin(angle)
    turn_ref[0:1, :] = jnp.cos(angle)
    turn_ref[1:2, :] = jnp.where(lane < HEAD_SIZE // 2, -sine, sine)
    slot = lax.broadcasted_iota(jnp.int32, mask_ref.shape, 1)
    mask_ref[...] = jnp.where(slot < length_ref[0], 0.0, -jnp.inf)


def turning(lengths, frequency, beside, more, after, cache_len):
    vmem = pl.BlockSpec(memory_space=pltpu.VMEM)
    return pl.pallas_call(
        turning_kernel,
        out_shape=(
            jax.ShapeDtypeStruct((8, HEAD_SIZE), jnp.float32),
            jax.ShapeDtypeStruct((1, cache_len), jnp.float32),
        ),
        in_specs=[
            pl.BlockSpec(memory_space=pltpu.SMEM),
            vmem,
            pl.BlockSpec(memory_space=pltpu.HBM),
            pl.BlockSpec(memory_space=pltpu.HBM),
            vmem,
        ],
        out_specs=(vmem, vmem),
        compiler_params=pltpu.CompilerParams(vmem_limit_bytes=2 * MIB),
        cost_estimate=pl.CostEstimate(flops=0, bytes_accessed=2 * beside.size, transcendentals=256),
        name="turning",
    )(lengths, frequency, in_hbm(beside), in_hbm(more), after)


def spread(depth, skip, chunk):
    ranges = [(at, min(chunk, depth - at)) for at in range(skip, depth, chunk)]
    if ranges and ranges[-1][1] >= 2 * LANES:
        start, size = ranges.pop()
        ranges += [(start, size - LANES), (start + size - LANES, LANES)]
    return ranges


def project_kernel(
    bits, rows_ref, other_ref, wq_hbm, first, wk, wv, *refs
):
    pieces, (wq, rows, sems) = refs[:FAN], refs[FAN:]
    skip = first.shape[0]
    ranges = spread(wq_hbm.shape[0], skip, CHUNK)
    copies = [
        copies_in(wq_hbm, wq, sems.at[i], start, size, start - skip)
        for i, (start, size) in enumerate(ranges)
    ]
    for group in copies:
        for copy in group:
            copy.start()

    slots = rows.shape[0]
    half = slots // 2
    turn = bit_reverse(lax.axis_index("gx"), bits)
    gy = lax.axis_index("gy")
    for ref, side in ((rows_ref, gy), (other_ref, 1 - gy)):
        block = ref[...].astype(jnp.float32)
        for t in range(half):
            slot = bit_reverse(t, bits) ^ turn ^ side
            rows[pl.ds(slot, 1), :] = block[t : t + 1, :]
    wide = rows[...]
    squares = jnp.sum(wide * wide, axis=1, keepdims=True)
    narrow = wide.astype(jnp.bfloat16)

    total = pieces[0].shape[1]
    each = slots // FAN
    flats = [ref.reshape(each * total, LANES) for ref in pieces]

    def put(first_block, part):
        for i in range(0, part.shape[1], LANES):
            for at, flat in enumerate(flats):
                flat[pl.ds(first_block + i // LANES, each, stride=total), :] = part[
                    at * each : (at + 1) * each, i : i + LANES
                ]

    at = wq.shape[1] // LANES
    for w in (wk, wv):
        put(at, jnp.dot(narrow, w[...], preferred_element_type=jnp.float32))
        at += w.shape[1] // LANES
    put(at, jnp.broadcast_to(squares, (slots, LANES)))
    put(at + 1, jnp.zeros((slots, (total - at - 1) * LANES), jnp.float32))

    sums = jnp.dot(narrow[:, :skip], first[...], preferred_element_type=jnp.float32)
    for (start, size), group in zip(ranges, copies):
        for copy in group:
            copy.wait()
        sums = sums + jnp.dot(
            narrow[:, start : start + size],
            wq[start - skip : start - skip + size, :],
            preferred_element_type=jnp.float32,
        )

    put(0, sums)


def project(rows, other, w_query, first, key_weight, value_weight, slots):
    bits = slots.bit_length() - 1
    depth, query_width = w_query.shape
    kv_width = key_weight.shape[1]
    used = (query_width + 2 * kv_width) // LANES + 1
    total = -(-used // 8) * 8
    skip = first.shape[0]
    piece = jax.ShapeDtypeStruct((slots // FAN, total, LANES), jnp.float32)
    hbm = pl.BlockSpec(memory_space=pltpu.HBM)
    whole = pl.BlockSpec(memory_space=pltpu.VMEM)
    return pl.pallas_call(
        functools.partial(project_kernel, bits),
        out_shape=(piece,) * FAN,
        in_specs=[whole, whole, hbm, whole, whole, whole],
        out_specs=(whole,) * FAN,
        scratch_shapes=[
            pltpu.VMEM((max(depth - skip, 16), query_width), jnp.bfloat16),
            pltpu.VMEM((slots, depth), jnp.float32),
            pltpu.SemaphoreType.DMA((max(1, len(spread(depth, skip, CHUNK))), PIECES)),
        ],
        compiler_params=pltpu.CompilerParams(vmem_limit_bytes=46 * MIB),
        cost_estimate=pl.CostEstimate(
            flops=2 * slots * depth * (query_width + 2 * kv_width),
            bytes_accessed=2 * depth * (query_width + 2 * kv_width),
            transcendentals=0,
        ),
        name="project",
    )(rows, other, in_hbm(w_query), first, key_weight, value_weight)


def attend_kernel(
    query_heads, kv_heads, pieces, beside_ref, turn_ref, live_ref, k_ref, v_ref, *refs
):
    heads_ref = refs[pieces]
    total = refs[0][0]
    for ref in refs[1:pieces]:
        total = total + ref[0]
    at = query_heads + 2 * kv_heads
    scale = lax.rsqrt(total[at : at + 1, :] / MODEL_WIDTH + 1e-05)
    turned = total[: query_heads + kv_heads] * scale
    half = HEAD_SIZE // 2
    swapped = jnp.concatenate([turned[:, half:], turned[:, :half]], axis=1)
    turned = (turned * turn_ref[0:1, :] + swapped * turn_ref[1:2, :]).astype(jnp.bfloat16)
    fresh_values = (total[query_heads + kv_heads : at] * scale).astype(jnp.bfloat16)
    group = query_heads // kv_heads
    factor = 1.0 / math.sqrt(HEAD_SIZE)
    side = 2 if kv_heads % 2 == 0 else 1
    for first in range(0, kv_heads, side):
        members = range(first, first + side)
        queries = [turned[head * group : (head + 1) * group] for head in members]
        empty = jnp.zeros((group, HEAD_SIZE), jnp.bfloat16)
        spread_out = jnp.concatenate(
            [
                jnp.concatenate([q if i == j else empty for j in range(side)], axis=1)
                for i, q in enumerate(queries)
            ],
            axis=0,
        )
        keys = jnp.concatenate([k_ref[0, head] for head in members], axis=1)
        values = jnp.concatenate([v_ref[0, head] for head in members], axis=1)
        scores = (
            lax.dot_general(
                spread_out, keys, (((1,), (1,)), ((), ())), preferred_element_type=jnp.float32
            )
            * factor
            + live_ref[...]
        )
        own = jnp.concatenate(
            [
                jnp.sum(
                    q.astype(jnp.float32)
                    * turned[query_heads + head : query_heads + head + 1].astype(jnp.float32),
                    axis=1,
                    keepdims=True,
                )
                for q, head in zip(queries, members)
            ],
            axis=0,
        ) * factor
        top = jnp.maximum(jnp.max(scores, axis=1, keepdims=True), own)
        exponent = jnp.exp(scores - top)
        own_exp = jnp.exp(own - top)
        mixed = jnp.dot(
            exponent.astype(jnp.bfloat16), values, preferred_element_type=jnp.float32
        )
        share = 1.0 / (jnp.sum(exponent, axis=1, keepdims=True) + own_exp)
        for i, head in enumerate(members):
            part = slice(i * group, (i + 1) * group)
            block = mixed[part, i * HEAD_SIZE : (i + 1) * HEAD_SIZE]
            block = block + own_exp[part] * fresh_values[head : head + 1].astype(jnp.float32)
            block = block * share[part]
            heads_ref[0, pl.ds(head * group, group), :] = block.astype(jnp.bfloat16)


def attend(parts, turn, live, k_cache, value_cache, query_heads, beside):
    kv_heads, cache_len = k_cache.shape[1:3]
    whole = pl.BlockSpec(memory_space=pltpu.VMEM)
    return pl.pallas_call(
        functools.partial(attend_kernel, query_heads, kv_heads, len(parts)),
        out_shape=jax.ShapeDtypeStruct((1, query_heads, HEAD_SIZE), jnp.bfloat16),
        in_specs=[pl.BlockSpec(memory_space=pltpu.HBM)] + [whole] * (4 + len(parts)),
        out_specs=whole,
        compiler_params=pltpu.CompilerParams(vmem_limit_bytes=12 * MIB),
        cost_estimate=pl.CostEstimate(
            flops=4 * query_heads * cache_len * HEAD_SIZE,
            bytes_accessed=4 * kv_heads * cache_len * HEAD_SIZE,
            transcendentals=query_heads * cache_len,
        ),
        name="attend",
    )(in_hbm(beside), turn, live, k_cache, value_cache, *parts)


def output_kernel(bits, places, turned, *refs):
    pieces = len(places)
    parts = refs[:pieces]
    w_ref, mine_ref, theirs_ref, flat, left = refs[pieces:]
    slots = left.shape[0]
    heads = flat.shape[0] // slots
    here = lax.axis_index("gx")
    for slot, ref in zip(places, parts):
        for i, row in enumerate(range(ref.shape[0])[::turned]):
            at = pl.multiple_of((here ^ bit_reverse(slot + i, bits)) * heads, heads)
            flat[pl.ds(at, heads), :] = ref[row].astype(jnp.float32)
    for head in range(heads):
        left[:, head * HEAD_SIZE : (head + 1) * HEAD_SIZE] = flat[
            pl.ds(head, slots, stride=heads), :
        ].astype(jnp.bfloat16)
    total = jnp.dot(left[...], w_ref[...], preferred_element_type=jnp.float32)
    half = slots // 2
    gy = lax.axis_index("gy")
    lower, upper = total[:half], total[half:]
    mine_ref[...] = jnp.where(gy == 0, lower, upper)
    theirs_ref[...] = jnp.where(gy == 0, upper, lower)


def output(parts, order, w_out, slots, turned=1):
    bits = slots.bit_length() - 1
    depth, width = w_out.shape
    heads = depth // HEAD_SIZE
    starts = [sum(x.shape[0] for x in parts[:i]) for i in range(len(parts))]
    places = tuple(starts[i] for i in order)
    parts = [parts[i] for i in order]
    whole = pl.BlockSpec(memory_space=pltpu.VMEM)
    piece = jax.ShapeDtypeStruct((slots // 2, width), jnp.float32)
    return pl.pallas_call(
        functools.partial(output_kernel, bits, places, turned),
        out_shape=(piece, piece),
        in_specs=[whole] * (len(parts) + 1),
        out_specs=(whole, whole),
        scratch_shapes=[
            pltpu.VMEM((slots * heads, HEAD_SIZE), jnp.float32),
            pltpu.VMEM((slots, depth), jnp.bfloat16),
        ],
        compiler_params=pltpu.CompilerParams(vmem_limit_bytes=12 * MIB),
        cost_estimate=pl.CostEstimate(
            flops=2 * slots * depth * width, bytes_accessed=2 * depth * width, transcendentals=0
        ),
        name="output",
    )(*parts, w_out)


def swap(block, axis, devices, mask):
    return lax.ppermute(block, axis, [(i, i ^ mask) for i in range(devices)])


def cross(block, devices, mask):
    pairs = [(i, i ^ (2 * mask + 1)) for i in range(2 * devices)]
    return lax.ppermute(block, ("gx", "gy"), pairs)


def fan(pieces, trade):
    masks = [bit_reverse(q, 2) for q in range(FAN)]
    arrived = [None] * FAN
    for q in sorted(range(1, FAN), key=lambda q: -masks[q]):
        arrived[q] = trade(pieces[q], masks[q])
    return arrived[1:]


def body(devices, activations, w_query, key_weight, value_weight, w_out, k_cache, value_cache, lengths):
    slots = devices
    query_heads = w_query.shape[1] // HEAD_SIZE
    other = swap(activations, "gy", 2, 1)
    depth = w_query.shape[0]
    first = stage_rows(w_query, min(FIRST, depth))
    pieces = project(activations, other, w_query, first, key_weight, value_weight, slots)
    half = HEAD_SIZE // 2
    frequency = jnp.power(
        jnp.float32(500000.0), -2.0 * jnp.arange(half, dtype=jnp.float32) / HEAD_SIZE
    )
    frequency = jnp.concatenate([frequency, frequency])[None, :]

    if devices == 2 * FAN:
        far = FAN
        arrived = fan(pieces, lambda block, mask: cross(block, devices, mask))
        beside = swap(pieces[0], "gy", 2, 1)
        turn, live = turning(lengths, frequency, w_out, w_query, pieces[3], k_cache.shape[2])
        leaving = [x[1:] for x in (*arrived, beside)]
        staying = [x[:1] for x in (*arrived, beside)]
        total = leaving[2] + (leaving[0] + (leaving[1] + leaving[3]))
        total, turn = lax.optimization_barrier((total, turn))
        crossed = cross(total, devices, far)
        beside = swap(staying[2] + (staying[0] + (staying[1] + staying[3])), "gy", 2, 1)
        parts = [crossed, beside]
        heads = attend(parts, turn, live, k_cache, value_cache, query_heads, w_out)
        crossed = cross(heads, devices, far)
        beside = swap(heads, "gy", 2, 1)
        held = jnp.concatenate([crossed, beside], axis=0)
        arrived = fan([held] * FAN, lambda block, mask: cross(block, devices, mask))
        parts = [heads, swap(crossed, "gy", 2, 1)] + arrived
        order, turned = (3, 4, 2, 1, 0), -1
    else:
        arrived = fan(pieces, lambda block, mask: swap(block, "gx", devices, mask))
        turn, live = turning(lengths, frequency, w_out, w_query, pieces[3], k_cache.shape[2])
        total = pieces[0] + (arrived[2] + (arrived[1] + arrived[0]))
        mask = FAN
        while total.shape[0] > 2:
            rest = total.shape[0] // 2
            total = total[:rest] + swap(total[rest:], "gx", devices, mask)
            mask *= 2
        parts = [total[:1], swap(total[1:], "gx", devices, mask)]
        heads = attend(parts, turn, live, k_cache, value_cache, query_heads, w_out)

        parts = [heads, swap(heads, "gx", devices, mask)]
        while mask > FAN:
            mask //= 2
            parts.append(swap(jnp.concatenate(parts, axis=0), "gx", devices, mask))
        held = jnp.concatenate(parts, axis=0)
        parts += fan([held] * FAN, lambda block, mask: swap(block, "gx", devices, mask))
        order, turned = range(len(parts))[::-1], 1
    mine, theirs = output(parts, order, w_out, slots, turned)
    return (mine + swap(theirs, "gy", 2, 1)).astype(jnp.bfloat16)


def solution(mesh):
    placed = (
        P(("groups", "gy"), "gx"),
        P("gx", "gy"),
        P("gx", "gy"),
        P("gx", "gy"),
        P("gy", "gx"),
        P(("groups", "gx"), "gy", None, None),
        P(("groups", "gx"), "gy", None, None),
        P(("groups", "gx")),
    )
    return jax.shard_map(
        functools.partial(body, mesh.shape["gx"]),
        mesh=mesh,
        in_specs=placed,
        out_specs=P(("groups", "gy"), "gx"),
        check_vma=False,
    )
```

```python
import functools
import math

import jax
import jax.numpy as jnp
from jax import lax
from jax.experimental import pallas as pl
from jax.experimental.pallas import tpu as pltpu
from jax.sharding import PartitionSpec as P

MODEL_WIDTH = 16384
LANES = 128
HEAD_SIZE = 128
CHUNK = 256
FIRST = 512
PIECES = 1
FAN = 4
MIB = 2**20


def bit_reverse(value, bits):
    turned = 0
    for bit in range(bits):
        turned = turned | (((value >> bit) & 1) << (bits - 1 - bit))
    return turned


def in_hbm(array):
    return pltpu.with_memory_space_constraint(array, pltpu.HBM)


def cut(start, size):
    if size % (16 * PIECES):
        return [(start, size)]
    return [(start + i * (size // PIECES), size // PIECES) for i in range(PIECES)]


def copies_in(src, dst, sems, start, size, offset):
    return [
        pltpu.make_async_copy(
            src.at[pl.ds(at, rows)], dst.at[pl.ds(at - start + offset, rows)], sems.at[i]
        )
        for i, (at, rows) in enumerate(cut(start, size))
    ]


def stage_kernel(rows, src, dst, sems):
    copies = copies_in(src, dst, sems, 0, rows, 0)
    for copy in copies:
        copy.start()
    for copy in copies:
        copy.wait()


def stage_rows(array, rows):
    vmem = pl.BlockSpec(memory_space=pltpu.VMEM)
    return pl.pallas_call(
        functools.partial(stage_kernel, rows),
        out_shape=jax.ShapeDtypeStruct((rows, array.shape[1]), array.dtype),
        in_specs=[pl.BlockSpec(memory_space=pltpu.HBM)],
        out_specs=vmem,
        scratch_shapes=[pltpu.SemaphoreType.DMA((PIECES,))],
        compiler_params=pltpu.CompilerParams(vmem_limit_bytes=16 * MIB),
        cost_estimate=pl.CostEstimate(
            flops=0, bytes_accessed=2 * rows * array.shape[1], transcendentals=0
        ),
        name="stage",
    )(in_hbm(array))


def turning_kernel(
    length_ref, frequency_ref, beside_ref, more_ref, after_ref, turn_ref, mask_ref
):
    position = length_ref[0].astype(jnp.float32)
    angle = position * frequency_ref[...]
    lane = lax.broadcasted_iota(jnp.int32, angle.shape, 1)
    sine = jnp.sin(angle)
    turn_ref[0:1, :] = jnp.cos(angle)
    turn_ref[1:2, :] = jnp.where(lane < HEAD_SIZE // 2, -sine, sine)
    slot = lax.broadcasted_iota(jnp.int32, mask_ref.shape, 1)
    mask_ref[...] = jnp.where(slot < length_ref[0], 0.0, -jnp.inf)


def turning(lengths, frequency, beside, more, after, cache_len):
    vmem = pl.BlockSpec(memory_space=pltpu.VMEM)
    return pl.pallas_call(
        turning_kernel,
        out_shape=(
            jax.ShapeDtypeStruct((8, HEAD_SIZE), jnp.float32),
            jax.ShapeDtypeStruct((1, cache_len), jnp.float32),
        ),
        in_specs=[
            pl.BlockSpec(memory_space=pltpu.SMEM),
            vmem,
            pl.BlockSpec(memory_space=pltpu.HBM),
            pl.BlockSpec(memory_space=pltpu.HBM),
            vmem,
        ],
        out_specs=(vmem, vmem),
        compiler_params=pltpu.CompilerParams(vmem_limit_bytes=2 * MIB),
        cost_estimate=pl.CostEstimate(flops=0, bytes_accessed=2 * beside.size, transcendentals=256),
        name="turning",
    )(lengths, frequency, in_hbm(beside), in_hbm(more), after)


def spread(depth, skip, chunk):
    ranges = [(at, min(chunk, depth - at)) for at in range(skip, depth, chunk)]
    if ranges and ranges[-1][1] >= 2 * LANES:
        start, size = ranges.pop()
        ranges += [(start, size - LANES), (start + size - LANES, LANES)]
    return ranges


def project_kernel(
    bits, rows_ref, other_ref, wq_hbm, first, wk, wv, *refs
):
    pieces, (wq, rows, sems) = refs[:FAN], refs[FAN:]
    skip = first.shape[0]
    ranges = spread(wq_hbm.shape[0], skip, CHUNK)
    copies = [
        copies_in(wq_hbm, wq, sems.at[i], start, size, start - skip)
        for i, (start, size) in enumerate(ranges)
    ]
    for group in copies:
        for copy in group:
            copy.start()

    slots = rows.shape[0]
    half = slots // 2
    turn = bit_reverse(lax.axis_index("gx"), bits)
    gy = lax.axis_index("gy")
    for ref, side in ((rows_ref, gy), (other_ref, 1 - gy)):
        block = ref[...].astype(jnp.float32)
        for t in range(half):
            slot = bit_reverse(t, bits) ^ turn ^ side
            rows[pl.ds(slot, 1), :] = block[t : t + 1, :]
    wide = rows[...]
    squares = jnp.sum(wide * wide, axis=1, keepdims=True)
    narrow = wide.astype(jnp.bfloat16)

    total = pieces[0].shape[1]
    each = slots // FAN
    flats = [ref.reshape(each * total, LANES) for ref in pieces]

    def put(first_block, part):
        for i in range(0, part.shape[1], LANES):
            for at, flat in enumerate(flats):
                flat[pl.ds(first_block + i // LANES, each, stride=total), :] = part[
                    at * each : (at + 1) * each, i : i + LANES
                ]

    at = wq.shape[1] // LANES
    for w in (wk, wv):
        put(at, jnp.dot(narrow, w[...], preferred_element_type=jnp.float32))
        at += w.shape[1] // LANES
    put(at, jnp.broadcast_to(squares, (slots, LANES)))
    put(at + 1, jnp.zeros((slots, (total - at - 1) * LANES), jnp.float32))

    sums = jnp.dot(narrow[:, :skip], first[...], preferred_element_type=jnp.float32)
    for (start, size), group in zip(ranges, copies):
        for copy in group:
            copy.wait()
        sums = sums + jnp.dot(
            narrow[:, start : start + size],
            wq[start - skip : start - skip + size, :],
            preferred_element_type=jnp.float32,
        )

    put(0, sums)


def project(rows, other, w_query, first, key_weight, value_weight, slots):
    bits = slots.bit_length() - 1
    depth, query_width = w_query.shape
    kv_width = key_weight.shape[1]
    used = (query_width + 2 * kv_width) // LANES + 1
    total = -(-used // 8) * 8
    skip = first.shape[0]
    piece = jax.ShapeDtypeStruct((slots // FAN, total, LANES), jnp.float32)
    hbm = pl.BlockSpec(memory_space=pltpu.HBM)
    whole = pl.BlockSpec(memory_space=pltpu.VMEM)
    return pl.pallas_call(
        functools.partial(project_kernel, bits),
        out_shape=(piece,) * FAN,
        in_specs=[whole, whole, hbm, whole, whole, whole],
        out_specs=(whole,) * FAN,
        scratch_shapes=[
            pltpu.VMEM((max(depth - skip, 16), query_width), jnp.bfloat16),
            pltpu.VMEM((slots, depth), jnp.float32),
            pltpu.SemaphoreType.DMA((max(1, len(spread(depth, skip, CHUNK))), PIECES)),
        ],
        compiler_params=pltpu.CompilerParams(vmem_limit_bytes=46 * MIB),
        cost_estimate=pl.CostEstimate(
            flops=2 * slots * depth * (query_width + 2 * kv_width),
            bytes_accessed=2 * depth * (query_width + 2 * kv_width),
            transcendentals=0,
        ),
        name="project",
    )(rows, other, in_hbm(w_query), first, key_weight, value_weight)


def attend_kernel(
    query_heads, kv_heads, pieces, beside_ref, turn_ref, live_ref, k_ref, v_ref, *refs
):
    heads_ref = refs[pieces]
    total = refs[0][0]
    for ref in refs[1:pieces]:
        total = total + ref[0]
    at = query_heads + 2 * kv_heads
    scale = lax.rsqrt(total[at : at + 1, :] / MODEL_WIDTH + 1e-05)
    turned = total[: query_heads + kv_heads] * scale
    half = HEAD_SIZE // 2
    swapped = jnp.concatenate([turned[:, half:], turned[:, :half]], axis=1)
    turned = (turned * turn_ref[0:1, :] + swapped * turn_ref[1:2, :]).astype(jnp.bfloat16)
    fresh_values = (total[query_heads + kv_heads : at] * scale).astype(jnp.bfloat16)
    group = query_heads // kv_heads
    factor = 1.0 / math.sqrt(HEAD_SIZE)
    side = 2 if kv_heads % 2 == 0 else 1
    for first in range(0, kv_heads, side):
        members = range(first, first + side)
        queries = [turned[head * group : (head + 1) * group] for head in members]
        empty = jnp.zeros((group, HEAD_SIZE), jnp.bfloat16)
        spread_out = jnp.concatenate(
            [
                jnp.concatenate([q if i == j else empty for j in range(side)], axis=1)
                for i, q in enumerate(queries)
            ],
            axis=0,
        )
        keys = jnp.concatenate([k_ref[0, head] for head in members], axis=1)
        values = jnp.concatenate([v_ref[0, head] for head in members], axis=1)
        scores = (
            lax.dot_general(
                spread_out, keys, (((1,), (1,)), ((), ())), preferred_element_type=jnp.float32
            )
            * factor
            + live_ref[...]
        )
        own = jnp.concatenate(
            [
                jnp.sum(
                    q.astype(jnp.float32)
                    * turned[query_heads + head : query_heads + head + 1].astype(jnp.float32),
                    axis=1,
                    keepdims=True,
                )
                for q, head in zip(queries, members)
            ],
            axis=0,
        ) * factor
        top = jnp.maximum(jnp.max(scores, axis=1, keepdims=True), own)
        exponent = jnp.exp(scores - top)
        own_exp = jnp.exp(own - top)
        mixed = jnp.dot(
            exponent.astype(jnp.bfloat16), values, preferred_element_type=jnp.float32
        )
        share = 1.0 / (jnp.sum(exponent, axis=1, keepdims=True) + own_exp)
        for i, head in enumerate(members):
            part = slice(i * group, (i + 1) * group)
            block = mixed[part, i * HEAD_SIZE : (i + 1) * HEAD_SIZE]
            block = block + own_exp[part] * fresh_values[head : head + 1].astype(jnp.float32)
            block = block * share[part]
            heads_ref[0, pl.ds(head * group, group), :] = block.astype(jnp.bfloat16)


def attend(parts, turn, live, k_cache, value_cache, query_heads, beside):
    kv_heads, cache_len = k_cache.shape[1:3]
    whole = pl.BlockSpec(memory_space=pltpu.VMEM)
    return pl.pallas_call(
        functools.partial(attend_kernel, query_heads, kv_heads, len(parts)),
        out_shape=jax.ShapeDtypeStruct((1, query_heads, HEAD_SIZE), jnp.bfloat16),
        in_specs=[pl.BlockSpec(memory_space=pltpu.HBM)] + [whole] * (4 + len(parts)),
        out_specs=whole,
        compiler_params=pltpu.CompilerParams(vmem_limit_bytes=12 * MIB),
        cost_estimate=pl.CostEstimate(
            flops=4 * query_heads * cache_len * HEAD_SIZE,
            bytes_accessed=4 * kv_heads * cache_len * HEAD_SIZE,
            transcendentals=query_heads * cache_len,
        ),
        name="attend",
    )(in_hbm(beside), turn, live, k_cache, value_cache, *parts)


def output_kernel(bits, places, turned, *refs):
    pieces = len(places)
    parts = refs[:pieces]
    w_ref, mine_ref, theirs_ref, flat, left = refs[pieces:]
    slots = left.shape[0]
    heads = flat.shape[0] // slots
    here = lax.axis_index("gx")
    for slot, ref in zip(places, parts):
        for i, row in enumerate(range(ref.shape[0])[::turned]):
            at = pl.multiple_of((here ^ bit_reverse(slot + i, bits)) * heads, heads)
            flat[pl.ds(at, heads), :] = ref[row].astype(jnp.float32)
    for head in range(heads):
        left[:, head * HEAD_SIZE : (head + 1) * HEAD_SIZE] = flat[
            pl.ds(head, slots, stride=heads), :
        ].astype(jnp.bfloat16)
    total = jnp.dot(left[...], w_ref[...], preferred_element_type=jnp.float32)
    half = slots // 2
    gy = lax.axis_index("gy")
    lower, upper = total[:half], total[half:]
    mine_ref[...] = jnp.where(gy == 0, lower, upper)
    theirs_ref[...] = jnp.where(gy == 0, upper, lower)


def output(parts, order, w_out, slots, turned=1):
    bits = slots.bit_length() - 1
    depth, width = w_out.shape
    heads = depth // HEAD_SIZE
    starts = [sum(x.shape[0] for x in parts[:i]) for i in range(len(parts))]
    places = tuple(starts[i] for i in order)
    parts = [parts[i] for i in order]
    whole = pl.BlockSpec(memory_space=pltpu.VMEM)
    piece = jax.ShapeDtypeStruct((slots // 2, width), jnp.float32)
    return pl.pallas_call(
        functools.partial(output_kernel, bits, places, turned),
        out_shape=(piece, piece),
        in_specs=[whole] * (len(parts) + 1),
        out_specs=(whole, whole),
        scratch_shapes=[
            pltpu.VMEM((slots * heads, HEAD_SIZE), jnp.float32),
            pltpu.VMEM((slots, depth), jnp.bfloat16),
        ],
        compiler_params=pltpu.CompilerParams(vmem_limit_bytes=12 * MIB),
        cost_estimate=pl.CostEstimate(
            flops=2 * slots * depth * width, bytes_accessed=2 * depth * width, transcendentals=0
        ),
        name="output",
    )(*parts, w_out)


def swap(block, axis, devices, mask):
    return lax.ppermute(block, axis, [(i, i ^ mask) for i in range(devices)])


def cross(block, devices, mask):
    pairs = [(i, i ^ (2 * mask + 1)) for i in range(2 * devices)]
    return lax.ppermute(block, ("gx", "gy"), pairs)


def fan(pieces, trade):
    masks = [bit_reverse(q, 2) for q in range(FAN)]
    arrived = [None] * FAN
    for q in sorted(range(1, FAN), key=lambda q: -masks[q]):
        arrived[q] = trade(pieces[q], masks[q])
    return arrived[1:]


def body(devices, activations, w_query, key_weight, value_weight, w_out, k_cache, value_cache, lengths):
    slots = devices
    query_heads = w_query.shape[1] // HEAD_SIZE
    other = swap(activations, "gy", 2, 1)
    depth = w_query.shape[0]
    first = stage_rows(w_query, min(FIRST, depth))
    pieces = project(activations, other, w_query, first, key_weight, value_weight, slots)
    half = HEAD_SIZE // 2
    frequency = jnp.power(
        jnp.float32(500000.0), -2.0 * jnp.arange(half, dtype=jnp.float32) / HEAD_SIZE
    )
    frequency = jnp.concatenate([frequency, frequency])[None, :]

    if devices == 2 * FAN:
        far = FAN
        arrived = fan(pieces, lambda block, mask: cross(block, devices, mask))
        beside = swap(pieces[0], "gy", 2, 1)
        turn, live = turning(lengths, frequency, w_out, w_query, pieces[3], k_cache.shape[2])
        leaving = [x[1:] for x in (*arrived, beside)]
        staying = [x[:1] for x in (*arrived, beside)]
        total = leaving[2] + (leaving[0] + (leaving[1] + leaving[3]))
        total, turn = lax.optimization_barrier((total, turn))
        crossed = cross(total, devices, far)
        beside = swap(staying[2] + (staying[0] + (staying[1] + staying[3])), "gy", 2, 1)
        parts = [crossed, beside]
        heads = attend(parts, turn, live, k_cache, value_cache, query_heads, w_out)
        crossed = cross(heads, devices, far)
        beside = swap(heads, "gy", 2, 1)
        held = jnp.concatenate([crossed, beside], axis=0)
        arrived = fan([held] * FAN, lambda block, mask: cross(block, devices, mask))
        parts = [heads, swap(crossed, "gy", 2, 1)] + arrived
        order, turned = (2, 4, 3, 1, 0), -1
    else:
        arrived = fan(pieces, lambda block, mask: swap(block, "gx", devices, mask))
        turn, live = turning(lengths, frequency, w_out, w_query, pieces[3], k_cache.shape[2])
        total = pieces[0] + (arrived[2] + (arrived[1] + arrived[0]))
        mask = FAN
        while total.shape[0] > 2:
            rest = total.shape[0] // 2
            total = total[:rest] + swap(total[rest:], "gx", devices, mask)
            mask *= 2
        parts = [total[:1], swap(total[1:], "gx", devices, mask)]
        heads = attend(parts, turn, live, k_cache, value_cache, query_heads, w_out)

        parts = [heads, swap(heads, "gx", devices, mask)]
        while mask > FAN:
            mask //= 2
            parts.append(swap(jnp.concatenate(parts, axis=0), "gx", devices, mask))
        held = jnp.concatenate(parts, axis=0)
        parts += fan([held] * FAN, lambda block, mask: swap(block, "gx", devices, mask))
        order, turned = range(len(parts))[::-1], 1
    mine, theirs = output(parts, order, w_out, slots, turned)
    return (mine + swap(theirs, "gy", 2, 1)).astype(jnp.bfloat16)


def solution(mesh):
    placed = (
        P(("groups", "gy"), "gx"),
        P("gx", "gy"),
        P("gx", "gy"),
        P("gx", "gy"),
        P("gy", "gx"),
        P(("groups", "gx"), "gy", None, None),
        P(("groups", "gx"), "gy", None, None),
        P(("groups", "gx")),
    )
    return jax.shard_map(
        functools.partial(body, mesh.shape["gx"]),
        mesh=mesh,
        in_specs=placed,
        out_specs=P(("groups", "gy"), "gx"),
        check_vma=False,
    )
```
